32 devices in a mesh: dp: 16 (over z, x, core), seq: 2 (over y).
Axes of the slice: x: 2, y: 2, z: 4, core: 2. Of those that a mesh axis runs over, the one named last changes fastest.
Arguments:
- q_proj: bfloat16 [16, 256, 4096], P('dp', 'seq'), may hold values from -200 to 200
- k_proj: bfloat16 [16, 256, 512], P('dp', 'seq'), may hold values from -6 to 6
- v_proj: bfloat16 [16, 256, 512], P('dp', 'seq'), may hold values from -6 to 6
- cache_k: bfloat16 [16, 1024, 512], P('dp', 'seq'), may hold values from -6 to 6
- cache_v: bfloat16 [16, 1024, 512], P('dp', 'seq'), may hold values from -6 to 6
- bias_q: bfloat16 [4096], replicated, may hold values from -3 to 3
- bias_k: bfloat16 [512], replicated, may hold values from -3 to 3
- bias_v: bfloat16 [512], replicated, may hold values from -3 to 3
- start: int32 [16], P('dp'), may hold values from 256 to 1024, as said below
- dout: bfloat16 [16, 256, 4096], P('dp', 'seq'), may hold values from -6 to 6
Outputs:
- attn_out: bfloat16 [16, 256, 4096], P('dp', 'seq')
- grad_q: bfloat16 [16, 256, 4096], P('dp', 'seq')
- grad_k: bfloat16 [16, 256, 512], P('dp', 'seq')
- grad_v: bfloat16 [16, 256, 512], P('dp', 'seq')
- grad_bias_q: float32 [4096], replicated
- grad_bias_k: float32 [512], replicated
- grad_bias_v: float32 [512], replicated
The draws below stay inside these ranges and needn't reach their ends.
Inputs may be any that keep to these rules, and one draw needn't show every extreme that they name: Cache slots at and beyond start hold no prefix; some sequence has a full prefix of 1024 slots.
All inputs are finite; a program needn't handle non-finite values.
Results may differ from the reference program's by a relative error of at most 0.04.
The reference program's roundings to bfloat16 on the way count: a program that leaves them out, or rounds other values in their place, can miss the bound.
Values may be sent and summed in bfloat16 or wider, within the bound.
No kernel may reach another device: no remote copies, remote signals or barrier semaphores. Data moves between devices by JAX's collectives and lax.ppermute only.
A program may use at most 128 MiB of HBM per device.

```python
import jax
import jax.numpy as jnp
from jax import lax

HQ = 32
KV = 4
HD = 128
PREFIX = 1024
GROUP = 8
LEN = 256
SEQS = 16


def draw_q_proj(key, part):
    first_key = jax.random.fold_in(jax.random.fold_in(key, 11), 0)
    values = jax.random.normal(first_key, (SEQS, LEN, HQ * HD), jnp.float32)
    values = jnp.clip(values, -6.0, 6.0)
    return values.astype(jnp.bfloat16)


def draw_start(key, part):
    values = jax.random.randint(jax.random.fold_in(key, 23), (SEQS,), PREFIX // 4, PREFIX + 1, dtype=jnp.int32)
    return values.at[0].set(PREFIX)


def steps_of(stream_key, shape, cuts, least, largest):
    loudness = 1.0
    for dim, blocks in cuts:
        draws = jax.random.uniform(jax.random.fold_in(jax.random.fold_in(stream_key, 6), dim), (blocks,), jnp.float32, least / len(cuts), largest / len(cuts))
        loudness = loudness * jnp.repeat(jnp.exp(draws), shape[dim] // blocks).reshape((-1,) + (1,) * (len(shape) - 1 - dim))
    return loudness


def bell_draw(rng, shape, deviation, limit, cuts=(), kind=jnp.bfloat16):
    entries = deviation * jax.random.normal(rng, shape, jnp.float32)
    if cuts:
        entries = entries * steps_of(rng, shape, cuts, -0.22, 0.18)
    return jnp.clip(entries, -limit, limit).astype(kind)


def setup_inputs(seed: int = 0) -> dict:
    splits = jax.random.split(jax.random.key(seed), 11)
    q_proj = draw_q_proj(jax.random.fold_in(splits[10], 71), 0)
    k_proj = bell_draw(splits[1], (SEQS, LEN, KV * HD), 1.0, 6.0, ((0, 16), (1, 2)))
    v_proj = bell_draw(splits[2], (SEQS, LEN, KV * HD), 1.0, 6.0, ((0, 16), (1, 2)))
    cache_k = bell_draw(splits[3], (SEQS, PREFIX, KV * HD), 1.0, 6.0, ((0, 16), (1, 2)))
    cache_v = bell_draw(splits[4], (SEQS, PREFIX, KV * HD), 1.0, 6.0, ((0, 16), (1, 2)))
    bias_q = bell_draw(splits[5], (HQ * HD,), 0.5, 3.0)
    bias_k = bell_draw(splits[6], (KV * HD,), 0.5, 3.0)
    bias_v = bell_draw(splits[7], (KV * HD,), 0.5, 3.0)
    start = draw_start(jax.random.fold_in(splits[10], 71), 0)
    dout = bell_draw(splits[9], (SEQS, LEN, HQ * HD), 1.0, 6.0, ((0, 16), (1, 2)))
    return dict(q_proj=q_proj, k_proj=k_proj, v_proj=v_proj, cache_k=cache_k, cache_v=cache_v, bias_q=bias_q, bias_k=bias_k, bias_v=bias_v, start=start, dout=dout)


def rotary_tables(positions, width):
    half = width // 2
    freqs = jnp.exp(-(2.0 * jnp.arange(half, dtype=jnp.float32) / width) * jnp.log(jnp.float32(1.0e6)))
    angles = positions.astype(jnp.float32)[:, None] * freqs[None, :]
    cosine = jnp.concatenate([jnp.cos(angles), jnp.cos(angles)], axis=1)
    sine = jnp.concatenate([jnp.sin(angles), jnp.sin(angles)], axis=1)
    return cosine[:, None, :], sine[:, None, :]


def rotary(values, positions):
    cosine, sine = rotary_tables(positions, values.shape[2])
    half = values.shape[2] // 2
    turned = jnp.concatenate([-values[:, :, half:], values[:, :, :half]], axis=2)
    return values * cosine + turned * sine


def rotary_back(grads, positions):
    cosine, sine = rotary_tables(positions, grads.shape[2])
    half = grads.shape[2] // 2
    scaled = grads * sine
    turned = jnp.concatenate([scaled[:, :, half:], -scaled[:, :, :half]], axis=2)
    return grads * cosine + turned


def attend(queries, cotangent, keys, values, first, row_zero, prefix):
    rows, heads, width = queries.shape
    key_count = keys.shape[0]
    slab = key_count - prefix
    head_block = max(1, min(512 // rows, GROUP, heads))
    row_block = min(rows, 512)
    scale = width ** -0.5
    key_index = jnp.arange(key_count, dtype=jnp.int32)

    def head_step(carry, head_slot):
        key_acc, value_acc = carry
        head_zero = head_slot * head_block
        owner = head_zero // GROUP
        key_one = lax.dynamic_index_in_dim(keys, owner, 1, keepdims=False).astype(jnp.float32)
        value_one = lax.dynamic_index_in_dim(values, owner, 1, keepdims=False).astype(jnp.float32)
        query_part = lax.dynamic_slice_in_dim(queries, head_zero, head_block, 1)
        cot_part = lax.dynamic_slice_in_dim(cotangent, head_zero, head_block, 1)

        def row_step(inner, row_slot):
            grad_key, grad_value = inner
            offset = row_slot * row_block
            query_rows = lax.dynamic_slice_in_dim(query_part, offset, row_block, 0).astype(jnp.float32)
            cot_rows = lax.dynamic_slice_in_dim(cot_part, offset, row_block, 0).astype(jnp.float32)
            query_index = row_zero + offset + jnp.arange(row_block, dtype=jnp.int32)
            allowed = jnp.where(key_index[None, :] < prefix, key_index[None, :] < first,
                                (key_index[None, :] - prefix) <= query_index[:, None])
            scores = jnp.einsum('rhd,kd->hrk', query_rows, key_one) * scale
            scores = jnp.where(allowed[None], scores, -1.0e30)
            highest = jnp.max(scores, axis=-1, keepdims=True)
            expo = jnp.exp(scores - highest)
            probs = expo / jnp.sum(expo, axis=-1, keepdims=True)
            probs_b = probs.astype(jnp.bfloat16)
            output = jnp.einsum('hrk,kd->rhd', probs_b.astype(jnp.float32), value_one).astype(jnp.bfloat16)
            delta = jnp.sum(cot_rows * output.astype(jnp.float32), axis=-1).T
            dprobs = jnp.einsum('rhd,kd->hrk', cot_rows, value_one)
            dscore = (probs * (dprobs - delta[:, :, None])).astype(jnp.bfloat16)
            dscore_f = dscore.astype(jnp.float32)
            grad_query = (jnp.einsum('hrk,kd->rhd', dscore_f, key_one) * scale).astype(jnp.bfloat16)
            grad_key = grad_key + jnp.einsum('hrk,rhd->kd', dscore_f[:, :, prefix:], query_rows) * scale
            grad_value = grad_value + jnp.einsum('hrk,rhd->kd', probs_b[:, :, prefix:].astype(jnp.float32), cot_rows)
            return (grad_key, grad_value), (output, grad_query)

        empty = jnp.zeros((slab, width), jnp.float32)
        (grad_key, grad_value), (outputs, grads) = lax.scan(row_step, (empty, empty),
                                                            jnp.arange(rows // row_block, dtype=jnp.int32))
        outputs = outputs.reshape(rows, head_block, width)
        grads = grads.reshape(rows, head_block, width)
        old_key = lax.dynamic_index_in_dim(key_acc, owner, 1, keepdims=False)
        old_value = lax.dynamic_index_in_dim(value_acc, owner, 1, keepdims=False)
        key_acc = lax.dynamic_update_index_in_dim(key_acc, old_key + grad_key, owner, 1)
        value_acc = lax.dynamic_update_index_in_dim(value_acc, old_value + grad_value, owner, 1)
        return (key_acc, value_acc), (outputs, grads)

    zeros_kv = jnp.zeros((slab, keys.shape[1], width), jnp.float32)
    (key_acc, value_acc), (outputs, grads) = lax.scan(head_step, (zeros_kv, zeros_kv),
                                                      jnp.arange(heads // head_block, dtype=jnp.int32))
    outputs = jnp.transpose(outputs, (1, 0, 2, 3)).reshape(rows, heads, width)
    grads = jnp.transpose(grads, (1, 0, 2, 3)).reshape(rows, heads, width)
    return outputs, grads, key_acc, value_acc


def reference(q_proj, k_proj, v_proj, cache_k, cache_v, bias_q, bias_k, bias_v, start, dout):
    def one_sequence(items):
        query_in, key_in, value_in, cached_k, cached_v, first, cot = items
        positions = first + jnp.arange(LEN, dtype=jnp.int32)
        queries = rotary((query_in.astype(jnp.float32) + bias_q.astype(jnp.float32)).reshape(LEN, HQ, HD), positions).astype(jnp.bfloat16)
        keys = rotary((key_in.astype(jnp.float32) + bias_k.astype(jnp.float32)).reshape(LEN, KV, HD), positions).astype(jnp.bfloat16)
        values = (value_in.astype(jnp.float32) + bias_v.astype(jnp.float32)).astype(jnp.bfloat16).reshape(LEN, KV, HD)
        all_keys = jnp.concatenate([cached_k.reshape(PREFIX, KV, HD), keys], axis=0)
        all_values = jnp.concatenate([cached_v.reshape(PREFIX, KV, HD), values], axis=0)
        outputs, dq_rot, dk_rot, dv_all = attend(queries, cot.reshape(LEN, HQ, HD), all_keys, all_values, first, 0, PREFIX)
        grad_query = rotary_back(dq_rot.astype(jnp.float32), positions)
        grad_key = rotary_back(dk_rot, positions)
        return (outputs.reshape(LEN, HQ * HD), grad_query.astype(jnp.bfloat16).reshape(LEN, HQ * HD),
                grad_key.astype(jnp.bfloat16).reshape(LEN, KV * HD), dv_all.astype(jnp.bfloat16).reshape(LEN, KV * HD),
                jnp.sum(grad_query, axis=0).reshape(HQ * HD), jnp.sum(grad_key, axis=0).reshape(KV * HD),
                jnp.sum(dv_all, axis=0).reshape(KV * HD))

    results = lax.map(one_sequence, (q_proj, k_proj, v_proj, cache_k, cache_v, start, dout))
    return (results[0], results[1], results[2], results[3],
            jnp.sum(results[4], axis=0), jnp.sum(results[5], axis=0), jnp.sum(results[6], axis=0))
```

```python
import functools
import math

import jax
import jax.numpy as jnp
from jax import lax
from jax.experimental import pallas as pl
from jax.experimental.pallas import tpu as pltpu
from jax.sharding import PartitionSpec as P

HQ = 32
KV = 4
HD = 128
GROUP = 8
HEADS = 4
NEG = -1e30


def turn(x):
    return pltpu.roll(x, HD // 2, 1)


def dot(a, b, dims):
    return lax.dot_general(a, b, (dims, ((), ())), preferred_element_type=jnp.float32)


NT = ((1,), (1,))
NN = ((1,), (0,))
TN = ((0,), (0,))


def pack_kernel(groups, ck_ref, cv_ref, *rest):
    outs, sems = rest[:-1], rest[-1]
    rows = ck_ref.shape[0]
    copies = []
    for slot, (g, out) in enumerate(zip(groups, outs)):
        for half, src in enumerate((ck_ref, cv_ref)):
            copy = pltpu.make_async_copy(
                src.at[:, pl.ds(g * HD, HD)],
                out.at[pl.ds(half * rows, rows)],
                sems.at[2 * slot + half],
            )
            copy.start()
            copies.append(copy)
    for copy in copies:
        copy.wait()


def pack(groups, ck, cv):
    rows = ck.shape[0]
    any_spec = pl.BlockSpec(memory_space=pl.ANY)
    return pl.pallas_call(
        functools.partial(pack_kernel, groups),
        out_shape=[jax.ShapeDtypeStruct((2 * rows, HD), ck.dtype) for _ in groups],
        in_specs=[any_spec] * 2,
        out_specs=[any_spec] * len(groups),
        scratch_shapes=[pltpu.SemaphoreType.DMA((2 * len(groups),))],
        cost_estimate=pl.CostEstimate(
            flops=0, bytes_accessed=8 * rows * HD * len(groups), transcendentals=0
        ),
        name="pack",
    )(ck, cv)


def attend_kernel(
    shards, chained,
    at_ref, q_ref, do_ref, bq_ref, cos_ref, sin_ref,
    ck_ref, cv_ref, kp_ref, vp_ref, bk_ref, bv_ref, *rest,
):
    far, rest = rest[: 2 * (shards - 1)], rest[2 * (shards - 1):]
    rest = rest[2 if chained else 0:]
    (out_ref, gq_ref, sq_ref, dk_ref, dv_ref, send_ref, sk_ref, sv_ref,
     keys, values, dkt, dvt) = rest
    step = pl.program_id(0)
    tokens = q_ref.shape[0]
    slots = ck_ref.shape[0]
    prefix = shards * slots
    slab = shards * tokens
    first = at_ref[0]
    rank = at_ref[1]

    @pl.when(step == 0)
    def _():
        keys[pl.ds(0, slots)] = ck_ref[...]
        values[pl.ds(0, slots)] = cv_ref[...]
        for s in range(1, shards):
            keys[pl.ds(s * slots, slots)] = far[s - 1][pl.ds(0, slots)]
            values[pl.ds(s * slots, slots)] = far[s - 1][pl.ds(slots, slots)]
        for s in range(shards):
            rows = pl.ds(s * tokens, tokens)
            if s == 0:
                kp, vp = kp_ref[...], vp_ref[...]
            else:
                block = far[shards - 1 + s - 1]
                kp, vp = block[0], block[1]
            k = kp.astype(jnp.float32) + bk_ref[...].astype(jnp.float32)
            k = k * cos_ref[rows, :] + turn(k) * sin_ref[rows, :]
            v = vp.astype(jnp.float32) + bv_ref[...].astype(jnp.float32)
            place = pl.ds(prefix + s * tokens, tokens)
            keys[place] = k.astype(jnp.bfloat16)
            values[place] = v.astype(jnp.bfloat16)
        dkt[...] = jnp.zeros_like(dkt)
        dvt[...] = jnp.zeros_like(dvt)

    cosine = cos_ref[pl.ds(0, tokens), :]
    sine = sin_ref[pl.ds(0, tokens), :]
    queries = []
    cots = []
    for h in range(HEADS):
        cols = pl.ds(h * HD, HD)
        x = q_ref[:, cols].astype(jnp.float32) + bq_ref[:, cols].astype(jnp.float32)
        x = x * cosine + turn(x) * sine
        queries.append(x.astype(jnp.bfloat16))
        cots.append(do_ref[:, cols])
    q = jnp.concatenate(queries, axis=0)
    do = jnp.concatenate(cots, axis=0)
    rows = HEADS * tokens

    scale = HD ** -0.5
    s = dot(q, keys[...], NT)
    parts = []
    col = lax.broadcasted_iota(jnp.int32, (1, slots), 1)
    for j in range(shards):
        owner = lax.rem(rank - j + shards, shards)
        part = s[:, j * slots:(j + 1) * slots]
        parts.append(jnp.where(col < first - owner * slots, part, NEG))
    part = s[:, prefix:prefix + tokens]
    token = lax.broadcasted_iota(jnp.int32, (rows, tokens), 0) & (tokens - 1)
    parts.append(jnp.where(lax.broadcasted_iota(jnp.int32, (rows, tokens), 1) <= token, part, NEG))
    for j in range(1, shards):
        part = s[:, prefix + j * tokens:prefix + (j + 1) * tokens]
        parts.append(jnp.where(rank >= j, part, NEG))
    s = jnp.concatenate(parts, axis=1)
    top = jnp.max(s, axis=1, keepdims=True)
    e = jnp.exp2((s - top) * (scale * math.log2(math.e)))
    p = e * (1.0 / jnp.sum(e, axis=1, keepdims=True))
    pb = p.astype(jnp.bfloat16)
    o = dot(pb, values[...], NN).astype(jnp.bfloat16)
    delta = jnp.sum(do.astype(jnp.float32) * o.astype(jnp.float32), axis=1, keepdims=True)
    dp = dot(do, values[...], NT)
    ds = (p * (dp - delta)).astype(jnp.bfloat16)
    dq = (dot(ds, keys[...], NN) * scale).astype(jnp.bfloat16).astype(jnp.float32)
    for h in range(HEADS):
        cols = pl.ds(h * HD, HD)
        part = slice(h * tokens, (h + 1) * tokens)
        out_ref[:, cols] = o[part]
        g = dq[part]
        g = g * cosine - turn(g) * sine
        gq_ref[:, cols] = g.astype(jnp.bfloat16)
        sq_ref[:, cols] = jnp.sum(g, axis=0, keepdims=True)
    dkt[...] += dot(q, ds[:, prefix:], TN)
    dvt[...] += dot(do, pb[:, prefix:], TN)

    @pl.when(step == pl.num_programs(0) - 1)
    def _():
        dk = dkt[...].T * scale
        dv = dvt[...].T
        gk = dk * cos_ref[...] - turn(dk) * sin_ref[...]
        dk_ref[...] = dk[:tokens]
        dv_ref[...] = dv[:tokens]
        for j in range(1, shards):
            block = slice(j * tokens, (j + 1) * tokens)
            send_ref[2 * (j - 1)] = dk[block].astype(jnp.bfloat16)
            send_ref[2 * (j - 1) + 1] = dv[block].astype(jnp.bfloat16)
        sk_ref[...] = jnp.sum(gk, axis=0, keepdims=True)
        sv_ref[...] = jnp.sum(dv, axis=0, keepdims=True)


def attend(g, shards, at, q, do, bq, cosine, sine, ck, cv, kp, vp, bk, bv, far, slabs, before):
    tokens, slots = q.shape[0], ck.shape[0]
    slab = shards * tokens
    total = slab + shards * slots
    steps = GROUP // HEADS
    width = HEADS * HD

    def wide(rows):
        return pl.BlockSpec((rows, width), lambda i: (0, g * steps + i))

    def column(rows):
        return pl.BlockSpec((rows, HD), lambda i: (0, g))

    def whole(shape):
        return pl.BlockSpec(shape, lambda i: (0,) * len(shape))

    in_specs = [
        pl.BlockSpec(memory_space=pltpu.SMEM),
        wide(tokens), wide(tokens), wide(1),
        whole((slab, HD)), whole((slab, HD)),
        column(slots), column(slots), column(tokens), column(tokens), column(1), column(1),
    ]
    in_specs += [whole(a.shape) for a in far]
    in_specs += [pl.BlockSpec((2, tokens, HD), lambda i: (0, 0, g)) for _ in slabs]
    aliases = {}
    if before is not None:
        aliases = {len(in_specs): 0, len(in_specs) + 1: 1}
        in_specs += [pl.BlockSpec(memory_space=pl.ANY)] * 2
    f32, b16 = jnp.float32, jnp.bfloat16
    flops = 2 * GROUP * tokens * HD * (4 * total + 2 * slab)
    return pl.pallas_call(
        functools.partial(attend_kernel, shards, before is not None),
        grid=(steps,),
        in_specs=in_specs,
        out_shape=[
            jax.ShapeDtypeStruct((tokens, HQ * HD), b16),
            jax.ShapeDtypeStruct((tokens, HQ * HD), b16),
            jax.ShapeDtypeStruct((1, GROUP * HD), f32),
            jax.ShapeDtypeStruct((tokens, HD), f32),
            jax.ShapeDtypeStruct((tokens, HD), f32),
            jax.ShapeDtypeStruct((max(2 * (shards - 1), 1), tokens, HD), b16),
            jax.ShapeDtypeStruct((1, HD), f32),
            jax.ShapeDtypeStruct((1, HD), f32),
        ],
        out_specs=[
            wide(tokens), wide(tokens),
            pl.BlockSpec((1, width), lambda i: (0, i)),
            whole((tokens, HD)), whole((tokens, HD)),
            whole((max(2 * (shards - 1), 1), tokens, HD)),
            whole((1, HD)), whole((1, HD)),
        ],
        scratch_shapes=[
            pltpu.VMEM((total, HD), b16), pltpu.VMEM((total, HD), b16),
            pltpu.VMEM((HD, slab), f32), pltpu.VMEM((HD, slab), f32),
        ],
        input_output_aliases=aliases,
        compiler_params=pltpu.CompilerParams(
            dimension_semantics=("arbitrary",), vmem_limit_bytes=40 * 1024 * 1024
        ),
        cost_estimate=pl.CostEstimate(
            flops=flops,
            bytes_accessed=8 * tokens * GROUP * HD + 8 * total * HD,
            transcendentals=GROUP * tokens * total,
        ),
        name="attend",
    )(at, q, do, bq, cosine, sine, ck, cv, kp, vp, bk, bv, *far, *slabs, *(before or ()))


def body(q_proj, k_proj, v_proj, cache_k, cache_v, bias_q, bias_k, bias_v, start, dout):
    shards = lax.axis_size("seq")
    rank = lax.axis_index("seq")
    tokens = q_proj.shape[1]
    first = start[0]
    ck, cv = cache_k[0], cache_v[0]

    def ring(x, s):
        return lax.ppermute(x, "seq", [(i, (i + s) % shards) for i in range(shards)])

    def later(x, s):
        return lax.ppermute(x, "seq", [(i, i + s) for i in range(shards - s)])

    def earlier(x, s):
        return lax.ppermute(x, "seq", [(i + s, i) for i in range(shards - s)])

    chunks = pack((0,), ck, cv) + pack(tuple(range(1, KV)), ck, cv)
    own = jnp.stack([k_proj[0], v_proj[0]])
    slabs = [later(own, s) for s in range(1, shards)]
    far = [[ring(chunk, s) for s in range(1, shards)] for chunk in chunks]

    owners = lax.rem(rank - jnp.arange(shards, dtype=jnp.int32) + shards, shards)
    positions = first + owners[:, None] * tokens + jnp.arange(tokens, dtype=jnp.int32)[None]
    freqs = jnp.exp(
        -(2.0 * jnp.arange(HD // 2, dtype=jnp.float32) / HD) * jnp.log(jnp.float32(1000000.0))
    )
    angles = positions.reshape(-1).astype(jnp.float32)[:, None] * freqs[None, :]
    c, n = jnp.cos(angles), jnp.sin(angles)
    cosine = jnp.concatenate([c, c], axis=1)
    sine = jnp.concatenate([-n, n], axis=1)
    at = jnp.stack([first, rank.astype(jnp.int32)])

    before = None
    sums_q, sums_k, sums_v, grads_k, grads_v = [], [], [], [], []
    for g in range(KV):
        out, gq, sq, dk, dv, send, sk, sv = attend(
            g, shards, at, q_proj[0], dout[0], bias_q[None], cosine, sine, ck, cv,
            k_proj[0], v_proj[0], bias_k[None], bias_v[None], far[g], slabs, before,
        )
        before = (out, gq)
        sums_q.append(sq[0])
        sums_k.append(sk[0])
        sums_v.append(sv[0])
        for s in range(1, shards):
            back = earlier(send[2 * (s - 1):2 * s], s).astype(jnp.float32)
            dk = dk + back[0]
            dv = dv + back[1]
        turned = jnp.concatenate([dk[:, HD // 2:], dk[:, :HD // 2]], axis=1)
        grads_k.append(dk * cosine[:tokens] - turned * sine[:tokens])
        grads_v.append(dv)
    sums = lax.psum(jnp.concatenate(sums_q + sums_k + sums_v), ("dp", "seq"))
    wide, narrow = HQ * HD, KV * HD
    return (
        out[None],
        gq[None],
        jnp.concatenate(grads_k, axis=1).astype(jnp.bfloat16)[None],
        jnp.concatenate(grads_v, axis=1).astype(jnp.bfloat16)[None],
        sums[:wide],
        sums[wide:wide + narrow],
        sums[wide + narrow:],
    )


def solution(mesh):
    split = P("dp", "seq", None)
    return jax.shard_map(
        body,
        mesh=mesh,
        in_specs=(split,) * 5 + (P(), P(), P(), P("dp"), split),
        out_specs=(split,) * 4 + (P(), P(), P()),
        check_vma=False,
    )
```

```python
import functools
import math

import jax
import jax.numpy as jnp
from jax import lax
from jax.experimental import pallas as pl
from jax.experimental.pallas import tpu as pltpu
from jax.sharding import PartitionSpec as P

HQ = 32
KV = 4
HD = 128
GROUP = 8
HEADS = 2
NEG = -1e30
SUMS = (GROUP + 2) * HD
VMEM = 56 * 1024 * 1024
F32, B16 = jnp.float32, jnp.bfloat16


def turn(x):
    return pltpu.roll(x, HD // 2, 1)


def dot(a, b, dims):
    return lax.dot_general(a, b, (dims, ((), ())), preferred_element_type=F32)


NT = ((1,), (1,))
NN = ((1,), (0,))
TN = ((0,), (0,))


def whole(shape):
    return pl.BlockSpec(shape, lambda i: (0,) * len(shape))


def column(rows, g):
    return pl.BlockSpec((rows, HD), lambda i: (0, g))


def params():
    return pltpu.CompilerParams(dimension_semantics=("arbitrary",), vmem_limit_bytes=VMEM)


def pack_kernel(ck_ref, cv_ref, *rest):
    out_ref = rest[-1] if len(rest) == 1 else rest[2]
    rows = ck_ref.shape[0]
    out_ref[pl.ds(0, rows)] = ck_ref[...]
    out_ref[pl.ds(rows, rows)] = cv_ref[...]
    if len(rest) > 1:
        kp_ref, vp_ref, _, slab_ref = rest
        slab_ref[0] = kp_ref[...]
        slab_ref[1] = vp_ref[...]


def pack(g, ck, cv, slab=()):
    rows = ck.shape[0]
    out_shape = [jax.ShapeDtypeStruct((2 * rows, HD), B16)]
    if slab:
        out_shape.append(jax.ShapeDtypeStruct((2,) + slab[0].shape, B16))
    return pl.pallas_call(
        pack_kernel,
        grid=(1,),
        in_specs=[column(rows, g)] * 2 + [whole(a.shape) for a in slab],
        out_specs=[whole(a.shape) for a in out_shape],
        out_shape=out_shape,
        compiler_params=params(),
        cost_estimate=pl.CostEstimate(flops=0, bytes_accessed=8 * rows * HD, transcendentals=0),
        name="pack",
    )(ck, cv, *slab)


def attend_kernel(
    shards, chained,
    at_ref, q_ref, do_ref, bq_ref, cos_ref, sin_ref,
    ck_ref, cv_ref, kp_ref, vp_ref, bk_ref, bv_ref, *rest,
):
    far, rest = rest[: 2 * (shards - 1)], rest[2 * (shards - 1):]
    rest = rest[chained:]
    out_ref, gq_ref, sums_ref, dk_ref, dv_ref, send_ref, keys, values = rest
    tokens = q_ref.shape[0]
    slots = ck_ref.shape[0]
    prefix = shards * slots
    slab = shards * tokens
    first = at_ref[0]
    rank = at_ref[1]
    cosine = cos_ref[pl.ds(0, tokens), :]
    sine = sin_ref[pl.ds(0, tokens), :]

    keys[pl.ds(0, slots)] = ck_ref[...]
    values[pl.ds(0, slots)] = cv_ref[...]
    for s in range(1, shards):
        keys[pl.ds(s * slots, slots)] = far[s - 1][pl.ds(0, slots)]
        values[pl.ds(s * slots, slots)] = far[s - 1][pl.ds(slots, slots)]
    for s in range(shards):
        rows = pl.ds(s * tokens, tokens)
        if s == 0:
            kp, vp = kp_ref[...], vp_ref[...]
        else:
            block = far[shards - 1 + s - 1]
            kp, vp = block[0], block[1]
        k = kp.astype(F32) + bk_ref[...].astype(F32)
        k = k * cos_ref[rows, :] + turn(k) * sin_ref[rows, :]
        v = vp.astype(F32) + bv_ref[...].astype(F32)
        place = pl.ds(prefix + s * tokens, tokens)
        keys[place] = k.astype(B16)
        values[place] = v.astype(B16)

    rows = HEADS * tokens
    scale = HD ** -0.5
    col = lax.broadcasted_iota(jnp.int32, (1, slots), 1)
    seen = [col < first - lax.rem(rank - j + shards, shards) * slots for j in range(shards)]
    token = lax.broadcasted_iota(jnp.int32, (rows, tokens), 0) & (tokens - 1)
    causal = lax.broadcasted_iota(jnp.int32, (rows, tokens), 1) <= token

    def scores(c):
        queries = []
        for h in range(c * HEADS, (c + 1) * HEADS):
            cols = pl.ds(h * HD, HD)
            x = q_ref[:, cols].astype(F32) + bq_ref[:, cols].astype(F32)
            x = x * cosine + turn(x) * sine
            queries.append(x.astype(B16))
        q = jnp.concatenate(queries, axis=0)
        do = jnp.concatenate(
            [do_ref[:, pl.ds(h * HD, HD)] for h in range(c * HEADS, (c + 1) * HEADS)], axis=0
        )
        s = dot(q, keys[...], NT)
        parts = []
        for j in range(shards):
            parts.append(jnp.where(seen[j], s[:, j * slots:(j + 1) * slots], NEG))
        parts.append(jnp.where(causal, s[:, prefix:prefix + tokens], NEG))
        for j in range(1, shards):
            part = s[:, prefix + j * tokens:prefix + (j + 1) * tokens]
            parts.append(jnp.where(rank >= j, part, NEG))
        return q, do, jnp.concatenate(parts, axis=1)

    def softmax(s):
        top = jnp.max(s, axis=1, keepdims=True)
        e = jnp.exp2((s - top) * (scale * math.log2(math.e)))
        return e * (1.0 / jnp.sum(e, axis=1, keepdims=True))

    def backward(c, q, do, p, dp):
        pb = p.astype(B16)
        o = dot(pb, values[...], NN).astype(B16)
        delta = jnp.sum(do.astype(F32) * o.astype(F32), axis=1, keepdims=True)
        ds = (p * (dp - delta)).astype(B16)
        dq = (dot(ds, keys[...], NN) * scale).astype(B16).astype(F32)
        for i in range(HEADS):
            h = c * HEADS + i
            cols = pl.ds(h * HD, HD)
            part = slice(i * tokens, (i + 1) * tokens)
            out_ref[:, cols] = o[part]
            g = dq[part]
            g = g * cosine - turn(g) * sine
            gq_ref[:, cols] = g.astype(B16)
            sums_ref[0, :, cols] = jnp.sum(g, axis=0, keepdims=True)
        return dot(q, ds[:, prefix:], TN), dot(do, pb[:, prefix:], TN)

    chains = GROUP // HEADS
    dkt = jnp.zeros((HD, slab), F32)
    dvt = jnp.zeros((HD, slab), F32)
    ready = scores(0)
    for c in range(chains):
        q, do, s = ready
        if c + 1 < chains:
            ready = scores(c + 1)
        dp = dot(do, values[...], NT)
        dk_part, dv_part = backward(c, q, do, softmax(s), dp)
        dkt += dk_part
        dvt += dv_part

    dk = dkt.T * scale
    dv = dvt.T
    gk = dk * cos_ref[...] - turn(dk) * sin_ref[...]
    dk_ref[...] = dk[:tokens]
    dv_ref[...] = dv[:tokens]
    for j in range(1, shards):
        block = slice(j * tokens, (j + 1) * tokens)
        send_ref[2 * (j - 1)] = dk[block].astype(B16)
        send_ref[2 * (j - 1) + 1] = dv[block].astype(B16)
    sums_ref[0, :, pl.ds(GROUP * HD, HD)] = jnp.sum(gk, axis=0, keepdims=True)
    sums_ref[0, :, pl.ds((GROUP + 1) * HD, HD)] = jnp.sum(dv, axis=0, keepdims=True)


def attend(g, shards, at, q, do, bq, cosine, sine, ck, cv, kp, vp, bk, bv, far, slabs, before):
    tokens, slots = q.shape[0], ck.shape[0]
    slab = shards * tokens
    total = slab + shards * slots
    width = GROUP * HD
    last = g == KV - 1
    sends = max(2 * (shards - 1), 1)

    def wide(rows):
        return pl.BlockSpec((rows, width), lambda i: (0, g))

    in_specs = [
        pl.BlockSpec(memory_space=pltpu.SMEM),
        wide(tokens), wide(tokens), wide(1),
        whole((slab, HD)), whole((slab, HD)),
        column(slots, g), column(slots, g), column(tokens, g), column(tokens, g),
        column(1, g), column(1, g),
    ]
    in_specs += [whole(a.shape) for a in far]
    in_specs += [pl.BlockSpec((2, tokens, HD), lambda i: (0, 0, g)) for _ in slabs]
    send_heads, send_place = (1, 0) if last else (KV - 1, g)
    out_shape = [
        jax.ShapeDtypeStruct((tokens, HQ * HD), B16),
        jax.ShapeDtypeStruct((tokens, HQ * HD), B16),
        jax.ShapeDtypeStruct((KV, 1, SUMS), F32),
        jax.ShapeDtypeStruct((tokens, KV * HD), F32),
        jax.ShapeDtypeStruct((tokens, KV * HD), F32),
        jax.ShapeDtypeStruct((sends, tokens, send_heads * HD), B16),
    ]
    out_specs = [
        wide(tokens), wide(tokens),
        pl.BlockSpec((1, 1, SUMS), lambda i: (g, 0, 0)),
        column(tokens, g), column(tokens, g),
        pl.BlockSpec((sends, tokens, HD), lambda i: (0, 0, send_place)),
    ]
    handed = [] if before is None else list(before[:5] if last else before)
    aliases = {len(in_specs) + i: i for i in range(len(handed))}
    in_specs += [pl.BlockSpec(memory_space=pl.ANY)] * len(handed)
    return pl.pallas_call(
        functools.partial(attend_kernel, shards, len(handed)),
        grid=(1,),
        in_specs=in_specs,
        out_shape=out_shape,
        out_specs=out_specs,
        scratch_shapes=[pltpu.VMEM((total, HD), B16), pltpu.VMEM((total, HD), B16)],
        input_output_aliases=aliases,
        compiler_params=params(),
        cost_estimate=pl.CostEstimate(
            flops=2 * GROUP * tokens * HD * (4 * total + 2 * slab),
            bytes_accessed=8 * tokens * GROUP * HD + 8 * total * HD,
            transcendentals=GROUP * tokens * total,
        ),
        name="attend",
    )(at, q, do, bq, cosine, sine, ck, cv, kp, vp, bk, bv, *far, *slabs, *handed)


def finish_kernel(shards, dk_ref, dv_ref, cos_ref, sin_ref, *rest):
    early, late = rest[: shards - 1], rest[shards - 1: 2 * (shards - 1)]
    gk_ref, gv_ref = rest[-2:]
    for g in range(KV):
        cols = pl.ds(g * HD, HD)
        dk = dk_ref[:, cols]
        dv = dv_ref[:, cols]
        for s in range(shards - 1):
            back, place = (late[s], pl.ds(0, HD)) if g == KV - 1 else (early[s], cols)
            dk = dk + back[0, :, place].astype(F32)
            dv = dv + back[1, :, place].astype(F32)
        gk_ref[:, cols] = (dk * cos_ref[...] - turn(dk) * sin_ref[...]).astype(B16)
        gv_ref[:, cols] = dv.astype(B16)


def finish(shards, dk, dv, cosine, sine, early, late):
    tokens = dk.shape[0]
    return pl.pallas_call(
        functools.partial(finish_kernel, shards),
        grid=(1,),
        in_specs=[whole(dk.shape)] * 2 + [whole((tokens, HD))] * 2
        + [whole(a.shape) for a in early + late],
        out_specs=[whole(dk.shape)] * 2,
        out_shape=[jax.ShapeDtypeStruct(dk.shape, B16)] * 2,
        compiler_params=params(),
        cost_estimate=pl.CostEstimate(flops=0, bytes_accessed=1 << 20, transcendentals=0),
        name="finish",
    )(dk, dv, cosine, sine, *early, *late)


def sum_over(x, axis):
    size = lax.axis_size(axis)
    if size & (size - 1):
        return lax.psum(x, axis)
    step = 1
    while step < size:
        x = x + lax.ppermute(x, axis, [(i, i ^ step) for i in range(size)])
        step *= 2
    return x


def body(q_proj, k_proj, v_proj, cache_k, cache_v, bias_q, bias_k, bias_v, start, dout):
    shards = lax.axis_size("seq")
    rank = lax.axis_index("seq")
    tokens = q_proj.shape[1]
    first = start[0]
    ck, cv, kp, vp = cache_k[0], cache_v[0], k_proj[0], v_proj[0]

    def ring(x, s):
        return lax.ppermute(x, "seq", [(i, (i + s) % shards) for i in range(shards)])

    def later(x, s):
        return lax.ppermute(x, "seq", [(i, i + s) for i in range(shards - s)])

    def earlier(x, s):
        return lax.ppermute(x, "seq", [(i + s, i) for i in range(shards - s)])

    chunk, own = pack(0, ck, cv, (kp, vp))
    chunks = [chunk] + [pack(g, ck, cv)[0] for g in range(1, KV)]
    slabs = [later(own, s) for s in range(1, shards)]
    far = [[ring(chunk, s) for s in range(1, shards)] for chunk in chunks]

    owners = lax.rem(rank - jnp.arange(shards, dtype=jnp.int32) + shards, shards)
    positions = first + owners[:, None] * tokens + jnp.arange(tokens, dtype=jnp.int32)[None]
    freqs = jnp.exp(
        -(2.0 * jnp.arange(HD // 2, dtype=F32) / HD) * jnp.log(jnp.float32(1000000.0))
    )
    angles = positions.reshape(-1).astype(F32)[:, None] * freqs[None, :]
    c, n = jnp.cos(angles), jnp.sin(angles)
    cosine = jnp.concatenate([c, c], axis=1)
    sine = jnp.concatenate([-n, n], axis=1)
    at = jnp.stack([first, rank.astype(jnp.int32)])

    before = None
    for g in range(KV):
        if g == KV - 1:
            early = [earlier(before[5][2 * (s - 1):2 * s], s) for s in range(1, shards)]
        before = attend(
            g, shards, at, q_proj[0], dout[0], bias_q[None], cosine, sine, ck, cv,
            kp, vp, bias_k[None], bias_v[None], far[g], slabs, before,
        )
    out, gq, sums, dk, dv, send = before
    late = [earlier(send[2 * (s - 1):2 * s], s) for s in range(1, shards)]
    sums = sum_over(sum_over(sums, "seq"), "dp")[:, 0]
    gk, gv = finish(shards, dk, dv, cosine, sine, early, late)
    wide = GROUP * HD
    return (
        out[None],
        gq[None],
        gk[None],
        gv[None],
        sums[:, :wide].reshape(-1),
        sums[:, wide:wide + HD].reshape(-1),
        sums[:, wide + HD:].reshape(-1),
    )


def solution(mesh):
    split = P("dp", "seq", None)
    return jax.shard_map(
        body,
        mesh=mesh,
        in_specs=(split,) * 5 + (P(), P(), P(), P("dp"), split),
        out_specs=(split,) * 4 + (P(), P(), P()),
        check_vma=False,
    )
```

```python
import functools
import math

import jax
import jax.numpy as jnp
from jax import lax
from jax.experimental import pallas as pl
from jax.experimental.pallas import tpu as pltpu
from jax.sharding import PartitionSpec as P

HQ = 32
KV = 4
HD = 128
GROUP = 8
HEADS = 2
NEG = -1e30
SUMS = HQ + 2 * KV
VMEM = 28 * 1024 * 1024
F32, B16 = jnp.float32, jnp.bfloat16


def turn(x):
    return pltpu.roll(x, HD // 2, 1)


def dot(a, b, dims):
    return lax.dot_general(a, b, (dims, ((), ())), preferred_element_type=F32)


NT = ((1,), (1,))
NN = ((1,), (0,))
TN = ((0,), (0,))


def whole(shape):
    return pl.BlockSpec(shape, lambda i: (0,) * len(shape))


def column(rows, g):
    return pl.BlockSpec((rows, HD), lambda i: (0, g))


def params():
    return pltpu.CompilerParams(dimension_semantics=("arbitrary",), vmem_limit_bytes=VMEM)


def pack_kernel(groups, ck_ref, cv_ref, *rest):
    outs = rest[len(rest) - len(groups) - (len(rest) > len(groups)):]
    rows = ck_ref.shape[0]
    width = ck_ref.shape[1] // len(groups)
    for i in range(len(groups)):
        cols = pl.ds(i * width, width)
        outs[i][pl.ds(0, rows)] = ck_ref[:, cols]
        outs[i][pl.ds(rows, rows)] = cv_ref[:, cols]
    if len(rest) > len(groups):
        kp_ref, vp_ref = rest[:2]
        outs[-1][0] = kp_ref[...]
        outs[-1][1] = vp_ref[...]


def pack(first, count, ck, cv, slab=()):
    rows = ck.shape[0]
    shapes = [(2 * rows, HD)] * count
    if slab:
        shapes.append((2,) + slab[0].shape)
    chunk = pl.BlockSpec((pl.Element(rows), pl.Element(count * HD)), lambda i: (0, first * HD))
    return pl.pallas_call(
        functools.partial(pack_kernel, range(count)),
        grid=(1,),
        in_specs=[chunk] * 2 + [whole(a.shape) for a in slab],
        out_specs=[pl.BlockSpec(memory_space=pltpu.VMEM)] * len(shapes),
        out_shape=[pltpu.VMEM(shape, B16) for shape in shapes],
        compiler_params=params(),
        cost_estimate=pl.CostEstimate(
            flops=0, bytes_accessed=8 * rows * HD * count, transcendentals=0
        ),
        name="pack",
    )(ck, cv, *slab)


def attend_kernel(
    g, shards, chained,
    first_ref, rank_ref, q_ref, do_ref, bq_ref, cos_ref, sin_ref,
    ck_ref, cv_ref, kp_ref, vp_ref, bk_ref, bv_ref, *rest,
):
    far, rest = rest[: 2 * (shards - 1)], rest[2 * (shards - 1):]
    old_sums_ref = rest[0] if g else None
    rest = rest[chained:]
    (out_ref, gq_ref, sums_ref, dk_ref, dv_ref, send_ref,
     keys, values, bias, dkt, dvt) = rest
    tokens = q_ref.shape[0]
    slots = ck_ref.shape[0]
    prefix = shards * slots
    slab = shards * tokens
    first = first_ref[0]
    rank = rank_ref[0]

    keys[pl.ds(0, slots)] = ck_ref[...]
    values[pl.ds(0, slots)] = cv_ref[...]
    for s in range(1, shards):
        keys[pl.ds(s * slots, slots)] = far[s - 1][pl.ds(0, slots)]
        values[pl.ds(s * slots, slots)] = far[s - 1][pl.ds(slots, slots)]
    bias_k = bk_ref[...].astype(F32)[g:g + 1]
    bias_v = bv_ref[...].astype(F32)[g:g + 1]
    for s in range(shards):
        rows = pl.ds(s * tokens, tokens)
        if s == 0:
            kp, vp = kp_ref[...], vp_ref[...]
        else:
            block = far[shards - 1 + s - 1]
            kp, vp = block[0], block[1]
        k = kp.astype(F32) + bias_k
        k = k * cos_ref[rows, :] + turn(k) * sin_ref[rows, :]
        v = vp.astype(F32) + bias_v
        place = pl.ds(prefix + s * tokens, tokens)
        keys[place] = k.astype(B16)
        values[place] = v.astype(B16)
    bias[...] = bq_ref[...].astype(F32)
    sums_ref[...] = jnp.zeros_like(sums_ref) if old_sums_ref is None else old_sums_ref[...]
    dkt[...] = jnp.zeros_like(dkt)
    dvt[...] = jnp.zeros_like(dvt)

    rows = HEADS * tokens
    scale = HD ** -0.5

    def scores(head):
        cosine = cos_ref[pl.ds(0, tokens), :]
        sine = sin_ref[pl.ds(0, tokens), :]
        queries, cots = [], []
        for h in range(HEADS):
            cols = pl.ds(pl.multiple_of((head + h) * HD, HD), HD)
            x = q_ref[:, cols].astype(F32) + bias[pl.ds(head + h, 1), :]
            x = x * cosine + turn(x) * sine
            queries.append(x.astype(B16))
            cots.append(do_ref[:, cols])
        q = jnp.concatenate(queries, axis=0)
        do = jnp.concatenate(cots, axis=0)
        s = dot(q, keys[...], NT)
        col = lax.broadcasted_iota(jnp.int32, (1, slots), 1)
        parts = []
        for j in range(shards):
            seen = col < first - lax.rem(rank - j + shards, shards) * slots
            parts.append(jnp.where(seen, s[:, j * slots:(j + 1) * slots], NEG))
        token = lax.broadcasted_iota(jnp.int32, (rows, tokens), 0) & (tokens - 1)
        causal = lax.broadcasted_iota(jnp.int32, (rows, tokens), 1) <= token
        parts.append(jnp.where(causal, s[:, prefix:prefix + tokens], NEG))
        for j in range(1, shards):
            part = s[:, prefix + j * tokens:prefix + (j + 1) * tokens]
            parts.append(jnp.where(rank >= j, part, NEG))
        return q, do, jnp.concatenate(parts, axis=1)

    def softmax(s):
        top = jnp.max(s, axis=1, keepdims=True)
        e = jnp.exp2((s - top) * (scale * math.log2(math.e)))
        return e * (1.0 / jnp.sum(e, axis=1, keepdims=True))

    def weigh(pb, do):
        o = dot(pb, values[...], NN).astype(B16)
        return o, jnp.sum(do.astype(F32) * o.astype(F32), axis=1, keepdims=True)

    def store(head, o, dq):
        cosine = cos_ref[pl.ds(0, tokens), :]
        sine = sin_ref[pl.ds(0, tokens), :]
        for h in range(HEADS):
            cols = pl.ds(pl.multiple_of((head + h) * HD, HD), HD)
            part = slice(h * tokens, (h + 1) * tokens)
            out_ref[:, cols] = o[part]
            x = dq[part]
            x = x * cosine - turn(x) * sine
            gq_ref[:, cols] = x.astype(B16)
            sums_ref[pl.ds(g * GROUP + head + h, 1), :] = jnp.sum(x, axis=0, keepdims=True)

    def query_grad(ds):
        return (dot(ds, keys[...], NN) * scale).astype(B16).astype(F32)

    def pair(i, carry):
        head_a = i * 2 * HEADS
        head_b = head_a + HEADS
        q_a, do_a, s_a = scores(head_a)
        q_b, do_b, s_b = scores(head_b)
        dp_a = dot(do_a, values[...], NT)
        p_a = softmax(s_a)
        pb_a = p_a.astype(B16)
        dp_b = dot(do_b, values[...], NT)
        o_a, delta_a = weigh(pb_a, do_a)
        p_b = softmax(s_b)
        pb_b = p_b.astype(B16)
        ds_a = (p_a * (dp_a - delta_a)).astype(B16)
        o_b, delta_b = weigh(pb_b, do_b)
        dq_a = query_grad(ds_a)
        dkt[...] += dot(q_a, ds_a[:, prefix:], TN)
        dvt[...] += dot(do_a, pb_a[:, prefix:], TN)
        ds_b = (p_b * (dp_b - delta_b)).astype(B16)
        store(head_a, o_a, dq_a)
        dq_b = query_grad(ds_b)
        dkt[...] += dot(q_b, ds_b[:, prefix:], TN)
        dvt[...] += dot(do_b, pb_b[:, prefix:], TN)
        store(head_b, o_b, dq_b)
        return carry

    lax.fori_loop(0, GROUP // (2 * HEADS), pair, 0)

    dk = dkt[...].T * scale
    dv = dvt[...].T
    gk = dk * cos_ref[...] - turn(dk) * sin_ref[...]
    dk_ref[...] = dk[:tokens]
    dv_ref[...] = dv[:tokens]
    for j in range(1, shards):
        block = slice(j * tokens, (j + 1) * tokens)
        send_ref[2 * (j - 1)] = dk[block].astype(B16)
        send_ref[2 * (j - 1) + 1] = dv[block].astype(B16)
    sums_ref[pl.ds(HQ + g, 1), :] = jnp.sum(gk, axis=0, keepdims=True)
    sums_ref[pl.ds(HQ + KV + g, 1), :] = jnp.sum(dv, axis=0, keepdims=True)


def attend(
    g, shards, first, rank, q, do, bq, cosine, sine, ck, cv, kp, vp, bk, bv, far, slabs, before
):
    tokens, slots = q.shape[0], ck.shape[0]
    slab = shards * tokens
    total = slab + shards * slots
    width = GROUP * HD
    last = g == KV - 1
    sends = max(2 * (shards - 1), 1)
    smem = pl.BlockSpec(memory_space=pltpu.SMEM)

    def wide(rows):
        return pl.BlockSpec((rows, width), lambda i: (0, g))

    in_specs = [
        smem, smem, wide(tokens), wide(tokens), pl.BlockSpec((GROUP, HD), lambda i: (g, 0)),
        whole((slab, HD)), whole((slab, HD)),
        column(slots, g), column(slots, g), column(tokens, g), column(tokens, g),
        whole((KV, HD)), whole((KV, HD)),
    ]
    in_specs += [whole(a.shape) for a in far]
    in_specs += [pl.BlockSpec((2, tokens, HD), lambda i: (0, 0, g)) for _ in slabs]
    send_heads, send_place = (1, 0) if last else (KV - 1, g)
    out_shape = [
        pltpu.HBM((tokens, HQ * HD), B16),
        pltpu.HBM((tokens, HQ * HD), B16),
        jax.ShapeDtypeStruct((SUMS, HD), F32),
        pltpu.HBM((tokens, KV * HD), F32),
        pltpu.HBM((tokens, KV * HD), F32),
        pltpu.HBM((sends, tokens, send_heads * HD), B16),
    ]
    out_specs = [
        wide(tokens), wide(tokens), whole((SUMS, HD)),
        column(tokens, g), column(tokens, g),
        pl.BlockSpec((sends, tokens, HD), lambda i: (0, 0, send_place)),
    ]
    handed = []
    aliases = {}
    if before is not None:
        out, gq, sums, dk, dv, send = before
        handed = [sums, out, gq, dk, dv] + ([] if last else [send])
        aliases = {len(in_specs) + 1 + i: j for i, j in enumerate((0, 1, 3, 4, 5)[:len(handed) - 1])}
        in_specs += [whole((SUMS, HD))] + [pl.BlockSpec(memory_space=pl.ANY)] * (len(handed) - 1)
    return pl.pallas_call(
        functools.partial(attend_kernel, g, shards, len(handed)),
        grid=(1,),
        in_specs=in_specs,
        out_shape=out_shape,
        out_specs=out_specs,
        scratch_shapes=[
            pltpu.VMEM((total, HD), B16), pltpu.VMEM((total, HD), B16),
            pltpu.VMEM((GROUP, HD), F32),
            pltpu.VMEM((HD, slab), F32), pltpu.VMEM((HD, slab), F32),
        ],
        input_output_aliases=aliases,
        compiler_params=params(),
        cost_estimate=pl.CostEstimate(
            flops=2 * GROUP * tokens * HD * (4 * total + 2 * slab),
            bytes_accessed=8 * tokens * GROUP * HD + 8 * total * HD,
            transcendentals=GROUP * tokens * total,
        ),
        name="attend",
    )(first, rank, q, do, bq, cosine, sine, ck, cv, kp, vp, bk, bv, *far, *slabs, *handed)


def finish_kernel(shards, dk_ref, dv_ref, cos_ref, sin_ref, *rest):
    early, late = rest[: shards - 1], rest[shards - 1: 2 * (shards - 1)]
    gk_ref, gv_ref = rest[-2:]
    for g in range(KV):
        cols = pl.ds(g * HD, HD)
        dk = dk_ref[:, cols]
        dv = dv_ref[:, cols]
        for s in range(shards - 1):
            back, place = (late[s], pl.ds(0, HD)) if g == KV - 1 else (early[s], cols)
            dk = dk + back[0, :, place].astype(F32)
            dv = dv + back[1, :, place].astype(F32)
        gk_ref[:, cols] = (dk * cos_ref[...] - turn(dk) * sin_ref[...]).astype(B16)
        gv_ref[:, cols] = dv.astype(B16)


def finish(shards, dk, dv, cosine, sine, early, late):
    tokens = dk.shape[0]
    return pl.pallas_call(
        functools.partial(finish_kernel, shards),
        grid=(1,),
        in_specs=[whole(dk.shape)] * 2 + [whole((tokens, HD))] * 2
        + [whole(a.shape) for a in early + late],
        out_specs=[whole(dk.shape)] * 2,
        out_shape=[jax.ShapeDtypeStruct(dk.shape, B16)] * 2,
        compiler_params=params(),
        cost_estimate=pl.CostEstimate(flops=0, bytes_accessed=1 << 20, transcendentals=0),
        name="finish",
    )(dk, dv, cosine, sine, *early, *late)


def body(q_proj, k_proj, v_proj, cache_k, cache_v, bias_q, bias_k, bias_v, start, dout):
    shards = lax.axis_size("seq")
    rank = lax.axis_index("seq").astype(jnp.int32)
    tokens = q_proj.shape[1]
    ck, cv, kp, vp = cache_k[0], cache_v[0], k_proj[0], v_proj[0]

    def ring(x, s):
        return lax.ppermute(x, "seq", [(i, (i + s) % shards) for i in range(shards)])

    def later(x, s):
        return lax.ppermute(x, "seq", [(i, i + s) for i in range(shards - s)])

    def earlier(x, s):
        return lax.ppermute(x, "seq", [(i + s, i) for i in range(shards - s)])

    chunk, own = pack(0, 1, ck, cv, (kp, vp))
    chunks = [chunk] + list(pack(1, KV - 1, ck, cv))
    slabs = [later(own, s) for s in range(1, shards)]
    far = [[ring(chunk, s) for s in range(1, shards)] for chunk in chunks]

    owners = lax.rem(rank - jnp.arange(shards, dtype=jnp.int32) + shards, shards)
    positions = start[0] + owners[:, None] * tokens + jnp.arange(tokens, dtype=jnp.int32)[None]
    lane = jnp.arange(HD, dtype=jnp.int32)
    freqs = jnp.exp(
        -(2.0 * (lane % (HD // 2)).astype(F32) / HD) * jnp.log(jnp.float32(1000000.0))
    )
    angles = positions.reshape(-1).astype(F32)[:, None] * freqs[None, :]
    cosine = jnp.cos(angles)
    sine = jnp.sin(angles) * jnp.where(lane < HD // 2, -1.0, 1.0).astype(F32)[None]

    before = None
    for g in range(KV):
        if g == KV - 1:
            early = [earlier(before[5][2 * (s - 1):2 * s], s) for s in range(1, shards)]
        before = attend(
            g, shards, start, rank.reshape(1), q_proj[0], dout[0], bias_q.reshape(HQ, HD),
            cosine, sine, ck, cv, kp, vp, bias_k.reshape(KV, HD), bias_v.reshape(KV, HD),
            far[g], slabs, before,
        )
    out, gq, sums, dk, dv, send = before
    late = [earlier(send[2 * (s - 1):2 * s], s) for s in range(1, shards)]
    gk, gv = finish(shards, dk, dv, cosine, sine, early, late)
    sums = jnp.sum(lax.all_gather(sums, ("dp", "seq")), axis=0)
    return (
        out[None],
        gq[None],
        gk[None],
        gv[None],
        sums[:HQ].reshape(-1),
        sums[HQ:HQ + KV].reshape(-1),
        sums[HQ + KV:].reshape(-1),
    )


def solution(mesh):
    split = P("dp", "seq", None)
    return jax.shard_map(
        body,
        mesh=mesh,
        in_specs=(split,) * 5 + (P(), P(), P(), P("dp"), split),
        out_specs=(split,) * 4 + (P(), P(), P()),
        check_vma=False,
    )
```

```python
import functools
import math

import jax
import jax.numpy as jnp
from jax import lax
from jax.experimental import pallas as pl
from jax.experimental.pallas import tpu as pltpu
from jax.sharding import PartitionSpec as P

HQ = 32
KV = 4
HD = 128
GROUP = 8
HEADS = 2
NEG = -1e30
SUMS = HQ + 2 * KV
VMEM = 28 * 1024 * 1024
F32, B16 = jnp.float32, jnp.bfloat16


def turn(x):
    return pltpu.roll(x, HD // 2, 1)


def dot(a, b, dims):
    return lax.dot_general(a, b, (dims, ((), ())), preferred_element_type=F32)


NT = ((1,), (1,))
NN = ((1,), (0,))
TN = ((0,), (0,))


def whole(shape):
    return pl.BlockSpec(shape, lambda i: (0,) * len(shape))


def column(rows, g):
    return pl.BlockSpec((rows, HD), lambda i: (0, g))


def params():
    return pltpu.CompilerParams(dimension_semantics=("arbitrary",), vmem_limit_bytes=VMEM)


def copy_chunk(g, ck_ref, cv_ref, out_ref):
    rows = ck_ref.shape[0]
    cols = pl.ds(g * HD, HD)
    out_ref[pl.ds(0, rows)] = ck_ref[:, cols]
    out_ref[pl.ds(rows, rows)] = cv_ref[:, cols]


def pack_kernel(ck_ref, cv_ref, *rest):
    copy_chunk(0, ck_ref, cv_ref, rest[-1])


def pack(g, ck, cv, *after):
    rows = ck.shape[0]
    return pl.pallas_call(
        pack_kernel,
        grid=(1,),
        in_specs=[column(rows, g)] * 2 + [pl.BlockSpec(memory_space=pl.ANY)] * len(after),
        out_specs=pl.BlockSpec(memory_space=pltpu.VMEM),
        out_shape=pltpu.VMEM((2 * rows, HD), B16),
        compiler_params=params(),
        cost_estimate=pl.CostEstimate(flops=0, bytes_accessed=8 * rows * HD, transcendentals=0),
        name="pack",
    )(ck, cv, *after)


def turn_back(x, cosine, sine):
    return x * cosine - turn(x) * sine


def finish_heads(heads, shards, tables, owns, backs, gk_ref, gv_ref):
    tokens = gk_ref.shape[0]
    cosine, sine = (t[pl.ds(0, tokens), :] for t in tables)
    for i in range(heads):
        dk, dv = owns[i][0], owns[i][1]
        for s in range(shards - 1):
            dk = dk + backs[s][2 * i].astype(F32)
            dv = dv + backs[s][2 * i + 1].astype(F32)
        cols = pl.ds(i * HD, HD)
        gk_ref[:, cols] = turn_back(dk, cosine, sine).astype(B16)
        gv_ref[:, cols] = dv.astype(B16)


def attend_kernel(g, shards, *refs):
    refs = list(refs)

    def take(count):
        taken = refs[:count]
        del refs[:count]
        return taken

    (first_ref, rank_ref, q_ref, do_ref, bq_ref, cos_ref, sin_ref,
     ck_ref, cv_ref, kp_ref, vp_ref, bk_ref, bv_ref) = take(13)
    far = take(shards - 1)
    far_k = take(shards - 1)
    far_v = take(shards - 1)
    old_sums_ref = take(1)[0] if g else None
    old_send = take(shards - 1) if g % 2 else []
    owns = take(2) if g == KV - 1 else []
    backs = take(shards - 1) if g == KV - 1 else []
    if g:
        take(2)
    out_ref, gq_ref, sums_ref, own_ref = take(4)
    send = take(shards - 1)
    pack_ref = take(1)[0] if g + 2 < KV else None
    gk_ref, gv_ref = take(2) if g == KV - 1 else (None, None)
    keys, values, keys_t, values_t, bias, dkt, dvt = refs
    tokens = q_ref.shape[0]
    slots = ck_ref.shape[0]
    prefix = shards * slots
    slab = shards * tokens
    first = first_ref[0]
    rank = rank_ref[0]
    mine = pl.ds(g * HD, HD)

    if pack_ref is not None:
        copy_chunk(g + 2, ck_ref, cv_ref, pack_ref)
    keys[pl.ds(0, slots)] = ck_ref[:, mine]
    values[pl.ds(0, slots)] = cv_ref[:, mine]
    for s in range(1, shards):
        keys[pl.ds(s * slots, slots)] = far[s - 1][pl.ds(0, slots)]
        values[pl.ds(s * slots, slots)] = far[s - 1][pl.ds(slots, slots)]
    bias_k = bk_ref[...].astype(F32)[g:g + 1]
    bias_v = bv_ref[...].astype(F32)[g:g + 1]
    for s in range(shards):
        rows = pl.ds(s * tokens, tokens)
        kp, vp = (kp_ref, vp_ref) if s == 0 else (far_k[s - 1], far_v[s - 1])
        k = kp[:, mine].astype(F32) + bias_k
        k = k * cos_ref[rows, :] + turn(k) * sin_ref[rows, :]
        v = vp[:, mine].astype(F32) + bias_v
        place = pl.ds(prefix + s * tokens, tokens)
        keys[place] = k.astype(B16)
        values[place] = v.astype(B16)
    keys_t[...] = keys[...].T
    values_t[...] = values[...].T
    bias[...] = bq_ref[...].astype(F32)[g * GROUP:(g + 1) * GROUP]
    sums_ref[...] = jnp.zeros_like(sums_ref) if old_sums_ref is None else old_sums_ref[...]
    dkt[...] = jnp.zeros_like(dkt)
    dvt[...] = jnp.zeros_like(dvt)

    rows = HEADS * tokens
    scale = HD ** -0.5

    def scores(head):
        cosine = cos_ref[pl.ds(0, tokens), :]
        sine = sin_ref[pl.ds(0, tokens), :]
        queries, cots = [], []
        for h in range(HEADS):
            cols = pl.ds(pl.multiple_of((g * GROUP + head + h) * HD, HD), HD)
            x = q_ref[:, cols].astype(F32) + bias[pl.ds(head + h, 1), :]
            x = x * cosine + turn(x) * sine
            queries.append(x.astype(B16))
            cots.append(do_ref[:, cols])
        q = jnp.concatenate(queries, axis=0)
        do = jnp.concatenate(cots, axis=0)
        s = dot(q, keys_t[...], NN)
        col = lax.broadcasted_iota(jnp.int32, (1, slots), 1)
        parts = []
        for j in range(shards):
            seen = col < first - lax.rem(rank - j + shards, shards) * slots
            parts.append(jnp.where(seen, s[:, j * slots:(j + 1) * slots], NEG))
        token = lax.broadcasted_iota(jnp.int32, (rows, tokens), 0) & (tokens - 1)
        causal = lax.broadcasted_iota(jnp.int32, (rows, tokens), 1) <= token
        parts.append(jnp.where(causal, s[:, prefix:prefix + tokens], NEG))
        for j in range(1, shards):
            part = s[:, prefix + j * tokens:prefix + (j + 1) * tokens]
            parts.append(jnp.where(rank >= j, part, NEG))
        return q, do, jnp.concatenate(parts, axis=1)

    def softmax(s):
        top = jnp.max(s, axis=1, keepdims=True)
        e = jnp.exp2((s - top) * (scale * math.log2(math.e)))
        return e * (1.0 / jnp.sum(e, axis=1, keepdims=True))

    def weigh(pb, do):
        o = dot(pb, values[...], NN).astype(B16)
        return o, jnp.sum(do.astype(F32) * o.astype(F32), axis=1, keepdims=True)

    def store(head, o, dq):
        cosine = cos_ref[pl.ds(0, tokens), :]
        sine = sin_ref[pl.ds(0, tokens), :]
        for h in range(HEADS):
            cols = pl.ds(pl.multiple_of((head + h) * HD, HD), HD)
            part = slice(h * tokens, (h + 1) * tokens)
            out_ref[:, cols] = o[part]
            x = turn_back(dq[part], cosine, sine)
            gq_ref[:, cols] = x.astype(B16)
            sums_ref[pl.ds(g * GROUP + head + h, 1), :] = jnp.sum(x, axis=0, keepdims=True)

    def query_grad(ds):
        return (dot(ds, keys[...], NN) * scale).astype(B16).astype(F32)

    def pair(i, carry):
        head_a = i * 2 * HEADS
        head_b = head_a + HEADS
        q_a, do_a, s_a = scores(head_a)
        q_b, do_b, s_b = scores(head_b)
        dp_a = dot(do_a, values_t[...], NN)
        p_a = softmax(s_a)
        pb_a = p_a.astype(B16)
        dp_b = dot(do_b, values_t[...], NN)
        o_a, delta_a = weigh(pb_a, do_a)
        p_b = softmax(s_b)
        pb_b = p_b.astype(B16)
        ds_a = (p_a * (dp_a - delta_a)).astype(B16)
        o_b, delta_b = weigh(pb_b, do_b)
        dq_a = query_grad(ds_a)
        dkt[...] += dot(q_a, ds_a[:, prefix:], TN)
        dvt[...] += dot(do_a, pb_a[:, prefix:], TN)
        ds_b = (p_b * (dp_b - delta_b)).astype(B16)
        store(head_a, o_a, dq_a)
        dq_b = query_grad(ds_b)
        dkt[...] += dot(q_b, ds_b[:, prefix:], TN)
        dvt[...] += dot(do_b, pb_b[:, prefix:], TN)
        store(head_b, o_b, dq_b)
        return carry

    lax.fori_loop(0, GROUP // (2 * HEADS), pair, 0)

    dk = dkt[...].T * scale
    dv = dvt[...].T
    gk = turn_back(dk, cos_ref[...], sin_ref[...])
    own_ref[0] = dk[:tokens]
    own_ref[1] = dv[:tokens]
    at = 2 * (g % 2)
    for j in range(1, shards):
        block = slice(j * tokens, (j + 1) * tokens)
        send[j - 1][at] = dk[block].astype(B16)
        send[j - 1][at + 1] = dv[block].astype(B16)
        if at:
            send[j - 1][pl.ds(0, at)] = old_send[j - 1][...]
    sums_ref[pl.ds(HQ + g, 1), :] = jnp.sum(gk, axis=0, keepdims=True)
    sums_ref[pl.ds(HQ + KV + g, 1), :] = jnp.sum(dv, axis=0, keepdims=True)
    if gk_ref is not None:
        finish_heads(2, shards, (cos_ref, sin_ref), owns, backs, gk_ref, gv_ref)


def attend(
    g, shards, first, rank, q, do, bq, cosine, sine, ck, cv, kp, vp, bk, bv, far, far_k, far_v,
    before, owns, backs,
):
    tokens, slots = q.shape[0], ck.shape[0]
    slab = shards * tokens
    total = slab + shards * slots
    last = g == KV - 1
    smem = pl.BlockSpec(memory_space=pltpu.SMEM)
    vmem = pl.BlockSpec(memory_space=pltpu.VMEM)
    anywhere = pl.BlockSpec(memory_space=pl.ANY)
    wide = pl.BlockSpec((tokens, GROUP * HD), lambda i: (0, g))
    half = pl.BlockSpec((tokens, 2 * HD), lambda i: (0, 0))

    args = [first, rank]
    placed = [q, do, bq, cosine, sine, ck, cv, kp, vp, bk, bv, *far, *far_k, *far_v]
    aliases = {}
    if before is not None:
        out, gq, sums, send = before
        placed.append(sums)
        if g % 2:
            placed += send
        if last:
            placed += [*owns[:2], *backs]
    args += placed
    in_specs = [smem] * 2 + [vmem] * len(placed)
    if before is not None:
        aliases = {len(args): 0, len(args) + 1: 1}
        args += [out, gq]
        in_specs += [anywhere] * 2
    out_shape = [
        pltpu.HBM((tokens, HQ * HD), B16),
        pltpu.HBM((tokens, HQ * HD), B16),
        pltpu.VMEM((SUMS, HD), F32),
        pltpu.VMEM((2, tokens, HD), F32),
    ]
    out_specs = [wide, wide, vmem, vmem]
    out_shape += [pltpu.VMEM((2 + 2 * (g % 2), tokens, HD), B16)] * (shards - 1)
    out_specs += [vmem] * (shards - 1)
    if g + 2 < KV:
        out_shape.append(pltpu.VMEM((2 * slots, HD), B16))
        out_specs.append(vmem)
    if last:
        out_shape += [pltpu.HBM((tokens, KV * HD), B16)] * 2
        out_specs += [half] * 2
    results = pl.pallas_call(
        functools.partial(attend_kernel, g, shards),
        grid=(1,),
        in_specs=in_specs,
        out_shape=out_shape,
        out_specs=out_specs,
        scratch_shapes=[
            pltpu.VMEM((total, HD), B16), pltpu.VMEM((total, HD), B16),
            pltpu.VMEM((HD, total), B16), pltpu.VMEM((HD, total), B16),
            pltpu.VMEM((GROUP, HD), F32),
            pltpu.VMEM((HD, slab), F32), pltpu.VMEM((HD, slab), F32),
        ],
        input_output_aliases=aliases,
        compiler_params=params(),
        cost_estimate=pl.CostEstimate(
            flops=2 * GROUP * tokens * HD * (4 * total + 2 * slab),
            bytes_accessed=8 * tokens * GROUP * HD + 8 * total * HD,
            transcendentals=GROUP * tokens * total,
        ),
        name="attend",
    )(*args)
    out, gq, sums, own = results[:4]
    send = results[4:4 + shards - 1]
    return (out, gq, sums, send), own, results[4 + shards - 1:]


def finish_kernel(shards, *refs):
    owns, backs = refs[2:4], refs[4:4 + shards - 1]
    finish_heads(2, shards, refs[:2], owns, backs, *refs[-2:])


def finish(shards, cosine, sine, owns, backs, gk, gv):
    tokens = gk.shape[0]
    vmem = pl.BlockSpec(memory_space=pltpu.VMEM)
    args = [cosine, sine, *owns, *backs]
    return pl.pallas_call(
        functools.partial(finish_kernel, shards),
        grid=(1,),
        in_specs=[vmem] * len(args) + [pl.BlockSpec(memory_space=pl.ANY)] * 2,
        out_specs=[pl.BlockSpec((tokens, 2 * HD), lambda i: (0, 1))] * 2,
        out_shape=[pltpu.HBM(gk.shape, B16)] * 2,
        input_output_aliases={len(args): 0, len(args) + 1: 1},
        compiler_params=params(),
        cost_estimate=pl.CostEstimate(flops=0, bytes_accessed=1 << 19, transcendentals=0),
        name="finish",
    )(*args, gk, gv)


def sum_everywhere(x, axes):
    devices = lax.axis_size(axes)
    copies = jnp.broadcast_to(x[None], (devices,) + x.shape)
    return jnp.sum(lax.all_to_all(copies, axes, 0, 0, tiled=True), axis=0)


def body(q_proj, k_proj, v_proj, cache_k, cache_v, bias_q, bias_k, bias_v, start, dout):
    shards = lax.axis_size("seq")
    rank = lax.axis_index("seq").astype(jnp.int32)
    tokens = q_proj.shape[1]
    ck, cv, kp, vp = cache_k[0], cache_v[0], k_proj[0], v_proj[0]

    def ring(x, s):
        return lax.ppermute(x, "seq", [(i, (i + s) % shards) for i in range(shards)])

    def later(x, s):
        return lax.ppermute(x, "seq", [(i, i + s) for i in range(shards - s)])

    def earlier(x, s):
        return lax.ppermute(x, "seq", [(i + s, i) for i in range(shards - s)])

    shifts = range(1, shards)
    far_k = [later(kp, s) for s in shifts]
    far_v = [later(vp, s) for s in shifts]
    hbm = functools.partial(pltpu.with_memory_space_constraint, memory_space=pltpu.HBM)
    chunk = pack(0, hbm(ck), hbm(cv))
    far = [[ring(chunk, s) for s in shifts]]

    owners = lax.rem(rank - jnp.arange(shards, dtype=jnp.int32) + shards, shards)
    positions = start[0] + owners[:, None] * tokens + jnp.arange(tokens, dtype=jnp.int32)[None]
    lane = jnp.arange(HD, dtype=jnp.int32)
    freqs = jnp.exp(
        -(2.0 * (lane % (HD // 2)).astype(F32) / HD) * jnp.log(jnp.float32(1000000.0))
    )
    angles = positions.reshape(-1).astype(F32)[:, None] * freqs[None, :]
    cosine = jnp.cos(angles)
    sine = jnp.sin(angles) * jnp.where(lane < HD // 2, -1.0, 1.0).astype(F32)[None]

    far.append([ring(pack(1, ck, cv, cosine), s) for s in shifts])
    before, owns, backs = None, [], []
    for g in range(KV):
        before, own, more = attend(
            g, shards, start, rank.reshape(1), q_proj[0], dout[0], bias_q.reshape(HQ, HD),
            cosine, sine, ck, cv, kp, vp, bias_k.reshape(KV, HD), bias_v.reshape(KV, HD),
            far[g], far_k, far_v, before, owns, backs,
        )
        owns.append(own)
        if g + 2 < KV:
            far.append([ring(more[0], s) for s in shifts])
        if g % 2:
            backs = [earlier(x, s) for s, x in zip(shifts, before[3])]
    out, gq, sums, _ = before
    gk, gv = finish(shards, cosine, sine, owns[2:], backs, *more)
    sums = sum_everywhere(sums, ("dp", "seq"))
    return (
        out[None],
        gq[None],
        gk[None],
        gv[None],
        sums[:HQ].reshape(-1),
        sums[HQ:HQ + KV].reshape(-1),
        sums[HQ + KV:].reshape(-1),
    )


def solution(mesh):
    split = P("dp", "seq", None)
    return jax.shard_map(
        body,
        mesh=mesh,
        in_specs=(split,) * 5 + (P(), P(), P(), P("dp"), split),
        out_specs=(split,) * 4 + (P(), P(), P()),
        check_vma=False,
    )
```

```python
import functools
import itertools
import math

import jax
import jax.numpy as jnp
from jax import lax
from jax.experimental import pallas as pl
from jax.experimental.pallas import tpu as pltpu
from jax.sharding import PartitionSpec as P

HQ = 32
KV = 4
HD = 128
GROUP = 8
HEADS = 2
NEG = -1e30
SUMS = HQ + 2 * KV
VMEM = 28 * 1024 * 1024
F32, B16 = jnp.float32, jnp.bfloat16


def turn(x):
    return pltpu.roll(x, HD // 2, 1)


def dot(a, b, dims):
    return lax.dot_general(a, b, (dims, ((), ())), preferred_element_type=F32)


NT = ((1,), (1,))
NN = ((1,), (0,))
TN = ((0,), (0,))


def whole(shape):
    return pl.BlockSpec(shape, lambda i: (0,) * len(shape))


def column(rows, g):
    return pl.BlockSpec((rows, HD), lambda i: (0, g))


def params():
    return pltpu.CompilerParams(dimension_semantics=("arbitrary",), vmem_limit_bytes=VMEM)


def copy_chunk(g, ck_ref, cv_ref, out_ref):
    rows = ck_ref.shape[0]
    cols = pl.ds(g * HD, HD)
    out_ref[pl.ds(0, rows)] = ck_ref[:, cols]
    out_ref[pl.ds(rows, rows)] = cv_ref[:, cols]


def pack_kernel(ck_ref, cv_ref, *rest):
    copy_chunk(0, ck_ref, cv_ref, rest[-1])


def pack(g, ck, cv, *after):
    rows = ck.shape[0]
    return pl.pallas_call(
        pack_kernel,
        grid=(1,),
        in_specs=[column(rows, g)] * 2 + [pl.BlockSpec(memory_space=pl.ANY)] * len(after),
        out_specs=pl.BlockSpec(memory_space=pltpu.VMEM),
        out_shape=pltpu.VMEM((2 * rows, HD), B16),
        compiler_params=params(),
        cost_estimate=pl.CostEstimate(flops=0, bytes_accessed=8 * rows * HD, transcendentals=0),
        name="pack",
    )(ck, cv, *after)


def turn_back(x, cosine, sine):
    return x * cosine - turn(x) * sine


def finish_heads(heads, shards, tables, owns, backs, gk_ref, gv_ref):
    tokens = gk_ref.shape[0]
    cosine, sine = (t[pl.ds(0, tokens), :] for t in tables)
    for i in range(heads):
        dk, dv = owns[i][0], owns[i][1]
        for s in range(shards - 1):
            dk = dk + backs[s][2 * i].astype(F32)
            dv = dv + backs[s][2 * i + 1].astype(F32)
        cols = pl.ds(i * HD, HD)
        gk_ref[:, cols] = turn_back(dk, cosine, sine).astype(B16)
        gv_ref[:, cols] = dv.astype(B16)


def prep_kernel(
    tokens, q_ref, do_ref, bq_ref, bk_ref, bv_ref, cos_ref, sin_ref, ck_ref, cv_ref,
    qs_ref, dos_ref, dot_ref, bias_ref, cos_t_ref, sin_t_ref, pack_ref,
):
    g = pl.program_id(0)
    cosine, sine = cos_ref[pl.ds(0, tokens), :], sin_ref[pl.ds(0, tokens), :]
    bias_q = bq_ref[...].astype(F32)

    @pl.when(g == 0)
    def _():
        bias_ref[pl.ds(0, KV), :] = bk_ref[...].astype(F32)
        bias_ref[pl.ds(KV, KV), :] = bv_ref[...].astype(F32)
        cos_t_ref[...] = cosine.T
        sin_t_ref[...] = sine.T
        copy_chunk(1, ck_ref, cv_ref, pack_ref)

    for h in range(GROUP):
        cols = pl.ds(h * HD, HD)
        rows = pl.ds(pl.multiple_of((g * GROUP + h) * tokens, tokens), tokens)
        x = q_ref[:, cols].astype(F32) + bias_q[h:h + 1]
        qs_ref[rows, :] = (x * cosine + turn(x) * sine).astype(B16)
        do = do_ref[:, cols]
        dos_ref[rows, :] = do
        chain, part = h // HEADS, h % HEADS
        place = pl.ds(pl.multiple_of((g * (GROUP // HEADS) + chain) * HD, HD), HD)
        dot_ref[place, pl.ds(part * tokens, tokens)] = do.T


def prep(q, do, bq, bk, bv, cosine, sine, ck, cv):
    tokens, slots = q.shape[0], ck.shape[0]
    vmem = pl.BlockSpec(memory_space=pltpu.VMEM)
    wide = pl.BlockSpec((tokens, GROUP * HD), lambda i: (0, i))
    out_shape = [
        pltpu.VMEM((HQ * tokens, HD), B16),
        pltpu.VMEM((HQ * tokens, HD), B16),
        pltpu.VMEM((HQ // HEADS * HD, HEADS * tokens), B16),
        pltpu.VMEM((2 * KV, HD), F32),
        pltpu.VMEM((HD, tokens), F32),
        pltpu.VMEM((HD, tokens), F32),
        pltpu.VMEM((2 * slots, HD), B16),
    ]
    return pl.pallas_call(
        functools.partial(prep_kernel, tokens),
        grid=(KV,),
        in_specs=[
            wide, wide, pl.BlockSpec((GROUP, HD), lambda i: (i, 0)),
            whole((KV, HD)), whole((KV, HD)), vmem, vmem, vmem, vmem,
        ],
        out_specs=[vmem] * len(out_shape),
        out_shape=out_shape,
        compiler_params=params(),
        cost_estimate=pl.CostEstimate(
            flops=4 * tokens * HQ * HD, bytes_accessed=12 * tokens * HQ * HD, transcendentals=0
        ),
        name="prep",
    )(q, do, bq, bk, bv, cosine, sine, ck, cv)


def alternate(first, second):
    pieces = [iter(first), iter(second)]
    while pieces:
        for piece in list(pieces):
            if next(piece, pieces) is pieces:
                pieces.remove(piece)


def fold(x, op):
    return op(x.reshape(x.shape[0] // 8, 8, x.shape[1]), axis=0)


def attend_kernel(g, shards, *refs):
    refs = list(refs)

    def take(count):
        taken = refs[:count]
        del refs[:count]
        return taken

    (first_ref, rank_ref, qs_ref, dos_ref, dot_ref, bias_ref, cos_t_ref, sin_t_ref,
     cos_ref, sin_ref, ck_ref, cv_ref, kp_ref, vp_ref) = take(14)
    far = take(shards - 1)
    far_k = take(shards - 1)
    far_v = take(shards - 1)
    old_sums_ref = take(1)[0] if g else None
    old_send = take(shards - 1) if g % 2 else []
    owns = take(2) if g == KV - 1 else []
    backs = take(shards - 1) if g == KV - 1 else []
    if g:
        take(2)
    out_ref, gq_ref, sums_ref, own_ref = take(4)
    send = take(shards - 1)
    pack_ref = take(1)[0] if g + 2 < KV else None
    gk_ref, gv_ref = take(2) if g == KV - 1 else (None, None)
    keys, values, keys_t, values_t, dk_acc, dv_acc = take(6)
    chains = [take(3), take(3)]
    tokens = kp_ref.shape[0]
    slots = ck_ref.shape[0]
    prefix = shards * slots
    slab = shards * tokens
    total = prefix + slab
    first = first_ref[0]
    rank = rank_ref[0]
    mine = pl.ds(g * HD, HD)

    if pack_ref is not None:
        copy_chunk(g + 2, ck_ref, cv_ref, pack_ref)
    keys[pl.ds(0, slots)] = ck_ref[:, mine]
    values[pl.ds(0, slots)] = cv_ref[:, mine]
    for s in range(1, shards):
        keys[pl.ds(s * slots, slots)] = far[s - 1][pl.ds(0, slots)]
        values[pl.ds(s * slots, slots)] = far[s - 1][pl.ds(slots, slots)]
    for s in range(shards):
        rows = pl.ds(s * tokens, tokens)
        kp, vp = (kp_ref, vp_ref) if s == 0 else (far_k[s - 1], far_v[s - 1])
        k = kp[:, mine].astype(F32) + bias_ref[g:g + 1, :]
        k = k * cos_ref[rows, :] + turn(k) * sin_ref[rows, :]
        v = vp[:, mine].astype(F32) + bias_ref[KV + g:KV + g + 1, :]
        place = pl.ds(prefix + s * tokens, tokens)
        keys[place] = k.astype(B16)
        values[place] = v.astype(B16)
    keys_t[...] = keys[...].T
    values_t[...] = values[...].T
    sums_ref[...] = jnp.zeros_like(sums_ref) if old_sums_ref is None else old_sums_ref[...]
    dk_acc[...] = jnp.zeros_like(dk_acc)
    dv_acc[...] = jnp.zeros_like(dv_acc)

    width = HEADS * tokens
    scale = HD ** -0.5
    blocks = range(0, total, tokens)
    tile = 2 * tokens
    tiles = range(0, total, tile)

    def allowed(start, s):
        row = lax.broadcasted_iota(jnp.int32, s.shape, 0)
        if start < prefix:
            owner = lax.rem(rank - start // slots + shards, shards)
            return row < first - owner * slots - start % slots
        if start < prefix + tokens:
            return row <= (lax.broadcasted_iota(jnp.int32, s.shape, 1) & (tokens - 1))
        return row < jnp.where(rank >= (start - prefix) // tokens, tokens, 0)

    class Chain:
        def __init__(self, index, scratch):
            self.index = index
            self.s, self.pb, self.ds = scratch
            self.rows = pl.ds(pl.multiple_of(index * width, width), width)
            self.top = jnp.full((8, width), NEG, F32)

        def scores(self):
            q = qs_ref[self.rows, :]
            for start in tiles:
                s = dot(keys[pl.ds(start, tile), :], q, NT)
                for i in range(0, tile, tokens):
                    part = s[i:i + tokens]
                    part = jnp.where(allowed(start + i, part), part, NEG)
                    self.s[pl.ds(start + i, tokens), :] = part
                    self.top = jnp.maximum(self.top, fold(part, jnp.max))
                yield

        def softmax(self):
            top = jnp.max(self.top, axis=0, keepdims=True)
            total_e = jnp.zeros((8, width), F32)
            for start in blocks:
                rows = pl.ds(start, tokens)
                e = jnp.exp2((self.s[rows, :] - top) * (scale * math.log2(math.e)))
                self.s[rows, :] = e
                total_e = total_e + fold(e, jnp.sum)
                yield
            self.inverse = 1.0 / jnp.sum(total_e, axis=0, keepdims=True)
            for start in blocks:
                rows = pl.ds(start, tokens)
                self.pb[rows, :] = (self.s[rows, :] * self.inverse).astype(B16)
                yield

        def heads(self):
            for i in range(HEADS):
                head = self.index * HEADS + i
                yield (
                    slice(i * tokens, (i + 1) * tokens),
                    pl.ds(pl.multiple_of((head - g * GROUP) * HD, HD), HD),
                    head,
                )

        def output(self):
            o = dot(values_t[...], self.pb[...], NN).astype(B16)
            place = pl.ds(pl.multiple_of(self.index * HD, HD), HD)
            do = dot_ref[place, :].astype(F32)
            self.delta = jnp.sum(do * o.astype(F32), axis=0, keepdims=True)
            yield
            for part, cols, _ in self.heads():
                out_ref[:, cols] = o[:, part].T
            yield

        def dscore(self):
            do = dos_ref[self.rows, :]
            for start in tiles:
                rows = pl.ds(start, tile)
                dp = dot(values[rows, :], do, NT)
                p = self.s[rows, :] * self.inverse
                self.ds[rows, :] = (p * (dp - self.delta)).astype(B16)
                yield

        def grads(self):
            last = pl.ds(prefix, slab)
            dk_acc[...] += dot(self.ds[last, :], qs_ref[self.rows, :], NN)
            dv_acc[...] += dot(self.pb[last, :], dos_ref[self.rows, :], NN)
            yield
            dq = (dot(keys_t[...], self.ds[...], NN) * scale).astype(B16).astype(F32)
            yield
            for part, cols, head in self.heads():
                x = dq[:, part]
                other = jnp.concatenate([x[HD // 2:], x[:HD // 2]], axis=0)
                x = (x * cos_t_ref[...] - other * sin_t_ref[...]).T
                gq_ref[:, cols] = x.astype(B16)
                sums_ref[pl.ds(head, 1), :] = jnp.sum(x, axis=0, keepdims=True)
            yield

    def pair(i, carry):
        index = g * (GROUP // HEADS) + 2 * i
        a, b = Chain(index, chains[0]), Chain(index + 1, chains[1])
        for _ in a.scores():
            pass
        alternate(b.scores(), a.softmax())
        alternate(itertools.chain(a.output(), a.dscore()), b.softmax())
        alternate(b.output(), a.grads())
        for _ in b.dscore():
            pass
        for _ in b.grads():
            pass
        return carry

    lax.fori_loop(0, GROUP // (2 * HEADS), pair, 0)

    dk = dk_acc[...] * scale
    dv = dv_acc[...]
    gk = turn_back(dk, cos_ref[...], sin_ref[...])
    own_ref[0] = dk[:tokens]
    own_ref[1] = dv[:tokens]
    at = 2 * (g % 2)
    for j in range(1, shards):
        block = slice(j * tokens, (j + 1) * tokens)
        send[j - 1][at] = dk[block].astype(B16)
        send[j - 1][at + 1] = dv[block].astype(B16)
        if at:
            send[j - 1][pl.ds(0, at)] = old_send[j - 1][...]
    sums_ref[pl.ds(HQ + g, 1), :] = jnp.sum(gk, axis=0, keepdims=True)
    sums_ref[pl.ds(HQ + KV + g, 1), :] = jnp.sum(dv, axis=0, keepdims=True)
    if gk_ref is not None:
        finish_heads(2, shards, (cos_ref, sin_ref), owns, backs, gk_ref, gv_ref)


def attend(
    g, shards, first, rank, prepared, cosine, sine, ck, cv, kp, vp, far, far_k, far_v,
    before, owns, backs,
):
    tokens, slots = kp.shape[0], ck.shape[0]
    slab = shards * tokens
    total = slab + shards * slots
    last = g == KV - 1
    smem = pl.BlockSpec(memory_space=pltpu.SMEM)
    vmem = pl.BlockSpec(memory_space=pltpu.VMEM)
    anywhere = pl.BlockSpec(memory_space=pl.ANY)
    wide = pl.BlockSpec((tokens, GROUP * HD), lambda i: (0, g))
    half = pl.BlockSpec((tokens, 2 * HD), lambda i: (0, 0))

    args = [first, rank]
    placed = [*prepared, cosine, sine, ck, cv, kp, vp, *far, *far_k, *far_v]
    aliases = {}
    if before is not None:
        out, gq, sums, send = before
        placed.append(sums)
        if g % 2:
            placed += send
        if last:
            placed += [*owns[:2], *backs]
    args += placed
    in_specs = [smem] * 2 + [vmem] * len(placed)
    if before is not None:
        aliases = {len(args): 0, len(args) + 1: 1}
        args += [out, gq]
        in_specs += [anywhere] * 2
    out_shape = [
        pltpu.HBM((tokens, HQ * HD), B16),
        pltpu.HBM((tokens, HQ * HD), B16),
        pltpu.VMEM((SUMS, HD), F32),
        pltpu.VMEM((2, tokens, HD), F32),
    ]
    out_specs = [wide, wide, vmem, vmem]
    out_shape += [pltpu.VMEM((2 + 2 * (g % 2), tokens, HD), B16)] * (shards - 1)
    out_specs += [vmem] * (shards - 1)
    if g + 2 < KV:
        out_shape.append(pltpu.VMEM((2 * slots, HD), B16))
        out_specs.append(vmem)
    if last:
        out_shape += [pltpu.HBM((tokens, KV * HD), B16)] * 2
        out_specs += [half] * 2
    results = pl.pallas_call(
        functools.partial(attend_kernel, g, shards),
        grid=(1,),
        in_specs=in_specs,
        out_shape=out_shape,
        out_specs=out_specs,
        scratch_shapes=[
            pltpu.VMEM((total, HD), B16), pltpu.VMEM((total, HD), B16),
            pltpu.VMEM((HD, total), B16), pltpu.VMEM((HD, total), B16),
            pltpu.VMEM((slab, HD), F32), pltpu.VMEM((slab, HD), F32),
        ] + [
            pltpu.VMEM((total, HEADS * tokens), kind) for kind in (F32, B16, B16) * 2
        ],
        input_output_aliases=aliases,
        compiler_params=params(),
        cost_estimate=pl.CostEstimate(
            flops=2 * GROUP * tokens * HD * (4 * total + 2 * slab),
            bytes_accessed=8 * tokens * GROUP * HD + 8 * total * HD,
            transcendentals=GROUP * tokens * total,
        ),
        name="attend",
    )(*args)
    out, gq, sums, own = results[:4]
    send = results[4:4 + shards - 1]
    return (out, gq, sums, send), own, results[4 + shards - 1:]


def finish_kernel(shards, *refs):
    owns, backs = refs[2:4], refs[4:4 + shards - 1]
    sums, other = refs[4 + shards - 1:4 + shards + 1]
    gk_ref, gv_ref, *parts = refs[-5:]
    finish_heads(2, shards, refs[:2], owns, backs, gk_ref, gv_ref)
    start = 0
    for part in parts:
        rows = pl.ds(start, part.shape[0])
        part[...] = sums[rows, :] + other[rows, :]
        start += part.shape[0]


def finish(shards, cosine, sine, owns, backs, sums, other, gk, gv):
    tokens = gk.shape[0]
    vmem = pl.BlockSpec(memory_space=pltpu.VMEM)
    args = [cosine, sine, *owns, *backs, sums, other]
    heads = [(HQ, HD), (KV, HD), (KV, HD)]
    return pl.pallas_call(
        functools.partial(finish_kernel, shards),
        grid=(1,),
        in_specs=[vmem] * len(args) + [pl.BlockSpec(memory_space=pl.ANY)] * 2,
        out_specs=[pl.BlockSpec((tokens, 2 * HD), lambda i: (0, 1))] * 2
        + [whole(shape) for shape in heads],
        out_shape=[pltpu.HBM(gk.shape, B16)] * 2 + [pltpu.HBM(shape, F32) for shape in heads],
        input_output_aliases={len(args): 0, len(args) + 1: 1},
        compiler_params=params(),
        cost_estimate=pl.CostEstimate(flops=0, bytes_accessed=1 << 19, transcendentals=0),
        name="finish",
    )(*args, gk, gv)


def exchanges(axis):
    size = lax.axis_size(axis)
    step = 1
    while step < size:
        yield axis, [(i, i ^ step) for i in range(size)]
        step *= 2


def sum_but_last(x, axes):
    other = None
    for axis in axes:
        for name, perm in exchanges(axis):
            x = x if other is None else x + other
            other = lax.ppermute(x, name, perm)
    return x, other


def body(q_proj, k_proj, v_proj, cache_k, cache_v, bias_q, bias_k, bias_v, start, dout):
    shards = lax.axis_size("seq")
    rank = lax.axis_index("seq").astype(jnp.int32)
    tokens = q_proj.shape[1]
    ck, cv, kp, vp = cache_k[0], cache_v[0], k_proj[0], v_proj[0]

    def ring(x, s):
        return lax.ppermute(x, "seq", [(i, (i + s) % shards) for i in range(shards)])

    def later(x, s):
        return lax.ppermute(x, "seq", [(i, i + s) for i in range(shards - s)])

    def earlier(x, s):
        return lax.ppermute(x, "seq", [(i + s, i) for i in range(shards - s)])

    shifts = range(1, shards)
    far_k = [later(kp, s) for s in shifts]
    far_v = [later(vp, s) for s in shifts]
    hbm = functools.partial(pltpu.with_memory_space_constraint, memory_space=pltpu.HBM)
    chunk = pack(0, hbm(ck), hbm(cv))
    far = [[ring(chunk, s) for s in shifts]]

    owners = lax.rem(rank - jnp.arange(shards, dtype=jnp.int32) + shards, shards)
    positions = start[0] + owners[:, None] * tokens + jnp.arange(tokens, dtype=jnp.int32)[None]
    lane = jnp.arange(HD, dtype=jnp.int32)
    freqs = jnp.exp(
        -(2.0 * (lane % (HD // 2)).astype(F32) / HD) * jnp.log(jnp.float32(1000000.0))
    )
    angles = positions.reshape(-1).astype(F32)[:, None] * freqs[None, :]
    cosine = jnp.cos(angles)
    sine = jnp.sin(angles) * jnp.where(lane < HD // 2, -1.0, 1.0).astype(F32)[None]

    *prepared, chunk = prep(
        hbm(q_proj[0]), hbm(dout[0]), hbm(bias_q.reshape(HQ, HD)),
        hbm(bias_k.reshape(KV, HD)), hbm(bias_v.reshape(KV, HD)), cosine, sine, ck, cv,
    )
    far.append([ring(chunk, s) for s in shifts])
    before, owns, backs = None, [], []
    for g in range(KV):
        before, own, more = attend(
            g, shards, start, rank.reshape(1), prepared, cosine, sine, ck, cv, kp, vp,
            far[g], far_k, far_v, before, owns, backs,
        )
        owns.append(own)
        if g + 2 < KV:
            far.append([ring(more[0], s) for s in shifts])
        if g % 2:
            backs = [earlier(x, s) for s, x in zip(shifts, before[3])]
    out, gq, sums, _ = before
    sums, other = sum_but_last(sums, ("dp", "seq"))
    gk, gv, *sums = finish(shards, cosine, sine, owns[2:], backs, sums, other, *more)
    return (out[None], gq[None], gk[None], gv[None], *[x.reshape(-1) for x in sums])


def solution(mesh):
    split = P("dp", "seq", None)
    return jax.shard_map(
        body,
        mesh=mesh,
        in_specs=(split,) * 5 + (P(), P(), P(), P("dp"), split),
        out_specs=(split,) * 4 + (P(), P(), P()),
        check_vma=False,
    )
```

```python
import functools
import itertools
import math

import jax
import jax.numpy as jnp
from jax import lax
from jax.experimental import pallas as pl
from jax.experimental.pallas import tpu as pltpu
from jax.sharding import PartitionSpec as P

HQ = 32
KV = 4
HD = 128
GROUP = 8
HEADS = 2
NEG = -1e30
SUMS = HQ + 2 * KV
VMEM = 28 * 1024 * 1024
F32, B16 = jnp.float32, jnp.bfloat16


def turn(x):
    return pltpu.roll(x, HD // 2, 1)


def dot(a, b, dims):
    return lax.dot_general(a, b, (dims, ((), ())), preferred_element_type=F32)


NN = ((1,), (0,))


def whole(shape):
    return pl.BlockSpec(shape, lambda i: (0,) * len(shape))


def column(rows, g):
    return pl.BlockSpec((rows, HD), lambda i: (0, g))


def params():
    return pltpu.CompilerParams(dimension_semantics=("arbitrary",), vmem_limit_bytes=VMEM)


def copy_chunk(g, ck_ref, cv_ref, out_ref):
    rows = ck_ref.shape[0]
    cols = pl.ds(g * HD, HD)
    out_ref[pl.ds(0, rows)] = ck_ref[:, cols]
    out_ref[pl.ds(rows, rows)] = cv_ref[:, cols]


def pack_kernel(ck_ref, cv_ref, *rest):
    copy_chunk(0, ck_ref, cv_ref, rest[-1])


def pack(g, ck, cv, *after):
    rows = ck.shape[0]
    return pl.pallas_call(
        pack_kernel,
        grid=(1,),
        in_specs=[column(rows, g)] * 2 + [pl.BlockSpec(memory_space=pl.ANY)] * len(after),
        out_specs=pl.BlockSpec(memory_space=pltpu.VMEM),
        out_shape=pltpu.VMEM((2 * rows, HD), B16),
        compiler_params=params(),
        cost_estimate=pl.CostEstimate(flops=0, bytes_accessed=8 * rows * HD, transcendentals=0),
        name="pack",
    )(ck, cv, *after)


def turn_back(x, cosine, sine):
    return x * cosine - turn(x) * sine


def finish_heads(heads, shards, tables, owns, backs, gk_ref, gv_ref):
    tokens = gk_ref.shape[0]
    cosine, sine = (t[pl.ds(0, tokens), :] for t in tables)
    for i in range(heads):
        dk, dv = owns[i][0], owns[i][1]
        for s in range(shards - 1):
            dk = dk + backs[s][2 * i].astype(F32)
            dv = dv + backs[s][2 * i + 1].astype(F32)
        cols = pl.ds(i * HD, HD)
        gk_ref[:, cols] = turn_back(dk, cosine, sine).astype(B16)
        gv_ref[:, cols] = dv.astype(B16)


def prep_kernel(
    tokens, q_ref, do_ref, bq_ref, bk_ref, bv_ref, cos_ref, sin_ref, ck_ref, cv_ref,
    qs_ref, qst_ref, dos_ref, dot_ref, bias_ref, cos_t_ref, sin_t_ref, ck_t_ref, cv_t_ref, pack_ref,
):
    g = pl.program_id(0)
    cosine, sine = cos_ref[pl.ds(0, tokens), :], sin_ref[pl.ds(0, tokens), :]
    bias_q = bq_ref[...].astype(F32)

    @pl.when(g == 0)
    def _():
        bias_ref[pl.ds(0, KV), :] = bk_ref[...].astype(F32)
        bias_ref[pl.ds(KV, KV), :] = bv_ref[...].astype(F32)
        cos_t_ref[...] = cosine.T
        sin_t_ref[...] = sine.T
        copy_chunk(1, ck_ref, cv_ref, pack_ref)

    for h in range(GROUP):
        cols = pl.ds(h * HD, HD)
        rows = pl.ds(pl.multiple_of((g * GROUP + h) * tokens, tokens), tokens)
        x = q_ref[:, cols].astype(F32) + bias_q[h:h + 1]
        x = (x * cosine + turn(x) * sine).astype(B16)
        qs_ref[rows, :] = x
        do = do_ref[:, cols]
        dos_ref[rows, :] = do
        chain, part = h // HEADS, h % HEADS
        place = pl.ds(pl.multiple_of((g * (GROUP // HEADS) + chain) * HD, HD), HD)
        qst_ref[place, pl.ds(part * tokens, tokens)] = x.T
        dot_ref[place, pl.ds(part * tokens, tokens)] = do.T
    mine = pl.ds(pl.multiple_of(g * HD, HD), HD)
    ck_t_ref[mine, :] = ck_ref[:, mine].T
    cv_t_ref[mine, :] = cv_ref[:, mine].T


def prep(q, do, bq, bk, bv, cosine, sine, ck, cv):
    tokens, slots = q.shape[0], ck.shape[0]
    vmem = pl.BlockSpec(memory_space=pltpu.VMEM)
    wide = pl.BlockSpec((tokens, GROUP * HD), lambda i: (0, i))
    stacked = pltpu.VMEM((HQ * tokens, HD), B16)
    turned = pltpu.VMEM((HQ // HEADS * HD, HEADS * tokens), B16)
    out_shape = [
        stacked, turned, stacked, turned,
        pltpu.VMEM((2 * KV, HD), F32),
        pltpu.VMEM((HD, tokens), F32),
        pltpu.VMEM((HD, tokens), F32),
        pltpu.VMEM((KV * HD, slots), B16),
        pltpu.VMEM((KV * HD, slots), B16),
        pltpu.VMEM((2 * slots, HD), B16),
    ]
    return pl.pallas_call(
        functools.partial(prep_kernel, tokens),
        grid=(KV,),
        in_specs=[
            wide, wide, pl.BlockSpec((GROUP, HD), lambda i: (i, 0)),
            whole((KV, HD)), whole((KV, HD)), vmem, vmem, vmem, vmem,
        ],
        out_specs=[vmem] * len(out_shape),
        out_shape=out_shape,
        compiler_params=params(),
        cost_estimate=pl.CostEstimate(
            flops=4 * tokens * HQ * HD, bytes_accessed=12 * tokens * HQ * HD, transcendentals=0
        ),
        name="prep",
    )(q, do, bq, bk, bv, cosine, sine, ck, cv)


def alternate(first, second):
    pieces = [iter(first), iter(second)]
    while pieces:
        for piece in list(pieces):
            if next(piece, pieces) is pieces:
                pieces.remove(piece)


def fold(x, op):
    return op(x.reshape(x.shape[0] // 8, 8, x.shape[1]), axis=0)


def attend_kernel(g, shards, *refs):
    refs = list(refs)

    def take(count):
        taken = refs[:count]
        del refs[:count]
        return taken

    (first_ref, rank_ref, qs_ref, qst_ref, dos_ref, dot_ref, bias_ref, cos_t_ref, sin_t_ref,
     ck_t_ref, cv_t_ref, cos_ref, sin_ref, ck_ref, cv_ref, kp_ref, vp_ref) = take(17)
    far = take(shards - 1)
    far_k = take(shards - 1)
    far_v = take(shards - 1)
    old_sums_ref = take(1)[0] if g else None
    old_send = take(shards - 1) if g % 2 else []
    owns = take(2) if g == KV - 1 else []
    backs = take(shards - 1) if g == KV - 1 else []
    if g:
        take(2)
    out_ref, gq_ref, sums_ref, own_ref = take(4)
    send = take(shards - 1)
    pack_ref = take(1)[0] if g + 2 < KV else None
    gk_ref, gv_ref = take(2) if g == KV - 1 else (None, None)
    keys, values, keys_t, values_t, dk_acc, dv_acc = take(6)
    chains = [take(3), take(3)]
    tokens = kp_ref.shape[0]
    slots = ck_ref.shape[0]
    prefix = shards * slots
    slab = shards * tokens
    total = prefix + slab
    first = first_ref[0]
    rank = rank_ref[0]
    mine = pl.ds(g * HD, HD)

    if pack_ref is not None:
        copy_chunk(g + 2, ck_ref, cv_ref, pack_ref)
    keys[pl.ds(0, slots)] = ck_ref[:, mine]
    values[pl.ds(0, slots)] = cv_ref[:, mine]
    for s in range(1, shards):
        keys[pl.ds(s * slots, slots)] = far[s - 1][pl.ds(0, slots)]
        values[pl.ds(s * slots, slots)] = far[s - 1][pl.ds(slots, slots)]
    for s in range(shards):
        rows = pl.ds(s * tokens, tokens)
        kp, vp = (kp_ref, vp_ref) if s == 0 else (far_k[s - 1], far_v[s - 1])
        k = kp[:, mine].astype(F32) + bias_ref[g:g + 1, :]
        k = k * cos_ref[rows, :] + turn(k) * sin_ref[rows, :]
        v = vp[:, mine].astype(F32) + bias_ref[KV + g:KV + g + 1, :]
        place = pl.ds(prefix + s * tokens, tokens)
        keys[place] = k.astype(B16)
        values[place] = v.astype(B16)
    keys_t[:, pl.ds(0, slots)] = ck_t_ref[mine, :]
    values_t[:, pl.ds(0, slots)] = cv_t_ref[mine, :]
    rest = pl.ds(slots, prefix - slots + slab)
    keys_t[:, rest] = keys[rest, :].T
    values_t[:, rest] = values[rest, :].T
    sums_ref[...] = jnp.zeros_like(sums_ref) if old_sums_ref is None else old_sums_ref[...]
    dk_acc[...] = jnp.zeros_like(dk_acc)
    dv_acc[...] = jnp.zeros_like(dv_acc)

    width = HEADS * tokens
    scale = HD ** -0.5
    blocks = range(0, total, tokens)
    tile = 2 * tokens
    tiles = range(0, total, tile)

    def allowed(start, s):
        row = lax.broadcasted_iota(jnp.int32, s.shape, 0)
        if start < prefix:
            owner = lax.rem(rank - start // slots + shards, shards)
            return row < first - owner * slots - start % slots
        if start < prefix + tokens:
            return row <= (lax.broadcasted_iota(jnp.int32, s.shape, 1) & (tokens - 1))
        return row < jnp.where(rank >= (start - prefix) // tokens, tokens, 0)

    class Chain:
        def __init__(self, index, scratch):
            self.index = index
            self.s, self.pb, self.ds = scratch
            self.rows = pl.ds(pl.multiple_of(index * width, width), width)
            self.place = pl.ds(pl.multiple_of(index * HD, HD), HD)
            self.top = jnp.full((8, width), NEG, F32)

        def scores(self):
            q = qst_ref[self.place, :]
            for start in tiles:
                s = dot(keys[pl.ds(start, tile), :], q, NN)
                for i in range(0, tile, tokens):
                    part = s[i:i + tokens]
                    part = jnp.where(allowed(start + i, part), part, NEG)
                    self.s[pl.ds(start + i, tokens), :] = part
                    self.top = jnp.maximum(self.top, fold(part, jnp.max))
                yield

        def softmax(self):
            top = jnp.max(self.top, axis=0, keepdims=True)
            total_e = jnp.zeros((8, width), F32)
            for start in blocks:
                rows = pl.ds(start, tokens)
                e = jnp.exp2((self.s[rows, :] - top) * (scale * math.log2(math.e)))
                self.s[rows, :] = e
                total_e = total_e + fold(e, jnp.sum)
                yield
            self.inverse = 1.0 / jnp.sum(total_e, axis=0, keepdims=True)
            for start in blocks:
                rows = pl.ds(start, tokens)
                self.pb[rows, :] = (self.s[rows, :] * self.inverse).astype(B16)
                yield

        def heads(self):
            for i in range(HEADS):
                head = self.index * HEADS + i
                yield (
                    slice(i * tokens, (i + 1) * tokens),
                    pl.ds(pl.multiple_of((head - g * GROUP) * HD, HD), HD),
                    head,
                )

        def output(self):
            o = dot(values_t[...], self.pb[...], NN).astype(B16)
            do = dot_ref[self.place, :].astype(F32)
            self.delta = jnp.sum(do * o.astype(F32), axis=0, keepdims=True)
            yield
            for part, cols, _ in self.heads():
                out_ref[:, cols] = o[:, part].T
            yield

        def dscore(self):
            do = dot_ref[self.place, :]
            for start in tiles:
                rows = pl.ds(start, tile)
                dp = dot(values[rows, :], do, NN)
                p = self.s[rows, :] * self.inverse
                self.ds[rows, :] = (p * (dp - self.delta)).astype(B16)
                yield

        def grads(self):
            last = pl.ds(prefix, slab)
            dk_acc[...] += dot(self.ds[last, :], qs_ref[self.rows, :], NN)
            dv_acc[...] += dot(self.pb[last, :], dos_ref[self.rows, :], NN)
            yield
            dq = (dot(keys_t[...], self.ds[...], NN) * scale).astype(B16).astype(F32)
            yield
            for part, cols, head in self.heads():
                x = dq[:, part]
                other = jnp.concatenate([x[HD // 2:], x[:HD // 2]], axis=0)
                x = (x * cos_t_ref[...] - other * sin_t_ref[...]).T
                gq_ref[:, cols] = x.astype(B16)
                sums_ref[pl.ds(head, 1), :] = jnp.sum(x, axis=0, keepdims=True)
            yield

    def pair(i, carry):
        index = g * (GROUP // HEADS) + 2 * i
        a, b = Chain(index, chains[0]), Chain(index + 1, chains[1])
        for _ in a.scores():
            pass
        alternate(b.scores(), a.softmax())
        alternate(itertools.chain(a.output(), a.dscore()), b.softmax())
        alternate(b.output(), a.grads())
        for _ in b.dscore():
            pass
        for _ in b.grads():
            pass
        return carry

    lax.fori_loop(0, GROUP // (2 * HEADS), pair, 0)

    dk = dk_acc[...] * scale
    dv = dv_acc[...]
    gk = turn_back(dk, cos_ref[...], sin_ref[...])
    own_ref[0] = dk[:tokens]
    own_ref[1] = dv[:tokens]
    at = 2 * (g % 2)
    for j in range(1, shards):
        block = slice(j * tokens, (j + 1) * tokens)
        send[j - 1][at] = dk[block].astype(B16)
        send[j - 1][at + 1] = dv[block].astype(B16)
        if at:
            send[j - 1][pl.ds(0, at)] = old_send[j - 1][...]
    sums_ref[pl.ds(HQ + g, 1), :] = jnp.sum(gk, axis=0, keepdims=True)
    sums_ref[pl.ds(HQ + KV + g, 1), :] = jnp.sum(dv, axis=0, keepdims=True)
    if gk_ref is not None:
        finish_heads(2, shards, (cos_ref, sin_ref), owns, backs, gk_ref, gv_ref)


def attend(
    g, shards, first, rank, prepared, cosine, sine, ck, cv, kp, vp, far, far_k, far_v,
    before, owns, backs,
):
    tokens, slots = kp.shape[0], ck.shape[0]
    slab = shards * tokens
    total = slab + shards * slots
    last = g == KV - 1
    smem = pl.BlockSpec(memory_space=pltpu.SMEM)
    vmem = pl.BlockSpec(memory_space=pltpu.VMEM)
    anywhere = pl.BlockSpec(memory_space=pl.ANY)
    wide = pl.BlockSpec((tokens, GROUP * HD), lambda i: (0, g))
    half = pl.BlockSpec((tokens, 2 * HD), lambda i: (0, 0))

    args = [first, rank]
    placed = [*prepared, cosine, sine, ck, cv, kp, vp, *far, *far_k, *far_v]
    aliases = {}
    if before is not None:
        out, gq, sums, send = before
        placed.append(sums)
        if g % 2:
            placed += send
        if last:
            placed += [*owns[:2], *backs]
    args += placed
    in_specs = [smem] * 2 + [vmem] * len(placed)
    if before is not None:
        aliases = {len(args): 0, len(args) + 1: 1}
        args += [out, gq]
        in_specs += [anywhere] * 2
    out_shape = [
        pltpu.HBM((tokens, HQ * HD), B16),
        pltpu.HBM((tokens, HQ * HD), B16),
        pltpu.VMEM((SUMS, HD), F32),
        pltpu.VMEM((2, tokens, HD), F32),
    ]
    out_specs = [wide, wide, vmem, vmem]
    out_shape += [pltpu.VMEM((2 + 2 * (g % 2), tokens, HD), B16)] * (shards - 1)
    out_specs += [vmem] * (shards - 1)
    if g + 2 < KV:
        out_shape.append(pltpu.VMEM((2 * slots, HD), B16))
        out_specs.append(vmem)
    if last:
        out_shape += [pltpu.HBM((tokens, KV * HD), B16)] * 2
        out_specs += [half] * 2
    results = pl.pallas_call(
        functools.partial(attend_kernel, g, shards),
        grid=(1,),
        in_specs=in_specs,
        out_shape=out_shape,
        out_specs=out_specs,
        scratch_shapes=[
            pltpu.VMEM((total, HD), B16), pltpu.VMEM((total, HD), B16),
            pltpu.VMEM((HD, total), B16), pltpu.VMEM((HD, total), B16),
            pltpu.VMEM((slab, HD), F32), pltpu.VMEM((slab, HD), F32),
        ] + [
            pltpu.VMEM((total, HEADS * tokens), kind) for kind in (F32, B16, B16) * 2
        ],
        input_output_aliases=aliases,
        compiler_params=params(),
        cost_estimate=pl.CostEstimate(
            flops=2 * GROUP * tokens * HD * (4 * total + 2 * slab),
            bytes_accessed=8 * tokens * GROUP * HD + 8 * total * HD,
            transcendentals=GROUP * tokens * total,
        ),
        name="attend",
    )(*args)
    out, gq, sums, own = results[:4]
    send = results[4:4 + shards - 1]
    return (out, gq, sums, send), own, results[4 + shards - 1:]


def finish_kernel(shards, *refs):
    owns, backs = refs[2:4], refs[4:4 + shards - 1]
    sums = refs[4 + shards - 1]
    gk_ref, gv_ref, *parts = refs[-5:]
    finish_heads(2, shards, refs[:2], owns, backs, gk_ref, gv_ref)
    start = 0
    for part in parts:
        rows = pl.ds(start, part.shape[0])
        part[...] = sums[rows, :]
        start += part.shape[0]


def finish(shards, cosine, sine, owns, backs, sums, gk, gv):
    tokens = gk.shape[0]
    vmem = pl.BlockSpec(memory_space=pltpu.VMEM)
    args = [cosine, sine, *owns, *backs, sums]
    heads = [(HQ, HD), (KV, HD), (KV, HD)]
    return pl.pallas_call(
        functools.partial(finish_kernel, shards),
        grid=(1,),
        in_specs=[vmem] * len(args) + [pl.BlockSpec(memory_space=pl.ANY)] * 2,
        out_specs=[pl.BlockSpec((tokens, 2 * HD), lambda i: (0, 1))] * 2
        + [whole(shape) for shape in heads],
        out_shape=[pltpu.HBM(gk.shape, B16)] * 2 + [pltpu.HBM(shape, F32) for shape in heads],
        input_output_aliases={len(args): 0, len(args) + 1: 1},
        compiler_params=params(),
        cost_estimate=pl.CostEstimate(flops=0, bytes_accessed=1 << 19, transcendentals=0),
        name="finish",
    )(*args, gk, gv)


def sum_everywhere(x, axes):
    devices = lax.axis_size(axes)
    if devices & (devices - 1):
        return lax.psum(x, axes)
    stride = 1
    while stride < devices:
        size = min(devices // stride, 8)
        groups = [
            [base + low + i * stride for i in range(size)]
            for base in range(0, devices, size * stride)
            for low in range(stride)
        ]
        copies = jnp.broadcast_to(x[None], (size,) + x.shape)
        got = lax.all_to_all(copies, axes, 0, 0, axis_index_groups=groups, tiled=True)
        x = jnp.sum(got, axis=0)
        stride *= size
    return x


def body(q_proj, k_proj, v_proj, cache_k, cache_v, bias_q, bias_k, bias_v, start, dout):
    shards = lax.axis_size("seq")
    rank = lax.axis_index("seq").astype(jnp.int32)
    tokens = q_proj.shape[1]
    ck, cv, kp, vp = cache_k[0], cache_v[0], k_proj[0], v_proj[0]

    def ring(x, s):
        return lax.ppermute(x, "seq", [(i, (i + s) % shards) for i in range(shards)])

    def later(x, s):
        return lax.ppermute(x, "seq", [(i, i + s) for i in range(shards - s)])

    def earlier(x, s):
        return lax.ppermute(x, "seq", [(i + s, i) for i in range(shards - s)])

    shifts = range(1, shards)
    far_k = [later(kp, s) for s in shifts]
    far_v = [later(vp, s) for s in shifts]
    hbm = functools.partial(pltpu.with_memory_space_constraint, memory_space=pltpu.HBM)
    chunk = pack(0, hbm(ck), hbm(cv))
    far = [[ring(chunk, s) for s in shifts]]

    owners = lax.rem(rank - jnp.arange(shards, dtype=jnp.int32) + shards, shards)
    positions = start[0] + owners[:, None] * tokens + jnp.arange(tokens, dtype=jnp.int32)[None]
    lane = jnp.arange(HD, dtype=jnp.int32)
    freqs = jnp.exp(
        -(2.0 * (lane % (HD // 2)).astype(F32) / HD) * jnp.log(jnp.float32(1000000.0))
    )
    angles = positions.reshape(-1).astype(F32)[:, None] * freqs[None, :]
    cosine = jnp.cos(angles)
    sine = jnp.sin(angles) * jnp.where(lane < HD // 2, -1.0, 1.0).astype(F32)[None]

    *prepared, chunk = prep(
        hbm(q_proj[0]), hbm(dout[0]), hbm(bias_q.reshape(HQ, HD)),
        hbm(bias_k.reshape(KV, HD)), hbm(bias_v.reshape(KV, HD)), cosine, sine, ck, cv,
    )
    far.append([ring(chunk, s) for s in shifts])
    before, owns, backs = None, [], []
    for g in range(KV):
        before, own, more = attend(
            g, shards, start, rank.reshape(1), prepared, cosine, sine, ck, cv, kp, vp,
            far[g], far_k, far_v, before, owns, backs,
        )
        owns.append(own)
        if g + 2 < KV:
            far.append([ring(more[0], s) for s in shifts])
        if g % 2:
            backs = [earlier(x, s) for s, x in zip(shifts, before[3])]
    out, gq, sums, _ = before
    sums = sum_everywhere(sums, ("dp", "seq"))
    gk, gv, *sums = finish(shards, cosine, sine, owns[2:], backs, sums, *more)
    return (out[None], gq[None], gk[None], gv[None], *[x.reshape(-1) for x in sums])


def solution(mesh):
    split = P("dp", "seq", None)
    return jax.shard_map(
        body,
        mesh=mesh,
        in_specs=(split,) * 5 + (P(), P(), P(), P("dp"), split),
        out_specs=(split,) * 4 + (P(), P(), P()),
        check_vma=False,
    )
```

```python
import functools
import itertools
import math

import jax
import jax.numpy as jnp
from jax import lax
from jax.experimental import pallas as pl
from jax.experimental.pallas import tpu as pltpu
from jax.sharding import PartitionSpec as P

HQ = 32
KV = 4
HD = 128
GROUP = 8
HEADS = 2
NEG = -1e30
SUMS = HQ + 2 * KV
VMEM = 28 * 1024 * 1024
F32, B16 = jnp.float32, jnp.bfloat16


def turn(x):
    return pltpu.roll(x, HD // 2, 1)


def dot(a, b, dims):
    return lax.dot_general(a, b, (dims, ((), ())), preferred_element_type=F32)


NN = ((1,), (0,))


def whole(shape):
    return pl.BlockSpec(shape, lambda i: (0,) * len(shape))


def column(rows, g):
    return pl.BlockSpec((rows, HD), lambda i: (0, g))


def params():
    return pltpu.CompilerParams(dimension_semantics=("arbitrary",), vmem_limit_bytes=VMEM)


def copy_chunk(g, ck_ref, cv_ref, out_ref):
    rows = ck_ref.shape[0]
    cols = pl.ds(g * HD, HD)
    out_ref[pl.ds(0, rows)] = ck_ref[:, cols]
    out_ref[pl.ds(rows, rows)] = cv_ref[:, cols]


def pack_kernel(ck_ref, cv_ref, *rest):
    copy_chunk(0, ck_ref, cv_ref, rest[-1])


def pack(g, ck, cv, *after):
    rows = ck.shape[0]
    return pl.pallas_call(
        pack_kernel,
        grid=(1,),
        in_specs=[column(rows, g)] * 2 + [pl.BlockSpec(memory_space=pl.ANY)] * len(after),
        out_specs=pl.BlockSpec(memory_space=pltpu.VMEM),
        out_shape=pltpu.VMEM((2 * rows, HD), B16),
        compiler_params=params(),
        cost_estimate=pl.CostEstimate(flops=0, bytes_accessed=8 * rows * HD, transcendentals=0),
        name="pack",
    )(ck, cv, *after)


def turn_back(x, cosine, sine):
    return x * cosine - turn(x) * sine


def finish_heads(heads, shards, tables, owns, backs, gk_ref, gv_ref):
    tokens = gk_ref.shape[0]
    cosine, sine = (t[pl.ds(0, tokens), :] for t in tables)
    for i in range(heads):
        dk, dv = owns[i][0], owns[i][1]
        for s in range(shards - 1):
            dk = dk + backs[s][2 * i].astype(F32)
            dv = dv + backs[s][2 * i + 1].astype(F32)
        cols = pl.ds(i * HD, HD)
        gk_ref[:, cols] = turn_back(dk, cosine, sine).astype(B16)
        gv_ref[:, cols] = dv.astype(B16)


def write_mask(first, rank, shards, slots, mask_ref):
    tokens = mask_ref.shape[1]
    row = lax.broadcasted_iota(jnp.int32, (tokens, tokens), 0)
    col = lax.broadcasted_iota(jnp.int32, (tokens, tokens), 1)
    prefix = shards * slots
    for start in range(0, mask_ref.shape[0], tokens):
        if start < prefix:
            owner = lax.rem(rank - start // slots + shards, shards)
            seen = row < first - owner * slots - start % slots
        elif start == prefix:
            seen = row <= col
        else:
            seen = row < jnp.where(rank >= (start - prefix) // tokens, tokens, 0)
        mask_ref[pl.ds(start, tokens), :] = jnp.where(seen, 0.0, NEG).astype(B16)


def prep_kernel(
    tokens, shards, first_ref, rank_ref, q_ref, do_ref, bq_ref, bk_ref, bv_ref, cos_ref, sin_ref, ck_ref, cv_ref,
    qs_ref, qst_ref, dos_ref, dot_ref, bias_ref, cos_t_ref, sin_t_ref, ck_t_ref, cv_t_ref, mask_ref, pack_ref,
):
    g = pl.program_id(0)
    cosine, sine = cos_ref[pl.ds(0, tokens), :], sin_ref[pl.ds(0, tokens), :]
    bias_q = bq_ref[...].astype(F32)

    @pl.when(g == 0)
    def _():
        bias_ref[pl.ds(0, KV), :] = bk_ref[...].astype(F32)
        bias_ref[pl.ds(KV, KV), :] = bv_ref[...].astype(F32)
        cos_t_ref[...] = cosine.T
        sin_t_ref[...] = sine.T
        copy_chunk(1, ck_ref, cv_ref, pack_ref)
        write_mask(first_ref[0], rank_ref[0], shards, ck_ref.shape[0], mask_ref)

    row = lax.broadcasted_iota(jnp.int32, (tokens, tokens), 0)
    col = lax.broadcasted_iota(jnp.int32, (tokens, tokens), 1)
    one_hot = jnp.where(row == col, 1.0, 0.0).astype(B16)
    for h in range(GROUP):
        cols = pl.ds(h * HD, HD)
        rows = pl.ds(pl.multiple_of((g * GROUP + h) * tokens, tokens), tokens)
        x = q_ref[:, cols].astype(F32) + bias_q[h:h + 1]
        x = (x * cosine + turn(x) * sine).astype(B16)
        qs_ref[rows, :] = x
        do = do_ref[:, cols]
        dos_ref[rows, :] = do
        chain, part = h // HEADS, h % HEADS
        place = pl.ds(pl.multiple_of((g * (GROUP // HEADS) + chain) * HD, HD), HD)
        depth = HD + tokens
        upper = pl.multiple_of((g * (GROUP // HEADS) + chain) * depth, depth)
        lower = pl.multiple_of(upper + HD, HD)
        qst_ref[pl.ds(upper, HD), pl.ds(part * tokens, tokens)] = x.T
        qst_ref[pl.ds(lower, tokens), pl.ds(part * tokens, tokens)] = one_hot
        dot_ref[place, pl.ds(part * tokens, tokens)] = do.T
    mine = pl.ds(pl.multiple_of(g * HD, HD), HD)
    ck_t_ref[mine, :] = ck_ref[:, mine].T
    cv_t_ref[mine, :] = cv_ref[:, mine].T


def prep(shards, first, rank, q, do, bq, bk, bv, cosine, sine, ck, cv):
    tokens, slots = q.shape[0], ck.shape[0]
    vmem = pl.BlockSpec(memory_space=pltpu.VMEM)
    wide = pl.BlockSpec((tokens, GROUP * HD), lambda i: (0, i))
    stacked = pltpu.VMEM((HQ * tokens, HD), B16)
    turned = pltpu.VMEM((HQ // HEADS * HD, HEADS * tokens), B16)
    deep = pltpu.VMEM((HQ // HEADS * (HD + tokens), HEADS * tokens), B16)
    out_shape = [
        stacked, deep, stacked, turned,
        pltpu.VMEM((2 * KV, HD), F32),
        pltpu.VMEM((HD, tokens), F32),
        pltpu.VMEM((HD, tokens), F32),
        pltpu.VMEM((KV * HD, slots), B16),
        pltpu.VMEM((KV * HD, slots), B16),
        pltpu.VMEM((shards * (slots + tokens), tokens), B16),
        pltpu.VMEM((2 * slots, HD), B16),
    ]
    return pl.pallas_call(
        functools.partial(prep_kernel, tokens, shards),
        grid=(KV,),
        in_specs=[pl.BlockSpec(memory_space=pltpu.SMEM)] * 2 + [
            wide, wide, pl.BlockSpec((GROUP, HD), lambda i: (i, 0)),
            whole((KV, HD)), whole((KV, HD)), vmem, vmem, vmem, vmem,
        ],
        out_specs=[vmem] * len(out_shape),
        out_shape=out_shape,
        compiler_params=params(),
        cost_estimate=pl.CostEstimate(
            flops=4 * tokens * HQ * HD, bytes_accessed=12 * tokens * HQ * HD, transcendentals=0
        ),
        name="prep",
    )(first, rank, q, do, bq, bk, bv, cosine, sine, ck, cv)


def alternate(first, second):
    pieces = [iter(first), iter(second)]
    while pieces:
        for piece in list(pieces):
            if next(piece, pieces) is pieces:
                pieces.remove(piece)


def fold(x, op):
    return op(x.reshape(x.shape[0] // 8, 8, x.shape[1]), axis=0)


def attend_kernel(g, shards, *refs):
    refs = list(refs)

    def take(count):
        taken = refs[:count]
        del refs[:count]
        return taken

    (qs_ref, qst_ref, dos_ref, dot_ref, bias_ref, cos_t_ref, sin_t_ref,
     ck_t_ref, cv_t_ref, mask_ref, cos_ref, sin_ref, ck_ref, cv_ref, kp_ref, vp_ref) = take(16)
    far = take(shards - 1)
    far_k = take(shards - 1)
    far_v = take(shards - 1)
    old_sums_ref = take(1)[0] if g else None
    old_send = take(shards - 1) if g % 2 else []
    owns = take(2) if g == KV - 1 else []
    backs = take(shards - 1) if g == KV - 1 else []
    if g:
        take(2)
    out_ref, gq_ref, sums_ref, own_ref = take(4)
    send = take(shards - 1)
    pack_ref = take(1)[0] if g + 2 < KV else None
    gk_ref, gv_ref = take(2) if g == KV - 1 else (None, None)
    keys, values, keys_t, values_t, dk_acc, dv_acc = take(6)
    chains = [take(4), take(4)]
    tokens = kp_ref.shape[0]
    slots = ck_ref.shape[0]
    prefix = shards * slots
    slab = shards * tokens
    total = prefix + slab
    mine = pl.ds(g * HD, HD)

    if pack_ref is not None:
        copy_chunk(g + 2, ck_ref, cv_ref, pack_ref)
    near, extra = pl.ds(0, HD), pl.ds(HD, tokens)
    keys[pl.ds(0, slots), near] = ck_ref[:, mine]
    values[pl.ds(0, slots), near] = cv_ref[:, mine]
    for s in range(1, shards):
        keys[pl.ds(s * slots, slots), near] = far[s - 1][pl.ds(0, slots)]
        values[pl.ds(s * slots, slots), near] = far[s - 1][pl.ds(slots, slots)]
    for s in range(shards):
        rows = pl.ds(s * tokens, tokens)
        kp, vp = (kp_ref, vp_ref) if s == 0 else (far_k[s - 1], far_v[s - 1])
        k = kp[:, mine].astype(F32) + bias_ref[g:g + 1, :]
        k = k * cos_ref[rows, :] + turn(k) * sin_ref[rows, :]
        v = vp[:, mine].astype(F32) + bias_ref[KV + g:KV + g + 1, :]
        place = pl.ds(prefix + s * tokens, tokens)
        keys[place, near] = k.astype(B16)
        values[place, near] = v.astype(B16)
    keys[:, extra] = mask_ref[...]
    values[:, extra] = jnp.ones_like(mask_ref)
    keys_t[:, pl.ds(0, slots)] = ck_t_ref[mine, :]
    values_t[:, pl.ds(0, slots)] = cv_t_ref[mine, :]
    rest = pl.ds(slots, prefix - slots + slab)
    keys_t[:, rest] = keys[rest, near].T
    values_t[:, rest] = values[rest, near].T
    for scratch in chains:
        scratch[3][...] = jnp.zeros_like(scratch[3])
    sums_ref[...] = jnp.zeros_like(sums_ref) if old_sums_ref is None else old_sums_ref[...]
    dk_acc[...] = jnp.zeros_like(dk_acc)
    dv_acc[...] = jnp.zeros_like(dv_acc)

    width = HEADS * tokens
    scale = HD ** -0.5
    blocks = range(0, total, tokens)

    class Chain:
        def __init__(self, index, scratch):
            self.index = index
            self.s, self.pb, self.ds, self.do = scratch
            self.rows = pl.ds(pl.multiple_of(index * width, width), width)
            self.place = pl.ds(pl.multiple_of(index * HD, HD), HD)
            self.top = jnp.full((8, width), NEG, F32)

        def scores(self):
            depth = HD + tokens
            s = dot(keys[...], qst_ref[pl.ds(pl.multiple_of(self.index * depth, depth), depth), :], NN)
            for start in blocks:
                part = s[start:start + tokens]
                self.s[pl.ds(start, tokens), :] = part
                self.top = jnp.maximum(self.top, fold(part, jnp.max))
                yield

        def softmax(self):
            top = jnp.max(self.top, axis=0, keepdims=True)
            total_e = jnp.zeros((8, width), F32)
            for start in blocks:
                rows = pl.ds(start, tokens)
                e = jnp.exp2((self.s[rows, :] - top) * (scale * math.log2(math.e)))
                self.s[rows, :] = e
                total_e = total_e + fold(e, jnp.sum)
                yield
            inverse = 1.0 / jnp.sum(total_e, axis=0, keepdims=True)
            for start in blocks:
                rows = pl.ds(start, tokens)
                p = self.s[rows, :] * inverse
                self.s[rows, :] = p
                self.pb[rows, :] = p.astype(B16)
                yield

        def heads(self):
            for i in range(HEADS):
                head = self.index * HEADS + i
                yield (
                    slice(i * tokens, (i + 1) * tokens),
                    pl.ds(pl.multiple_of((head - g * GROUP) * HD, HD), HD),
                    head,
                )

        def output(self):
            o = dot(values_t[...], self.pb[...], NN).astype(B16)
            do = dot_ref[self.place, :]
            self.do[pl.ds(0, HD), :] = do
            left = -jnp.sum(do.astype(F32) * o.astype(F32), axis=0, keepdims=True)
            row = lax.broadcasted_iota(jnp.int32, (16, width), 0)
            terms = jnp.zeros((16, width), F32)
            for i in range(3):
                term = left.astype(B16).astype(F32)
                left = left - term
                terms = jnp.where(row == i, term, terms)
            self.do[pl.ds(HD, 16), :] = terms.astype(B16)
            yield
            for part, cols, _ in self.heads():
                out_ref[:, cols] = o[:, part].T
            yield

        def dscore(self):
            dp = dot(values[...], self.do[...], NN)
            for start in blocks:
                rows = pl.ds(start, tokens)
                self.ds[rows, :] = (self.s[rows, :] * dp[start:start + tokens]).astype(B16)
                yield

        def grads(self):
            last = pl.ds(prefix, slab)
            dk_acc[...] += dot(self.ds[last, :], qs_ref[self.rows, :], NN)
            dv_acc[...] += dot(self.pb[last, :], dos_ref[self.rows, :], NN)
            yield
            dq = (dot(keys_t[...], self.ds[...], NN) * scale).astype(B16).astype(F32)
            yield
            for part, cols, head in self.heads():
                x = dq[:, part]
                other = jnp.concatenate([x[HD // 2:], x[:HD // 2]], axis=0)
                x = (x * cos_t_ref[...] - other * sin_t_ref[...]).T
                gq_ref[:, cols] = x.astype(B16)
                sums_ref[pl.ds(head, 1), :] = jnp.sum(x, axis=0, keepdims=True)
            yield

    def pair(i, carry):
        index = g * (GROUP // HEADS) + 2 * i
        a, b = Chain(index, chains[0]), Chain(index + 1, chains[1])
        for _ in a.scores():
            pass
        alternate(b.scores(), a.softmax())
        alternate(itertools.chain(a.output(), a.dscore()), b.softmax())
        alternate(b.output(), a.grads())
        for _ in b.dscore():
            pass
        for _ in b.grads():
            pass
        return carry

    lax.fori_loop(0, GROUP // (2 * HEADS), pair, 0)

    dk = dk_acc[...] * scale
    dv = dv_acc[...]
    gk = turn_back(dk, cos_ref[...], sin_ref[...])
    own_ref[0] = dk[:tokens]
    own_ref[1] = dv[:tokens]
    at = 2 * (g % 2)
    for j in range(1, shards):
        block = slice(j * tokens, (j + 1) * tokens)
        send[j - 1][at] = dk[block].astype(B16)
        send[j - 1][at + 1] = dv[block].astype(B16)
        if at:
            send[j - 1][pl.ds(0, at)] = old_send[j - 1][...]
    sums_ref[pl.ds(HQ + g, 1), :] = jnp.sum(gk, axis=0, keepdims=True)
    sums_ref[pl.ds(HQ + KV + g, 1), :] = jnp.sum(dv, axis=0, keepdims=True)
    if gk_ref is not None:
        finish_heads(2, shards, (cos_ref, sin_ref), owns, backs, gk_ref, gv_ref)


def attend(
    g, shards, prepared, cosine, sine, ck, cv, kp, vp, far, far_k, far_v,
    before, owns, backs,
):
    tokens, slots = kp.shape[0], ck.shape[0]
    slab = shards * tokens
    total = slab + shards * slots
    last = g == KV - 1
    vmem = pl.BlockSpec(memory_space=pltpu.VMEM)
    anywhere = pl.BlockSpec(memory_space=pl.ANY)
    wide = pl.BlockSpec((tokens, GROUP * HD), lambda i: (0, g))
    half = pl.BlockSpec((tokens, 2 * HD), lambda i: (0, 0))

    placed = [*prepared, cosine, sine, ck, cv, kp, vp, *far, *far_k, *far_v]
    aliases = {}
    if before is not None:
        out, gq, sums, send = before
        placed.append(sums)
        if g % 2:
            placed += send
        if last:
            placed += [*owns[:2], *backs]
    args = list(placed)
    in_specs = [vmem] * len(placed)
    if before is not None:
        aliases = {len(args): 0, len(args) + 1: 1}
        args += [out, gq]
        in_specs += [anywhere] * 2
    out_shape = [
        pltpu.HBM((tokens, HQ * HD), B16),
        pltpu.HBM((tokens, HQ * HD), B16),
        pltpu.VMEM((SUMS, HD), F32),
        pltpu.VMEM((2, tokens, HD), F32),
    ]
    out_specs = [wide, wide, vmem, vmem]
    out_shape += [pltpu.VMEM((2 + 2 * (g % 2), tokens, HD), B16)] * (shards - 1)
    out_specs += [vmem] * (shards - 1)
    if g + 2 < KV:
        out_shape.append(pltpu.VMEM((2 * slots, HD), B16))
        out_specs.append(vmem)
    if last:
        out_shape += [pltpu.HBM((tokens, KV * HD), B16)] * 2
        out_specs += [half] * 2
    results = pl.pallas_call(
        functools.partial(attend_kernel, g, shards),
        grid=(1,),
        in_specs=in_specs,
        out_shape=out_shape,
        out_specs=out_specs,
        scratch_shapes=[
            pltpu.VMEM((total, HD + tokens), B16), pltpu.VMEM((total, HD + tokens), B16),
            pltpu.VMEM((HD, total), B16), pltpu.VMEM((HD, total), B16),
            pltpu.VMEM((slab, HD), F32), pltpu.VMEM((slab, HD), F32),
        ] + [
            pltpu.VMEM((rows, HEADS * tokens), kind)
            for rows, kind in ((total, F32), (total, B16), (total, B16), (HD + tokens, B16)) * 2
        ],
        input_output_aliases=aliases,
        compiler_params=params(),
        cost_estimate=pl.CostEstimate(
            flops=2 * GROUP * tokens * HD * (4 * total + 2 * slab),
            bytes_accessed=8 * tokens * GROUP * HD + 8 * total * HD,
            transcendentals=GROUP * tokens * total,
        ),
        name="attend",
    )(*args)
    out, gq, sums, own = results[:4]
    send = results[4:4 + shards - 1]
    return (out, gq, sums, send), own, results[4 + shards - 1:]


def finish_kernel(shards, *refs):
    owns, backs = refs[2:4], refs[4:4 + shards - 1]
    sums, other = refs[4 + shards - 1:4 + shards + 1]
    gk_ref, gv_ref, *parts = refs[-5:]
    finish_heads(2, shards, refs[:2], owns, backs, gk_ref, gv_ref)
    start = 0
    for part in parts:
        rows = pl.ds(start, part.shape[0])
        part[...] = sums[rows, :] + other[rows, :]
        start += part.shape[0]


def finish(shards, cosine, sine, owns, backs, sums, other, gk, gv):
    tokens = gk.shape[0]
    vmem = pl.BlockSpec(memory_space=pltpu.VMEM)
    args = [cosine, sine, *owns, *backs, sums, other]
    heads = [(HQ, HD), (KV, HD), (KV, HD)]
    return pl.pallas_call(
        functools.partial(finish_kernel, shards),
        grid=(1,),
        in_specs=[vmem] * len(args) + [pl.BlockSpec(memory_space=pl.ANY)] * 2,
        out_specs=[pl.BlockSpec((tokens, 2 * HD), lambda i: (0, 1))] * 2
        + [whole(shape) for shape in heads],
        out_shape=[pltpu.HBM(gk.shape, B16)] * 2 + [pltpu.HBM(shape, F32) for shape in heads],
        input_output_aliases={len(args): 0, len(args) + 1: 1},
        compiler_params=params(),
        cost_estimate=pl.CostEstimate(flops=0, bytes_accessed=1 << 19, transcendentals=0),
        name="finish",
    )(*args, gk, gv)


def exchanges(axis):
    size = lax.axis_size(axis)
    step = 1
    while step < size:
        yield axis, [(i, i ^ step) for i in range(size)]
        step *= 2


def sum_but_last(x, axes):
    other = None
    for axis in axes:
        for name, perm in exchanges(axis):
            x = x if other is None else x + other
            other = lax.ppermute(x, name, perm)
    return x, other


def body(q_proj, k_proj, v_proj, cache_k, cache_v, bias_q, bias_k, bias_v, start, dout):
    shards = lax.axis_size("seq")
    rank = lax.axis_index("seq").astype(jnp.int32)
    tokens = q_proj.shape[1]
    ck, cv, kp, vp = cache_k[0], cache_v[0], k_proj[0], v_proj[0]

    def ring(x, s):
        return lax.ppermute(x, "seq", [(i, (i + s) % shards) for i in range(shards)])

    def later(x, s):
        return lax.ppermute(x, "seq", [(i, i + s) for i in range(shards - s)])

    def earlier(x, s):
        return lax.ppermute(x, "seq", [(i + s, i) for i in range(shards - s)])

    shifts = range(1, shards)
    far_k = [later(kp, s) for s in shifts]
    far_v = [later(vp, s) for s in shifts]
    hbm = functools.partial(pltpu.with_memory_space_constraint, memory_space=pltpu.HBM)
    chunk = pack(0, hbm(ck), hbm(cv))
    far = [[ring(chunk, s) for s in shifts]]

    owners = lax.rem(rank - jnp.arange(shards, dtype=jnp.int32) + shards, shards)
    positions = start[0] + owners[:, None] * tokens + jnp.arange(tokens, dtype=jnp.int32)[None]
    lane = jnp.arange(HD, dtype=jnp.int32)
    freqs = jnp.exp(
        -(2.0 * (lane % (HD // 2)).astype(F32) / HD) * jnp.log(jnp.float32(1000000.0))
    )
    angles = positions.reshape(-1).astype(F32)[:, None] * freqs[None, :]
    cosine = jnp.cos(angles)
    sine = jnp.sin(angles) * jnp.where(lane < HD // 2, -1.0, 1.0).astype(F32)[None]

    *prepared, chunk = prep(
        shards, start, rank.reshape(1), hbm(q_proj[0]), hbm(dout[0]), hbm(bias_q.reshape(HQ, HD)),
        hbm(bias_k.reshape(KV, HD)), hbm(bias_v.reshape(KV, HD)), cosine, sine, ck, cv,
    )
    far.append([ring(chunk, s) for s in shifts])
    before, owns, backs = None, [], []
    for g in range(KV):
        before, own, more = attend(
            g, shards, prepared, cosine, sine, ck, cv, kp, vp,
            far[g], far_k, far_v, before, owns, backs,
        )
        owns.append(own)
        if g + 2 < KV:
            far.append([ring(more[0], s) for s in shifts])
        if g % 2:
            backs = [earlier(x, s) for s, x in zip(shifts, before[3])]
    out, gq, sums, _ = before
    sums, other = sum_but_last(sums, ("dp", "seq"))
    gk, gv, *sums = finish(shards, cosine, sine, owns[2:], backs, sums, other, *more)
    return (out[None], gq[None], gk[None], gv[None], *[x.reshape(-1) for x in sums])


def solution(mesh):
    split = P("dp", "seq", None)
    return jax.shard_map(
        body,
        mesh=mesh,
        in_specs=(split,) * 5 + (P(), P(), P(), P("dp"), split),
        out_specs=(split,) * 4 + (P(), P(), P()),
        check_vma=False,
    )
```

```python
import functools
import itertools
import math

import jax
import jax.numpy as jnp
from jax import lax
from jax.experimental import pallas as pl
from jax.experimental.pallas import tpu as pltpu
from jax.sharding import PartitionSpec as P

HQ = 32
KV = 4
HD = 128
GROUP = 8
HEADS = 2
NEG = -1e30
SUMS = HQ + 2 * KV
VMEM = 28 * 1024 * 1024
F32, B16 = jnp.float32, jnp.bfloat16


def turn(x):
    return pltpu.roll(x, HD // 2, 1)


def dot(a, b, dims):
    return lax.dot_general(a, b, (dims, ((), ())), preferred_element_type=F32)


NN = ((1,), (0,))


def whole(shape):
    return pl.BlockSpec(shape, lambda i: (0,) * len(shape))


def column(rows, g):
    return pl.BlockSpec((rows, HD), lambda i: (0, g))


def params():
    return pltpu.CompilerParams(dimension_semantics=("arbitrary",), vmem_limit_bytes=VMEM)


def copy_chunk(g, ck_ref, cv_ref, out_ref):
    rows = ck_ref.shape[0]
    cols = pl.ds(g * HD, HD)
    out_ref[pl.ds(0, rows)] = ck_ref[:, cols]
    out_ref[pl.ds(rows, rows)] = cv_ref[:, cols]


def pack_kernel(ck_ref, cv_ref, *rest):
    copy_chunk(0, ck_ref, cv_ref, rest[-1])


def pack(g, ck, cv, *after):
    rows = ck.shape[0]
    return pl.pallas_call(
        pack_kernel,
        grid=(1,),
        in_specs=[column(rows, g)] * 2 + [pl.BlockSpec(memory_space=pl.ANY)] * len(after),
        out_specs=pl.BlockSpec(memory_space=pltpu.VMEM),
        out_shape=pltpu.VMEM((2 * rows, HD), B16),
        compiler_params=params(),
        cost_estimate=pl.CostEstimate(flops=0, bytes_accessed=8 * rows * HD, transcendentals=0),
        name="pack",
    )(ck, cv, *after)


def turn_back(x, cosine, sine):
    return x * cosine - turn(x) * sine


def finish_heads(heads, shards, tables, owns, backs, gk_ref, gv_ref):
    tokens = gk_ref.shape[0]
    cosine, sine = (t[pl.ds(0, tokens), :] for t in tables)
    for i in range(heads):
        dk, dv = owns[i][0], owns[i][1]
        for s in range(shards - 1):
            dk = dk + backs[s][2 * i].astype(F32)
            dv = dv + backs[s][2 * i + 1].astype(F32)
        cols = pl.ds(i * HD, HD)
        gk_ref[:, cols] = turn_back(dk, cosine, sine).astype(B16)
        gv_ref[:, cols] = dv.astype(B16)


def prep_kernel(
    tokens, q_ref, do_ref, bq_ref, bk_ref, bv_ref, cos_ref, sin_ref, ck_ref, cv_ref,
    qs_ref, qst_ref, dos_ref, dot_ref, bias_ref, cos_t_ref, sin_t_ref, ck_t_ref, cv_t_ref, pack_ref,
):
    g = pl.program_id(0)
    cosine, sine = cos_ref[pl.ds(0, tokens), :], sin_ref[pl.ds(0, tokens), :]
    bias_q = bq_ref[...].astype(F32)

    @pl.when(g == 0)
    def _():
        bias_ref[pl.ds(0, KV), :] = bk_ref[...].astype(F32)
        bias_ref[pl.ds(KV, KV), :] = bv_ref[...].astype(F32)
        cos_t_ref[...] = cosine.T
        sin_t_ref[...] = sine.T
        copy_chunk(1, ck_ref, cv_ref, pack_ref)

    for h in range(GROUP):
        cols = pl.ds(h * HD, HD)
        rows = pl.ds(pl.multiple_of((g * GROUP + h) * tokens, tokens), tokens)
        x = q_ref[:, cols].astype(F32) + bias_q[h:h + 1]
        x = (x * cosine + turn(x) * sine).astype(B16)
        qs_ref[rows, :] = x
        do = do_ref[:, cols]
        dos_ref[rows, :] = do
        chain, part = h // HEADS, h % HEADS
        place = pl.ds(pl.multiple_of((g * (GROUP // HEADS) + chain) * HD, HD), HD)
        qst_ref[place, pl.ds(part * tokens, tokens)] = x.T
        dot_ref[place, pl.ds(part * tokens, tokens)] = do.T
    mine = pl.ds(pl.multiple_of(g * HD, HD), HD)
    ck_t_ref[mine, :] = ck_ref[:, mine].T
    cv_t_ref[mine, :] = cv_ref[:, mine].T


def prep(q, do, bq, bk, bv, cosine, sine, ck, cv):
    tokens, slots = q.shape[0], ck.shape[0]
    vmem = pl.BlockSpec(memory_space=pltpu.VMEM)
    wide = pl.BlockSpec((tokens, GROUP * HD), lambda i: (0, i))
    stacked = pltpu.VMEM((HQ * tokens, HD), B16)
    turned = pltpu.VMEM((HQ // HEADS * HD, HEADS * tokens), B16)
    out_shape = [
        stacked, turned, stacked, turned,
        pltpu.VMEM((2 * KV, HD), F32),
        pltpu.VMEM((HD, tokens), F32),
        pltpu.VMEM((HD, tokens), F32),
        pltpu.VMEM((KV * HD, slots), B16),
        pltpu.VMEM((KV * HD, slots), B16),
        pltpu.VMEM((2 * slots, HD), B16),
    ]
    return pl.pallas_call(
        functools.partial(prep_kernel, tokens),
        grid=(KV,),
        in_specs=[
            wide, wide, pl.BlockSpec((GROUP, HD), lambda i: (i, 0)),
            whole((KV, HD)), whole((KV, HD)), vmem, vmem, vmem, vmem,
        ],
        out_specs=[vmem] * len(out_shape),
        out_shape=out_shape,
        compiler_params=params(),
        cost_estimate=pl.CostEstimate(
            flops=4 * tokens * HQ * HD, bytes_accessed=12 * tokens * HQ * HD, transcendentals=0
        ),
        name="prep",
    )(q, do, bq, bk, bv, cosine, sine, ck, cv)


def fold(x, op):
    return op(x.reshape(x.shape[0] // 8, 8, x.shape[1]), axis=0)


def attend_kernel(g, shards, *refs):
    refs = list(refs)

    def take(count):
        taken = refs[:count]
        del refs[:count]
        return taken

    (first_ref, rank_ref, qs_ref, qst_ref, dos_ref, dot_ref, bias_ref, cos_t_ref, sin_t_ref,
     ck_t_ref, cv_t_ref, cos_ref, sin_ref, ck_ref, cv_ref, kp_ref, vp_ref) = take(17)
    far = take(shards - 1)
    far_k = take(shards - 1)
    far_v = take(shards - 1)
    old_sums_ref = take(1)[0] if g else None
    old_send = take(shards - 1) if g % 2 else []
    owns = take(2) if g == KV - 1 else []
    backs = take(shards - 1) if g == KV - 1 else []
    if g:
        take(2)
    out_ref, gq_ref, sums_ref, own_ref = take(4)
    send = take(shards - 1)
    pack_ref = take(1)[0] if g + 2 < KV else None
    gk_ref, gv_ref = take(2) if g == KV - 1 else (None, None)
    keys, values, keys_t, values_t, dk_acc, dv_acc = take(6)
    chains = [take(3), take(3)]
    tokens = kp_ref.shape[0]
    slots = ck_ref.shape[0]
    prefix = shards * slots
    slab = shards * tokens
    total = prefix + slab
    first = first_ref[0]
    rank = rank_ref[0]
    mine = pl.ds(g * HD, HD)

    if pack_ref is not None:
        copy_chunk(g + 2, ck_ref, cv_ref, pack_ref)
    keys[pl.ds(0, slots)] = ck_ref[:, mine]
    values[pl.ds(0, slots)] = cv_ref[:, mine]
    for s in range(1, shards):
        keys[pl.ds(s * slots, slots)] = far[s - 1][pl.ds(0, slots)]
        values[pl.ds(s * slots, slots)] = far[s - 1][pl.ds(slots, slots)]
    for s in range(shards):
        rows = pl.ds(s * tokens, tokens)
        kp, vp = (kp_ref, vp_ref) if s == 0 else (far_k[s - 1], far_v[s - 1])
        k = kp[:, mine].astype(F32) + bias_ref[g:g + 1, :]
        k = k * cos_ref[rows, :] + turn(k) * sin_ref[rows, :]
        v = vp[:, mine].astype(F32) + bias_ref[KV + g:KV + g + 1, :]
        place = pl.ds(prefix + s * tokens, tokens)
        keys[place] = k.astype(B16)
        values[place] = v.astype(B16)
    keys_t[:, pl.ds(0, slots)] = ck_t_ref[mine, :]
    values_t[:, pl.ds(0, slots)] = cv_t_ref[mine, :]
    rest = pl.ds(slots, prefix - slots + slab)
    keys_t[:, rest] = keys[rest, :].T
    values_t[:, rest] = values[rest, :].T
    sums_ref[...] = jnp.zeros_like(sums_ref) if old_sums_ref is None else old_sums_ref[...]
    dk_acc[...] = jnp.zeros_like(dk_acc)
    dv_acc[...] = jnp.zeros_like(dv_acc)

    width = HEADS * tokens
    scale = HD ** -0.5
    blocks = range(0, total, tokens)
    tile = 2 * tokens
    tiles = range(0, total, tile)

    def allowed(start, s):
        row = lax.broadcasted_iota(jnp.int32, s.shape, 0)
        if start < prefix:
            owner = lax.rem(rank - start // slots + shards, shards)
            return row < first - owner * slots - start % slots
        if start < prefix + tokens:
            return row <= (lax.broadcasted_iota(jnp.int32, s.shape, 1) & (tokens - 1))
        return row < jnp.where(rank >= (start - prefix) // tokens, tokens, 0)

    class Chain:
        def __init__(self, index, scratch):
            self.index = index
            self.s, self.pb, self.ds = scratch
            self.rows = pl.ds(pl.multiple_of(index * width, width), width)
            self.place = pl.ds(pl.multiple_of(index * HD, HD), HD)
            self.top = jnp.full((8, width), NEG, F32)

        def scores(self):
            q = qst_ref[self.place, :]
            for start in tiles:
                s = dot(keys[pl.ds(start, tile), :], q, NN)
                for i in range(0, tile, tokens):
                    part = s[i:i + tokens]
                    part = jnp.where(allowed(start + i, part), part, NEG)
                    self.s[pl.ds(start + i, tokens), :] = part
                    self.top = jnp.maximum(self.top, fold(part, jnp.max))
                yield

        def exponents(self):
            top = jnp.max(self.top, axis=0, keepdims=True)
            self.weight = jnp.zeros((8, width), F32)
            for start in tiles:
                rows = pl.ds(start, tile)
                e = jnp.exp2((self.s[rows, :] - top) * (scale * math.log2(math.e)))
                self.s[rows, :] = e
                self.weight = self.weight + fold(e, jnp.sum)
                yield

        def probs(self):
            inverse = 1.0 / jnp.sum(self.weight, axis=0, keepdims=True)
            for start in tiles:
                rows = pl.ds(start, tile)
                p = self.s[rows, :] * inverse
                self.s[rows, :] = p
                self.pb[rows, :] = p.astype(B16)
                yield

        def output(self):
            o = jnp.zeros((HD, width), F32)
            for start in tiles:
                rows = pl.ds(start, tile)
                o = o + dot(values_t[:, rows], self.pb[rows, :], NN)
                yield
            self.o = o.astype(B16)
            do = dot_ref[self.place, :].astype(F32)
            self.delta = jnp.sum(do * self.o.astype(F32), axis=0, keepdims=True)

        def heads(self):
            for i in range(HEADS):
                head = self.index * HEADS + i
                yield (
                    slice(i * tokens, (i + 1) * tokens),
                    pl.ds(pl.multiple_of((head - g * GROUP) * HD, HD), HD),
                    head,
                )

        def dscores(self):
            do = dot_ref[self.place, :]
            for start in tiles:
                rows = pl.ds(start, tile)
                dp = dot(values[rows, :], do, NN)
                self.ds[rows, :] = (self.s[rows, :] * (dp - self.delta)).astype(B16)
                yield

        def query_grad(self):
            dq = jnp.zeros((HD, width), F32)
            for start in tiles:
                rows = pl.ds(start, tile)
                dq = dq + dot(keys_t[:, rows], self.ds[rows, :], NN)
                yield
            self.dq = (dq * scale).astype(B16).astype(F32)

        def slab_grads(self):
            last = pl.ds(prefix, slab)
            dv_acc[...] += dot(self.pb[last, :], dos_ref[self.rows, :], NN)
            dk_acc[...] += dot(self.ds[last, :], qs_ref[self.rows, :], NN)

        def store(self):
            for part, cols, head in self.heads():
                out_ref[:, cols] = self.o[:, part].T
                x = self.dq[:, part]
                other = jnp.concatenate([x[HD // 2:], x[:HD // 2]], axis=0)
                x = (x * cos_t_ref[...] - other * sin_t_ref[...]).T
                gq_ref[:, cols] = x.astype(B16)
                sums_ref[pl.ds(head, 1), :] = jnp.sum(x, axis=0, keepdims=True)

    def together(*works):
        for _ in itertools.zip_longest(*works):
            pass

    def pair(i, carry):
        index = g * (GROUP // HEADS) + 2 * i
        a, b = Chain(index, chains[0]), Chain(index + 1, chains[1])
        together(a.scores())
        together(b.scores(), a.exponents())
        together(a.probs(), b.exponents(), a.output())
        together(a.dscores(), b.probs(), a.query_grad(), b.output())
        together(b.dscores(), b.query_grad())
        a.slab_grads()
        a.store()
        b.slab_grads()
        b.store()
        return carry

    lax.fori_loop(0, GROUP // (2 * HEADS), pair, 0)

    dk = dk_acc[...] * scale
    dv = dv_acc[...]
    gk = turn_back(dk, cos_ref[...], sin_ref[...])
    own_ref[0] = dk[:tokens]
    own_ref[1] = dv[:tokens]
    at = 2 * (g % 2)
    for j in range(1, shards):
        block = slice(j * tokens, (j + 1) * tokens)
        send[j - 1][at] = dk[block].astype(B16)
        send[j - 1][at + 1] = dv[block].astype(B16)
        if at:
            send[j - 1][pl.ds(0, at)] = old_send[j - 1][...]
    sums_ref[pl.ds(HQ + g, 1), :] = jnp.sum(gk, axis=0, keepdims=True)
    sums_ref[pl.ds(HQ + KV + g, 1), :] = jnp.sum(dv, axis=0, keepdims=True)
    if gk_ref is not None:
        finish_heads(2, shards, (cos_ref, sin_ref), owns, backs, gk_ref, gv_ref)


def attend(
    g, shards, first, rank, prepared, cosine, sine, ck, cv, kp, vp, far, far_k, far_v,
    before, owns, backs,
):
    tokens, slots = kp.shape[0], ck.shape[0]
    slab = shards * tokens
    total = slab + shards * slots
    last = g == KV - 1
    smem = pl.BlockSpec(memory_space=pltpu.SMEM)
    vmem = pl.BlockSpec(memory_space=pltpu.VMEM)
    anywhere = pl.BlockSpec(memory_space=pl.ANY)
    wide = pl.BlockSpec((tokens, GROUP * HD), lambda i: (0, g))
    half = pl.BlockSpec((tokens, 2 * HD), lambda i: (0, 0))

    args = [first, rank]
    placed = [*prepared, cosine, sine, ck, cv, kp, vp, *far, *far_k, *far_v]
    aliases = {}
    if before is not None:
        out, gq, sums, send = before
        placed.append(sums)
        if g % 2:
            placed += send
        if last:
            placed += [*owns[:2], *backs]
    args += placed
    in_specs = [smem] * 2 + [vmem] * len(placed)
    if before is not None:
        aliases = {len(args): 0, len(args) + 1: 1}
        args += [out, gq]
        in_specs += [anywhere] * 2
    out_shape = [
        pltpu.HBM((tokens, HQ * HD), B16),
        pltpu.HBM((tokens, HQ * HD), B16),
        pltpu.VMEM((SUMS, HD), F32),
        pltpu.VMEM((2, tokens, HD), F32),
    ]
    out_specs = [wide, wide, vmem, vmem]
    out_shape += [pltpu.VMEM((2 + 2 * (g % 2), tokens, HD), B16)] * (shards - 1)
    out_specs += [vmem] * (shards - 1)
    if g + 2 < KV:
        out_shape.append(pltpu.VMEM((2 * slots, HD), B16))
        out_specs.append(vmem)
    if last:
        out_shape += [pltpu.HBM((tokens, KV * HD), B16)] * 2
        out_specs += [half] * 2
    results = pl.pallas_call(
        functools.partial(attend_kernel, g, shards),
        grid=(1,),
        in_specs=in_specs,
        out_shape=out_shape,
        out_specs=out_specs,
        scratch_shapes=[
            pltpu.VMEM((total, HD), B16), pltpu.VMEM((total, HD), B16),
            pltpu.VMEM((HD, total), B16), pltpu.VMEM((HD, total), B16),
            pltpu.VMEM((slab, HD), F32), pltpu.VMEM((slab, HD), F32),
        ] + [
            pltpu.VMEM((total, HEADS * tokens), kind) for kind in (F32, B16, B16) * 2
        ],
        input_output_aliases=aliases,
        compiler_params=params(),
        cost_estimate=pl.CostEstimate(
            flops=2 * GROUP * tokens * HD * (4 * total + 2 * slab),
            bytes_accessed=8 * tokens * GROUP * HD + 8 * total * HD,
            transcendentals=GROUP * tokens * total,
        ),
        name="attend",
    )(*args)
    out, gq, sums, own = results[:4]
    send = results[4:4 + shards - 1]
    return (out, gq, sums, send), own, results[4 + shards - 1:]


def finish_kernel(shards, *refs):
    owns, backs = refs[2:4], refs[4:4 + shards - 1]
    sums = refs[4 + shards - 1:-7]
    gk_ref, gv_ref, *parts = refs[-5:]
    finish_heads(2, shards, refs[:2], owns, backs, gk_ref, gv_ref)
    start = 0
    for part in parts:
        rows = pl.ds(start, part.shape[0])
        part[...] = add_up([ref[rows, :] for ref in sums])
        start += part.shape[0]


def finish(shards, cosine, sine, owns, backs, sums, gk, gv):
    tokens = gk.shape[0]
    vmem = pl.BlockSpec(memory_space=pltpu.VMEM)
    args = [cosine, sine, *owns, *backs, *sums]
    heads = [(HQ, HD), (KV, HD), (KV, HD)]
    return pl.pallas_call(
        functools.partial(finish_kernel, shards),
        grid=(1,),
        in_specs=[vmem] * len(args) + [pl.BlockSpec(memory_space=pl.ANY)] * 2,
        out_specs=[pl.BlockSpec((tokens, 2 * HD), lambda i: (0, 1))] * 2
        + [whole(shape) for shape in heads],
        out_shape=[pltpu.HBM(gk.shape, B16)] * 2 + [pltpu.HBM(shape, F32) for shape in heads],
        input_output_aliases={len(args): 0, len(args) + 1: 1},
        compiler_params=params(),
        cost_estimate=pl.CostEstimate(flops=0, bytes_accessed=1 << 19, transcendentals=0),
        name="finish",
    )(*args, gk, gv)


def add_up(parts):
    while len(parts) > 1:
        parts = [a + b for a, b in zip(parts[::2], parts[1::2])]
    return parts[0]


def sum_but_last(x, axes, near):
    devices = lax.axis_size(axes)
    bits = [1 << i for i in range(devices.bit_length() - 1) if 1 << i != near]
    stages = [[near]] + [bits[i:i + 2] for i in range(0, len(bits), 2)]
    parts = [x]
    for stage in stages:
        x = add_up(parts)
        parts = [x]
        for flip in [sum(c) for n in (1, 2) for c in itertools.combinations(stage, n)]:
            parts.append(lax.ppermute(x, axes, [(i, i ^ flip) for i in range(devices)]))
    return parts


def body(q_proj, k_proj, v_proj, cache_k, cache_v, bias_q, bias_k, bias_v, start, dout):
    shards = lax.axis_size("seq")
    rank = lax.axis_index("seq").astype(jnp.int32)
    tokens = q_proj.shape[1]
    ck, cv, kp, vp = cache_k[0], cache_v[0], k_proj[0], v_proj[0]

    def ring(x, s):
        return lax.ppermute(x, "seq", [(i, (i + s) % shards) for i in range(shards)])

    def later(x, s):
        return lax.ppermute(x, "seq", [(i, i + s) for i in range(shards - s)])

    def earlier(x, s):
        return lax.ppermute(x, "seq", [(i + s, i) for i in range(shards - s)])

    shifts = range(1, shards)
    far_k = [later(kp, s) for s in shifts]
    far_v = [later(vp, s) for s in shifts]
    hbm = functools.partial(pltpu.with_memory_space_constraint, memory_space=pltpu.HBM)
    chunk = pack(0, hbm(ck), hbm(cv))
    far = [[ring(chunk, s) for s in shifts]]

    owners = lax.rem(rank - jnp.arange(shards, dtype=jnp.int32) + shards, shards)
    positions = start[0] + owners[:, None] * tokens + jnp.arange(tokens, dtype=jnp.int32)[None]
    lane = jnp.arange(HD, dtype=jnp.int32)
    freqs = jnp.exp(
        -(2.0 * (lane % (HD // 2)).astype(F32) / HD) * jnp.log(jnp.float32(1000000.0))
    )
    angles = positions.reshape(-1).astype(F32)[:, None] * freqs[None, :]
    cosine = jnp.cos(angles)
    sine = jnp.sin(angles) * jnp.where(lane < HD // 2, -1.0, 1.0).astype(F32)[None]

    *prepared, chunk = prep(
        hbm(q_proj[0]), hbm(dout[0]), hbm(bias_q.reshape(HQ, HD)),
        hbm(bias_k.reshape(KV, HD)), hbm(bias_v.reshape(KV, HD)), cosine, sine, ck, cv,
    )
    far.append([ring(chunk, s) for s in shifts])
    before, owns, backs = None, [], []
    for g in range(KV):
        before, own, more = attend(
            g, shards, start, rank.reshape(1), prepared, cosine, sine, ck, cv, kp, vp,
            far[g], far_k, far_v, before, owns, backs,
        )
        owns.append(own)
        if g + 2 < KV:
            far.append([ring(more[0], s) for s in shifts])
        if g % 2:
            backs = [earlier(x, s) for s, x in zip(shifts, before[3])]
    out, gq, sums, _ = before
    parts = sum_but_last(sums, ("dp", "seq"), shards)
    gk, gv, *sums = finish(shards, cosine, sine, owns[2:], backs, parts, *more)
    return (out[None], gq[None], gk[None], gv[None], *[x.reshape(-1) for x in sums])


def solution(mesh):
    split = P("dp", "seq", None)
    return jax.shard_map(
        body,
        mesh=mesh,
        in_specs=(split,) * 5 + (P(), P(), P(), P("dp"), split),
        out_specs=(split,) * 4 + (P(), P(), P()),
        check_vma=False,
    )
```

```python
import functools
import itertools
import math

import jax
import jax.numpy as jnp
from jax import lax
from jax.experimental import pallas as pl
from jax.experimental.pallas import tpu as pltpu
from jax.sharding import PartitionSpec as P

HQ = 32
KV = 4
HD = 128
GROUP = 8
HEADS = 4
NEG = -1e30
SUMS = HQ + 2 * KV
VMEM = 28 * 1024 * 1024
F32, B16 = jnp.float32, jnp.bfloat16


def turn(x):
    return pltpu.roll(x, HD // 2, 1)


def dot(a, b, dims):
    return lax.dot_general(a, b, (dims, ((), ())), preferred_element_type=F32)


NN = ((1,), (0,))


def whole(shape):
    return pl.BlockSpec(shape, lambda i: (0,) * len(shape))


def column(rows, g):
    return pl.BlockSpec((rows, HD), lambda i: (0, g))


def params():
    return pltpu.CompilerParams(dimension_semantics=("arbitrary",), vmem_limit_bytes=VMEM)


def copy_chunk(g, ck_ref, cv_ref, out_ref):
    rows = ck_ref.shape[0]
    cols = pl.ds(g * HD, HD)
    out_ref[pl.ds(0, rows)] = ck_ref[:, cols]
    out_ref[pl.ds(rows, rows)] = cv_ref[:, cols]


def pack_kernel(ck_ref, cv_ref, *rest):
    copy_chunk(0, ck_ref, cv_ref, rest[-1])


def pack(g, ck, cv, *after):
    rows = ck.shape[0]
    return pl.pallas_call(
        pack_kernel,
        grid=(1,),
        in_specs=[column(rows, g)] * 2 + [pl.BlockSpec(memory_space=pl.ANY)] * len(after),
        out_specs=pl.BlockSpec(memory_space=pltpu.VMEM),
        out_shape=pltpu.VMEM((2 * rows, HD), B16),
        compiler_params=params(),
        cost_estimate=pl.CostEstimate(flops=0, bytes_accessed=8 * rows * HD, transcendentals=0),
        name="pack",
    )(ck, cv, *after)


def turn_back(x, cosine, sine):
    return x * cosine - turn(x) * sine


def finish_heads(heads, shards, tables, owns, backs, gk_ref, gv_ref):
    tokens = gk_ref.shape[0]
    cosine, sine = (t[pl.ds(0, tokens), :] for t in tables)
    for i in range(heads):
        dk, dv = owns[i][0], owns[i][1]
        for s in range(shards - 1):
            dk = dk + backs[s][2 * i].astype(F32)
            dv = dv + backs[s][2 * i + 1].astype(F32)
        cols = pl.ds(i * HD, HD)
        gk_ref[:, cols] = turn_back(dk, cosine, sine).astype(B16)
        gv_ref[:, cols] = dv.astype(B16)


def prep_kernel(
    tokens, q_ref, do_ref, bq_ref, bk_ref, bv_ref, cos_ref, sin_ref, ck_ref, cv_ref,
    qs_ref, qst_ref, dos_ref, dot_ref, bias_ref, cos_t_ref, sin_t_ref, ck_t_ref, cv_t_ref, pack_ref,
):
    g = pl.program_id(0)
    cosine, sine = cos_ref[pl.ds(0, tokens), :], sin_ref[pl.ds(0, tokens), :]
    bias_q = bq_ref[...].astype(F32)

    @pl.when(g == 0)
    def _():
        bias_ref[pl.ds(0, KV), :] = bk_ref[...].astype(F32)
        bias_ref[pl.ds(KV, KV), :] = bv_ref[...].astype(F32)
        cos_t_ref[...] = cosine.T
        sin_t_ref[...] = sine.T
        copy_chunk(1, ck_ref, cv_ref, pack_ref)

    for h in range(GROUP):
        cols = pl.ds(h * HD, HD)
        rows = pl.ds(pl.multiple_of((g * GROUP + h) * tokens, tokens), tokens)
        x = q_ref[:, cols].astype(F32) + bias_q[h:h + 1]
        x = (x * cosine + turn(x) * sine).astype(B16)
        qs_ref[rows, :] = x
        do = do_ref[:, cols]
        dos_ref[rows, :] = do
        chain, part = h // HEADS, h % HEADS
        place = pl.ds(pl.multiple_of((g * (GROUP // HEADS) + chain) * HD, HD), HD)
        qst_ref[place, pl.ds(part * tokens, tokens)] = x.T
        dot_ref[place, pl.ds(part * tokens, tokens)] = do.T
    mine = pl.ds(pl.multiple_of(g * HD, HD), HD)
    ck_t_ref[mine, :] = ck_ref[:, mine].T
    cv_t_ref[mine, :] = cv_ref[:, mine].T


def prep(q, do, bq, bk, bv, cosine, sine, ck, cv):
    tokens, slots = q.shape[0], ck.shape[0]
    vmem = pl.BlockSpec(memory_space=pltpu.VMEM)
    wide = pl.BlockSpec((tokens, GROUP * HD), lambda i: (0, i))
    stacked = pltpu.VMEM((HQ * tokens, HD), B16)
    turned = pltpu.VMEM((HQ // HEADS * HD, HEADS * tokens), B16)
    out_shape = [
        stacked, turned, stacked, turned,
        pltpu.VMEM((2 * KV, HD), F32),
        pltpu.VMEM((HD, tokens), F32),
        pltpu.VMEM((HD, tokens), F32),
        pltpu.VMEM((KV * HD, slots), B16),
        pltpu.VMEM((KV * HD, slots), B16),
        pltpu.VMEM((2 * slots, HD), B16),
    ]
    return pl.pallas_call(
        functools.partial(prep_kernel, tokens),
        grid=(KV,),
        in_specs=[
            wide, wide, pl.BlockSpec((GROUP, HD), lambda i: (i, 0)),
            whole((KV, HD)), whole((KV, HD)), vmem, vmem, vmem, vmem,
        ],
        out_specs=[vmem] * len(out_shape),
        out_shape=out_shape,
        compiler_params=params(),
        cost_estimate=pl.CostEstimate(
            flops=4 * tokens * HQ * HD, bytes_accessed=12 * tokens * HQ * HD, transcendentals=0
        ),
        name="prep",
    )(q, do, bq, bk, bv, cosine, sine, ck, cv)


def fold(x, op):
    return op(x.reshape(x.shape[0] // 8, 8, x.shape[1]), axis=0)


def attend_kernel(g, shards, *refs):
    refs = list(refs)

    def take(count):
        taken = refs[:count]
        del refs[:count]
        return taken

    (first_ref, rank_ref, qs_ref, qst_ref, dos_ref, dot_ref, bias_ref, cos_t_ref, sin_t_ref,
     ck_t_ref, cv_t_ref, cos_ref, sin_ref, ck_ref, cv_ref, kp_ref, vp_ref) = take(17)
    far = take(shards - 1)
    far_k = take(shards - 1)
    far_v = take(shards - 1)
    old_sums_ref = take(1)[0] if g else None
    old_send = take(shards - 1) if g % 2 else []
    owns = take(2) if g == KV - 1 else []
    backs = take(shards - 1) if g == KV - 1 else []
    if g:
        take(2)
    out_ref, gq_ref, sums_ref, own_ref = take(4)
    send = take(shards - 1)
    pack_ref = take(1)[0] if g + 2 < KV else None
    gk_ref, gv_ref = take(2) if g == KV - 1 else (None, None)
    keys, values, keys_t, values_t, dk_acc, dv_acc = take(6)
    scratch = take(3)
    tokens = kp_ref.shape[0]
    slots = ck_ref.shape[0]
    prefix = shards * slots
    slab = shards * tokens
    total = prefix + slab
    first = first_ref[0]
    rank = rank_ref[0]
    mine = pl.ds(g * HD, HD)

    if pack_ref is not None:
        copy_chunk(g + 2, ck_ref, cv_ref, pack_ref)
    keys[pl.ds(0, slots)] = ck_ref[:, mine]
    values[pl.ds(0, slots)] = cv_ref[:, mine]
    for s in range(1, shards):
        keys[pl.ds(s * slots, slots)] = far[s - 1][pl.ds(0, slots)]
        values[pl.ds(s * slots, slots)] = far[s - 1][pl.ds(slots, slots)]
    for s in range(shards):
        rows = pl.ds(s * tokens, tokens)
        kp, vp = (kp_ref, vp_ref) if s == 0 else (far_k[s - 1], far_v[s - 1])
        k = kp[:, mine].astype(F32) + bias_ref[g:g + 1, :]
        k = k * cos_ref[rows, :] + turn(k) * sin_ref[rows, :]
        v = vp[:, mine].astype(F32) + bias_ref[KV + g:KV + g + 1, :]
        place = pl.ds(prefix + s * tokens, tokens)
        keys[place] = k.astype(B16)
        values[place] = v.astype(B16)
    keys_t[:, pl.ds(0, slots)] = ck_t_ref[mine, :]
    values_t[:, pl.ds(0, slots)] = cv_t_ref[mine, :]
    rest = pl.ds(slots, prefix - slots + slab)
    keys_t[:, rest] = keys[rest, :].T
    values_t[:, rest] = values[rest, :].T
    sums_ref[...] = jnp.zeros_like(sums_ref) if old_sums_ref is None else old_sums_ref[...]
    dk_acc[...] = jnp.zeros_like(dk_acc)
    dv_acc[...] = jnp.zeros_like(dv_acc)

    width = HEADS * tokens
    scale = HD ** -0.5
    blocks = range(0, total, tokens)
    def allowed(start, s):
        row = lax.broadcasted_iota(jnp.int32, s.shape, 0)
        if start < prefix:
            owner = lax.rem(rank - start // slots + shards, shards)
            return row < first - owner * slots - start % slots
        if start < prefix + tokens:
            return row <= (lax.broadcasted_iota(jnp.int32, s.shape, 1) & (tokens - 1))
        return row < jnp.where(rank >= (start - prefix) // tokens, tokens, 0)

    class Chain:
        def __init__(self, index):
            self.index = index
            self.s, self.pb, self.ds = scratch
            self.rows = pl.ds(pl.multiple_of(index * width, width), width)
            self.place = pl.ds(pl.multiple_of(index * HD, HD), HD)
            self.top = jnp.full((8, width), NEG, F32)

        def scores(self):
            s = dot(keys[...], qst_ref[self.place, :], NN)
            for start in blocks:
                part = s[start:start + tokens]
                part = jnp.where(allowed(start, part), part, NEG)
                self.s[pl.ds(start, tokens), :] = part
                self.top = jnp.maximum(self.top, fold(part, jnp.max))

        def probs(self):
            top = jnp.max(self.top, axis=0, keepdims=True)
            weight = jnp.zeros((8, width), F32)
            for start in blocks:
                rows = pl.ds(start, tokens)
                e = jnp.exp2((self.s[rows, :] - top) * (scale * math.log2(math.e)))
                self.s[rows, :] = e
                weight = weight + fold(e, jnp.sum)
            inverse = 1.0 / jnp.sum(weight, axis=0, keepdims=True)
            for start in blocks:
                rows = pl.ds(start, tokens)
                p = self.s[rows, :] * inverse
                self.s[rows, :] = p
                self.pb[rows, :] = p.astype(B16)

        def output(self):
            self.o = dot(values_t[...], self.pb[...], NN).astype(B16)
            do = dot_ref[self.place, :].astype(F32)
            self.delta = jnp.sum(do * self.o.astype(F32), axis=0, keepdims=True)

        def heads(self):
            for i in range(HEADS):
                head = self.index * HEADS + i
                yield (
                    slice(i * tokens, (i + 1) * tokens),
                    pl.ds(pl.multiple_of((head - g * GROUP) * HD, HD), HD),
                    head,
                )

        def dscores(self):
            dp = dot(values[...], dot_ref[self.place, :], NN)
            for start in blocks:
                rows = pl.ds(start, tokens)
                part = dp[start:start + tokens]
                self.ds[rows, :] = (self.s[rows, :] * (part - self.delta)).astype(B16)

        def query_grad(self):
            self.dq = (dot(keys_t[...], self.ds[...], NN) * scale).astype(B16).astype(F32)

        def slab_grads(self):
            last = pl.ds(prefix, slab)
            dv_acc[...] += dot(self.pb[last, :], dos_ref[self.rows, :], NN)
            dk_acc[...] += dot(self.ds[last, :], qs_ref[self.rows, :], NN)

        def store(self):
            for part, cols, head in self.heads():
                out_ref[:, cols] = self.o[:, part].T
                x = self.dq[:, part]
                other = jnp.concatenate([x[HD // 2:], x[:HD // 2]], axis=0)
                x = (x * cos_t_ref[...] - other * sin_t_ref[...]).T
                gq_ref[:, cols] = x.astype(B16)
                sums_ref[pl.ds(head, 1), :] = jnp.sum(x, axis=0, keepdims=True)

    def heads_step(i, carry):
        chain = Chain(g * (GROUP // HEADS) + i)
        chain.scores()
        chain.probs()
        chain.output()
        chain.dscores()
        chain.query_grad()
        chain.slab_grads()
        chain.store()
        return carry

    lax.fori_loop(0, GROUP // HEADS, heads_step, 0)

    dk = dk_acc[...] * scale
    dv = dv_acc[...]
    gk = turn_back(dk, cos_ref[...], sin_ref[...])
    own_ref[0] = dk[:tokens]
    own_ref[1] = dv[:tokens]
    at = 2 * (g % 2)
    for j in range(1, shards):
        block = slice(j * tokens, (j + 1) * tokens)
        send[j - 1][at] = dk[block].astype(B16)
        send[j - 1][at + 1] = dv[block].astype(B16)
        if at:
            send[j - 1][pl.ds(0, at)] = old_send[j - 1][...]
    sums_ref[pl.ds(HQ + g, 1), :] = jnp.sum(gk, axis=0, keepdims=True)
    sums_ref[pl.ds(HQ + KV + g, 1), :] = jnp.sum(dv, axis=0, keepdims=True)
    if gk_ref is not None:
        finish_heads(2, shards, (cos_ref, sin_ref), owns, backs, gk_ref, gv_ref)


def attend(
    g, shards, first, rank, prepared, cosine, sine, ck, cv, kp, vp, far, far_k, far_v,
    before, owns, backs,
):
    tokens, slots = kp.shape[0], ck.shape[0]
    slab = shards * tokens
    total = slab + shards * slots
    last = g == KV - 1
    smem = pl.BlockSpec(memory_space=pltpu.SMEM)
    vmem = pl.BlockSpec(memory_space=pltpu.VMEM)
    anywhere = pl.BlockSpec(memory_space=pl.ANY)
    wide = pl.BlockSpec((tokens, GROUP * HD), lambda i: (0, g))
    half = pl.BlockSpec((tokens, 2 * HD), lambda i: (0, 0))

    args = [first, rank]
    placed = [*prepared, cosine, sine, ck, cv, kp, vp, *far, *far_k, *far_v]
    aliases = {}
    if before is not None:
        out, gq, sums, send = before
        placed.append(sums)
        if g % 2:
            placed += send
        if last:
            placed += [*owns[:2], *backs]
    args += placed
    in_specs = [smem] * 2 + [vmem] * len(placed)
    if before is not None:
        aliases = {len(args): 0, len(args) + 1: 1}
        args += [out, gq]
        in_specs += [anywhere] * 2
    out_shape = [
        pltpu.HBM((tokens, HQ * HD), B16),
        pltpu.HBM((tokens, HQ * HD), B16),
        pltpu.VMEM((SUMS, HD), F32),
        pltpu.VMEM((2, tokens, HD), F32),
    ]
    out_specs = [wide, wide, vmem, vmem]
    out_shape += [pltpu.VMEM((2 + 2 * (g % 2), tokens, HD), B16)] * (shards - 1)
    out_specs += [vmem] * (shards - 1)
    if g + 2 < KV:
        out_shape.append(pltpu.VMEM((2 * slots, HD), B16))
        out_specs.append(vmem)
    if last:
        out_shape += [pltpu.HBM((tokens, KV * HD), B16)] * 2
        out_specs += [half] * 2
    results = pl.pallas_call(
        functools.partial(attend_kernel, g, shards),
        grid=(1,),
        in_specs=in_specs,
        out_shape=out_shape,
        out_specs=out_specs,
        scratch_shapes=[
            pltpu.VMEM((total, HD), B16), pltpu.VMEM((total, HD), B16),
            pltpu.VMEM((HD, total), B16), pltpu.VMEM((HD, total), B16),
            pltpu.VMEM((slab, HD), F32), pltpu.VMEM((slab, HD), F32),
        ] + [
            pltpu.VMEM((total, HEADS * tokens), kind) for kind in (F32, B16, B16)
        ],
        input_output_aliases=aliases,
        compiler_params=params(),
        cost_estimate=pl.CostEstimate(
            flops=2 * GROUP * tokens * HD * (4 * total + 2 * slab),
            bytes_accessed=8 * tokens * GROUP * HD + 8 * total * HD,
            transcendentals=GROUP * tokens * total,
        ),
        name="attend",
    )(*args)
    out, gq, sums, own = results[:4]
    send = results[4:4 + shards - 1]
    return (out, gq, sums, send), own, results[4 + shards - 1:]


def finish_kernel(shards, *refs):
    owns, backs = refs[2:4], refs[4:4 + shards - 1]
    sums = refs[4 + shards - 1:-7]
    gk_ref, gv_ref, *parts = refs[-5:]
    finish_heads(2, shards, refs[:2], owns, backs, gk_ref, gv_ref)
    start = 0
    for part in parts:
        rows = pl.ds(start, part.shape[0])
        part[...] = add_up([ref[rows, :] for ref in sums])
        start += part.shape[0]


def finish(shards, cosine, sine, owns, backs, sums, gk, gv):
    tokens = gk.shape[0]
    vmem = pl.BlockSpec(memory_space=pltpu.VMEM)
    args = [cosine, sine, *owns, *backs, *sums]
    heads = [(HQ, HD), (KV, HD), (KV, HD)]
    return pl.pallas_call(
        functools.partial(finish_kernel, shards),
        grid=(1,),
        in_specs=[vmem] * len(args) + [pl.BlockSpec(memory_space=pl.ANY)] * 2,
        out_specs=[pl.BlockSpec((tokens, 2 * HD), lambda i: (0, 1))] * 2
        + [whole(shape) for shape in heads],
        out_shape=[pltpu.HBM(gk.shape, B16)] * 2 + [pltpu.HBM(shape, F32) for shape in heads],
        input_output_aliases={len(args): 0, len(args) + 1: 1},
        compiler_params=params(),
        cost_estimate=pl.CostEstimate(flops=0, bytes_accessed=1 << 19, transcendentals=0),
        name="finish",
    )(*args, gk, gv)


def add_up(parts):
    while len(parts) > 1:
        parts = [a + b for a, b in zip(parts[::2], parts[1::2])]
    return parts[0]


def sum_but_last(x, axes, near):
    devices = lax.axis_size(axes)
    bits = [1 << i for i in range(devices.bit_length() - 1) if 1 << i != near]
    stages = [[near]] + [bits[i:i + 2] for i in range(0, len(bits), 2)]
    parts = [x]
    for stage in stages:
        x = add_up(parts)
        parts = [x]
        for flip in [sum(c) for n in (1, 2) for c in itertools.combinations(stage, n)]:
            parts.append(lax.ppermute(x, axes, [(i, i ^ flip) for i in range(devices)]))
    return parts


def body(q_proj, k_proj, v_proj, cache_k, cache_v, bias_q, bias_k, bias_v, start, dout):
    shards = lax.axis_size("seq")
    rank = lax.axis_index("seq").astype(jnp.int32)
    tokens = q_proj.shape[1]
    ck, cv, kp, vp = cache_k[0], cache_v[0], k_proj[0], v_proj[0]

    def ring(x, s):
        return lax.ppermute(x, "seq", [(i, (i + s) % shards) for i in range(shards)])

    def later(x, s):
        return lax.ppermute(x, "seq", [(i, i + s) for i in range(shards - s)])

    def earlier(x, s):
        return lax.ppermute(x, "seq", [(i + s, i) for i in range(shards - s)])

    shifts = range(1, shards)
    far_k = [later(kp, s) for s in shifts]
    far_v = [later(vp, s) for s in shifts]
    hbm = functools.partial(pltpu.with_memory_space_constraint, memory_space=pltpu.HBM)
    chunk = pack(0, hbm(ck), hbm(cv))
    far = [[ring(chunk, s) for s in shifts]]

    owners = lax.rem(rank - jnp.arange(shards, dtype=jnp.int32) + shards, shards)
    positions = start[0] + owners[:, None] * tokens + jnp.arange(tokens, dtype=jnp.int32)[None]
    lane = jnp.arange(HD, dtype=jnp.int32)
    freqs = jnp.exp(
        -(2.0 * (lane % (HD // 2)).astype(F32) / HD) * jnp.log(jnp.float32(1000000.0))
    )
    angles = positions.reshape(-1).astype(F32)[:, None] * freqs[None, :]
    cosine = jnp.cos(angles)
    sine = jnp.sin(angles) * jnp.where(lane < HD // 2, -1.0, 1.0).astype(F32)[None]

    *prepared, chunk = prep(
        hbm(q_proj[0]), hbm(dout[0]), hbm(bias_q.reshape(HQ, HD)),
        hbm(bias_k.reshape(KV, HD)), hbm(bias_v.reshape(KV, HD)), cosine, sine, ck, cv,
    )
    far.append([ring(chunk, s) for s in shifts])
    before, owns, backs = None, [], []
    for g in range(KV):
        before, own, more = attend(
            g, shards, start, rank.reshape(1), prepared, cosine, sine, ck, cv, kp, vp,
            far[g], far_k, far_v, before, owns, backs,
        )
        owns.append(own)
        if g + 2 < KV:
            far.append([ring(more[0], s) for s in shifts])
        if g % 2:
            backs = [earlier(x, s) for s, x in zip(shifts, before[3])]
    out, gq, sums, _ = before
    parts = sum_but_last(sums, ("dp", "seq"), shards)
    gk, gv, *sums = finish(shards, cosine, sine, owns[2:], backs, parts, *more)
    return (out[None], gq[None], gk[None], gv[None], *[x.reshape(-1) for x in sums])


def solution(mesh):
    split = P("dp", "seq", None)
    return jax.shard_map(
        body,
        mesh=mesh,
        in_specs=(split,) * 5 + (P(), P(), P(), P("dp"), split),
        out_specs=(split,) * 4 + (P(), P(), P()),
        check_vma=False,
    )
```

```python
import functools
import itertools
import math

import jax
import jax.numpy as jnp
from jax import lax
from jax.experimental import pallas as pl
from jax.experimental.pallas import tpu as pltpu
from jax.sharding import PartitionSpec as P

HQ = 32
KV = 4
HD = 128
GROUP = 8
HEADS = 4
NEG = -1e30
SUMS = HQ + 2 * KV
VMEM = 28 * 1024 * 1024
F32, B16 = jnp.float32, jnp.bfloat16


def turn(x):
    return pltpu.roll(x, HD // 2, 1)


def dot(a, b, dims):
    return lax.dot_general(a, b, (dims, ((), ())), preferred_element_type=F32)


NN = ((1,), (0,))


def whole(shape):
    return pl.BlockSpec(shape, lambda i: (0,) * len(shape))


def column(rows, g):
    return pl.BlockSpec((rows, HD), lambda i: (0, g))


def params():
    return pltpu.CompilerParams(dimension_semantics=("arbitrary",), vmem_limit_bytes=VMEM)


def copy_chunk(g, ck_ref, cv_ref, out_ref):
    rows = ck_ref.shape[0]
    cols = pl.ds(g * HD, HD)
    out_ref[pl.ds(0, rows)] = ck_ref[:, cols]
    out_ref[pl.ds(rows, rows)] = cv_ref[:, cols]


def pack_kernel(g, with_slab, *refs):
    out_ref = refs[-1]
    if with_slab:
        ck_ref, cv_ref, kp_ref, vp_ref = refs[:4]
        rows, tokens = ck_ref.shape[0], kp_ref.shape[0]
        out_ref[pl.ds(2 * rows, tokens)] = kp_ref[...]
        out_ref[pl.ds(2 * rows + tokens, tokens)] = vp_ref[...]
        copy_chunk(0, ck_ref, cv_ref, out_ref)
    else:
        copy_chunk(g, *refs[:2], out_ref)


def pack(g, ck, cv, slab=(), after=()):
    rows = 2 * ck.shape[0] + sum(x.shape[0] for x in slab)
    vmem = pl.BlockSpec(memory_space=pltpu.VMEM)
    in_specs = [column(x.shape[0], g) for x in (ck, cv, *slab)] if slab else [vmem] * 2
    return pl.pallas_call(
        functools.partial(pack_kernel, g, bool(slab)),
        grid=(1,),
        in_specs=in_specs + [pl.BlockSpec(memory_space=pl.ANY)] * len(after),
        out_specs=vmem,
        out_shape=pltpu.VMEM((rows, HD), B16),
        compiler_params=params(),
        cost_estimate=pl.CostEstimate(flops=0, bytes_accessed=4 * rows * HD, transcendentals=0),
        name="pack",
    )(ck, cv, *slab, *after)


def turn_back(x, cosine, sine):
    return x * cosine - turn(x) * sine


def finish_heads(heads, shards, tables, owns, backs, gk_ref, gv_ref):
    tokens = gk_ref.shape[0]
    cosine, sine = (t[pl.ds(0, tokens), :] for t in tables)
    for i in range(heads):
        dk, dv = owns[i][0], owns[i][1]
        for s in range(shards - 1):
            dk = dk + backs[s][2 * i].astype(F32)
            dv = dv + backs[s][2 * i + 1].astype(F32)
        cols = pl.ds(i * HD, HD)
        gk_ref[:, cols] = turn_back(dk, cosine, sine).astype(B16)
        gv_ref[:, cols] = dv.astype(B16)


def prep_kernel(
    tokens, q_ref, do_ref, bq_ref, bk_ref, bv_ref, cos_ref, sin_ref, ck_ref, cv_ref,
    kp_ref, vp_ref, qs_ref, qst_ref, dos_ref, dot_ref, bias_ref, cos_t_ref, sin_t_ref, ck_t_ref, cv_t_ref, pack_ref, slab_ref,
):
    g = pl.program_id(0)
    cosine, sine = cos_ref[pl.ds(0, tokens), :], sin_ref[pl.ds(0, tokens), :]
    bias_q = bq_ref[...].astype(F32)

    @pl.when(g == 0)
    def _():
        bias_ref[pl.ds(0, KV), :] = bk_ref[...].astype(F32)
        bias_ref[pl.ds(KV, KV), :] = bv_ref[...].astype(F32)
        cos_t_ref[...] = cosine.T
        sin_t_ref[...] = sine.T
        copy_chunk(1, ck_ref, cv_ref, pack_ref)
        others = pl.ds(HD, (KV - 1) * HD)
        slab_ref[0] = kp_ref[:, others]
        slab_ref[1] = vp_ref[:, others]

    for h in range(GROUP):
        cols = pl.ds(h * HD, HD)
        rows = pl.ds(pl.multiple_of((g * GROUP + h) * tokens, tokens), tokens)
        x = q_ref[:, cols].astype(F32) + bias_q[h:h + 1]
        x = (x * cosine + turn(x) * sine).astype(B16)
        qs_ref[rows, :] = x
        do = do_ref[:, cols]
        dos_ref[rows, :] = do
        chain, part = h // HEADS, h % HEADS
        place = pl.ds(pl.multiple_of((g * (GROUP // HEADS) + chain) * HD, HD), HD)
        qst_ref[place, pl.ds(part * tokens, tokens)] = x.T
        dot_ref[place, pl.ds(part * tokens, tokens)] = do.T
    mine = pl.ds(pl.multiple_of(g * HD, HD), HD)
    ck_t_ref[mine, :] = ck_ref[:, mine].T
    cv_t_ref[mine, :] = cv_ref[:, mine].T


def prep(q, do, bq, bk, bv, cosine, sine, ck, cv, kp, vp):
    tokens, slots = q.shape[0], ck.shape[0]
    vmem = pl.BlockSpec(memory_space=pltpu.VMEM)
    wide = pl.BlockSpec((tokens, GROUP * HD), lambda i: (0, i))
    stacked = pltpu.VMEM((HQ * tokens, HD), B16)
    turned = pltpu.VMEM((HQ // HEADS * HD, HEADS * tokens), B16)
    out_shape = [
        stacked, turned, stacked, turned,
        pltpu.VMEM((2 * KV, HD), F32),
        pltpu.VMEM((HD, tokens), F32),
        pltpu.VMEM((HD, tokens), F32),
        pltpu.VMEM((KV * HD, slots), B16),
        pltpu.VMEM((KV * HD, slots), B16),
        pltpu.VMEM((2 * slots, HD), B16),
        pltpu.VMEM((2, tokens, (KV - 1) * HD), B16),
    ]
    return pl.pallas_call(
        functools.partial(prep_kernel, tokens),
        grid=(KV,),
        in_specs=[
            wide, wide, pl.BlockSpec((GROUP, HD), lambda i: (i, 0)),
            whole((KV, HD)), whole((KV, HD)), *[vmem] * 6,
        ],
        out_specs=[vmem] * len(out_shape),
        out_shape=out_shape,
        compiler_params=params(),
        cost_estimate=pl.CostEstimate(
            flops=4 * tokens * HQ * HD, bytes_accessed=12 * tokens * HQ * HD, transcendentals=0
        ),
        name="prep",
    )(q, do, bq, bk, bv, cosine, sine, ck, cv, kp, vp)


def fold(x, op):
    return op(x.reshape(x.shape[0] // 8, 8, x.shape[1]), axis=0)


def attend_kernel(g, shards, *refs):
    refs = list(refs)

    def take(count):
        taken = refs[:count]
        del refs[:count]
        return taken

    (first_ref, rank_ref, qs_ref, qst_ref, dos_ref, dot_ref, bias_ref, cos_t_ref, sin_t_ref,
     ck_t_ref, cv_t_ref, cos_ref, sin_ref, ck_ref, cv_ref, kp_ref, vp_ref) = take(17)
    far = take(shards - 1)
    far_slab = take(shards - 1) if g else []
    old_sums_ref = take(1)[0] if g else None
    old_send = take(shards - 1) if g % 2 else []
    owns = take(2) if g == KV - 1 else []
    backs = take(shards - 1) if g == KV - 1 else []
    if g:
        take(2)
    out_ref, gq_ref, sums_ref, own_ref = take(4)
    send = take(shards - 1)
    pack_ref = take(1)[0] if g == 0 else None
    gk_ref, gv_ref = take(2) if g == KV - 1 else (None, None)
    keys, values, keys_t, values_t, dk_acc, dv_acc = take(6)
    scratch = take(3)
    tokens = kp_ref.shape[0]
    slots = ck_ref.shape[0]
    prefix = shards * slots
    slab = shards * tokens
    total = prefix + slab
    first = first_ref[0]
    rank = rank_ref[0]
    mine = pl.ds(g * HD, HD)

    if pack_ref is not None:
        copy_chunk(g + 2, ck_ref, cv_ref, pack_ref)
    keys[pl.ds(0, slots)] = ck_ref[:, mine]
    values[pl.ds(0, slots)] = cv_ref[:, mine]
    for s in range(1, shards):
        keys[pl.ds(s * slots, slots)] = far[s - 1][pl.ds(0, slots)]
        values[pl.ds(s * slots, slots)] = far[s - 1][pl.ds(slots, slots)]
    for s in range(shards):
        rows = pl.ds(s * tokens, tokens)
        if s == 0:
            kp, vp = kp_ref[:, mine], vp_ref[:, mine]
        elif g == 0:
            kp, vp = (far[s - 1][pl.ds(2 * slots + i * tokens, tokens)] for i in range(2))
        else:
            kp, vp = (far_slab[s - 1][i, :, pl.ds((g - 1) * HD, HD)] for i in range(2))
        k = kp.astype(F32) + bias_ref[g:g + 1, :]
        k = k * cos_ref[rows, :] + turn(k) * sin_ref[rows, :]
        v = vp.astype(F32) + bias_ref[KV + g:KV + g + 1, :]
        place = pl.ds(prefix + s * tokens, tokens)
        keys[place] = k.astype(B16)
        values[place] = v.astype(B16)
    keys_t[:, pl.ds(0, slots)] = ck_t_ref[mine, :]
    values_t[:, pl.ds(0, slots)] = cv_t_ref[mine, :]
    rest = pl.ds(slots, prefix - slots + slab)
    keys_t[:, rest] = keys[rest, :].T
    values_t[:, rest] = values[rest, :].T
    sums_ref[...] = jnp.zeros_like(sums_ref) if old_sums_ref is None else old_sums_ref[...]
    dk_acc[...] = jnp.zeros_like(dk_acc)
    dv_acc[...] = jnp.zeros_like(dv_acc)

    width = HEADS * tokens
    scale = HD ** -0.5
    blocks = range(0, total, tokens)
    def allowed(start, s):
        row = lax.broadcasted_iota(jnp.int32, s.shape, 0)
        if start < prefix:
            owner = lax.rem(rank - start // slots + shards, shards)
            return row < first - owner * slots - start % slots
        if start < prefix + tokens:
            return row <= (lax.broadcasted_iota(jnp.int32, s.shape, 1) & (tokens - 1))
        return row < jnp.where(rank >= (start - prefix) // tokens, tokens, 0)

    class Chain:
        def __init__(self, index):
            self.index = index
            self.s, self.pb, self.ds = scratch
            self.rows = pl.ds(pl.multiple_of(index * width, width), width)
            self.place = pl.ds(pl.multiple_of(index * HD, HD), HD)
            self.top = jnp.full((8, width), NEG, F32)

        def scores(self):
            s = dot(keys[...], qst_ref[self.place, :], NN)
            for start in blocks:
                part = s[start:start + tokens]
                part = jnp.where(allowed(start, part), part, NEG)
                self.s[pl.ds(start, tokens), :] = part
                self.top = jnp.maximum(self.top, fold(part, jnp.max))

        def exponents(self):
            top = jnp.max(self.top, axis=0, keepdims=True)
            weight = jnp.zeros((8, width), F32)
            for start in blocks:
                rows = pl.ds(start, tokens)
                e = jnp.exp2((self.s[rows, :] - top) * (scale * math.log2(math.e)))
                self.s[rows, :] = e
                self.pb[rows, :] = e.astype(B16)
                weight = weight + fold(e, jnp.sum)
            self.inverse = 1.0 / jnp.sum(weight, axis=0, keepdims=True)

        def output(self):
            self.o = (dot(values_t[...], self.pb[...], NN) * self.inverse).astype(B16)
            do = dot_ref[self.place, :].astype(F32)
            self.delta = jnp.sum(do * self.o.astype(F32), axis=0, keepdims=True)

        def heads(self):
            for i in range(HEADS):
                head = self.index * HEADS + i
                yield (
                    slice(i * tokens, (i + 1) * tokens),
                    pl.ds(pl.multiple_of((head - g * GROUP) * HD, HD), HD),
                    head,
                )

        def dscores(self):
            dp = dot(values[...], dot_ref[self.place, :], NN)
            for start in blocks:
                rows = pl.ds(start, tokens)
                p = self.s[rows, :] * self.inverse
                self.ds[rows, :] = (p * (dp[start:start + tokens] - self.delta)).astype(B16)
                if start >= prefix:
                    self.pb[rows, :] = p.astype(B16)

        def query_grad(self):
            self.dq = (dot(keys_t[...], self.ds[...], NN) * scale).astype(B16).astype(F32)

        def slab_grads(self):
            last = pl.ds(prefix, slab)
            dv_acc[...] += dot(self.pb[last, :], dos_ref[self.rows, :], NN)
            dk_acc[...] += dot(self.ds[last, :], qs_ref[self.rows, :], NN)

        def store(self):
            for part, cols, head in self.heads():
                out_ref[:, cols] = self.o[:, part].T
                x = self.dq[:, part]
                other = jnp.concatenate([x[HD // 2:], x[:HD // 2]], axis=0)
                x = (x * cos_t_ref[...] - other * sin_t_ref[...]).T
                gq_ref[:, cols] = x.astype(B16)
                sums_ref[pl.ds(head, 1), :] = jnp.sum(x, axis=0, keepdims=True)

    def heads_step(i, carry):
        chain = Chain(g * (GROUP // HEADS) + i)
        chain.scores()
        chain.exponents()
        chain.output()
        chain.dscores()
        chain.query_grad()
        chain.slab_grads()
        chain.store()
        return carry

    lax.fori_loop(0, GROUP // HEADS, heads_step, 0)

    dk = dk_acc[...] * scale
    dv = dv_acc[...]
    gk = turn_back(dk, cos_ref[...], sin_ref[...])
    own_ref[0] = dk[:tokens]
    own_ref[1] = dv[:tokens]
    at = 2 * (g % 2)
    for j in range(1, shards):
        block = slice(j * tokens, (j + 1) * tokens)
        send[j - 1][at] = dk[block].astype(B16)
        send[j - 1][at + 1] = dv[block].astype(B16)
        if at:
            send[j - 1][pl.ds(0, at)] = old_send[j - 1][...]
    sums_ref[pl.ds(HQ + g, 1), :] = jnp.sum(gk, axis=0, keepdims=True)
    sums_ref[pl.ds(HQ + KV + g, 1), :] = jnp.sum(dv, axis=0, keepdims=True)
    if gk_ref is not None:
        finish_heads(2, shards, (cos_ref, sin_ref), owns, backs, gk_ref, gv_ref)


def attend(
    g, shards, first, rank, prepared, cosine, sine, ck, cv, kp, vp, far, far_slab,
    before, owns, backs,
):
    tokens, slots = kp.shape[0], ck.shape[0]
    slab = shards * tokens
    total = slab + shards * slots
    last = g == KV - 1
    smem = pl.BlockSpec(memory_space=pltpu.SMEM)
    vmem = pl.BlockSpec(memory_space=pltpu.VMEM)
    anywhere = pl.BlockSpec(memory_space=pl.ANY)
    wide = pl.BlockSpec((tokens, GROUP * HD), lambda i: (0, g))
    half = pl.BlockSpec((tokens, 2 * HD), lambda i: (0, 0))

    args = [first, rank]
    placed = [*prepared, cosine, sine, ck, cv, kp, vp, *far, *far_slab]
    aliases = {}
    if before is not None:
        out, gq, sums, send = before
        placed.append(sums)
        if g % 2:
            placed += send
        if last:
            placed += [*owns[:2], *backs]
    args += placed
    in_specs = [smem] * 2 + [vmem] * len(placed)
    if before is not None:
        aliases = {len(args): 0, len(args) + 1: 1}
        args += [out, gq]
        in_specs += [anywhere] * 2
    out_shape = [
        pltpu.HBM((tokens, HQ * HD), B16),
        pltpu.HBM((tokens, HQ * HD), B16),
        pltpu.VMEM((SUMS, HD), F32),
        pltpu.VMEM((2, tokens, HD), F32),
    ]
    out_specs = [wide, wide, vmem, vmem]
    out_shape += [pltpu.VMEM((2 + 2 * (g % 2), tokens, HD), B16)] * (shards - 1)
    out_specs += [vmem] * (shards - 1)
    if g == 0:
        out_shape.append(pltpu.VMEM((2 * slots, HD), B16))
        out_specs.append(vmem)
    if last:
        out_shape += [pltpu.HBM((tokens, KV * HD), B16)] * 2
        out_specs += [half] * 2
    results = pl.pallas_call(
        functools.partial(attend_kernel, g, shards),
        grid=(1,),
        in_specs=in_specs,
        out_shape=out_shape,
        out_specs=out_specs,
        scratch_shapes=[
            pltpu.VMEM((total, HD), B16), pltpu.VMEM((total, HD), B16),
            pltpu.VMEM((HD, total), B16), pltpu.VMEM((HD, total), B16),
            pltpu.VMEM((slab, HD), F32), pltpu.VMEM((slab, HD), F32),
        ] + [
            pltpu.VMEM((total, HEADS * tokens), kind) for kind in (F32, B16, B16)
        ],
        input_output_aliases=aliases,
        compiler_params=params(),
        cost_estimate=pl.CostEstimate(
            flops=2 * GROUP * tokens * HD * (4 * total + 2 * slab),
            bytes_accessed=8 * tokens * GROUP * HD + 8 * total * HD,
            transcendentals=GROUP * tokens * total,
        ),
        name="attend",
    )(*args)
    out, gq, sums, own = results[:4]
    send = results[4:4 + shards - 1]
    return (out, gq, sums, send), own, results[4 + shards - 1:]


def finish_kernel(shards, *refs):
    owns, backs = refs[2:4], refs[4:4 + shards - 1]
    sums = refs[4 + shards - 1:-7]
    gk_ref, gv_ref, *parts = refs[-5:]
    finish_heads(2, shards, refs[:2], owns, backs, gk_ref, gv_ref)
    start = 0
    for part in parts:
        rows = pl.ds(start, part.shape[0])
        part[...] = add_up([ref[rows, :] for ref in sums])
        start += part.shape[0]


def finish(shards, cosine, sine, owns, backs, sums, gk, gv):
    tokens = gk.shape[0]
    vmem = pl.BlockSpec(memory_space=pltpu.VMEM)
    args = [cosine, sine, *owns, *backs, *sums]
    heads = [(HQ, HD), (KV, HD), (KV, HD)]
    return pl.pallas_call(
        functools.partial(finish_kernel, shards),
        grid=(1,),
        in_specs=[vmem] * len(args) + [pl.BlockSpec(memory_space=pl.ANY)] * 2,
        out_specs=[pl.BlockSpec((tokens, 2 * HD), lambda i: (0, 1))] * 2
        + [whole(shape) for shape in heads],
        out_shape=[pltpu.HBM(gk.shape, B16)] * 2 + [pltpu.HBM(shape, F32) for shape in heads],
        input_output_aliases={len(args): 0, len(args) + 1: 1},
        compiler_params=params(),
        cost_estimate=pl.CostEstimate(flops=0, bytes_accessed=1 << 19, transcendentals=0),
        name="finish",
    )(*args, gk, gv)


def add_up(parts):
    while len(parts) > 1:
        parts = [a + b for a, b in zip(parts[::2], parts[1::2])]
    return parts[0]


def sum_but_last(x, axes, near):
    devices = lax.axis_size(axes)
    bits = [1 << i for i in range(devices.bit_length() - 1) if 1 << i != near]
    stages = [[near]] + [bits[i:i + 2] for i in range(0, len(bits), 2)]
    parts = [x]
    for stage in stages:
        x = add_up(parts)
        parts = [x]
        for flip in [sum(c) for n in (1, 2) for c in itertools.combinations(stage, n)]:
            parts.append(lax.ppermute(x, axes, [(i, i ^ flip) for i in range(devices)]))
    return parts


def body(q_proj, k_proj, v_proj, cache_k, cache_v, bias_q, bias_k, bias_v, start, dout):
    shards = lax.axis_size("seq")
    rank = lax.axis_index("seq").astype(jnp.int32)
    tokens = q_proj.shape[1]
    shifts = range(1, shards)
    ck, cv, kp, vp = cache_k[0], cache_v[0], k_proj[0], v_proj[0]

    def ring(x, s):
        return lax.ppermute(x, "seq", [(i, (i + s) % shards) for i in range(shards)])

    def later(x, s):
        return lax.ppermute(x, "seq", [(i, i + s) for i in range(shards - s)])

    def earlier(x, s):
        return lax.ppermute(x, "seq", [(i + s, i) for i in range(shards - s)])

    hbm = functools.partial(pltpu.with_memory_space_constraint, memory_space=pltpu.HBM)
    chunk = pack(0, hbm(ck), hbm(cv), (hbm(kp), hbm(vp)))
    far = [[ring(chunk, s) for s in shifts]]

    owners = lax.rem(rank - jnp.arange(shards, dtype=jnp.int32) + shards, shards)
    positions = start[0] + owners[:, None] * tokens + jnp.arange(tokens, dtype=jnp.int32)[None]
    lane = jnp.arange(HD, dtype=jnp.int32)
    freqs = jnp.exp(
        -(2.0 * (lane % (HD // 2)).astype(F32) / HD) * jnp.log(jnp.float32(1000000.0))
    )
    angles = positions.reshape(-1).astype(F32)[:, None] * freqs[None, :]
    cosine = jnp.cos(angles)
    sine = jnp.sin(angles) * jnp.where(lane < HD // 2, -1.0, 1.0).astype(F32)[None]

    *prepared, chunk, own = prep(
        hbm(q_proj[0]), hbm(dout[0]), hbm(bias_q.reshape(HQ, HD)),
        hbm(bias_k.reshape(KV, HD)), hbm(bias_v.reshape(KV, HD)), cosine, sine, ck, cv, kp, vp,
    )
    far.append([ring(chunk, s) for s in shifts])
    far_slab = [later(own, s) for s in shifts]
    before, owns, backs = None, [], []
    for g in range(KV):
        if g == 1:
            chunk = pack(KV - 1, ck, cv, after=far[1])
            far.append([ring(chunk, s) for s in shifts])
        before, own, more = attend(
            g, shards, start, rank.reshape(1), prepared, cosine, sine, ck, cv, kp, vp,
            far[g], far_slab if g else [], before, owns, backs,
        )
        owns.append(own)
        if g == 0:
            far.append([ring(more[0], s) for s in shifts])
        if g % 2:
            backs = [earlier(x, s) for s, x in zip(shifts, before[3])]
    out, gq, sums, _ = before
    parts = sum_but_last(sums, ("dp", "seq"), shards)
    gk, gv, *sums = finish(shards, cosine, sine, owns[2:], backs, parts, *more)
    return (out[None], gq[None], gk[None], gv[None], *[x.reshape(-1) for x in sums])


def solution(mesh):
    split = P("dp", "seq", None)
    return jax.shard_map(
        body,
        mesh=mesh,
        in_specs=(split,) * 5 + (P(), P(), P(), P("dp"), split),
        out_specs=(split,) * 4 + (P(), P(), P()),
        check_vma=False,
    )
```

```python
import functools
import itertools
import math

import jax
import jax.numpy as jnp
from jax import lax
from jax.experimental import pallas as pl
from jax.experimental.pallas import tpu as pltpu
from jax.sharding import PartitionSpec as P

HQ = 32
KV = 4
HD = 128
GROUP = 8
HEADS = 4
NEG = -1e30
SUMS = HQ + 2 * KV
VMEM = 28 * 1024 * 1024
F32, B16 = jnp.float32, jnp.bfloat16


def turn(x):
    return pltpu.roll(x, HD // 2, 1)


def dot(a, b, dims):
    return lax.dot_general(a, b, (dims, ((), ())), preferred_element_type=F32)


NN = ((1,), (0,))


def whole(shape):
    return pl.BlockSpec(shape, lambda i: (0,) * len(shape))


def column(rows, g):
    return pl.BlockSpec((rows, HD), lambda i: (0, g))


def params():
    return pltpu.CompilerParams(dimension_semantics=("arbitrary",), vmem_limit_bytes=VMEM)


def copy_chunk(cols, sources, out_ref):
    start = 0
    for ref in sources:
        rows = ref.shape[0]
        out_ref[pl.ds(start, rows)] = ref[:, cols]
        start += rows


def pack_kernel(*refs):
    copy_chunk(pl.ds(0, HD), refs[:-1], refs[-1])


def pack(sources):
    rows = sum(x.shape[0] for x in sources)
    return pl.pallas_call(
        pack_kernel,
        grid=(1,),
        in_specs=[column(x.shape[0], 0) for x in sources],
        out_specs=pl.BlockSpec(memory_space=pltpu.VMEM),
        out_shape=pltpu.VMEM((rows, HD), B16),
        compiler_params=params(),
        cost_estimate=pl.CostEstimate(flops=0, bytes_accessed=4 * rows * HD, transcendentals=0),
        name="pack",
    )(*sources)


def turn_back(x, cosine, sine):
    return x * cosine - turn(x) * sine


def prep_kernel(
    tokens, q_ref, do_ref, bq_ref, bk_ref, bv_ref, cos_ref, sin_ref, ck_ref, cv_ref,
    kp_ref, vp_ref, qs_ref, qst_ref, dos_ref, dot_ref, bias_ref, cos_t_ref, sin_t_ref, ck_t_ref, cv_t_ref, pack_ref,
):
    g = pl.program_id(0)
    cosine, sine = cos_ref[pl.ds(0, tokens), :], sin_ref[pl.ds(0, tokens), :]
    bias_q = bq_ref[...].astype(F32)

    @pl.when(g == 0)
    def _():
        bias_ref[pl.ds(0, KV), :] = bk_ref[...].astype(F32)
        bias_ref[pl.ds(KV, KV), :] = bv_ref[...].astype(F32)
        cos_t_ref[...] = cosine.T
        sin_t_ref[...] = sine.T
        copy_chunk(pl.ds(HD, HD), (ck_ref, cv_ref, kp_ref, vp_ref), pack_ref)

    for h in range(GROUP):
        cols = pl.ds(h * HD, HD)
        rows = pl.ds(pl.multiple_of((g * GROUP + h) * tokens, tokens), tokens)
        x = q_ref[:, cols].astype(F32) + bias_q[h:h + 1]
        x = (x * cosine + turn(x) * sine).astype(B16)
        qs_ref[rows, :] = x
        do = do_ref[:, cols]
        dos_ref[rows, :] = do
        chain, part = h // HEADS, h % HEADS
        place = pl.ds(pl.multiple_of((g * (GROUP // HEADS) + chain) * HD, HD), HD)
        qst_ref[place, pl.ds(part * tokens, tokens)] = x.T
        dot_ref[place, pl.ds(part * tokens, tokens)] = do.T
    mine = pl.ds(pl.multiple_of(g * HD, HD), HD)
    ck_t_ref[mine, :] = ck_ref[:, mine].T
    cv_t_ref[mine, :] = cv_ref[:, mine].T


def prep(q, do, bq, bk, bv, cosine, sine, ck, cv, kp, vp):
    tokens, slots = q.shape[0], ck.shape[0]
    vmem = pl.BlockSpec(memory_space=pltpu.VMEM)
    wide = pl.BlockSpec((tokens, GROUP * HD), lambda i: (0, i))
    stacked = pltpu.VMEM((HQ * tokens, HD), B16)
    turned = pltpu.VMEM((HQ // HEADS * HD, HEADS * tokens), B16)
    out_shape = [
        stacked, turned, stacked, turned,
        pltpu.VMEM((2 * KV, HD), F32),
        pltpu.VMEM((HD, tokens), F32),
        pltpu.VMEM((HD, tokens), F32),
        pltpu.VMEM((KV * HD, slots), B16),
        pltpu.VMEM((KV * HD, slots), B16),
        pltpu.VMEM((2 * (slots + tokens), HD), B16),
    ]
    return pl.pallas_call(
        functools.partial(prep_kernel, tokens),
        grid=(KV,),
        in_specs=[
            wide, wide, pl.BlockSpec((GROUP, HD), lambda i: (i, 0)),
            whole((KV, HD)), whole((KV, HD)), *[vmem] * 6,
        ],
        out_specs=[vmem] * len(out_shape),
        out_shape=out_shape,
        compiler_params=params(),
        cost_estimate=pl.CostEstimate(
            flops=4 * tokens * HQ * HD, bytes_accessed=12 * tokens * HQ * HD, transcendentals=0
        ),
        name="prep",
    )(q, do, bq, bk, bv, cosine, sine, ck, cv, kp, vp)


def fold(x, op):
    return op(x.reshape(x.shape[0] // 8, 8, x.shape[1]), axis=0)


def attend_kernel(g, shards, *refs):
    refs = list(refs)

    def take(count):
        taken = refs[:count]
        del refs[:count]
        return taken

    (first_ref, rank_ref, qs_ref, qst_ref, dos_ref, dot_ref, bias_ref, cos_t_ref, sin_t_ref,
     ck_t_ref, cv_t_ref, cos_ref, sin_ref, ck_ref, cv_ref, kp_ref, vp_ref) = take(17)
    far = take(shards - 1)
    old_sums_ref = take(1)[0] if g else None
    old_send = take(shards - 1) if g else []
    if g:
        take(2)
    out_ref, gq_ref, sums_ref, own_ref = take(4)
    send = take(shards - 1)
    pack_ref = take(1)[0] if g + 2 < KV else None
    keys, values, keys_t, values_t, dk_acc, dv_acc = take(6)
    scratch = [take(3) for _ in range(GROUP // HEADS)]
    tokens = kp_ref.shape[0]
    slots = ck_ref.shape[0]
    prefix = shards * slots
    slab = shards * tokens
    total = prefix + slab
    first = first_ref[0]
    rank = rank_ref[0]
    mine = pl.ds(g * HD, HD)

    if pack_ref is not None:
        copy_chunk(pl.ds((g + 2) * HD, HD), (ck_ref, cv_ref, kp_ref, vp_ref), pack_ref)
    keys[pl.ds(0, slots)] = ck_ref[:, mine]
    values[pl.ds(0, slots)] = cv_ref[:, mine]
    for s in range(1, shards):
        keys[pl.ds(s * slots, slots)] = far[s - 1][pl.ds(0, slots)]
        values[pl.ds(s * slots, slots)] = far[s - 1][pl.ds(slots, slots)]
    for s in range(shards):
        rows = pl.ds(s * tokens, tokens)
        if s == 0:
            kp, vp = kp_ref[:, mine], vp_ref[:, mine]
        else:
            kp, vp = (far[s - 1][pl.ds(2 * slots + i * tokens, tokens)] for i in range(2))
        k = kp.astype(F32) + bias_ref[g:g + 1, :]
        k = k * cos_ref[rows, :] + turn(k) * sin_ref[rows, :]
        v = vp.astype(F32) + bias_ref[KV + g:KV + g + 1, :]
        place = pl.ds(prefix + s * tokens, tokens)
        keys[place] = k.astype(B16)
        values[place] = v.astype(B16)
    keys_t[:, pl.ds(0, slots)] = ck_t_ref[mine, :]
    values_t[:, pl.ds(0, slots)] = cv_t_ref[mine, :]
    rest = pl.ds(slots, prefix - slots + slab)
    keys_t[:, rest] = keys[rest, :].T
    values_t[:, rest] = values[rest, :].T
    sums_ref[...] = jnp.zeros_like(sums_ref) if old_sums_ref is None else old_sums_ref[...]
    dk_acc[...] = jnp.zeros_like(dk_acc)
    dv_acc[...] = jnp.zeros_like(dv_acc)

    width = HEADS * tokens
    scale = HD ** -0.5
    blocks = range(0, total, tokens)
    def allowed(start, s):
        row = lax.broadcasted_iota(jnp.int32, s.shape, 0)
        if start < prefix:
            owner = lax.rem(rank - start // slots + shards, shards)
            return row < first - owner * slots - start % slots
        if start < prefix + tokens:
            return row <= (lax.broadcasted_iota(jnp.int32, s.shape, 1) & (tokens - 1))
        return row < jnp.where(rank >= (start - prefix) // tokens, tokens, 0)

    class Chain:
        def __init__(self, index):
            self.index = g * (GROUP // HEADS) + index
            self.s, self.pb, self.ds = scratch[index]
            index = self.index
            self.rows = pl.ds(pl.multiple_of(index * width, width), width)
            self.place = pl.ds(pl.multiple_of(index * HD, HD), HD)
            self.top = jnp.full((8, width), NEG, F32)

        def scores(self):
            s = dot(keys[...], qst_ref[self.place, :], NN)
            for start in blocks:
                part = s[start:start + tokens]
                part = jnp.where(allowed(start, part), part, NEG)
                self.s[pl.ds(start, tokens), :] = part
                self.top = jnp.maximum(self.top, fold(part, jnp.max))

        def exponents(self):
            top = jnp.max(self.top, axis=0, keepdims=True)
            weight = jnp.zeros((8, width), F32)
            for start in blocks:
                rows = pl.ds(start, tokens)
                e = jnp.exp2((self.s[rows, :] - top) * (scale * math.log2(math.e)))
                self.s[rows, :] = e
                weight = weight + fold(e, jnp.sum)
            self.inverse = 1.0 / jnp.sum(weight, axis=0, keepdims=True)

        def probs(self):
            for start in blocks:
                rows = pl.ds(start, tokens)
                p = self.s[rows, :] * self.inverse
                self.s[rows, :] = p
                self.pb[rows, :] = p.astype(B16)

        def output(self):
            self.o = dot(values_t[...], self.pb[...], NN).astype(B16)
            do = dot_ref[self.place, :].astype(F32)
            self.delta = jnp.sum(do * self.o.astype(F32), axis=0, keepdims=True)

        def heads(self):
            for i in range(HEADS):
                head = self.index * HEADS + i
                yield (
                    slice(i * tokens, (i + 1) * tokens),
                    pl.ds(pl.multiple_of((head - g * GROUP) * HD, HD), HD),
                    head,
                )

        def dprobs(self):
            self.dp = dot(values[...], dot_ref[self.place, :], NN)

        def dscores(self):
            for start in blocks:
                rows = pl.ds(start, tokens)
                part = self.dp[start:start + tokens]
                self.ds[rows, :] = (self.s[rows, :] * (part - self.delta)).astype(B16)

        def query_grad(self):
            self.dq = (dot(keys_t[...], self.ds[...], NN) * scale).astype(B16).astype(F32)

        def slab_grads(self):
            last = pl.ds(prefix, slab)
            dv_acc[...] += dot(self.pb[last, :], dos_ref[self.rows, :], NN)
            dk_acc[...] += dot(self.ds[last, :], qs_ref[self.rows, :], NN)

        def store(self):
            for part, cols, head in self.heads():
                out_ref[:, cols] = self.o[:, part].T
                x = self.dq[:, part]
                other = jnp.concatenate([x[HD // 2:], x[:HD // 2]], axis=0)
                x = (x * cos_t_ref[...] - other * sin_t_ref[...]).T
                gq_ref[:, cols] = x.astype(B16)
                sums_ref[pl.ds(head, 1), :] = jnp.sum(x, axis=0, keepdims=True)

    steps = [
        Chain.scores, Chain.exponents, Chain.dprobs, Chain.probs, Chain.output,
        Chain.dscores, Chain.query_grad, Chain.slab_grads, Chain.store,
    ]
    group = [Chain(i) for i in range(GROUP // HEADS)]
    for turn_of in range(len(steps) + len(group) - 1):
        for i, chain in reversed(list(enumerate(group))):
            if 0 <= turn_of - i < len(steps):
                steps[turn_of - i](chain)

    dk = dk_acc[...] * scale
    dv = dv_acc[...]
    gk = turn_back(dk, cos_ref[...], sin_ref[...])
    own_ref[0] = dk[:tokens]
    own_ref[1] = dv[:tokens]
    at = 2 * g
    for j in range(1, shards):
        block = slice(j * tokens, (j + 1) * tokens)
        send[j - 1][at] = dk[block].astype(B16)
        send[j - 1][at + 1] = dv[block].astype(B16)
        if g:
            send[j - 1][pl.ds(0, at)] = old_send[j - 1][...]
    sums_ref[pl.ds(HQ + g, 1), :] = jnp.sum(gk, axis=0, keepdims=True)
    sums_ref[pl.ds(HQ + KV + g, 1), :] = jnp.sum(dv, axis=0, keepdims=True)


def attend(
    g, shards, first, rank, prepared, cosine, sine, ck, cv, kp, vp, far, before
):
    tokens, slots = kp.shape[0], ck.shape[0]
    slab = shards * tokens
    total = slab + shards * slots
    smem = pl.BlockSpec(memory_space=pltpu.SMEM)
    vmem = pl.BlockSpec(memory_space=pltpu.VMEM)
    anywhere = pl.BlockSpec(memory_space=pl.ANY)
    wide = pl.BlockSpec((tokens, GROUP * HD), lambda i: (0, g))

    args = [first, rank]
    placed = [*prepared, cosine, sine, ck, cv, kp, vp, *far]
    aliases = {}
    if before is not None:
        out, gq, sums, send = before
        placed += [sums, *send]
    args += placed
    in_specs = [smem] * 2 + [vmem] * len(placed)
    if before is not None:
        aliases = {len(args): 0, len(args) + 1: 1}
        args += [out, gq]
        in_specs += [anywhere] * 2
    out_shape = [
        pltpu.HBM((tokens, HQ * HD), B16),
        pltpu.HBM((tokens, HQ * HD), B16),
        pltpu.VMEM((SUMS, HD), F32),
        pltpu.VMEM((2, tokens, HD), F32),
    ]
    out_specs = [wide, wide, vmem, vmem]
    out_shape += [pltpu.VMEM((2 * g + 2, tokens, HD), B16)] * (shards - 1)
    out_specs += [vmem] * (shards - 1)
    if g + 2 < KV:
        out_shape.append(pltpu.VMEM((2 * (slots + tokens), HD), B16))
        out_specs.append(vmem)
    results = pl.pallas_call(
        functools.partial(attend_kernel, g, shards),
        grid=(1,),
        in_specs=in_specs,
        out_shape=out_shape,
        out_specs=out_specs,
        scratch_shapes=[
            pltpu.VMEM((total, HD), B16), pltpu.VMEM((total, HD), B16),
            pltpu.VMEM((HD, total), B16), pltpu.VMEM((HD, total), B16),
            pltpu.VMEM((slab, HD), F32), pltpu.VMEM((slab, HD), F32),
        ] + [
            pltpu.VMEM((total, HEADS * tokens), kind) for kind in (F32, B16, B16) * (GROUP // HEADS)
        ],
        input_output_aliases=aliases,
        compiler_params=params(),
        cost_estimate=pl.CostEstimate(
            flops=2 * GROUP * tokens * HD * (4 * total + 2 * slab),
            bytes_accessed=8 * tokens * GROUP * HD + 8 * total * HD,
            transcendentals=GROUP * tokens * total,
        ),
        name="attend",
    )(*args)
    out, gq, sums, own = results[:4]
    send = results[4:4 + shards - 1]
    return (out, gq, sums, send), own, results[4 + shards - 1:]


def finish_kernel(shards, *refs):
    cos_ref, sin_ref, *refs = refs
    owns, refs = refs[:KV], refs[KV:]
    backs, refs = refs[:shards - 1], refs[shards - 1:]
    sums, (gk_ref, gv_ref, *parts) = refs[:-5], refs[-5:]
    tokens = gk_ref.shape[0]
    cosine, sine = cos_ref[pl.ds(0, tokens), :], sin_ref[pl.ds(0, tokens), :]
    for g in range(KV):
        dk, dv = owns[g][0], owns[g][1]
        for back in backs:
            dk = dk + back[2 * g].astype(F32)
            dv = dv + back[2 * g + 1].astype(F32)
        cols = pl.ds(g * HD, HD)
        gk_ref[:, cols] = turn_back(dk, cosine, sine).astype(B16)
        gv_ref[:, cols] = dv.astype(B16)
    start = 0
    for part in parts:
        rows = pl.ds(start, part.shape[0])
        part[...] = add_up([ref[rows, :] for ref in sums])
        start += part.shape[0]


def finish(shards, tokens, cosine, sine, owns, backs, sums):
    vmem = pl.BlockSpec(memory_space=pltpu.VMEM)
    args = [cosine, sine, *owns, *backs, *sums]
    shapes = [((tokens, KV * HD), B16)] * 2 + [((rows, HD), F32) for rows in (HQ, KV, KV)]
    return pl.pallas_call(
        functools.partial(finish_kernel, shards),
        grid=(1,),
        in_specs=[vmem] * len(args),
        out_specs=[whole(shape) for shape, _ in shapes],
        out_shape=[pltpu.HBM(shape, kind) for shape, kind in shapes],
        compiler_params=params(),
        cost_estimate=pl.CostEstimate(flops=0, bytes_accessed=1 << 19, transcendentals=0),
        name="finish",
    )(*args)


def add_up(parts):
    while len(parts) > 1:
        parts = [a + b for a, b in zip(parts[::2], parts[1::2])]
    return parts[0]


def sum_but_last(x, axes, near):
    devices = lax.axis_size(axes)
    bits = [1 << i for i in reversed(range(devices.bit_length() - 1)) if 1 << i != near]
    stages = [[near]] + [bits[i:i + 2] for i in range(0, len(bits), 2)]
    parts = [x]
    for stage in stages:
        x = add_up(parts)
        parts = [x]
        for flip in [sum(c) for n in (1, 2) for c in itertools.combinations(stage, n)]:
            parts.append(lax.ppermute(x, axes, [(i, i ^ flip) for i in range(devices)]))
    return parts


def body(q_proj, k_proj, v_proj, cache_k, cache_v, bias_q, bias_k, bias_v, start, dout):
    shards = lax.axis_size("seq")
    rank = lax.axis_index("seq").astype(jnp.int32)
    tokens = q_proj.shape[1]
    shifts = range(1, shards)
    ck, cv, kp, vp = cache_k[0], cache_v[0], k_proj[0], v_proj[0]

    def ring(x, s):
        return lax.ppermute(x, "seq", [(i, (i + s) % shards) for i in range(shards)])

    def earlier(x, s):
        return lax.ppermute(x, "seq", [(i + s, i) for i in range(shards - s)])

    hbm = functools.partial(pltpu.with_memory_space_constraint, memory_space=pltpu.HBM)
    chunk = pack([hbm(x) for x in (ck, cv, kp, vp)])
    far = [[ring(chunk, s) for s in shifts]]

    owners = lax.rem(rank - jnp.arange(shards, dtype=jnp.int32) + shards, shards)
    positions = start[0] + owners[:, None] * tokens + jnp.arange(tokens, dtype=jnp.int32)[None]
    lane = jnp.arange(HD, dtype=jnp.int32)
    freqs = jnp.exp(
        -(2.0 * (lane % (HD // 2)).astype(F32) / HD) * jnp.log(jnp.float32(1000000.0))
    )
    angles = positions.reshape(-1).astype(F32)[:, None] * freqs[None, :]
    cosine = jnp.cos(angles)
    sine = jnp.sin(angles) * jnp.where(lane < HD // 2, -1.0, 1.0).astype(F32)[None]

    *prepared, chunk = prep(
        hbm(q_proj[0]), hbm(dout[0]), hbm(bias_q.reshape(HQ, HD)),
        hbm(bias_k.reshape(KV, HD)), hbm(bias_v.reshape(KV, HD)), cosine, sine, ck, cv, kp, vp,
    )
    far.append([ring(chunk, s) for s in shifts])
    before, owns = None, []
    for g in range(KV):
        before, own, more = attend(
            g, shards, start, rank.reshape(1), prepared, cosine, sine, ck, cv, kp, vp,
            far[g], before,
        )
        owns.append(own)
        far += [[ring(chunk, s) for s in shifts] for chunk in more]
    out, gq, sums, send = before
    backs = [earlier(x, s) for s, x in zip(shifts, send)]
    sums = sum_but_last(sums, ("dp", "seq"), shards)
    gk, gv, *sums = finish(shards, tokens, cosine, sine, owns, backs, sums)
    return (out[None], gq[None], gk[None], gv[None], *[x.reshape(-1) for x in sums])


def solution(mesh):
    split = P("dp", "seq", None)
    return jax.shard_map(
        body,
        mesh=mesh,
        in_specs=(split,) * 5 + (P(), P(), P(), P("dp"), split),
        out_specs=(split,) * 4 + (P(), P(), P()),
        check_vma=False,
    )
```

```python
import functools
import itertools
import math

import jax
import jax.numpy as jnp
from jax import lax
from jax.experimental import pallas as pl
from jax.experimental.pallas import tpu as pltpu
from jax.sharding import PartitionSpec as P

HQ = 32
KV = 4
HD = 128
GROUP = 8
HEADS = 4
NEG = -1e30
SUMS = HQ + 2 * KV
VMEM = 28 * 1024 * 1024
F32, B16 = jnp.float32, jnp.bfloat16


def turn(x):
    return pltpu.roll(x, HD // 2, 1)


def dot(a, b, dims):
    return lax.dot_general(a, b, (dims, ((), ())), preferred_element_type=F32)


NN = ((1,), (0,))


def whole(shape):
    return pl.BlockSpec(shape, lambda i: (0,) * len(shape))


def column(rows, g):
    return pl.BlockSpec((rows, HD), lambda i: (0, g))


def params():
    return pltpu.CompilerParams(dimension_semantics=("arbitrary",), vmem_limit_bytes=VMEM)


def copy_chunk(cols, sources, out_ref):
    start = 0
    for ref in sources:
        rows = ref.shape[0]
        out_ref[pl.ds(start, rows)] = ref[:, cols]
        start += rows


def pack_kernel(*refs):
    copy_chunk(pl.ds(0, HD), refs[:-1], refs[-1])


def pack(sources):
    rows = sum(x.shape[0] for x in sources)
    return pl.pallas_call(
        pack_kernel,
        grid=(1,),
        in_specs=[column(x.shape[0], 0) for x in sources],
        out_specs=pl.BlockSpec(memory_space=pltpu.VMEM),
        out_shape=pltpu.VMEM((rows, HD), B16),
        compiler_params=params(),
        cost_estimate=pl.CostEstimate(flops=0, bytes_accessed=4 * rows * HD, transcendentals=0),
        name="pack",
    )(*sources)


def turn_back(x, cosine, sine):
    return x * cosine - turn(x) * sine


def prep_kernel(
    tokens, q_ref, do_ref, bq_ref, bk_ref, bv_ref, cos_ref, sin_ref, ck_ref, cv_ref,
    kp_ref, vp_ref, qs_ref, qst_ref, dos_ref, dot_ref, bias_ref, cos_t_ref, sin_t_ref, ck_t_ref, cv_t_ref, pack_ref,
):
    g = pl.program_id(0)
    cosine, sine = cos_ref[pl.ds(0, tokens), :], sin_ref[pl.ds(0, tokens), :]
    bias_q = bq_ref[...].astype(F32)

    @pl.when(g == 0)
    def _():
        bias_ref[pl.ds(0, KV), :] = bk_ref[...].astype(F32)
        bias_ref[pl.ds(KV, KV), :] = bv_ref[...].astype(F32)
        cos_t_ref[...] = cosine.T
        sin_t_ref[...] = sine.T
        copy_chunk(pl.ds(HD, HD), (ck_ref, cv_ref, kp_ref, vp_ref), pack_ref)

    for h in range(GROUP):
        cols = pl.ds(h * HD, HD)
        rows = pl.ds(pl.multiple_of((g * GROUP + h) * tokens, tokens), tokens)
        x = q_ref[:, cols].astype(F32) + bias_q[h:h + 1]
        x = (x * cosine + turn(x) * sine).astype(B16)
        qs_ref[rows, :] = x
        do = do_ref[:, cols]
        dos_ref[rows, :] = do
        chain, part = h // HEADS, h % HEADS
        place = pl.ds(pl.multiple_of((g * (GROUP // HEADS) + chain) * HD, HD), HD)
        qst_ref[place, pl.ds(part * tokens, tokens)] = x.T
        dot_ref[place, pl.ds(part * tokens, tokens)] = do.T
    mine = pl.ds(pl.multiple_of(g * HD, HD), HD)
    ck_t_ref[mine, :] = ck_ref[:, mine].T
    cv_t_ref[mine, :] = cv_ref[:, mine].T


def prep(q, do, bq, bk, bv, cosine, sine, ck, cv, kp, vp):
    tokens, slots = q.shape[0], ck.shape[0]
    vmem = pl.BlockSpec(memory_space=pltpu.VMEM)
    wide = pl.BlockSpec((tokens, GROUP * HD), lambda i: (0, i))
    stacked = pltpu.VMEM((HQ * tokens, HD), B16)
    turned = pltpu.VMEM((HQ // HEADS * HD, HEADS * tokens), B16)
    out_shape = [
        stacked, turned, stacked, turned,
        pltpu.VMEM((2 * KV, HD), F32),
        pltpu.VMEM((HD, tokens), F32),
        pltpu.VMEM((HD, tokens), F32),
        pltpu.VMEM((KV * HD, slots), B16),
        pltpu.VMEM((KV * HD, slots), B16),
        pltpu.VMEM((2 * (slots + tokens), HD), B16),
    ]
    return pl.pallas_call(
        functools.partial(prep_kernel, tokens),
        grid=(KV,),
        in_specs=[
            wide, wide, pl.BlockSpec((GROUP, HD), lambda i: (i, 0)),
            whole((KV, HD)), whole((KV, HD)), *[vmem] * 6,
        ],
        out_specs=[vmem] * len(out_shape),
        out_shape=out_shape,
        compiler_params=params(),
        cost_estimate=pl.CostEstimate(
            flops=4 * tokens * HQ * HD, bytes_accessed=12 * tokens * HQ * HD, transcendentals=0
        ),
        name="prep",
    )(q, do, bq, bk, bv, cosine, sine, ck, cv, kp, vp)


def fold(x, op):
    return op(x.reshape(x.shape[0] // 8, 8, x.shape[1]), axis=0)


def allowed(start, s, first, rank, shards, slots, tokens):
    shift, at = divmod(start, slots + tokens)
    row = lax.broadcasted_iota(jnp.int32, s.shape, 0)
    if at < slots:
        owner = lax.rem(rank - shift + shards, shards)
        return row < first - owner * slots - at
    if shift == 0:
        return row <= (lax.broadcasted_iota(jnp.int32, s.shape, 1) & (tokens - 1))
    return row < jnp.where(rank >= shift, tokens, 0)


def slab_rows(g, sources, bias_ref, cosine, sine):
    kp, vp = sources
    k = kp.astype(F32) + bias_ref[g:g + 1, :]
    v = vp.astype(F32) + bias_ref[KV + g:KV + g + 1, :]
    return (k * cosine + turn(k) * sine).astype(B16), v.astype(B16)


def ahead_kernel(
    g, shards, first_ref, rank_ref, qst_ref, dot_ref, bias_ref, cos_ref, sin_ref,
    ck_ref, cv_ref, kp_ref, vp_ref, s_ref, dp_ref, top_ref, keys, values,
):
    tokens, slots, width = kp_ref.shape[0], ck_ref.shape[0], qst_ref.shape[1]
    owned = slots + tokens
    mine = pl.ds(g * HD, HD)
    rows = pl.ds(0, tokens)
    k, v = slab_rows(
        g, (kp_ref[:, mine], vp_ref[:, mine]), bias_ref, cos_ref[rows, :], sin_ref[rows, :]
    )
    keys[pl.ds(0, slots)] = ck_ref[:, mine]
    keys[pl.ds(slots, tokens)] = k
    values[pl.ds(0, slots)] = cv_ref[:, mine]
    values[pl.ds(slots, tokens)] = v
    for i in range(GROUP // HEADS):
        place = pl.ds((g * (GROUP // HEADS) + i) * HD, HD)
        s = dot(keys[...], qst_ref[place, :], NN)
        top = jnp.full((8, width), NEG, F32)
        for start in range(0, owned, tokens):
            part = s[start:start + tokens]
            seen = allowed(start, part, first_ref[0], rank_ref[0], shards, slots, tokens)
            part = jnp.where(seen, part, NEG)
            s_ref[i, pl.ds(start, tokens), :] = part
            top = jnp.maximum(top, fold(part, jnp.max))
        top_ref[i] = top
        dp_ref[i] = dot(values[...], dot_ref[place, :], NN)


def look_ahead(g, shards, first, rank, qst, dot_t, bias, cosine, sine, ck, cv, kp, vp):
    tokens, slots, width = kp.shape[0], ck.shape[0], qst.shape[1]
    owned = slots + tokens
    chains = GROUP // HEADS
    smem = pl.BlockSpec(memory_space=pltpu.SMEM)
    vmem = pl.BlockSpec(memory_space=pltpu.VMEM)
    args = [first, rank, qst, dot_t, bias, cosine, sine, ck, cv, kp, vp]
    return pl.pallas_call(
        functools.partial(ahead_kernel, g, shards),
        grid=(1,),
        in_specs=[smem] * 2 + [vmem] * (len(args) - 2),
        out_specs=[vmem] * 3,
        out_shape=[
            pltpu.VMEM((chains, owned, width), F32),
            pltpu.VMEM((chains, owned, width), F32),
            pltpu.VMEM((chains, 8, width), F32),
        ],
        scratch_shapes=[pltpu.VMEM((owned, HD), B16)] * 2,
        compiler_params=params(),
        cost_estimate=pl.CostEstimate(
            flops=4 * GROUP * tokens * HD * owned, bytes_accessed=8 * GROUP * tokens * owned,
            transcendentals=0,
        ),
        name="ahead",
    )(*args)


def attend_kernel(g, shards, *refs):
    refs = list(refs)

    def take(count):
        taken = refs[:count]
        del refs[:count]
        return taken

    (first_ref, rank_ref, qs_ref, qst_ref, dos_ref, dot_ref, bias_ref, cos_t_ref, sin_t_ref,
     ck_t_ref, cv_t_ref, cos_ref, sin_ref, ck_ref, cv_ref, kp_ref, vp_ref) = take(17)
    far = take(shards - 1)
    ahead = take(3) if g == KV - 1 else []
    if g == 0:
        take(1)
    old_sums_ref = take(1)[0] if g else None
    old_send = take(shards - 1) if g else []
    if 0 < g < KV - 1:
        take(2)
    out_ref, gq_ref, sums_ref, own_ref = take(4)
    send = take(shards - 1)
    pack_ref = take(1)[0] if g + 2 < KV else None
    keys, values, keys_t, values_t, dk_acc, dv_acc = take(6)
    scratch = [take(3) for _ in range(GROUP // HEADS)]
    tokens = kp_ref.shape[0]
    slots = ck_ref.shape[0]
    owned = slots + tokens
    total = shards * owned
    known = owned if ahead else 0
    first = first_ref[0]
    rank = rank_ref[0]
    mine = pl.ds(g * HD, HD)

    if pack_ref is not None:
        copy_chunk(pl.ds((g + 2) * HD, HD), (ck_ref, cv_ref, kp_ref, vp_ref), pack_ref)
    for s in range(shards):
        at = s * owned
        rows = pl.ds(s * tokens, tokens)
        if s == 0:
            sources = [ref[:, mine] for ref in (ck_ref, cv_ref, kp_ref, vp_ref)]
        else:
            sources = [
                far[s - 1][pl.ds(*part)] for part in
                ((0, slots), (slots, slots), (2 * slots, tokens), (2 * slots + tokens, tokens))
            ]
        k, v = slab_rows(g, sources[2:], bias_ref, cos_ref[rows, :], sin_ref[rows, :])
        for (natural, transposed), cache, own in zip(
            ((keys, keys_t), (values, values_t)), sources[:2], (k, v)
        ):
            if s or not ahead:
                natural[pl.ds(at, slots)] = cache
                natural[pl.ds(at + slots, tokens)] = own
            transposed[:, pl.ds(at + slots, tokens)] = own.T
            if s:
                transposed[:, pl.ds(at, slots)] = cache.T
    keys_t[:, pl.ds(0, slots)] = ck_t_ref[mine, :]
    values_t[:, pl.ds(0, slots)] = cv_t_ref[mine, :]
    sums_ref[...] = jnp.zeros_like(sums_ref) if old_sums_ref is None else old_sums_ref[...]
    dk_acc[...] = jnp.zeros_like(dk_acc)
    dv_acc[...] = jnp.zeros_like(dv_acc)

    width = HEADS * tokens
    scale = HD ** -0.5
    blocks = range(0, total, tokens)

    class Chain:
        def __init__(self, index):
            self.index = g * (GROUP // HEADS) + index
            self.s, self.pb, self.ds = scratch[index]
            index = self.index
            self.rows = pl.ds(pl.multiple_of(index * width, width), width)
            self.place = pl.ds(pl.multiple_of(index * HD, HD), HD)
            self.ahead = [ref.at[self.index % len(scratch)] for ref in ahead]
            self.top = self.ahead[2][...] if ahead else jnp.full((8, width), NEG, F32)

        def scores(self):
            s = dot(keys[pl.ds(known, total - known), :], qst_ref[self.place, :], NN)
            for start in blocks[known // tokens:]:
                part = s[start - known:start - known + tokens]
                seen = allowed(start, part, first, rank, shards, slots, tokens)
                part = jnp.where(seen, part, NEG)
                self.s[pl.ds(start, tokens), :] = part
                self.top = jnp.maximum(self.top, fold(part, jnp.max))

        def exponents(self):
            top = jnp.max(self.top, axis=0, keepdims=True)
            weight = jnp.zeros((8, width), F32)
            for start in blocks:
                rows = pl.ds(start, tokens)
                s = (self.ahead[0] if start < known else self.s)[rows, :]
                e = jnp.exp2((s - top) * (scale * math.log2(math.e)))
                self.s[rows, :] = e
                weight = weight + fold(e, jnp.sum)
            self.inverse = 1.0 / jnp.sum(weight, axis=0, keepdims=True)

        def probs(self):
            for start in blocks:
                rows = pl.ds(start, tokens)
                p = self.s[rows, :] * self.inverse
                self.s[rows, :] = p
                self.pb[rows, :] = p.astype(B16)

        def output(self):
            self.o = dot(values_t[...], self.pb[...], NN).astype(B16)
            do = dot_ref[self.place, :].astype(F32)
            self.delta = jnp.sum(do * self.o.astype(F32), axis=0, keepdims=True)

        def heads(self):
            for i in range(HEADS):
                head = self.index * HEADS + i
                yield (
                    slice(i * tokens, (i + 1) * tokens),
                    pl.ds(pl.multiple_of((head - g * GROUP) * HD, HD), HD),
                    head,
                )

        def dprobs(self):
            rows = pl.ds(known, total - known)
            self.dp = dot(values[rows, :], dot_ref[self.place, :], NN)

        def dscores(self):
            for start in blocks:
                rows = pl.ds(start, tokens)
                if start < known:
                    part = self.ahead[1][rows, :]
                else:
                    part = self.dp[start - known:start - known + tokens]
                self.ds[rows, :] = (self.s[rows, :] * (part - self.delta)).astype(B16)

        def query_grad(self):
            self.dq = (dot(keys_t[...], self.ds[...], NN) * scale).astype(B16).astype(F32)

        def slab_grads(self):
            for s in range(shards):
                rows = pl.ds(s * owned + slots, tokens)
                place = pl.ds(s * tokens, tokens)
                dv_acc[place, :] += dot(self.pb[rows, :], dos_ref[self.rows, :], NN)
                dk_acc[place, :] += dot(self.ds[rows, :], qs_ref[self.rows, :], NN)

        def store(self):
            for part, cols, head in self.heads():
                out_ref[:, cols] = self.o[:, part].T
                x = self.dq[:, part]
                other = jnp.concatenate([x[HD // 2:], x[:HD // 2]], axis=0)
                x = (x * cos_t_ref[...] - other * sin_t_ref[...]).T
                gq_ref[:, cols] = x.astype(B16)
                sums_ref[pl.ds(head, 1), :] = jnp.sum(x, axis=0, keepdims=True)

    steps = [
        Chain.scores, Chain.exponents, Chain.dprobs, Chain.probs, Chain.output,
        Chain.dscores, Chain.query_grad, Chain.slab_grads, Chain.store,
    ]
    group = [Chain(i) for i in range(GROUP // HEADS)]
    for turn_of in range(len(steps) + len(group) - 1):
        for i, chain in reversed(list(enumerate(group))):
            if 0 <= turn_of - i < len(steps):
                steps[turn_of - i](chain)

    dk = dk_acc[...] * scale
    dv = dv_acc[...]
    gk = turn_back(dk, cos_ref[...], sin_ref[...])
    own_ref[0] = dk[:tokens]
    own_ref[1] = dv[:tokens]
    at = 2 * g
    for j in range(1, shards):
        block = slice(j * tokens, (j + 1) * tokens)
        send[j - 1][at] = dk[block].astype(B16)
        send[j - 1][at + 1] = dv[block].astype(B16)
        if g:
            send[j - 1][pl.ds(0, at)] = old_send[j - 1][...]
    sums_ref[pl.ds(HQ + g, 1), :] = jnp.sum(gk, axis=0, keepdims=True)
    sums_ref[pl.ds(HQ + KV + g, 1), :] = jnp.sum(dv, axis=0, keepdims=True)


def attend(
    g, shards, first, rank, prepared, cosine, sine, ck, cv, kp, vp, far, ahead, before
):
    tokens, slots = kp.shape[0], ck.shape[0]
    slab = shards * tokens
    total = slab + shards * slots
    smem = pl.BlockSpec(memory_space=pltpu.SMEM)
    vmem = pl.BlockSpec(memory_space=pltpu.VMEM)
    anywhere = pl.BlockSpec(memory_space=pl.ANY)
    wide = pl.BlockSpec((tokens, GROUP * HD), lambda i: (0, g))

    args = [first, rank]
    placed = [*prepared, cosine, sine, ck, cv, kp, vp, *far]
    placed += ahead if g == KV - 1 else ahead[2:] if g == 0 else []
    aliases = {}
    if before is not None:
        out, gq, sums, send = before
        placed += [sums, *send]
    args += placed
    in_specs = [smem] * 2 + [vmem] * len(placed)
    last = g == KV - 1
    if before is not None and not last:
        aliases = {len(args): 0, len(args) + 1: 1}
        args += [out, gq]
        in_specs += [anywhere] * 2
    kept = pltpu.VMEM((tokens, GROUP * HD), B16) if last else pltpu.HBM((tokens, HQ * HD), B16)
    out_shape = [
        kept, kept,
        pltpu.VMEM((SUMS, HD), F32),
        pltpu.VMEM((2, tokens, HD), F32),
    ]
    out_specs = [vmem if last else wide] * 2 + [vmem, vmem]
    out_shape += [pltpu.VMEM((2 * g + 2, tokens, HD), B16)] * (shards - 1)
    out_specs += [vmem] * (shards - 1)
    if g + 2 < KV:
        out_shape.append(pltpu.VMEM((2 * (slots + tokens), HD), B16))
        out_specs.append(vmem)
    results = pl.pallas_call(
        functools.partial(attend_kernel, g, shards),
        grid=(1,),
        in_specs=in_specs,
        out_shape=out_shape,
        out_specs=out_specs,
        scratch_shapes=[
            pltpu.VMEM((total, HD), B16), pltpu.VMEM((total, HD), B16),
            pltpu.VMEM((HD, total), B16), pltpu.VMEM((HD, total), B16),
            pltpu.VMEM((slab, HD), F32), pltpu.VMEM((slab, HD), F32),
        ] + [
            pltpu.VMEM((total, HEADS * tokens), kind) for kind in (F32, B16, B16) * (GROUP // HEADS)
        ],
        input_output_aliases=aliases,
        compiler_params=params(),
        cost_estimate=pl.CostEstimate(
            flops=2 * GROUP * tokens * HD * (4 * total + 2 * slab),
            bytes_accessed=8 * tokens * GROUP * HD + 8 * total * HD,
            transcendentals=GROUP * tokens * total,
        ),
        name="attend",
    )(*args)
    out, gq, sums, own = results[:4]
    send = results[4:4 + shards - 1]
    return (out, gq, sums, send), own, results[4 + shards - 1:]


def finish_kernel(shards, *refs):
    cos_ref, sin_ref, *refs = refs
    owns, refs = refs[:KV], refs[KV:]
    backs, refs = refs[:shards - 1], refs[shards - 1:]
    out_part, gq_part, _, _, out_ref, gq_ref, gk_ref, gv_ref = refs
    out_ref[...] = out_part[...]
    gq_ref[...] = gq_part[...]
    tokens = gk_ref.shape[0]
    cosine, sine = cos_ref[pl.ds(0, tokens), :], sin_ref[pl.ds(0, tokens), :]
    for g in range(KV):
        dk, dv = owns[g][0], owns[g][1]
        for back in backs:
            dk = dk + back[2 * g].astype(F32)
            dv = dv + back[2 * g + 1].astype(F32)
        cols = pl.ds(g * HD, HD)
        gk_ref[:, cols] = turn_back(dk, cosine, sine).astype(B16)
        gv_ref[:, cols] = dv.astype(B16)


def finish(shards, cosine, sine, owns, backs, parts, out, gq):
    tokens = out.shape[0]
    args = [cosine, sine, *owns, *backs, *parts]
    wide = pl.BlockSpec((tokens, GROUP * HD), lambda i: (0, KV - 1))
    narrow = (tokens, KV * HD)
    return pl.pallas_call(
        functools.partial(finish_kernel, shards),
        grid=(1,),
        in_specs=[pl.BlockSpec(memory_space=pltpu.VMEM)] * len(args)
        + [pl.BlockSpec(memory_space=pl.ANY)] * 2,
        out_specs=[wide, wide, whole(narrow), whole(narrow)],
        out_shape=[pltpu.HBM(out.shape, B16)] * 2 + [pltpu.HBM(narrow, B16)] * 2,
        input_output_aliases={len(args): 0, len(args) + 1: 1},
        compiler_params=params(),
        cost_estimate=pl.CostEstimate(flops=0, bytes_accessed=1 << 21, transcendentals=0),
        name="finish",
    )(*args, out, gq)


def sums_kernel(*refs):
    sums, parts = refs[:-4], refs[-3:]
    start = 0
    for part in parts:
        rows = pl.ds(start, part.shape[0])
        part[...] = add_up([ref[rows, :] for ref in sums])
        start += part.shape[0]


def last_sums(sums, after):
    shapes = [(rows, HD) for rows in (HQ, KV, KV)]
    return pl.pallas_call(
        sums_kernel,
        grid=(1,),
        in_specs=[pl.BlockSpec(memory_space=pltpu.VMEM)] * len(sums)
        + [pl.BlockSpec(memory_space=pl.ANY)],
        out_specs=[whole(shape) for shape in shapes],
        out_shape=[pltpu.HBM(shape, F32) for shape in shapes],
        compiler_params=params(),
        cost_estimate=pl.CostEstimate(flops=0, bytes_accessed=1 << 17, transcendentals=0),
        name="sums",
    )(*sums, after)


def add_up(parts):
    while len(parts) > 1:
        parts = [a + b for a, b in zip(parts[::2], parts[1::2])]
    return parts[0]


def sum_but_last(x, axes, near):
    devices = lax.axis_size(axes)
    bits = [1 << i for i in reversed(range(devices.bit_length() - 1)) if 1 << i != near]
    stages = [[near]] + [bits[i:i + 2] for i in range(0, len(bits), 2)]
    parts = [x]
    for stage in stages:
        x = add_up(parts)
        parts = [x]
        for flip in [sum(c) for n in (1, 2) for c in itertools.combinations(stage, n)]:
            parts.append(lax.ppermute(x, axes, [(i, i ^ flip) for i in range(devices)]))
    return parts


def body(q_proj, k_proj, v_proj, cache_k, cache_v, bias_q, bias_k, bias_v, start, dout):
    shards = lax.axis_size("seq")
    rank = lax.axis_index("seq").astype(jnp.int32)
    tokens = q_proj.shape[1]
    shifts = range(1, shards)
    ck, cv, kp, vp = cache_k[0], cache_v[0], k_proj[0], v_proj[0]

    def ring(x, s):
        return lax.ppermute(x, "seq", [(i, (i + s) % shards) for i in range(shards)])

    def earlier(x, s):
        return lax.ppermute(x, "seq", [(i + s, i) for i in range(shards - s)])

    hbm = functools.partial(pltpu.with_memory_space_constraint, memory_space=pltpu.HBM)
    chunk = pack([hbm(x) for x in (ck, cv, kp, vp)])
    far = [[ring(chunk, s) for s in shifts]]

    owners = lax.rem(rank - jnp.arange(shards, dtype=jnp.int32) + shards, shards)
    positions = start[0] + owners[:, None] * tokens + jnp.arange(tokens, dtype=jnp.int32)[None]
    lane = jnp.arange(HD, dtype=jnp.int32)
    freqs = jnp.exp(
        -(2.0 * (lane % (HD // 2)).astype(F32) / HD) * jnp.log(jnp.float32(1000000.0))
    )
    angles = positions.reshape(-1).astype(F32)[:, None] * freqs[None, :]
    cosine = jnp.cos(angles)
    sine = jnp.sin(angles) * jnp.where(lane < HD // 2, -1.0, 1.0).astype(F32)[None]

    *prepared, chunk = prep(
        hbm(q_proj[0]), hbm(dout[0]), hbm(bias_q.reshape(HQ, HD)),
        hbm(bias_k.reshape(KV, HD)), hbm(bias_v.reshape(KV, HD)), cosine, sine, ck, cv, kp, vp,
    )
    far.append([ring(chunk, s) for s in shifts])
    qst, dot_t, bias = prepared[1], prepared[3], prepared[4]
    ahead = look_ahead(
        KV - 1, shards, start, rank.reshape(1), qst, dot_t, bias, cosine, sine, ck, cv, kp, vp
    )
    before, owns = None, []
    for g in range(KV):
        before, own, more = attend(
            g, shards, start, rank.reshape(1), prepared, cosine, sine, ck, cv, kp, vp,
            far[g], ahead, before,
        )
        if g == KV - 2:
            out, gq = before[:2]
        owns.append(own)
        far += [[ring(chunk, s) for s in shifts] for chunk in more]
    *columns, sums, send = before
    backs = [earlier(x, s) for s, x in zip(shifts, send)]
    sums = sum_but_last(sums, ("dp", "seq"), shards)
    out, gq, gk, gv = finish(shards, cosine, sine, owns, backs, columns, out, gq)
    sums = last_sums(sums, gk)
    return (out[None], gq[None], gk[None], gv[None], *[x.reshape(-1) for x in sums])


def solution(mesh):
    split = P("dp", "seq", None)
    return jax.shard_map(
        body,
        mesh=mesh,
        in_specs=(split,) * 5 + (P(), P(), P(), P("dp"), split),
        out_specs=(split,) * 4 + (P(), P(), P()),
        check_vma=False,
    )
```

```python
import functools
import itertools
import math

import jax
import jax.numpy as jnp
from jax import lax
from jax.experimental import pallas as pl
from jax.experimental.pallas import tpu as pltpu
from jax.sharding import PartitionSpec as P

HQ = 32
KV = 4
HD = 128
GROUP = 8
HEADS = 4
NEG = -1e30
SUMS = HQ + 2 * KV
VMEM = 28 * 1024 * 1024
F32, B16 = jnp.float32, jnp.bfloat16


def turn(x):
    return pltpu.roll(x, HD // 2, 1)


def dot(a, b, dims):
    return lax.dot_general(a, b, (dims, ((), ())), preferred_element_type=F32)


NN = ((1,), (0,))


def whole(shape):
    return pl.BlockSpec(shape, lambda i: (0,) * len(shape))


def column(rows, g):
    return pl.BlockSpec((rows, HD), lambda i: (0, g))


def params():
    return pltpu.CompilerParams(dimension_semantics=("arbitrary",), vmem_limit_bytes=VMEM)


def copy_chunk(cols, sources, out_ref):
    start = 0
    for ref in sources:
        rows = ref.shape[0]
        out_ref[pl.ds(start, rows)] = ref[:, cols]
        start += rows


def pack_kernel(*refs):
    copy_chunk(pl.ds(0, HD), refs[:-1], refs[-1])


def pack(sources):
    rows = sum(x.shape[0] for x in sources)
    return pl.pallas_call(
        pack_kernel,
        grid=(1,),
        in_specs=[column(x.shape[0], 0) for x in sources],
        out_specs=pl.BlockSpec(memory_space=pltpu.VMEM),
        out_shape=pltpu.VMEM((rows, HD), B16),
        compiler_params=params(),
        cost_estimate=pl.CostEstimate(flops=0, bytes_accessed=4 * rows * HD, transcendentals=0),
        name="pack",
    )(*sources)


def turn_back(x, cosine, sine):
    return x * cosine - turn(x) * sine


def prep_kernel(
    q_ref, do_ref, bq_ref, bk_ref, bv_ref, cos_ref, sin_ref, ck_ref, cv_ref, kp_ref, vp_ref,
    qs_ref, qst_ref, dos_ref, dot_ref, bias_ref, cos_t_ref, sin_t_ref, ck_t_ref, cv_t_ref,
    ck_out, cv_out, kp_out, vp_out, pack_ref,
):
    g = pl.program_id(0)
    tokens = q_ref.shape[0]
    cosine, sine = cos_ref[pl.ds(0, tokens), :], sin_ref[pl.ds(0, tokens), :]
    bias_q = bq_ref[...].astype(F32)
    own = (ck_ref, cv_ref, kp_ref, vp_ref)

    @pl.when(g == 0)
    def _():
        bias_ref[pl.ds(0, KV), :] = bk_ref[...].astype(F32)
        bias_ref[pl.ds(KV, KV), :] = bv_ref[...].astype(F32)
        cos_t_ref[...] = cosine.T
        sin_t_ref[...] = sine.T

    @pl.when(g == 1)
    def _():
        copy_chunk(pl.ds(0, HD), own, pack_ref)

    for h in range(GROUP):
        cols = pl.ds(h * HD, HD)
        rows = pl.ds(pl.multiple_of((g * GROUP + h) * tokens, tokens), tokens)
        x = q_ref[:, cols].astype(F32) + bias_q[h:h + 1]
        x = (x * cosine + turn(x) * sine).astype(B16)
        qs_ref[rows, :] = x
        do = do_ref[:, cols]
        dos_ref[rows, :] = do
        chain, part = h // HEADS, h % HEADS
        place = pl.ds(pl.multiple_of((g * (GROUP // HEADS) + chain) * HD, HD), HD)
        qst_ref[place, pl.ds(part * tokens, tokens)] = x.T
        dot_ref[place, pl.ds(part * tokens, tokens)] = do.T
    mine = pl.ds(pl.multiple_of(g * HD, HD), HD)
    ck_t_ref[mine, :] = ck_ref[...].T
    cv_t_ref[mine, :] = cv_ref[...].T
    for ref, out in zip(own, (ck_out, cv_out, kp_out, vp_out)):
        out[:, mine] = ref[...]


def prep(q, do, bq, bk, bv, cosine, sine, own):
    tokens, slots = q.shape[0], own[0].shape[0]
    vmem = pl.BlockSpec(memory_space=pltpu.VMEM)
    wide = pl.BlockSpec((tokens, GROUP * HD), lambda i: (0, i))
    stacked = pltpu.VMEM((HQ * tokens, HD), B16)
    turned = pltpu.VMEM((HQ // HEADS * HD, HEADS * tokens), B16)
    out_shape = [
        stacked, turned, stacked, turned,
        pltpu.VMEM((2 * KV, HD), F32),
        pltpu.VMEM((HD, tokens), F32),
        pltpu.VMEM((HD, tokens), F32),
        pltpu.VMEM((KV * HD, slots), B16),
        pltpu.VMEM((KV * HD, slots), B16),
        *[pltpu.VMEM(x.shape, B16) for x in own],
        pltpu.VMEM((2 * (slots + tokens), HD), B16),
    ]
    return pl.pallas_call(
        prep_kernel,
        grid=(KV,),
        in_specs=[
            wide, wide, pl.BlockSpec((GROUP, HD), lambda i: (i, 0)),
            whole((KV, HD)), whole((KV, HD)), vmem, vmem,
            *[pl.BlockSpec((x.shape[0], HD), lambda i: (0, i)) for x in own],
        ],
        out_specs=[vmem] * len(out_shape),
        out_shape=out_shape,
        compiler_params=params(),
        cost_estimate=pl.CostEstimate(
            flops=4 * tokens * HQ * HD, bytes_accessed=12 * tokens * HQ * HD, transcendentals=0
        ),
        name="prep",
    )(q, do, bq, bk, bv, cosine, sine, *own)


def fold(x, op):
    return op(x.reshape(x.shape[0] // 8, 8, x.shape[1]), axis=0)


def allowed(start, s, first, rank, shards, slots, tokens):
    shift, at = divmod(start, slots + tokens)
    row = lax.broadcasted_iota(jnp.int32, s.shape, 0)
    if at < slots:
        owner = lax.rem(rank - shift + shards, shards)
        return row < first - owner * slots - at
    if shift == 0:
        return row <= (lax.broadcasted_iota(jnp.int32, s.shape, 1) & (tokens - 1))
    return row < jnp.where(rank >= shift, tokens, 0)


def slab_rows(g, sources, bias_ref, cosine, sine):
    kp, vp = sources
    k = kp.astype(F32) + bias_ref[g:g + 1, :]
    v = vp.astype(F32) + bias_ref[KV + g:KV + g + 1, :]
    return (k * cosine + turn(k) * sine).astype(B16), v.astype(B16)


def ahead_kernel(
    g, shards, first_ref, rank_ref, qst_ref, dot_ref, bias_ref, cos_ref, sin_ref,
    ck_ref, cv_ref, kp_ref, vp_ref, s_ref, dp_ref, top_ref, keys, values,
):
    tokens, slots, width = kp_ref.shape[0], ck_ref.shape[0], qst_ref.shape[1]
    owned = slots + tokens
    mine = pl.ds(g * HD, HD)
    rows = pl.ds(0, tokens)
    k, v = slab_rows(
        g, (kp_ref[:, mine], vp_ref[:, mine]), bias_ref, cos_ref[rows, :], sin_ref[rows, :]
    )
    keys[pl.ds(0, slots)] = ck_ref[:, mine]
    keys[pl.ds(slots, tokens)] = k
    values[pl.ds(0, slots)] = cv_ref[:, mine]
    values[pl.ds(slots, tokens)] = v
    for i in range(GROUP // HEADS):
        place = pl.ds((g * (GROUP // HEADS) + i) * HD, HD)
        s = dot(keys[...], qst_ref[place, :], NN)
        top = jnp.full((8, width), NEG, F32)
        for start in range(0, owned, tokens):
            part = s[start:start + tokens]
            seen = allowed(start, part, first_ref[0], rank_ref[0], shards, slots, tokens)
            part = jnp.where(seen, part, NEG)
            s_ref[i, pl.ds(start, tokens), :] = part
            top = jnp.maximum(top, fold(part, jnp.max))
        top_ref[i] = top
        dp_ref[i] = dot(values[...], dot_ref[place, :], NN)


def look_ahead(g, shards, first, rank, qst, dot_t, bias, cosine, sine, ck, cv, kp, vp):
    tokens, slots, width = kp.shape[0], ck.shape[0], qst.shape[1]
    owned = slots + tokens
    chains = GROUP // HEADS
    smem = pl.BlockSpec(memory_space=pltpu.SMEM)
    vmem = pl.BlockSpec(memory_space=pltpu.VMEM)
    args = [first, rank, qst, dot_t, bias, cosine, sine, ck, cv, kp, vp]
    return pl.pallas_call(
        functools.partial(ahead_kernel, g, shards),
        grid=(1,),
        in_specs=[smem] * 2 + [vmem] * (len(args) - 2),
        out_specs=[vmem] * 3,
        out_shape=[
            pltpu.VMEM((chains, owned, width), F32),
            pltpu.VMEM((chains, owned, width), F32),
            pltpu.VMEM((chains, 8, width), F32),
        ],
        scratch_shapes=[pltpu.VMEM((owned, HD), B16)] * 2,
        compiler_params=params(),
        cost_estimate=pl.CostEstimate(
            flops=4 * GROUP * tokens * HD * owned, bytes_accessed=8 * GROUP * tokens * owned,
            transcendentals=0,
        ),
        name="ahead",
    )(*args)


def attend_kernel(g, shards, *refs):
    refs = list(refs)

    def take(count):
        taken = refs[:count]
        del refs[:count]
        return taken

    (first_ref, rank_ref, qs_ref, qst_ref, dos_ref, dot_ref, bias_ref, cos_t_ref, sin_t_ref,
     ck_t_ref, cv_t_ref, cos_ref, sin_ref, ck_ref, cv_ref, kp_ref, vp_ref) = take(17)
    far = take(shards - 1)
    ahead = take(3)
    if g + 1 < KV:
        take(1)
    old_sums_ref = take(1)[0] if g else None
    old_send = take(shards - 1) if g else []
    if 0 < g < KV - 1:
        take(2)
    out_ref, gq_ref, sums_ref, own_ref = take(4)
    send = take(shards - 1)
    pack_ref = take(1)[0] if g + 2 < KV else None
    keys, values, keys_t, values_t, dk_acc, dv_acc = take(6)
    scratch = [take(3) for _ in range(GROUP // HEADS)]
    tokens = kp_ref.shape[0]
    slots = ck_ref.shape[0]
    owned = slots + tokens
    total = shards * owned
    known = owned
    first = first_ref[0]
    rank = rank_ref[0]
    mine = pl.ds(g * HD, HD)

    if pack_ref is not None:
        copy_chunk(pl.ds((g + 2) * HD, HD), (ck_ref, cv_ref, kp_ref, vp_ref), pack_ref)
    for s in range(shards):
        at = s * owned
        rows = pl.ds(s * tokens, tokens)
        if s == 0:
            sources = [ref[:, mine] for ref in (ck_ref, cv_ref, kp_ref, vp_ref)]
        else:
            sources = [
                far[s - 1][pl.ds(*part)] for part in
                ((0, slots), (slots, slots), (2 * slots, tokens), (2 * slots + tokens, tokens))
            ]
        k, v = slab_rows(g, sources[2:], bias_ref, cos_ref[rows, :], sin_ref[rows, :])
        for (natural, transposed), cache, own in zip(
            ((keys, keys_t), (values, values_t)), sources[:2], (k, v)
        ):
            if s:
                natural[pl.ds(at, slots)] = cache
                natural[pl.ds(at + slots, tokens)] = own
            transposed[:, pl.ds(at + slots, tokens)] = own.T
            if s:
                transposed[:, pl.ds(at, slots)] = cache.T
    keys_t[:, pl.ds(0, slots)] = ck_t_ref[mine, :]
    values_t[:, pl.ds(0, slots)] = cv_t_ref[mine, :]
    sums_ref[...] = jnp.zeros_like(sums_ref) if old_sums_ref is None else old_sums_ref[...]
    dk_acc[...] = jnp.zeros_like(dk_acc)
    dv_acc[...] = jnp.zeros_like(dv_acc)

    width = HEADS * tokens
    scale = HD ** -0.5
    blocks = range(0, total, tokens)

    class Chain:
        def __init__(self, index):
            self.index = g * (GROUP // HEADS) + index
            self.s, self.pb, self.ds = scratch[index]
            index = self.index
            self.rows = pl.ds(pl.multiple_of(index * width, width), width)
            self.place = pl.ds(pl.multiple_of(index * HD, HD), HD)
            self.ahead = [ref.at[self.index % len(scratch)] for ref in ahead]
            self.top = self.ahead[2][...]

        def scores(self):
            s = dot(keys[pl.ds(known, total - known), :], qst_ref[self.place, :], NN)
            for start in blocks[known // tokens:]:
                part = s[start - known:start - known + tokens]
                seen = allowed(start, part, first, rank, shards, slots, tokens)
                part = jnp.where(seen, part, NEG)
                self.s[pl.ds(start, tokens), :] = part
                self.top = jnp.maximum(self.top, fold(part, jnp.max))

        def exponents(self):
            top = jnp.max(self.top, axis=0, keepdims=True)
            weight = jnp.zeros((8, width), F32)
            for start in blocks:
                rows = pl.ds(start, tokens)
                s = (self.ahead[0] if start < known else self.s)[rows, :]
                e = jnp.exp2((s - top) * (scale * math.log2(math.e)))
                self.s[rows, :] = e
                weight = weight + fold(e, jnp.sum)
            self.inverse = 1.0 / jnp.sum(weight, axis=0, keepdims=True)

        def probs(self):
            for start in blocks:
                rows = pl.ds(start, tokens)
                p = self.s[rows, :] * self.inverse
                self.s[rows, :] = p
                self.pb[rows, :] = p.astype(B16)

        def output(self):
            self.o = dot(values_t[...], self.pb[...], NN).astype(B16)
            do = dot_ref[self.place, :].astype(F32)
            self.delta = jnp.sum(do * self.o.astype(F32), axis=0, keepdims=True)

        def heads(self):
            for i in range(HEADS):
                head = self.index * HEADS + i
                yield (
                    slice(i * tokens, (i + 1) * tokens),
                    pl.ds(pl.multiple_of((head - g * GROUP) * HD, HD), HD),
                    head,
                )

        def dprobs(self):
            rows = pl.ds(known, total - known)
            self.dp = dot(values[rows, :], dot_ref[self.place, :], NN)

        def dscores(self):
            for start in blocks:
                rows = pl.ds(start, tokens)
                if start < known:
                    part = self.ahead[1][rows, :]
                else:
                    part = self.dp[start - known:start - known + tokens]
                self.ds[rows, :] = (self.s[rows, :] * (part - self.delta)).astype(B16)

        def query_grad(self):
            self.dq = (dot(keys_t[...], self.ds[...], NN) * scale).astype(B16).astype(F32)

        def slab_grads(self):
            for s in range(shards):
                rows = pl.ds(s * owned + slots, tokens)
                place = pl.ds(s * tokens, tokens)
                dv_acc[place, :] += dot(self.pb[rows, :], dos_ref[self.rows, :], NN)
                dk_acc[place, :] += dot(self.ds[rows, :], qs_ref[self.rows, :], NN)

        def store(self):
            for part, cols, head in self.heads():
                out_ref[:, cols] = self.o[:, part].T
                x = self.dq[:, part]
                other = jnp.concatenate([x[HD // 2:], x[:HD // 2]], axis=0)
                x = (x * cos_t_ref[...] - other * sin_t_ref[...]).T
                gq_ref[:, cols] = x.astype(B16)
                sums_ref[pl.ds(head, 1), :] = jnp.sum(x, axis=0, keepdims=True)

    steps = [
        Chain.scores, Chain.exponents, Chain.dprobs, Chain.probs, Chain.output,
        Chain.dscores, Chain.query_grad, Chain.slab_grads, Chain.store,
    ]
    group = [Chain(i) for i in range(GROUP // HEADS)]
    for turn_of in range(len(steps) + len(group) - 1):
        for i, chain in reversed(list(enumerate(group))):
            if 0 <= turn_of - i < len(steps):
                steps[turn_of - i](chain)

    dk = dk_acc[...] * scale
    dv = dv_acc[...]
    gk = turn_back(dk, cos_ref[...], sin_ref[...])
    own_ref[0] = dk[:tokens]
    own_ref[1] = dv[:tokens]
    at = 2 * g
    for j in range(1, shards):
        block = slice(j * tokens, (j + 1) * tokens)
        send[j - 1][at] = dk[block].astype(B16)
        send[j - 1][at + 1] = dv[block].astype(B16)
        if g:
            send[j - 1][pl.ds(0, at)] = old_send[j - 1][...]
    sums_ref[pl.ds(HQ + g, 1), :] = jnp.sum(gk, axis=0, keepdims=True)
    sums_ref[pl.ds(HQ + KV + g, 1), :] = jnp.sum(dv, axis=0, keepdims=True)


def attend(
    g, shards, first, rank, prepared, cosine, sine, ck, cv, kp, vp, far, ahead, before
):
    tokens, slots = kp.shape[0], ck.shape[0]
    slab = shards * tokens
    total = slab + shards * slots
    smem = pl.BlockSpec(memory_space=pltpu.SMEM)
    vmem = pl.BlockSpec(memory_space=pltpu.VMEM)
    anywhere = pl.BlockSpec(memory_space=pl.ANY)
    wide = pl.BlockSpec((tokens, GROUP * HD), lambda i: (0, g))

    args = [first, rank]
    placed = [*prepared, cosine, sine, ck, cv, kp, vp, *far]
    placed += [*ahead[g], *[x[2] for x in ahead[g + 1:g + 2]]]
    aliases = {}
    if before is not None:
        out, gq, sums, send = before
        placed += [sums, *send]
    args += placed
    in_specs = [smem] * 2 + [vmem] * len(placed)
    last = g == KV - 1
    if before is not None and not last:
        aliases = {len(args): 0, len(args) + 1: 1}
        args += [out, gq]
        in_specs += [anywhere] * 2
    kept = pltpu.VMEM((tokens, GROUP * HD), B16) if last else pltpu.HBM((tokens, HQ * HD), B16)
    out_shape = [
        kept, kept,
        pltpu.VMEM((SUMS, HD), F32),
        pltpu.VMEM((2, tokens, HD), F32),
    ]
    out_specs = [vmem if last else wide] * 2 + [vmem, vmem]
    out_shape += [pltpu.VMEM((2 * g + 2, tokens, HD), B16)] * (shards - 1)
    out_specs += [vmem] * (shards - 1)
    if g + 2 < KV:
        out_shape.append(pltpu.VMEM((2 * (slots + tokens), HD), B16))
        out_specs.append(vmem)
    results = pl.pallas_call(
        functools.partial(attend_kernel, g, shards),
        grid=(1,),
        in_specs=in_specs,
        out_shape=out_shape,
        out_specs=out_specs,
        scratch_shapes=[
            pltpu.VMEM((total, HD), B16), pltpu.VMEM((total, HD), B16),
            pltpu.VMEM((HD, total), B16), pltpu.VMEM((HD, total), B16),
            pltpu.VMEM((slab, HD), F32), pltpu.VMEM((slab, HD), F32),
        ] + [
            pltpu.VMEM((total, HEADS * tokens), kind) for kind in (F32, B16, B16) * (GROUP // HEADS)
        ],
        input_output_aliases=aliases,
        compiler_params=params(),
        cost_estimate=pl.CostEstimate(
            flops=2 * GROUP * tokens * HD * (4 * total + 2 * slab),
            bytes_accessed=8 * tokens * GROUP * HD + 8 * total * HD,
            transcendentals=GROUP * tokens * total,
        ),
        name="attend",
    )(*args)
    out, gq, sums, own = results[:4]
    send = results[4:4 + shards - 1]
    return (out, gq, sums, send), own, results[4 + shards - 1:]


def finish_kernel(shards, *refs):
    cos_ref, sin_ref, *refs = refs
    owns, refs = refs[:KV], refs[KV:]
    backs, refs = refs[:shards - 1], refs[shards - 1:]
    out_part, gq_part, _, _, out_ref, gq_ref, gk_ref, gv_ref = refs
    out_ref[...] = out_part[...]
    gq_ref[...] = gq_part[...]
    tokens = gk_ref.shape[0]
    cosine, sine = cos_ref[pl.ds(0, tokens), :], sin_ref[pl.ds(0, tokens), :]
    for g in range(KV):
        dk, dv = owns[g][0], owns[g][1]
        for back in backs:
            dk = dk + back[2 * g].astype(F32)
            dv = dv + back[2 * g + 1].astype(F32)
        cols = pl.ds(g * HD, HD)
        gk_ref[:, cols] = turn_back(dk, cosine, sine).astype(B16)
        gv_ref[:, cols] = dv.astype(B16)


def finish(shards, cosine, sine, owns, backs, parts, out, gq):
    tokens = out.shape[0]
    args = [cosine, sine, *owns, *backs, *parts]
    wide = pl.BlockSpec((tokens, GROUP * HD), lambda i: (0, KV - 1))
    narrow = (tokens, KV * HD)
    return pl.pallas_call(
        functools.partial(finish_kernel, shards),
        grid=(1,),
        in_specs=[pl.BlockSpec(memory_space=pltpu.VMEM)] * len(args)
        + [pl.BlockSpec(memory_space=pl.ANY)] * 2,
        out_specs=[wide, wide, whole(narrow), whole(narrow)],
        out_shape=[pltpu.HBM(out.shape, B16)] * 2 + [pltpu.HBM(narrow, B16)] * 2,
        input_output_aliases={len(args): 0, len(args) + 1: 1},
        compiler_params=params(),
        cost_estimate=pl.CostEstimate(flops=0, bytes_accessed=1 << 21, transcendentals=0),
        name="finish",
    )(*args, out, gq)


def sums_kernel(*refs):
    sums, parts = refs[:-4], refs[-3:]
    start = 0
    for part in parts:
        rows = pl.ds(start, part.shape[0])
        part[...] = add_up([ref[rows, :] for ref in sums])
        start += part.shape[0]


def last_sums(sums, after):
    shapes = [(rows, HD) for rows in (HQ, KV, KV)]
    return pl.pallas_call(
        sums_kernel,
        grid=(1,),
        in_specs=[pl.BlockSpec(memory_space=pltpu.VMEM)] * len(sums)
        + [pl.BlockSpec(memory_space=pl.ANY)],
        out_specs=[whole(shape) for shape in shapes],
        out_shape=[pltpu.HBM(shape, F32) for shape in shapes],
        compiler_params=params(),
        cost_estimate=pl.CostEstimate(flops=0, bytes_accessed=1 << 17, transcendentals=0),
        name="sums",
    )(*sums, after)


def add_up(parts):
    while len(parts) > 1:
        parts = [a + b for a, b in zip(parts[::2], parts[1::2])]
    return parts[0]


def sum_but_last(x, axes, near):
    devices = lax.axis_size(axes)
    bits = [1 << i for i in reversed(range(devices.bit_length() - 1)) if 1 << i != near]
    stages = [[near]] + [bits[i:i + 2] for i in range(0, len(bits), 2)]
    parts = [x]
    for stage in stages:
        x = add_up(parts)
        parts = [x]
        for flip in [sum(c) for n in (1, 2) for c in itertools.combinations(stage, n)]:
            parts.append(lax.ppermute(x, axes, [(i, i ^ flip) for i in range(devices)]))
    return parts


def body(q_proj, k_proj, v_proj, cache_k, cache_v, bias_q, bias_k, bias_v, start, dout):
    shards = lax.axis_size("seq")
    rank = lax.axis_index("seq").astype(jnp.int32)
    tokens = q_proj.shape[1]
    shifts = range(1, shards)

    def ring(x, s):
        return lax.ppermute(x, "seq", [(i, (i + s) % shards) for i in range(shards)])

    def earlier(x, s):
        return lax.ppermute(x, "seq", [(i + s, i) for i in range(shards - s)])

    hbm = functools.partial(pltpu.with_memory_space_constraint, memory_space=pltpu.HBM)
    own = [hbm(x[0]) for x in (cache_k, cache_v, k_proj, v_proj)]
    chunk = pack(own)
    far = [[ring(chunk, s) for s in shifts]]

    owners = lax.rem(rank - jnp.arange(shards, dtype=jnp.int32) + shards, shards)
    positions = start[0] + owners[:, None] * tokens + jnp.arange(tokens, dtype=jnp.int32)[None]
    lane = jnp.arange(HD, dtype=jnp.int32)
    freqs = jnp.exp(
        -(2.0 * (lane % (HD // 2)).astype(F32) / HD) * jnp.log(jnp.float32(1000000.0))
    )
    angles = positions.reshape(-1).astype(F32)[:, None] * freqs[None, :]
    cosine = jnp.cos(angles)
    sine = jnp.sin(angles) * jnp.where(lane < HD // 2, -1.0, 1.0).astype(F32)[None]

    *prepared, ck, cv, kp, vp, chunk = prep(
        hbm(q_proj[0]), hbm(dout[0]), hbm(bias_q.reshape(HQ, HD)),
        hbm(bias_k.reshape(KV, HD)), hbm(bias_v.reshape(KV, HD)), cosine, sine, own,
    )
    far.append([ring(chunk, s) for s in shifts])
    qst, dot_t, bias = prepared[1], prepared[3], prepared[4]
    ahead = [
        look_ahead(
            g, shards, start, rank.reshape(1), qst, dot_t, bias, cosine, sine, ck, cv, kp, vp
        )
        for g in range(KV)
    ]
    before, owns = None, []
    for g in range(KV):
        before, own, more = attend(
            g, shards, start, rank.reshape(1), prepared, cosine, sine, ck, cv, kp, vp,
            far[g], ahead, before,
        )
        if g == KV - 2:
            out, gq = before[:2]
        owns.append(own)
        far += [[ring(chunk, s) for s in shifts] for chunk in more]
    *columns, sums, send = before
    backs = [earlier(x, s) for s, x in zip(shifts, send)]
    sums = sum_but_last(sums, ("dp", "seq"), shards)
    out, gq, gk, gv = finish(shards, cosine, sine, owns, backs, columns, out, gq)
    sums = last_sums(sums, hbm(gk))
    return (out[None], gq[None], gk[None], gv[None], *[x.reshape(-1) for x in sums])


def solution(mesh):
    split = P("dp", "seq", None)
    return jax.shard_map(
        body,
        mesh=mesh,
        in_specs=(split,) * 5 + (P(), P(), P(), P("dp"), split),
        out_specs=(split,) * 4 + (P(), P(), P()),
        check_vma=False,
    )
```

```python
import functools
import itertools
import math

import jax
import jax.numpy as jnp
from jax import lax
from jax.experimental import pallas as pl
from jax.experimental.pallas import tpu as pltpu
from jax.sharding import PartitionSpec as P

HQ = 32
KV = 4
HD = 128
GROUP = 8
HEADS = 4
NEG = -1e30
SUMS = HQ + 2 * KV
VMEM = 28 * 1024 * 1024
F32, B16 = jnp.float32, jnp.bfloat16


def turn(x):
    return pltpu.roll(x, HD // 2, 1)


def dot(a, b, dims):
    return lax.dot_general(a, b, (dims, ((), ())), preferred_element_type=F32)


NN = ((1,), (0,))


def whole(shape):
    return pl.BlockSpec(shape, lambda i: (0,) * len(shape))


def column(rows, g):
    return pl.BlockSpec((rows, HD), lambda i: (0, g))


def params():
    return pltpu.CompilerParams(dimension_semantics=("arbitrary",), vmem_limit_bytes=VMEM)


def copy_chunk(cols, sources, out_ref):
    start = 0
    for ref in sources:
        rows = ref.shape[0]
        out_ref[pl.ds(start, rows)] = ref[:, cols]
        start += rows


def pack_kernel(*refs):
    copy_chunk(pl.ds(0, HD), refs[:-1], refs[-1])


def pack(sources):
    rows = sum(x.shape[0] for x in sources)
    return pl.pallas_call(
        pack_kernel,
        grid=(1,),
        in_specs=[column(x.shape[0], 0) for x in sources],
        out_specs=pl.BlockSpec(memory_space=pltpu.VMEM),
        out_shape=pltpu.VMEM((rows, HD), B16),
        compiler_params=params(),
        cost_estimate=pl.CostEstimate(flops=0, bytes_accessed=4 * rows * HD, transcendentals=0),
        name="pack",
    )(*sources)


def turn_back(x, cosine, sine):
    return x * cosine - turn(x) * sine


def prep_kernel(
    q_ref, do_ref, bq_ref, bk_ref, bv_ref, cos_ref, sin_ref, ck_ref, cv_ref, kp_ref, vp_ref,
    qs_ref, qst_ref, dos_ref, dot_ref, bias_ref, cos_t_ref, sin_t_ref, ck_t_ref, cv_t_ref,
    ck_out, cv_out, kp_out, vp_out, pack_ref,
):
    g = pl.program_id(0)
    tokens = q_ref.shape[0]
    cosine, sine = cos_ref[pl.ds(0, tokens), :], sin_ref[pl.ds(0, tokens), :]
    bias_q = bq_ref[...].astype(F32)
    own = (ck_ref, cv_ref, kp_ref, vp_ref)

    @pl.when(g == 0)
    def _():
        bias_ref[pl.ds(0, KV), :] = bk_ref[...].astype(F32)
        bias_ref[pl.ds(KV, KV), :] = bv_ref[...].astype(F32)
        cos_t_ref[...] = cosine.T
        sin_t_ref[...] = sine.T

    @pl.when(g == 1)
    def _():
        copy_chunk(pl.ds(0, HD), own, pack_ref)

    for h in range(GROUP):
        cols = pl.ds(h * HD, HD)
        rows = pl.ds(pl.multiple_of((g * GROUP + h) * tokens, tokens), tokens)
        x = q_ref[:, cols].astype(F32) + bias_q[h:h + 1]
        x = (x * cosine + turn(x) * sine).astype(B16)
        qs_ref[rows, :] = x
        do = do_ref[:, cols]
        dos_ref[rows, :] = do
        chain, part = h // HEADS, h % HEADS
        place = pl.ds(pl.multiple_of((g * (GROUP // HEADS) + chain) * HD, HD), HD)
        qst_ref[place, pl.ds(part * tokens, tokens)] = x.T
        dot_ref[place, pl.ds(part * tokens, tokens)] = do.T
    mine = pl.ds(pl.multiple_of(g * HD, HD), HD)
    ck_t_ref[mine, :] = ck_ref[...].T
    cv_t_ref[mine, :] = cv_ref[...].T
    for ref, out in zip(own, (ck_out, cv_out, kp_out, vp_out)):
        out[:, mine] = ref[...]


def prep(q, do, bq, bk, bv, cosine, sine, own):
    tokens, slots = q.shape[0], own[0].shape[0]
    vmem = pl.BlockSpec(memory_space=pltpu.VMEM)
    wide = pl.BlockSpec((tokens, GROUP * HD), lambda i: (0, i))
    stacked = pltpu.VMEM((HQ * tokens, HD), B16)
    turned = pltpu.VMEM((HQ // HEADS * HD, HEADS * tokens), B16)
    out_shape = [
        stacked, turned, stacked, turned,
        pltpu.VMEM((2 * KV, HD), F32),
        pltpu.VMEM((HD, tokens), F32),
        pltpu.VMEM((HD, tokens), F32),
        pltpu.VMEM((KV * HD, slots), B16),
        pltpu.VMEM((KV * HD, slots), B16),
        *[pltpu.VMEM(x.shape, B16) for x in own],
        pltpu.VMEM((2 * (slots + tokens), HD), B16),
    ]
    return pl.pallas_call(
        prep_kernel,
        grid=(KV,),
        in_specs=[
            wide, wide, pl.BlockSpec((GROUP, HD), lambda i: (i, 0)),
            whole((KV, HD)), whole((KV, HD)), vmem, vmem,
            *[pl.BlockSpec((x.shape[0], HD), lambda i: (0, i)) for x in own],
        ],
        out_specs=[vmem] * len(out_shape),
        out_shape=out_shape,
        compiler_params=params(),
        cost_estimate=pl.CostEstimate(
            flops=4 * tokens * HQ * HD, bytes_accessed=12 * tokens * HQ * HD, transcendentals=0
        ),
        name="prep",
    )(q, do, bq, bk, bv, cosine, sine, *own)


def fold(x, op):
    return op(x.reshape(x.shape[0] // 8, 8, x.shape[1]), axis=0)


def allowed(start, s, first, rank, shards, slots, tokens):
    shift, at = divmod(start, slots + tokens)
    row = lax.broadcasted_iota(jnp.int32, s.shape, 0)
    if at < slots:
        owner = lax.rem(rank - shift + shards, shards)
        return row < first - owner * slots - at
    if shift == 0:
        return row <= (lax.broadcasted_iota(jnp.int32, s.shape, 1) & (tokens - 1))
    return row < jnp.where(rank >= shift, tokens, 0)


def slab_rows(g, sources, bias_ref, cosine, sine):
    kp, vp = sources
    k = kp.astype(F32) + bias_ref[g:g + 1, :]
    v = vp.astype(F32) + bias_ref[KV + g:KV + g + 1, :]
    return (k * cosine + turn(k) * sine).astype(B16), v.astype(B16)


def ahead_kernel(
    g, shards, first_ref, rank_ref, qst_ref, dot_ref, bias_ref, cos_ref, sin_ref,
    ck_ref, cv_ref, kp_ref, vp_ref, s_ref, dp_ref, top_ref, keys, values,
):
    tokens, slots, width = kp_ref.shape[0], ck_ref.shape[0], qst_ref.shape[1]
    owned = slots + tokens
    mine = pl.ds(g * HD, HD)
    rows = pl.ds(0, tokens)
    k, v = slab_rows(
        g, (kp_ref[:, mine], vp_ref[:, mine]), bias_ref, cos_ref[rows, :], sin_ref[rows, :]
    )
    keys[pl.ds(0, slots)] = ck_ref[:, mine]
    keys[pl.ds(slots, tokens)] = k
    values[pl.ds(0, slots)] = cv_ref[:, mine]
    values[pl.ds(slots, tokens)] = v
    for i in range(GROUP // HEADS):
        place = pl.ds((g * (GROUP // HEADS) + i) * HD, HD)
        s = dot(keys[...], qst_ref[place, :], NN)
        top = jnp.full((8, width), NEG, F32)
        for start in range(0, owned, tokens):
            part = s[start:start + tokens]
            seen = allowed(start, part, first_ref[0], rank_ref[0], shards, slots, tokens)
            part = jnp.where(seen, part, NEG)
            s_ref[i, pl.ds(start, tokens), :] = part
            top = jnp.maximum(top, fold(part, jnp.max))
        top_ref[i] = top
        dp_ref[i] = dot(values[...], dot_ref[place, :], NN)


def look_ahead(g, shards, first, rank, qst, dot_t, bias, cosine, sine, ck, cv, kp, vp):
    tokens, slots, width = kp.shape[0], ck.shape[0], qst.shape[1]
    owned = slots + tokens
    chains = GROUP // HEADS
    smem = pl.BlockSpec(memory_space=pltpu.SMEM)
    vmem = pl.BlockSpec(memory_space=pltpu.VMEM)
    args = [first, rank, qst, dot_t, bias, cosine, sine, ck, cv, kp, vp]
    return pl.pallas_call(
        functools.partial(ahead_kernel, g, shards),
        grid=(1,),
        in_specs=[smem] * 2 + [vmem] * (len(args) - 2),
        out_specs=[vmem] * 3,
        out_shape=[
            pltpu.VMEM((chains, owned, width), F32),
            pltpu.VMEM((chains, owned, width), F32),
            pltpu.VMEM((chains, 8, width), F32),
        ],
        scratch_shapes=[pltpu.VMEM((owned, HD), B16)] * 2,
        compiler_params=params(),
        cost_estimate=pl.CostEstimate(
            flops=4 * GROUP * tokens * HD * owned, bytes_accessed=8 * GROUP * tokens * owned,
            transcendentals=0,
        ),
        name="ahead",
    )(*args)


def attend_kernel(g, shards, *refs):
    refs = list(refs)

    def take(count):
        taken = refs[:count]
        del refs[:count]
        return taken

    (first_ref, rank_ref, qs_ref, qst_ref, dos_ref, dot_ref, bias_ref, cos_t_ref, sin_t_ref,
     ck_t_ref, cv_t_ref, cos_ref, sin_ref, ck_ref, cv_ref, kp_ref, vp_ref) = take(17)
    far = take(shards - 1)
    ahead = take(3)
    if g + 1 < KV:
        take(1)
    old_sums_ref = take(1)[0] if g else None
    old_send = take(shards - 1) if 0 < g < KV - 1 else []
    if 0 < g < KV - 1:
        take(2)
    out_ref, gq_ref, sums_ref, own_ref = take(4)
    send = take(shards - 1)
    pack_ref = take(1)[0] if g + 2 < KV else None
    keys, values, keys_t, values_t, dk_acc, dv_acc = take(6)
    scratch = [take(3) for _ in range(GROUP // HEADS)]
    tokens = kp_ref.shape[0]
    slots = ck_ref.shape[0]
    owned = slots + tokens
    total = shards * owned
    known = owned
    first = first_ref[0]
    rank = rank_ref[0]
    mine = pl.ds(g * HD, HD)

    if pack_ref is not None:
        copy_chunk(pl.ds((g + 2) * HD, HD), (ck_ref, cv_ref, kp_ref, vp_ref), pack_ref)
    for s in range(shards):
        at = s * owned
        rows = pl.ds(s * tokens, tokens)
        if s == 0:
            sources = [ref[:, mine] for ref in (ck_ref, cv_ref, kp_ref, vp_ref)]
        else:
            sources = [
                far[s - 1][pl.ds(*part)] for part in
                ((0, slots), (slots, slots), (2 * slots, tokens), (2 * slots + tokens, tokens))
            ]
        k, v = slab_rows(g, sources[2:], bias_ref, cos_ref[rows, :], sin_ref[rows, :])
        for (natural, transposed), cache, own in zip(
            ((keys, keys_t), (values, values_t)), sources[:2], (k, v)
        ):
            if s:
                natural[pl.ds(at, slots)] = cache
                natural[pl.ds(at + slots, tokens)] = own
            transposed[:, pl.ds(at + slots, tokens)] = own.T
            if s:
                transposed[:, pl.ds(at, slots)] = cache.T
    keys_t[:, pl.ds(0, slots)] = ck_t_ref[mine, :]
    values_t[:, pl.ds(0, slots)] = cv_t_ref[mine, :]
    sums_ref[...] = jnp.zeros_like(sums_ref) if old_sums_ref is None else old_sums_ref[...]
    dk_acc[...] = jnp.zeros_like(dk_acc)
    dv_acc[...] = jnp.zeros_like(dv_acc)

    width = HEADS * tokens
    scale = HD ** -0.5
    blocks = range(0, total, tokens)

    class Chain:
        def __init__(self, index):
            self.index = g * (GROUP // HEADS) + index
            self.s, self.pb, self.ds = scratch[index]
            index = self.index
            self.rows = pl.ds(pl.multiple_of(index * width, width), width)
            self.place = pl.ds(pl.multiple_of(index * HD, HD), HD)
            self.ahead = [ref.at[self.index % len(scratch)] for ref in ahead]
            self.top = self.ahead[2][...]

        def scores(self):
            s = dot(keys[pl.ds(known, total - known), :], qst_ref[self.place, :], NN)
            for start in blocks[known // tokens:]:
                part = s[start - known:start - known + tokens]
                seen = allowed(start, part, first, rank, shards, slots, tokens)
                part = jnp.where(seen, part, NEG)
                self.s[pl.ds(start, tokens), :] = part
                self.top = jnp.maximum(self.top, fold(part, jnp.max))

        def exponents(self):
            top = jnp.max(self.top, axis=0, keepdims=True)
            weight = jnp.zeros((8, width), F32)
            for start in blocks:
                rows = pl.ds(start, tokens)
                s = (self.ahead[0] if start < known else self.s)[rows, :]
                e = jnp.exp2((s - top) * (scale * math.log2(math.e)))
                self.s[rows, :] = e
                weight = weight + fold(e, jnp.sum)
            self.inverse = 1.0 / jnp.sum(weight, axis=0, keepdims=True)

        def probs(self):
            for start in blocks:
                rows = pl.ds(start, tokens)
                p = self.s[rows, :] * self.inverse
                self.s[rows, :] = p
                self.pb[rows, :] = p.astype(B16)

        def output(self):
            self.o = dot(values_t[...], self.pb[...], NN).astype(B16)
            do = dot_ref[self.place, :].astype(F32)
            self.delta = jnp.sum(do * self.o.astype(F32), axis=0, keepdims=True)

        def heads(self):
            for i in range(HEADS):
                head = self.index * HEADS + i
                yield (
                    slice(i * tokens, (i + 1) * tokens),
                    pl.ds(pl.multiple_of((head - g * GROUP) * HD, HD), HD),
                    head,
                )

        def dprobs(self):
            rows = pl.ds(known, total - known)
            self.dp = dot(values[rows, :], dot_ref[self.place, :], NN)

        def dscores(self):
            for start in blocks:
                rows = pl.ds(start, tokens)
                if start < known:
                    part = self.ahead[1][rows, :]
                else:
                    part = self.dp[start - known:start - known + tokens]
                self.ds[rows, :] = (self.s[rows, :] * (part - self.delta)).astype(B16)

        def query_grad(self):
            self.dq = (dot(keys_t[...], self.ds[...], NN) * scale).astype(B16).astype(F32)

        def slab_grads(self):
            for s in range(shards):
                rows = pl.ds(s * owned + slots, tokens)
                place = pl.ds(s * tokens, tokens)
                dv_acc[place, :] += dot(self.pb[rows, :], dos_ref[self.rows, :], NN)
                dk_acc[place, :] += dot(self.ds[rows, :], qs_ref[self.rows, :], NN)

        def store(self):
            for part, cols, head in self.heads():
                out_ref[:, cols] = self.o[:, part].T
                x = self.dq[:, part]
                other = jnp.concatenate([x[HD // 2:], x[:HD // 2]], axis=0)
                x = (x * cos_t_ref[...] - other * sin_t_ref[...]).T
                gq_ref[:, cols] = x.astype(B16)
                sums_ref[pl.ds(head, 1), :] = jnp.sum(x, axis=0, keepdims=True)

    steps = [
        Chain.scores, Chain.exponents, Chain.dprobs, Chain.probs, Chain.output,
        Chain.dscores, Chain.query_grad, Chain.slab_grads, Chain.store,
    ]
    group = [Chain(i) for i in range(GROUP // HEADS)]
    for turn_of in range(len(steps) + len(group) - 1):
        for i, chain in reversed(list(enumerate(group))):
            if 0 <= turn_of - i < len(steps):
                steps[turn_of - i](chain)

    dk = dk_acc[...] * scale
    dv = dv_acc[...]
    gk = turn_back(dk, cos_ref[...], sin_ref[...])
    own_ref[0] = dk[:tokens]
    own_ref[1] = dv[:tokens]
    at = 2 * g if g < KV - 1 else 0
    for j in range(1, shards):
        block = slice(j * tokens, (j + 1) * tokens)
        send[j - 1][at] = dk[block].astype(B16)
        send[j - 1][at + 1] = dv[block].astype(B16)
        if at:
            send[j - 1][pl.ds(0, at)] = old_send[j - 1][...]
    sums_ref[pl.ds(HQ + g, 1), :] = jnp.sum(gk, axis=0, keepdims=True)
    sums_ref[pl.ds(HQ + KV + g, 1), :] = jnp.sum(dv, axis=0, keepdims=True)


def attend(
    g, shards, first, rank, prepared, cosine, sine, ck, cv, kp, vp, far, ahead, before
):
    tokens, slots = kp.shape[0], ck.shape[0]
    slab = shards * tokens
    total = slab + shards * slots
    smem = pl.BlockSpec(memory_space=pltpu.SMEM)
    vmem = pl.BlockSpec(memory_space=pltpu.VMEM)
    anywhere = pl.BlockSpec(memory_space=pl.ANY)
    wide = pl.BlockSpec((tokens, GROUP * HD), lambda i: (0, g))

    last = g == KV - 1
    args = [first, rank]
    placed = [*prepared, cosine, sine, ck, cv, kp, vp, *far]
    placed += [*ahead[g], *[x[2] for x in ahead[g + 1:g + 2]]]
    aliases = {}
    if before is not None:
        out, gq, sums, send = before
        placed += [sums, *([] if last else send)]
    args += placed
    in_specs = [smem] * 2 + [vmem] * len(placed)
    if before is not None and not last:
        aliases = {len(args): 0, len(args) + 1: 1}
        args += [out, gq]
        in_specs += [anywhere] * 2
    kept = pltpu.VMEM((tokens, GROUP * HD), B16) if last else pltpu.HBM((tokens, HQ * HD), B16)
    out_shape = [
        kept, kept,
        pltpu.VMEM((SUMS, HD), F32),
        pltpu.VMEM((2, tokens, HD), F32),
    ]
    out_specs = [vmem if last else wide] * 2 + [vmem, vmem]
    out_shape += [pltpu.VMEM((2 if last else 2 * g + 2, tokens, HD), B16)] * (shards - 1)
    out_specs += [vmem] * (shards - 1)
    if g + 2 < KV:
        out_shape.append(pltpu.VMEM((2 * (slots + tokens), HD), B16))
        out_specs.append(vmem)
    results = pl.pallas_call(
        functools.partial(attend_kernel, g, shards),
        grid=(1,),
        in_specs=in_specs,
        out_shape=out_shape,
        out_specs=out_specs,
        scratch_shapes=[
            pltpu.VMEM((total, HD), B16), pltpu.VMEM((total, HD), B16),
            pltpu.VMEM((HD, total), B16), pltpu.VMEM((HD, total), B16),
            pltpu.VMEM((slab, HD), F32), pltpu.VMEM((slab, HD), F32),
        ] + [
            pltpu.VMEM((total, HEADS * tokens), kind) for kind in (F32, B16, B16) * (GROUP // HEADS)
        ],
        input_output_aliases=aliases,
        compiler_params=params(),
        cost_estimate=pl.CostEstimate(
            flops=2 * GROUP * tokens * HD * (4 * total + 2 * slab),
            bytes_accessed=8 * tokens * GROUP * HD + 8 * total * HD,
            transcendentals=GROUP * tokens * total,
        ),
        name="attend",
    )(*args)
    out, gq, sums, own = results[:4]
    send = results[4:4 + shards - 1]
    return (out, gq, sums, send), own, results[4 + shards - 1:]


def place_kernel(out_part, gq_part, _, __, out_ref, gq_ref):
    out_ref[...] = out_part[...]
    gq_ref[...] = gq_part[...]


def place(parts, out, gq):
    wide = pl.BlockSpec((out.shape[0], GROUP * HD), lambda i: (0, KV - 1))
    return pl.pallas_call(
        place_kernel,
        grid=(1,),
        in_specs=[pl.BlockSpec(memory_space=pltpu.VMEM)] * 2
        + [pl.BlockSpec(memory_space=pl.ANY)] * 2,
        out_specs=[wide, wide],
        out_shape=[pltpu.HBM(out.shape, B16)] * 2,
        input_output_aliases={2: 0, 3: 1},
        compiler_params=params(),
        cost_estimate=pl.CostEstimate(flops=0, bytes_accessed=1 << 21, transcendentals=0),
        name="place",
    )(*parts, out, gq)


def finish_kernel(shards, *refs):
    cos_ref, sin_ref, *refs = refs
    owns, refs = refs[:KV], refs[KV:]
    early, late = refs[:shards - 1], refs[shards - 1:2 * (shards - 1)]
    sums = refs[2 * (shards - 1):-6]
    gk_ref, gv_ref, *parts = refs[-5:]
    tokens = gk_ref.shape[0]
    cosine, sine = cos_ref[pl.ds(0, tokens), :], sin_ref[pl.ds(0, tokens), :]
    for g in range(KV):
        dk, dv = owns[g][0], owns[g][1]
        last = g == KV - 1
        for back in late if last else early:
            dk = dk + back[0 if last else 2 * g].astype(F32)
            dv = dv + back[1 if last else 2 * g + 1].astype(F32)
        cols = pl.ds(g * HD, HD)
        gk_ref[:, cols] = turn_back(dk, cosine, sine).astype(B16)
        gv_ref[:, cols] = dv.astype(B16)
    start = 0
    for part in parts:
        rows = pl.ds(start, part.shape[0])
        part[...] = add_up([ref[rows, :] for ref in sums])
        start += part.shape[0]


def finish(shards, cosine, sine, owns, early, late, sums, after):
    tokens = owns[0].shape[1]
    args = [cosine, sine, *owns, *early, *late, *sums]
    shapes = [((tokens, KV * HD), B16)] * 2 + [((rows, HD), F32) for rows in (HQ, KV, KV)]
    return pl.pallas_call(
        functools.partial(finish_kernel, shards),
        grid=(1,),
        in_specs=[pl.BlockSpec(memory_space=pltpu.VMEM)] * len(args)
        + [pl.BlockSpec(memory_space=pl.ANY)],
        out_specs=[whole(shape) for shape, _ in shapes],
        out_shape=[pltpu.HBM(shape, kind) for shape, kind in shapes],
        compiler_params=params(),
        cost_estimate=pl.CostEstimate(flops=0, bytes_accessed=1 << 19, transcendentals=0),
        name="finish",
    )(*args, after)


def join_kernel(a_ref, b_ref, *refs):
    refs[-1][...] = a_ref[...] + b_ref[...]


def join(parts, held):
    args = [*parts, *held]
    return pl.pallas_call(
        join_kernel,
        grid=(1,),
        in_specs=[pl.BlockSpec(memory_space=pltpu.VMEM)] * len(args),
        out_specs=pl.BlockSpec(memory_space=pltpu.VMEM),
        out_shape=pltpu.VMEM(parts[0].shape, parts[0].dtype),
        compiler_params=params(),
        cost_estimate=pl.CostEstimate(flops=0, bytes_accessed=1 << 16, transcendentals=0),
        name="join",
    )(*args)


def add_up(parts):
    while len(parts) > 1:
        parts = [a + b for a, b in zip(parts[::2], parts[1::2])]
    return parts[0]


def sum_but_last(x, axes, near, held):
    devices = lax.axis_size(axes)
    bits = [1 << i for i in reversed(range(devices.bit_length() - 1)) if 1 << i != near]
    stages = [[near]] + [bits[i:i + 2] for i in range(0, len(bits), 2)]
    parts = [x]
    for i, stage in enumerate(stages):
        x = join(parts, held) if i == 1 else add_up(parts)
        parts = [x]
        for flip in [sum(c) for n in (1, 2) for c in itertools.combinations(stage, n)]:
            parts.append(lax.ppermute(x, axes, [(i, i ^ flip) for i in range(devices)]))
    return parts


def body(q_proj, k_proj, v_proj, cache_k, cache_v, bias_q, bias_k, bias_v, start, dout):
    shards = lax.axis_size("seq")
    rank = lax.axis_index("seq").astype(jnp.int32)
    tokens = q_proj.shape[1]
    shifts = range(1, shards)

    def ring(x, s):
        return lax.ppermute(x, "seq", [(i, (i + s) % shards) for i in range(shards)])

    def earlier(x, s):
        return lax.ppermute(x, "seq", [(i + s, i) for i in range(shards - s)])

    hbm = functools.partial(pltpu.with_memory_space_constraint, memory_space=pltpu.HBM)
    own = [hbm(x[0]) for x in (cache_k, cache_v, k_proj, v_proj)]
    chunk = pack(own)
    far = [[ring(chunk, s) for s in shifts]]

    owners = lax.rem(rank - jnp.arange(shards, dtype=jnp.int32) + shards, shards)
    positions = start[0] + owners[:, None] * tokens + jnp.arange(tokens, dtype=jnp.int32)[None]
    lane = jnp.arange(HD, dtype=jnp.int32)
    freqs = jnp.exp(
        -(2.0 * (lane % (HD // 2)).astype(F32) / HD) * jnp.log(jnp.float32(1000000.0))
    )
    angles = positions.reshape(-1).astype(F32)[:, None] * freqs[None, :]
    cosine = jnp.cos(angles)
    sine = jnp.sin(angles) * jnp.where(lane < HD // 2, -1.0, 1.0).astype(F32)[None]

    *prepared, ck, cv, kp, vp, chunk = prep(
        hbm(q_proj[0]), hbm(dout[0]), hbm(bias_q.reshape(HQ, HD)),
        hbm(bias_k.reshape(KV, HD)), hbm(bias_v.reshape(KV, HD)), cosine, sine, own,
    )
    far.append([ring(chunk, s) for s in shifts])
    qst, dot_t, bias = prepared[1], prepared[3], prepared[4]
    ahead = [
        look_ahead(
            g, shards, start, rank.reshape(1), qst, dot_t, bias, cosine, sine, ck, cv, kp, vp
        )
        for g in range(KV)
    ]
    before, owns = None, []
    for g in range(KV):
        before, own, more = attend(
            g, shards, start, rank.reshape(1), prepared, cosine, sine, ck, cv, kp, vp,
            far[g], ahead, before,
        )
        if g == KV - 2:
            out, gq = before[:2]
            early = [earlier(x, s) for s, x in zip(shifts, before[3])]
        owns.append(own)
        far += [[ring(chunk, s) for s in shifts] for chunk in more]
    *columns, sums, send = before
    late = [earlier(x, s) for s, x in zip(shifts, send)]
    sums = sum_but_last(sums, ("dp", "seq"), shards, early)
    out, gq = place(columns, out, gq)
    gk, gv, *sums = finish(shards, cosine, sine, owns, early, late, sums, hbm(out))
    return (out[None], gq[None], gk[None], gv[None], *[x.reshape(-1) for x in sums])


def solution(mesh):
    split = P("dp", "seq", None)
    return jax.shard_map(
        body,
        mesh=mesh,
        in_specs=(split,) * 5 + (P(), P(), P(), P("dp"), split),
        out_specs=(split,) * 4 + (P(), P(), P()),
        check_vma=False,
    )
```

```python
import functools
import itertools
import math

import jax
import jax.numpy as jnp
from jax import lax
from jax.experimental import pallas as pl
from jax.experimental.pallas import tpu as pltpu
from jax.sharding import PartitionSpec as P

HQ = 32
KV = 4
HD = 128
GROUP = 8
HEADS = 4
NEG = -1e30
SUMS = HQ + 2 * KV
VMEM = 28 * 1024 * 1024
F32, B16 = jnp.float32, jnp.bfloat16


def turn(x):
    return pltpu.roll(x, HD // 2, 1)


def dot(a, b, dims):
    return lax.dot_general(a, b, (dims, ((), ())), preferred_element_type=F32)


NN = ((1,), (0,))


def whole(shape):
    return pl.BlockSpec(shape, lambda i: (0,) * len(shape))


def column(rows, g):
    return pl.BlockSpec((rows, HD), lambda i: (0, g))


def params():
    return pltpu.CompilerParams(dimension_semantics=("arbitrary",), vmem_limit_bytes=VMEM)


def copy_chunk(cols, sources, out_ref):
    start = 0
    for ref in sources:
        rows = ref.shape[0]
        out_ref[pl.ds(start, rows)] = ref[:, cols]
        start += rows


def pack_kernel(*refs):
    copy_chunk(pl.ds(0, HD), refs[:-1], refs[-1])


def pack(sources):
    rows = sum(x.shape[0] for x in sources)
    return pl.pallas_call(
        pack_kernel,
        grid=(1,),
        in_specs=[column(x.shape[0], 0) for x in sources],
        out_specs=pl.BlockSpec(memory_space=pltpu.VMEM),
        out_shape=pltpu.VMEM((rows, HD), B16),
        compiler_params=params(),
        cost_estimate=pl.CostEstimate(flops=0, bytes_accessed=4 * rows * HD, transcendentals=0),
        name="pack",
    )(*sources)


def turn_back(x, cosine, sine):
    return x * cosine - turn(x) * sine


def prep_kernel(
    q_ref, do_ref, bq_ref, bk_ref, bv_ref, cos_ref, sin_ref, ck_ref, cv_ref, kp_ref, vp_ref,
    qs_ref, qst_ref, dos_ref, dot_ref, bias_ref, cos_t_ref, sin_t_ref, ck_t_ref, cv_t_ref,
    ck_out, cv_out, kp_out, vp_out, pack_ref,
):
    g = pl.program_id(0)
    tokens = q_ref.shape[0]
    cosine, sine = cos_ref[pl.ds(0, tokens), :], sin_ref[pl.ds(0, tokens), :]
    bias_q = bq_ref[...].astype(F32)
    own = (ck_ref, cv_ref, kp_ref, vp_ref)

    @pl.when(g == 0)
    def _():
        bias_ref[pl.ds(0, KV), :] = bk_ref[...].astype(F32)
        bias_ref[pl.ds(KV, KV), :] = bv_ref[...].astype(F32)
        cos_t_ref[...] = cosine.T
        sin_t_ref[...] = sine.T

    @pl.when(g == 1)
    def _():
        copy_chunk(pl.ds(0, HD), own, pack_ref)

    for h in range(GROUP):
        cols = pl.ds(h * HD, HD)
        rows = pl.ds(pl.multiple_of((g * GROUP + h) * tokens, tokens), tokens)
        x = q_ref[:, cols].astype(F32) + bias_q[h:h + 1]
        x = (x * cosine + turn(x) * sine).astype(B16)
        qs_ref[rows, :] = x
        do = do_ref[:, cols]
        dos_ref[rows, :] = do
        chain, part = h // HEADS, h % HEADS
        place = pl.ds(pl.multiple_of((g * (GROUP // HEADS) + chain) * HD, HD), HD)
        qst_ref[place, pl.ds(part * tokens, tokens)] = x.T
        dot_ref[place, pl.ds(part * tokens, tokens)] = do.T
    mine = pl.ds(pl.multiple_of(g * HD, HD), HD)
    ck_t_ref[mine, :] = ck_ref[...].T
    cv_t_ref[mine, :] = cv_ref[...].T
    for ref, out in zip(own, (ck_out, cv_out, kp_out, vp_out)):
        out[:, mine] = ref[...]


def prep(q, do, bq, bk, bv, cosine, sine, own):
    tokens, slots = q.shape[0], own[0].shape[0]
    vmem = pl.BlockSpec(memory_space=pltpu.VMEM)
    wide = pl.BlockSpec((tokens, GROUP * HD), lambda i: (0, i))
    stacked = pltpu.VMEM((HQ * tokens, HD), B16)
    turned = pltpu.VMEM((HQ // HEADS * HD, HEADS * tokens), B16)
    out_shape = [
        stacked, turned, stacked, turned,
        pltpu.VMEM((2 * KV, HD), F32),
        pltpu.VMEM((HD, tokens), F32),
        pltpu.VMEM((HD, tokens), F32),
        pltpu.VMEM((KV * HD, slots), B16),
        pltpu.VMEM((KV * HD, slots), B16),
        *[pltpu.VMEM(x.shape, B16) for x in own],
        pltpu.VMEM((2 * (slots + tokens), HD), B16),
    ]
    return pl.pallas_call(
        prep_kernel,
        grid=(KV,),
        in_specs=[
            wide, wide, pl.BlockSpec((GROUP, HD), lambda i: (i, 0)),
            whole((KV, HD)), whole((KV, HD)), vmem, vmem,
            *[pl.BlockSpec((x.shape[0], HD), lambda i: (0, i)) for x in own],
        ],
        out_specs=[vmem] * len(out_shape),
        out_shape=out_shape,
        compiler_params=params(),
        cost_estimate=pl.CostEstimate(
            flops=4 * tokens * HQ * HD, bytes_accessed=12 * tokens * HQ * HD, transcendentals=0
        ),
        name="prep",
    )(q, do, bq, bk, bv, cosine, sine, *own)


def fold(x, op):
    return op(x.reshape(x.shape[0] // 8, 8, x.shape[1]), axis=0)


def allowed(start, s, first, rank, shards, slots, tokens):
    shift, at = divmod(start, slots + tokens)
    row = lax.broadcasted_iota(jnp.int32, s.shape, 0)
    if at < slots:
        owner = lax.rem(rank - shift + shards, shards)
        return row < first - owner * slots - at
    if shift == 0:
        return row <= (lax.broadcasted_iota(jnp.int32, s.shape, 1) & (tokens - 1))
    return row < jnp.where(rank >= shift, tokens, 0)


def slab_rows(g, sources, bias_ref, cosine, sine):
    kp, vp = sources
    k = kp.astype(F32) + bias_ref[g:g + 1, :]
    v = vp.astype(F32) + bias_ref[KV + g:KV + g + 1, :]
    return (k * cosine + turn(k) * sine).astype(B16), v.astype(B16)


def ahead_kernel(
    g, shards, first_ref, rank_ref, qst_ref, dot_ref, bias_ref, cos_ref, sin_ref,
    ck_ref, cv_ref, kp_ref, vp_ref, s_ref, dp_ref, top_ref, keys, values,
):
    tokens, slots, width = kp_ref.shape[0], ck_ref.shape[0], qst_ref.shape[1]
    owned = slots + tokens
    mine = pl.ds(g * HD, HD)
    rows = pl.ds(0, tokens)
    k, v = slab_rows(
        g, (kp_ref[:, mine], vp_ref[:, mine]), bias_ref, cos_ref[rows, :], sin_ref[rows, :]
    )
    keys[pl.ds(0, slots)] = ck_ref[:, mine]
    keys[pl.ds(slots, tokens)] = k
    values[pl.ds(0, slots)] = cv_ref[:, mine]
    values[pl.ds(slots, tokens)] = v
    for i in range(GROUP // HEADS):
        place = pl.ds((g * (GROUP // HEADS) + i) * HD, HD)
        s = dot(keys[...], qst_ref[place, :], NN)
        top = jnp.full((8, width), NEG, F32)
        for start in range(0, owned, tokens):
            part = s[start:start + tokens]
            seen = allowed(start, part, first_ref[0], rank_ref[0], shards, slots, tokens)
            part = jnp.where(seen, part, NEG)
            s_ref[i, pl.ds(start, tokens), :] = part
            top = jnp.maximum(top, fold(part, jnp.max))
        top_ref[i] = top
        dp_ref[i] = dot(values[...], dot_ref[place, :], NN)


def look_ahead(g, shards, first, rank, qst, dot_t, bias, cosine, sine, ck, cv, kp, vp):
    tokens, slots, width = kp.shape[0], ck.shape[0], qst.shape[1]
    owned = slots + tokens
    chains = GROUP // HEADS
    smem = pl.BlockSpec(memory_space=pltpu.SMEM)
    vmem = pl.BlockSpec(memory_space=pltpu.VMEM)
    args = [first, rank, qst, dot_t, bias, cosine, sine, ck, cv, kp, vp]
    return pl.pallas_call(
        functools.partial(ahead_kernel, g, shards),
        grid=(1,),
        in_specs=[smem] * 2 + [vmem] * (len(args) - 2),
        out_specs=[vmem] * 3,
        out_shape=[
            pltpu.VMEM((chains, owned, width), F32),
            pltpu.VMEM((chains, owned, width), F32),
            pltpu.VMEM((chains, 8, width), F32),
        ],
        scratch_shapes=[pltpu.VMEM((owned, HD), B16)] * 2,
        compiler_params=params(),
        cost_estimate=pl.CostEstimate(
            flops=4 * GROUP * tokens * HD * owned, bytes_accessed=8 * GROUP * tokens * owned,
            transcendentals=0,
        ),
        name="ahead",
    )(*args)


def attend_kernel(g, shards, *refs):
    refs = list(refs)

    def take(count):
        taken = refs[:count]
        del refs[:count]
        return taken

    (first_ref, rank_ref, qs_ref, qst_ref, dos_ref, dot_ref, bias_ref, cos_t_ref, sin_t_ref,
     ck_t_ref, cv_t_ref, cos_ref, sin_ref, ck_ref, cv_ref, kp_ref, vp_ref) = take(17)
    far = take(shards - 1)
    ahead = take(3)
    if g + 1 < KV:
        take(1)
    old_sums_ref = take(1)[0] if g else None
    old_send = take(shards - 1) if g else []
    if 0 < g < KV - 1:
        take(2)
    out_ref, gq_ref, sums_ref, own_ref = take(4)
    send = take(shards - 1)
    pack_ref = take(1)[0] if g + 2 < KV else None
    keys, values, keys_t, values_t, dk_acc, dv_acc = take(6)
    scratch = [take(3) for _ in range(GROUP // HEADS)]
    tokens = kp_ref.shape[0]
    slots = ck_ref.shape[0]
    owned = slots + tokens
    total = shards * owned
    known = owned
    first = first_ref[0]
    rank = rank_ref[0]
    mine = pl.ds(g * HD, HD)

    if pack_ref is not None:
        copy_chunk(pl.ds((g + 2) * HD, HD), (ck_ref, cv_ref, kp_ref, vp_ref), pack_ref)
    for s in range(shards):
        at = s * owned
        rows = pl.ds(s * tokens, tokens)
        if s == 0:
            sources = [ref[:, mine] for ref in (ck_ref, cv_ref, kp_ref, vp_ref)]
        else:
            sources = [
                far[s - 1][pl.ds(*part)] for part in
                ((0, slots), (slots, slots), (2 * slots, tokens), (2 * slots + tokens, tokens))
            ]
        k, v = slab_rows(g, sources[2:], bias_ref, cos_ref[rows, :], sin_ref[rows, :])
        for (natural, transposed), cache, own in zip(
            ((keys, keys_t), (values, values_t)), sources[:2], (k, v)
        ):
            if s:
                natural[pl.ds(at, slots)] = cache
                natural[pl.ds(at + slots, tokens)] = own
            transposed[:, pl.ds(at + slots, tokens)] = own.T
            if s:
                transposed[:, pl.ds(at, slots)] = cache.T
    keys_t[:, pl.ds(0, slots)] = ck_t_ref[mine, :]
    values_t[:, pl.ds(0, slots)] = cv_t_ref[mine, :]
    sums_ref[...] = jnp.zeros_like(sums_ref) if old_sums_ref is None else old_sums_ref[...]
    dk_acc[...] = jnp.zeros_like(dk_acc)
    dv_acc[...] = jnp.zeros_like(dv_acc)

    width = HEADS * tokens
    scale = HD ** -0.5
    blocks = range(0, total, tokens)

    class Chain:
        def __init__(self, index):
            self.index = g * (GROUP // HEADS) + index
            self.s, self.pb, self.ds = scratch[index]
            index = self.index
            self.rows = pl.ds(pl.multiple_of(index * width, width), width)
            self.place = pl.ds(pl.multiple_of(index * HD, HD), HD)
            self.ahead = [ref.at[self.index % len(scratch)] for ref in ahead]
            self.top = self.ahead[2][...]

        def scores(self):
            s = dot(keys[pl.ds(known, total - known), :], qst_ref[self.place, :], NN)
            for start in blocks[known // tokens:]:
                part = s[start - known:start - known + tokens]
                seen = allowed(start, part, first, rank, shards, slots, tokens)
                part = jnp.where(seen, part, NEG)
                self.s[pl.ds(start, tokens), :] = part
                self.top = jnp.maximum(self.top, fold(part, jnp.max))

        def exponents(self):
            top = jnp.max(self.top, axis=0, keepdims=True)
            weight = jnp.zeros((8, width), F32)
            for start in blocks:
                rows = pl.ds(start, tokens)
                s = (self.ahead[0] if start < known else self.s)[rows, :]
                e = jnp.exp2((s - top) * (scale * math.log2(math.e)))
                self.s[rows, :] = e
                weight = weight + fold(e, jnp.sum)
            self.inverse = 1.0 / jnp.sum(weight, axis=0, keepdims=True)

        def probs(self):
            for start in blocks:
                rows = pl.ds(start, tokens)
                p = self.s[rows, :] * self.inverse
                self.s[rows, :] = p
                self.pb[rows, :] = p.astype(B16)

        def output(self):
            self.o = dot(values_t[...], self.pb[...], NN).astype(B16)
            do = dot_ref[self.place, :].astype(F32)
            self.delta = jnp.sum(do * self.o.astype(F32), axis=0, keepdims=True)

        def heads(self):
            for i in range(HEADS):
                head = self.index * HEADS + i
                yield (
                    slice(i * tokens, (i + 1) * tokens),
                    pl.ds(pl.multiple_of((head - g * GROUP) * HD, HD), HD),
                    head,
                )

        def dprobs(self):
            rows = pl.ds(known, total - known)
            self.dp = dot(values[rows, :], dot_ref[self.place, :], NN)

        def dscores(self):
            for start in blocks:
                rows = pl.ds(start, tokens)
                if start < known:
                    part = self.ahead[1][rows, :]
                else:
                    part = self.dp[start - known:start - known + tokens]
                self.ds[rows, :] = (self.s[rows, :] * (part - self.delta)).astype(B16)

        def query_grad(self):
            self.dq = (dot(keys_t[...], self.ds[...], NN) * scale).astype(B16).astype(F32)

        def slab_grads(self):
            for s in range(shards):
                rows = pl.ds(s * owned + slots, tokens)
                place = pl.ds(s * tokens, tokens)
                dv_acc[place, :] += dot(self.pb[rows, :], dos_ref[self.rows, :], NN)
                dk_acc[place, :] += dot(self.ds[rows, :], qs_ref[self.rows, :], NN)

        def store(self):
            for part, cols, head in self.heads():
                out_ref[:, cols] = self.o[:, part].T
                x = self.dq[:, part]
                other = jnp.concatenate([x[HD // 2:], x[:HD // 2]], axis=0)
                x = (x * cos_t_ref[...] - other * sin_t_ref[...]).T
                gq_ref[:, cols] = x.astype(B16)
                sums_ref[pl.ds(head, 1), :] = jnp.sum(x, axis=0, keepdims=True)

    steps = [
        Chain.scores, Chain.exponents, Chain.dprobs, Chain.probs, Chain.output,
        Chain.dscores, Chain.query_grad, Chain.slab_grads, Chain.store,
    ]
    group = [Chain(i) for i in range(GROUP // HEADS)]
    for turn_of in range(len(steps) + len(group) - 1):
        for i, chain in reversed(list(enumerate(group))):
            if 0 <= turn_of - i < len(steps):
                steps[turn_of - i](chain)

    dk = dk_acc[...] * scale
    dv = dv_acc[...]
    gk = turn_back(dk, cos_ref[...], sin_ref[...])
    own_ref[0] = dk[:tokens]
    own_ref[1] = dv[:tokens]
    at = 2 * g
    for j in range(1, shards):
        block = slice(j * tokens, (j + 1) * tokens)
        send[j - 1][at] = dk[block].astype(B16)
        send[j - 1][at + 1] = dv[block].astype(B16)
        if at:
            send[j - 1][pl.ds(0, at)] = old_send[j - 1][...]
    sums_ref[pl.ds(HQ + g, 1), :] = jnp.sum(gk, axis=0, keepdims=True)
    sums_ref[pl.ds(HQ + KV + g, 1), :] = jnp.sum(dv, axis=0, keepdims=True)


def attend(
    g, shards, first, rank, prepared, cosine, sine, ck, cv, kp, vp, far, ahead, before
):
    tokens, slots = kp.shape[0], ck.shape[0]
    slab = shards * tokens
    total = slab + shards * slots
    smem = pl.BlockSpec(memory_space=pltpu.SMEM)
    vmem = pl.BlockSpec(memory_space=pltpu.VMEM)
    anywhere = pl.BlockSpec(memory_space=pl.ANY)
    wide = pl.BlockSpec((tokens, GROUP * HD), lambda i: (0, g))

    last = g == KV - 1
    args = [first, rank]
    placed = [*prepared, cosine, sine, ck, cv, kp, vp, *far]
    placed += [*ahead[g], *[x[2] for x in ahead[g + 1:g + 2]]]
    aliases = {}
    if before is not None:
        out, gq, sums, send = before
        placed += [sums, *send]
    args += placed
    in_specs = [smem] * 2 + [vmem] * len(placed)
    if before is not None and not last:
        aliases = {len(args): 0, len(args) + 1: 1}
        args += [out, gq]
        in_specs += [anywhere] * 2
    kept = pltpu.VMEM((tokens, GROUP * HD), B16) if last else pltpu.HBM((tokens, HQ * HD), B16)
    out_shape = [
        kept, kept,
        pltpu.VMEM((SUMS, HD), F32),
        pltpu.VMEM((2, tokens, HD), F32),
    ]
    out_specs = [vmem if last else wide] * 2 + [vmem, vmem]
    out_shape += [pltpu.VMEM((2 * g + 2, tokens, HD), B16)] * (shards - 1)
    out_specs += [vmem] * (shards - 1)
    if g + 2 < KV:
        out_shape.append(pltpu.VMEM((2 * (slots + tokens), HD), B16))
        out_specs.append(vmem)
    results = pl.pallas_call(
        functools.partial(attend_kernel, g, shards),
        grid=(1,),
        in_specs=in_specs,
        out_shape=out_shape,
        out_specs=out_specs,
        scratch_shapes=[
            pltpu.VMEM((total, HD), B16), pltpu.VMEM((total, HD), B16),
            pltpu.VMEM((HD, total), B16), pltpu.VMEM((HD, total), B16),
            pltpu.VMEM((slab, HD), F32), pltpu.VMEM((slab, HD), F32),
        ] + [
            pltpu.VMEM((total, HEADS * tokens), kind) for kind in (F32, B16, B16) * (GROUP // HEADS)
        ],
        input_output_aliases=aliases,
        compiler_params=params(),
        cost_estimate=pl.CostEstimate(
            flops=2 * GROUP * tokens * HD * (4 * total + 2 * slab),
            bytes_accessed=8 * tokens * GROUP * HD + 8 * total * HD,
            transcendentals=GROUP * tokens * total,
        ),
        name="attend",
    )(*args)
    out, gq, sums, own = results[:4]
    send = results[4:4 + shards - 1]
    return (out, gq, sums, send), own, results[4 + shards - 1:]


def place_kernel(out_part, gq_part, _, __, out_ref, gq_ref):
    out_ref[...] = out_part[...]
    gq_ref[...] = gq_part[...]


def place(parts, out, gq):
    wide = pl.BlockSpec((out.shape[0], GROUP * HD), lambda i: (0, KV - 1))
    return pl.pallas_call(
        place_kernel,
        grid=(1,),
        in_specs=[pl.BlockSpec(memory_space=pltpu.VMEM)] * 2
        + [pl.BlockSpec(memory_space=pl.ANY)] * 2,
        out_specs=[wide, wide],
        out_shape=[pltpu.HBM(out.shape, B16)] * 2,
        input_output_aliases={2: 0, 3: 1},
        compiler_params=params(),
        cost_estimate=pl.CostEstimate(flops=0, bytes_accessed=1 << 21, transcendentals=0),
        name="place",
    )(*parts, out, gq)


def finish_kernel(shards, *refs):
    cos_ref, sin_ref, *refs = refs
    owns, refs = refs[:KV], refs[KV:]
    backs, sums = refs[:shards - 1], refs[shards - 1:-6]
    gk_ref, gv_ref, *parts = refs[-5:]
    tokens = gk_ref.shape[0]
    cosine, sine = cos_ref[pl.ds(0, tokens), :], sin_ref[pl.ds(0, tokens), :]
    for g in range(KV):
        dk, dv = owns[g][0], owns[g][1]
        for back in backs:
            dk = dk + back[2 * g].astype(F32)
            dv = dv + back[2 * g + 1].astype(F32)
        cols = pl.ds(g * HD, HD)
        gk_ref[:, cols] = turn_back(dk, cosine, sine).astype(B16)
        gv_ref[:, cols] = dv.astype(B16)
    start = 0
    for part in parts:
        rows = pl.ds(start, part.shape[0])
        part[...] = add_up([ref[rows, :] for ref in sums])
        start += part.shape[0]


def finish(shards, cosine, sine, owns, backs, sums, after):
    tokens = owns[0].shape[1]
    args = [cosine, sine, *owns, *backs, *sums]
    shapes = [((tokens, KV * HD), B16)] * 2 + [((rows, HD), F32) for rows in (HQ, KV, KV)]
    return pl.pallas_call(
        functools.partial(finish_kernel, shards),
        grid=(1,),
        in_specs=[pl.BlockSpec(memory_space=pltpu.VMEM)] * len(args)
        + [pl.BlockSpec(memory_space=pl.ANY)],
        out_specs=[whole(shape) for shape, _ in shapes],
        out_shape=[pltpu.HBM(shape, kind) for shape, kind in shapes],
        compiler_params=params(),
        cost_estimate=pl.CostEstimate(flops=0, bytes_accessed=1 << 19, transcendentals=0),
        name="finish",
    )(*args, after)


def add_up(parts):
    while len(parts) > 1:
        parts = [a + b for a, b in zip(parts[::2], parts[1::2])]
    return parts[0]


def sum_but_last(x, axes, near):
    devices = lax.axis_size(axes)
    bits = [1 << i for i in reversed(range(devices.bit_length() - 1)) if 1 << i != near]
    stages = [[near]] + [bits[i:i + 2] for i in range(0, len(bits), 2)]
    parts = [x]
    for stage in stages:
        x = add_up(parts)
        parts = [x]
        for flip in [sum(c) for n in (1, 2) for c in itertools.combinations(stage, n)]:
            parts.append(lax.ppermute(x, axes, [(i, i ^ flip) for i in range(devices)]))
    return parts


def body(q_proj, k_proj, v_proj, cache_k, cache_v, bias_q, bias_k, bias_v, start, dout):
    shards = lax.axis_size("seq")
    rank = lax.axis_index("seq").astype(jnp.int32)
    tokens = q_proj.shape[1]
    shifts = range(1, shards)

    def ring(x, s):
        return lax.ppermute(x, "seq", [(i, (i + s) % shards) for i in range(shards)])

    def earlier(x, s):
        return lax.ppermute(x, "seq", [(i + s, i) for i in range(shards - s)])

    hbm = functools.partial(pltpu.with_memory_space_constraint, memory_space=pltpu.HBM)
    own = [hbm(x[0]) for x in (cache_k, cache_v, k_proj, v_proj)]
    chunk = pack(own)
    far = [[ring(chunk, s) for s in shifts]]

    owners = lax.rem(rank - jnp.arange(shards, dtype=jnp.int32) + shards, shards)
    positions = start[0] + owners[:, None] * tokens + jnp.arange(tokens, dtype=jnp.int32)[None]
    lane = jnp.arange(HD, dtype=jnp.int32)
    freqs = jnp.exp(
        -(2.0 * (lane % (HD // 2)).astype(F32) / HD) * jnp.log(jnp.float32(1000000.0))
    )
    angles = positions.reshape(-1).astype(F32)[:, None] * freqs[None, :]
    cosine = jnp.cos(angles)
    sine = jnp.sin(angles) * jnp.where(lane < HD // 2, -1.0, 1.0).astype(F32)[None]

    *prepared, ck, cv, kp, vp, chunk = prep(
        hbm(q_proj[0]), hbm(dout[0]), hbm(bias_q.reshape(HQ, HD)),
        hbm(bias_k.reshape(KV, HD)), hbm(bias_v.reshape(KV, HD)), cosine, sine, own,
    )
    far.append([ring(chunk, s) for s in shifts])
    qst, dot_t, bias = prepared[1], prepared[3], prepared[4]
    ahead = [
        look_ahead(
            g, shards, start, rank.reshape(1), qst, dot_t, bias, cosine, sine, ck, cv, kp, vp
        )
        for g in range(KV)
    ]
    before, owns = None, []
    for g in range(KV):
        before, own, more = attend(
            g, shards, start, rank.reshape(1), prepared, cosine, sine, ck, cv, kp, vp,
            far[g], ahead, before,
        )
        if g == KV - 2:
            out, gq = before[:2]
        owns.append(own)
        far += [[ring(chunk, s) for s in shifts] for chunk in more]
    *columns, sums, send = before
    backs = [earlier(x, s) for s, x in zip(shifts, send)]
    sums = sum_but_last(sums, ("dp", "seq"), shards)
    out, gq = place(columns, out, gq)
    gk, gv, *sums = finish(shards, cosine, sine, owns, backs, sums, hbm(out))
    return (out[None], gq[None], gk[None], gv[None], *[x.reshape(-1) for x in sums])


def solution(mesh):
    split = P("dp", "seq", None)
    return jax.shard_map(
        body,
        mesh=mesh,
        in_specs=(split,) * 5 + (P(), P(), P(), P("dp"), split),
        out_specs=(split,) * 4 + (P(), P(), P()),
        check_vma=False,
    )
```

```python
import functools
import itertools
import math

import jax
import jax.numpy as jnp
from jax import lax
from jax.experimental import pallas as pl
from jax.experimental.pallas import tpu as pltpu
from jax.sharding import PartitionSpec as P

HQ = 32
KV = 4
HD = 128
GROUP = 8
HEADS = 4
NEG = -1e30
SUMS = HQ + 2 * KV
VMEM = 28 * 1024 * 1024
F32, B16 = jnp.float32, jnp.bfloat16


def turn(x):
    return pltpu.roll(x, HD // 2, 1)


def dot(a, b, dims):
    return lax.dot_general(a, b, (dims, ((), ())), preferred_element_type=F32)


NN = ((1,), (0,))


def whole(shape):
    return pl.BlockSpec(shape, lambda i: (0,) * len(shape))


def column(rows, g):
    return pl.BlockSpec((rows, HD), lambda i: (0, g))


def params():
    return pltpu.CompilerParams(dimension_semantics=("arbitrary",), vmem_limit_bytes=VMEM)


def copy_chunk(cols, sources, out_ref):
    start = 0
    for ref in sources:
        rows = ref.shape[0]
        out_ref[pl.ds(start, rows)] = ref[:, cols]
        start += rows


def pack_kernel(*refs):
    copy_chunk(pl.ds(0, HD), refs[:-1], refs[-1])


def pack(sources):
    rows = sum(x.shape[0] for x in sources)
    return pl.pallas_call(
        pack_kernel,
        grid=(1,),
        in_specs=[column(x.shape[0], 0) for x in sources],
        out_specs=pl.BlockSpec(memory_space=pltpu.VMEM),
        out_shape=pltpu.VMEM((rows, HD), B16),
        compiler_params=params(),
        cost_estimate=pl.CostEstimate(flops=0, bytes_accessed=4 * rows * HD, transcendentals=0),
        name="pack",
    )(*sources)


def turn_back(x, cosine, sine):
    return x * cosine - turn(x) * sine


def prep_kernel(
    q_ref, do_ref, bq_ref, bk_ref, bv_ref, cos_ref, sin_ref, ck_ref, cv_ref, kp_ref, vp_ref,
    qs_ref, qst_ref, dos_ref, dot_ref, bias_ref, cos_t_ref, sin_t_ref, ck_t_ref, cv_t_ref,
    ck_out, cv_out, kp_out, vp_out, pack_ref,
):
    g = pl.program_id(0)
    tokens = q_ref.shape[0]
    cosine, sine = cos_ref[pl.ds(0, tokens), :], sin_ref[pl.ds(0, tokens), :]
    bias_q = bq_ref[...].astype(F32)
    own = (ck_ref, cv_ref, kp_ref, vp_ref)

    @pl.when(g == 0)
    def _():
        bias_ref[pl.ds(0, KV), :] = bk_ref[...].astype(F32)
        bias_ref[pl.ds(KV, KV), :] = bv_ref[...].astype(F32)
        cos_t_ref[...] = cosine.T
        sin_t_ref[...] = sine.T

    @pl.when(g == 1)
    def _():
        copy_chunk(pl.ds(0, HD), own, pack_ref)

    for h in range(GROUP):
        cols = pl.ds(h * HD, HD)
        rows = pl.ds(pl.multiple_of((g * GROUP + h) * tokens, tokens), tokens)
        x = q_ref[:, cols].astype(F32) + bias_q[h:h + 1]
        x = (x * cosine + turn(x) * sine).astype(B16)
        qs_ref[rows, :] = x
        do = do_ref[:, cols]
        dos_ref[rows, :] = do
        chain, part = h // HEADS, h % HEADS
        place = pl.ds(pl.multiple_of((g * (GROUP // HEADS) + chain) * HD, HD), HD)
        qst_ref[place, pl.ds(part * tokens, tokens)] = x.T
        dot_ref[place, pl.ds(part * tokens, tokens)] = do.T
    mine = pl.ds(pl.multiple_of(g * HD, HD), HD)
    ck_t_ref[mine, :] = ck_ref[...].T
    cv_t_ref[mine, :] = cv_ref[...].T
    for ref, out in zip(own, (ck_out, cv_out, kp_out, vp_out)):
        out[:, mine] = ref[...]


def prep(q, do, bq, bk, bv, cosine, sine, own):
    tokens, slots = q.shape[0], own[0].shape[0]
    vmem = pl.BlockSpec(memory_space=pltpu.VMEM)
    wide = pl.BlockSpec((tokens, GROUP * HD), lambda i: (0, i))
    stacked = pltpu.VMEM((HQ * tokens, HD), B16)
    turned = pltpu.VMEM((HQ // HEADS * HD, HEADS * tokens), B16)
    out_shape = [
        stacked, turned, stacked, turned,
        pltpu.VMEM((2 * KV, HD), F32),
        pltpu.VMEM((HD, tokens), F32),
        pltpu.VMEM((HD, tokens), F32),
        pltpu.VMEM((KV * HD, slots), B16),
        pltpu.VMEM((KV * HD, slots), B16),
        *[pltpu.VMEM(x.shape, B16) for x in own],
        pltpu.VMEM((2 * (slots + tokens), HD), B16),
    ]
    return pl.pallas_call(
        prep_kernel,
        grid=(KV,),
        in_specs=[
            wide, wide, pl.BlockSpec((GROUP, HD), lambda i: (i, 0)),
            whole((KV, HD)), whole((KV, HD)), vmem, vmem,
            *[pl.BlockSpec((x.shape[0], HD), lambda i: (0, i)) for x in own],
        ],
        out_specs=[vmem] * len(out_shape),
        out_shape=out_shape,
        compiler_params=params(),
        cost_estimate=pl.CostEstimate(
            flops=4 * tokens * HQ * HD, bytes_accessed=12 * tokens * HQ * HD, transcendentals=0
        ),
        name="prep",
    )(q, do, bq, bk, bv, cosine, sine, *own)


def fold(x, op):
    return op(x.reshape(x.shape[0] // 8, 8, x.shape[1]), axis=0)


def allowed(start, s, first, rank, shards, slots, tokens):
    shift, at = divmod(start, slots + tokens)
    row = lax.broadcasted_iota(jnp.int32, s.shape, 0)
    if at < slots:
        owner = lax.rem(rank - shift + shards, shards)
        return row < first - owner * slots - at
    if shift == 0:
        return row <= (lax.broadcasted_iota(jnp.int32, s.shape, 1) & (tokens - 1))
    return row < jnp.where(rank >= shift, tokens, 0)


def slab_rows(g, sources, bias_ref, cosine, sine):
    kp, vp = sources
    k = kp.astype(F32) + bias_ref[g:g + 1, :]
    v = vp.astype(F32) + bias_ref[KV + g:KV + g + 1, :]
    return (k * cosine + turn(k) * sine).astype(B16), v.astype(B16)


def ahead_kernel(
    g, shards, first_ref, rank_ref, qst_ref, dot_ref, bias_ref, cos_ref, sin_ref,
    ck_ref, cv_ref, kp_ref, vp_ref, s_ref, dp_ref, top_ref, keys, values,
):
    tokens, slots, width = kp_ref.shape[0], ck_ref.shape[0], qst_ref.shape[1]
    owned = slots + tokens
    mine = pl.ds(g * HD, HD)
    rows = pl.ds(0, tokens)
    k, v = slab_rows(
        g, (kp_ref[:, mine], vp_ref[:, mine]), bias_ref, cos_ref[rows, :], sin_ref[rows, :]
    )
    keys[pl.ds(0, slots)] = ck_ref[:, mine]
    keys[pl.ds(slots, tokens)] = k
    values[pl.ds(0, slots)] = cv_ref[:, mine]
    values[pl.ds(slots, tokens)] = v
    for i in range(GROUP // HEADS):
        place = pl.ds((g * (GROUP // HEADS) + i) * HD, HD)
        s = dot(keys[...], qst_ref[place, :], NN)
        top = jnp.full((8, width), NEG, F32)
        for start in range(0, owned, tokens):
            part = s[start:start + tokens]
            seen = allowed(start, part, first_ref[0], rank_ref[0], shards, slots, tokens)
            part = jnp.where(seen, part, NEG)
            s_ref[i, pl.ds(start, tokens), :] = part
            top = jnp.maximum(top, fold(part, jnp.max))
        top_ref[i] = top
        dp_ref[i] = dot(values[...], dot_ref[place, :], NN)


def look_ahead(g, shards, first, rank, qst, dot_t, bias, cosine, sine, ck, cv, kp, vp):
    tokens, slots, width = kp.shape[0], ck.shape[0], qst.shape[1]
    owned = slots + tokens
    chains = GROUP // HEADS
    smem = pl.BlockSpec(memory_space=pltpu.SMEM)
    vmem = pl.BlockSpec(memory_space=pltpu.VMEM)
    args = [first, rank, qst, dot_t, bias, cosine, sine, ck, cv, kp, vp]
    return pl.pallas_call(
        functools.partial(ahead_kernel, g, shards),
        grid=(1,),
        in_specs=[smem] * 2 + [vmem] * (len(args) - 2),
        out_specs=[vmem] * 3,
        out_shape=[
            pltpu.VMEM((chains, owned, width), F32),
            pltpu.VMEM((chains, owned, width), F32),
            pltpu.VMEM((chains, 8, width), F32),
        ],
        scratch_shapes=[pltpu.VMEM((owned, HD), B16)] * 2,
        compiler_params=params(),
        cost_estimate=pl.CostEstimate(
            flops=4 * GROUP * tokens * HD * owned, bytes_accessed=8 * GROUP * tokens * owned,
            transcendentals=0,
        ),
        name="ahead",
    )(*args)


def attend_kernel(g, shards, *refs):
    refs = list(refs)

    def take(count):
        taken = refs[:count]
        del refs[:count]
        return taken

    (first_ref, rank_ref, qs_ref, qst_ref, dos_ref, dot_ref, bias_ref, cos_t_ref, sin_t_ref,
     ck_t_ref, cv_t_ref, cos_ref, sin_ref, ck_ref, cv_ref, kp_ref, vp_ref) = take(17)
    far = take(shards - 1)
    ahead = take(3)
    if g + 1 < KV:
        take(1)
    old_sums_ref = take(1)[0] if g else None
    old_send = take(shards - 1) if g else []
    if 0 < g < KV - 1:
        take(2)
    out_ref, gq_ref, sums_ref, own_ref = take(4)
    send = take(shards - 1)
    pack_ref = take(1)[0] if g + 2 < KV else None
    keys, values, keys_t, values_t, dk_acc, dv_acc = take(6)
    scratch = [take(3) for _ in range(GROUP // HEADS)]
    tokens = kp_ref.shape[0]
    slots = ck_ref.shape[0]
    owned = slots + tokens
    total = shards * owned
    known = owned
    first = first_ref[0]
    rank = rank_ref[0]
    mine = pl.ds(g * HD, HD)

    if pack_ref is not None:
        copy_chunk(pl.ds((g + 2) * HD, HD), (ck_ref, cv_ref, kp_ref, vp_ref), pack_ref)
    for s in range(shards):
        at = s * owned
        rows = pl.ds(s * tokens, tokens)
        if s == 0:
            sources = [ref[:, mine] for ref in (ck_ref, cv_ref, kp_ref, vp_ref)]
        else:
            sources = [
                far[s - 1][pl.ds(*part)] for part in
                ((0, slots), (slots, slots), (2 * slots, tokens), (2 * slots + tokens, tokens))
            ]
        k, v = slab_rows(g, sources[2:], bias_ref, cos_ref[rows, :], sin_ref[rows, :])
        for (natural, transposed), cache, own in zip(
            ((keys, keys_t), (values, values_t)), sources[:2], (k, v)
        ):
            if s:
                natural[pl.ds(at, slots)] = cache
                natural[pl.ds(at + slots, tokens)] = own
            transposed[:, pl.ds(at + slots, tokens)] = own.T
            if s:
                transposed[:, pl.ds(at, slots)] = cache.T
    keys_t[:, pl.ds(0, slots)] = ck_t_ref[mine, :]
    values_t[:, pl.ds(0, slots)] = cv_t_ref[mine, :]
    sums_ref[...] = jnp.zeros_like(sums_ref) if old_sums_ref is None else old_sums_ref[...]
    dk_acc[...] = jnp.zeros_like(dk_acc)
    dv_acc[...] = jnp.zeros_like(dv_acc)

    width = HEADS * tokens
    scale = HD ** -0.5
    blocks = range(0, total, tokens)

    class Chain:
        def __init__(self, index):
            self.index = g * (GROUP // HEADS) + index
            self.s, self.pb, self.ds = scratch[index]
            index = self.index
            self.rows = pl.ds(pl.multiple_of(index * width, width), width)
            self.place = pl.ds(pl.multiple_of(index * HD, HD), HD)
            self.ahead = [ref.at[self.index % len(scratch)] for ref in ahead]
            self.top = self.ahead[2][...]

        def scores(self):
            s = dot(keys[pl.ds(known, total - known), :], qst_ref[self.place, :], NN)
            for start in blocks[known // tokens:]:
                part = s[start - known:start - known + tokens]
                seen = allowed(start, part, first, rank, shards, slots, tokens)
                part = jnp.where(seen, part, NEG)
                self.s[pl.ds(start, tokens), :] = part
                self.top = jnp.maximum(self.top, fold(part, jnp.max))

        def exponents(self):
            top = jnp.max(self.top, axis=0, keepdims=True)
            weight = jnp.zeros((8, width), F32)
            for start in blocks:
                rows = pl.ds(start, tokens)
                s = (self.ahead[0] if start < known else self.s)[rows, :]
                e = jnp.exp2((s - top) * (scale * math.log2(math.e)))
                self.s[rows, :] = e
                weight = weight + fold(e, jnp.sum)
            self.inverse = 1.0 / jnp.sum(weight, axis=0, keepdims=True)

        def probs(self):
            for start in blocks:
                rows = pl.ds(start, tokens)
                p = self.s[rows, :] * self.inverse
                self.s[rows, :] = p
                self.pb[rows, :] = p.astype(B16)

        def output(self):
            self.o = dot(values_t[...], self.pb[...], NN).astype(B16)
            do = dot_ref[self.place, :].astype(F32)
            self.delta = jnp.sum(do * self.o.astype(F32), axis=0, keepdims=True)

        def heads(self):
            for i in range(HEADS):
                head = self.index * HEADS + i
                yield (
                    slice(i * tokens, (i + 1) * tokens),
                    pl.ds(pl.multiple_of((head - g * GROUP) * HD, HD), HD),
                    head,
                )

        def dprobs(self):
            rows = pl.ds(known, total - known)
            self.dp = dot(values[rows, :], dot_ref[self.place, :], NN)

        def dscores(self):
            for start in blocks:
                rows = pl.ds(start, tokens)
                if start < known:
                    part = self.ahead[1][rows, :]
                else:
                    part = self.dp[start - known:start - known + tokens]
                self.ds[rows, :] = (self.s[rows, :] * (part - self.delta)).astype(B16)

        def query_grad(self):
            self.dq = (dot(keys_t[...], self.ds[...], NN) * scale).astype(B16).astype(F32)

        def slab_grads(self):
            for s in range(shards):
                rows = pl.ds(s * owned + slots, tokens)
                place = pl.ds(s * tokens, tokens)
                dv_acc[place, :] += dot(self.pb[rows, :], dos_ref[self.rows, :], NN)
                dk_acc[place, :] += dot(self.ds[rows, :], qs_ref[self.rows, :], NN)

        def store(self):
            for part, cols, head in self.heads():
                out_ref[:, cols] = self.o[:, part].T
                x = self.dq[:, part]
                other = jnp.concatenate([x[HD // 2:], x[:HD // 2]], axis=0)
                x = (x * cos_t_ref[...] - other * sin_t_ref[...]).T
                gq_ref[:, cols] = x.astype(B16)
                sums_ref[pl.ds(head, 1), :] = jnp.sum(x, axis=0, keepdims=True)

    steps = [
        Chain.scores, Chain.exponents, Chain.dprobs, Chain.probs, Chain.output,
        Chain.dscores, Chain.query_grad, Chain.slab_grads, Chain.store,
    ]
    group = [Chain(i) for i in range(GROUP // HEADS)]
    for turn_of in range(len(steps) + len(group) - 1):
        for i, chain in reversed(list(enumerate(group))):
            if 0 <= turn_of - i < len(steps):
                steps[turn_of - i](chain)

    dk = dk_acc[...] * scale
    dv = dv_acc[...]
    gk = turn_back(dk, cos_ref[...], sin_ref[...])
    own_ref[0] = dk[:tokens]
    own_ref[1] = dv[:tokens]
    at = 2 * g
    for j in range(1, shards):
        block = slice(j * tokens, (j + 1) * tokens)
        send[j - 1][at] = dk[block].astype(B16)
        send[j - 1][at + 1] = dv[block].astype(B16)
        if g:
            send[j - 1][pl.ds(0, at)] = old_send[j - 1][...]
    sums_ref[pl.ds(HQ + g, 1), :] = jnp.sum(gk, axis=0, keepdims=True)
    sums_ref[pl.ds(HQ + KV + g, 1), :] = jnp.sum(dv, axis=0, keepdims=True)


def attend(
    g, shards, first, rank, prepared, cosine, sine, ck, cv, kp, vp, far, ahead, before
):
    tokens, slots = kp.shape[0], ck.shape[0]
    slab = shards * tokens
    total = slab + shards * slots
    smem = pl.BlockSpec(memory_space=pltpu.SMEM)
    vmem = pl.BlockSpec(memory_space=pltpu.VMEM)
    anywhere = pl.BlockSpec(memory_space=pl.ANY)
    wide = pl.BlockSpec((tokens, GROUP * HD), lambda i: (0, g))

    args = [first, rank]
    placed = [*prepared, cosine, sine, ck, cv, kp, vp, *far]
    placed += [*ahead[g], *[x[2] for x in ahead[g + 1:g + 2]]]
    aliases = {}
    if before is not None:
        out, gq, sums, send = before
        placed += [sums, *send]
    args += placed
    in_specs = [smem] * 2 + [vmem] * len(placed)
    last = g == KV - 1
    if before is not None and not last:
        aliases = {len(args): 0, len(args) + 1: 1}
        args += [out, gq]
        in_specs += [anywhere] * 2
    kept = pltpu.VMEM((tokens, GROUP * HD), B16) if last else pltpu.HBM((tokens, HQ * HD), B16)
    out_shape = [
        kept, kept,
        pltpu.VMEM((SUMS, HD), F32),
        pltpu.VMEM((2, tokens, HD), F32),
    ]
    out_specs = [vmem if last else wide] * 2 + [vmem, vmem]
    out_shape += [pltpu.VMEM((2 * g + 2, tokens, HD), B16)] * (shards - 1)
    out_specs += [vmem] * (shards - 1)
    if g + 2 < KV:
        out_shape.append(pltpu.VMEM((2 * (slots + tokens), HD), B16))
        out_specs.append(vmem)
    results = pl.pallas_call(
        functools.partial(attend_kernel, g, shards),
        grid=(1,),
        in_specs=in_specs,
        out_shape=out_shape,
        out_specs=out_specs,
        scratch_shapes=[
            pltpu.VMEM((total, HD), B16), pltpu.VMEM((total, HD), B16),
            pltpu.VMEM((HD, total), B16), pltpu.VMEM((HD, total), B16),
            pltpu.VMEM((slab, HD), F32), pltpu.VMEM((slab, HD), F32),
        ] + [
            pltpu.VMEM((total, HEADS * tokens), kind) for kind in (F32, B16, B16) * (GROUP // HEADS)
        ],
        input_output_aliases=aliases,
        compiler_params=params(),
        cost_estimate=pl.CostEstimate(
            flops=2 * GROUP * tokens * HD * (4 * total + 2 * slab),
            bytes_accessed=8 * tokens * GROUP * HD + 8 * total * HD,
            transcendentals=GROUP * tokens * total,
        ),
        name="attend",
    )(*args)
    out, gq, sums, own = results[:4]
    send = results[4:4 + shards - 1]
    return (out, gq, sums, send), own, results[4 + shards - 1:]


def finish_kernel(shards, *refs):
    cos_ref, sin_ref, *refs = refs
    owns, refs = refs[:KV], refs[KV:]
    backs, refs = refs[:shards - 1], refs[shards - 1:]
    out_part, gq_part, _, _, out_ref, gq_ref, gk_ref, gv_ref = refs
    out_ref[...] = out_part[...]
    gq_ref[...] = gq_part[...]
    tokens = gk_ref.shape[0]
    cosine, sine = cos_ref[pl.ds(0, tokens), :], sin_ref[pl.ds(0, tokens), :]
    for g in range(KV):
        dk, dv = owns[g][0], owns[g][1]
        for back in backs:
            dk = dk + back[2 * g].astype(F32)
            dv = dv + back[2 * g + 1].astype(F32)
        cols = pl.ds(g * HD, HD)
        gk_ref[:, cols] = turn_back(dk, cosine, sine).astype(B16)
        gv_ref[:, cols] = dv.astype(B16)


def finish(shards, cosine, sine, owns, backs, parts, out, gq):
    tokens = out.shape[0]
    args = [cosine, sine, *owns, *backs, *parts]
    wide = pl.BlockSpec((tokens, GROUP * HD), lambda i: (0, KV - 1))
    narrow = (tokens, KV * HD)
    return pl.pallas_call(
        functools.partial(finish_kernel, shards),
        grid=(1,),
        in_specs=[pl.BlockSpec(memory_space=pltpu.VMEM)] * len(args)
        + [pl.BlockSpec(memory_space=pl.ANY)] * 2,
        out_specs=[wide, wide, whole(narrow), whole(narrow)],
        out_shape=[pltpu.HBM(out.shape, B16)] * 2 + [pltpu.HBM(narrow, B16)] * 2,
        input_output_aliases={len(args): 0, len(args) + 1: 1},
        compiler_params=params(),
        cost_estimate=pl.CostEstimate(flops=0, bytes_accessed=1 << 21, transcendentals=0),
        name="finish",
    )(*args, out, gq)


def sums_kernel(*refs):
    sums, parts = refs[:-4], refs[-3:]
    start = 0
    for part in parts:
        rows = pl.ds(start, part.shape[0])
        part[...] = add_up([ref[rows, :] for ref in sums])
        start += part.shape[0]


def last_sums(sums, after):
    shapes = [(rows, HD) for rows in (HQ, KV, KV)]
    return pl.pallas_call(
        sums_kernel,
        grid=(1,),
        in_specs=[pl.BlockSpec(memory_space=pltpu.VMEM)] * len(sums)
        + [pl.BlockSpec(memory_space=pl.ANY)],
        out_specs=[whole(shape) for shape in shapes],
        out_shape=[pltpu.HBM(shape, F32) for shape in shapes],
        compiler_params=params(),
        cost_estimate=pl.CostEstimate(flops=0, bytes_accessed=1 << 17, transcendentals=0),
        name="sums",
    )(*sums, after)


def add_up(parts):
    while len(parts) > 1:
        parts = [a + b for a, b in zip(parts[::2], parts[1::2])]
    return parts[0]


def join_kernel(count, *refs):
    refs[-1][...] = add_up([ref[...] for ref in refs[:count]])


def join(parts, held):
    args = [*parts, *held]
    return pl.pallas_call(
        functools.partial(join_kernel, len(parts)),
        grid=(1,),
        in_specs=[pl.BlockSpec(memory_space=pltpu.VMEM)] * len(args),
        out_specs=pl.BlockSpec(memory_space=pltpu.VMEM),
        out_shape=pltpu.VMEM(parts[0].shape, parts[0].dtype),
        compiler_params=params(),
        cost_estimate=pl.CostEstimate(flops=0, bytes_accessed=1 << 16, transcendentals=0),
        name="join",
    )(*args)


def sum_but_last(x, axes, near, held):
    devices = lax.axis_size(axes)
    bits = [1 << i for i in reversed(range(devices.bit_length() - 1)) if 1 << i != near]
    stages = [[near]] + [bits[i:i + 2] for i in range(0, len(bits), 2)]
    parts = [x]
    for i, stage in enumerate(stages):
        x = join(parts, held) if i == 2 else add_up(parts)
        parts = [x]
        for flip in [sum(c) for n in (1, 2) for c in itertools.combinations(stage, n)]:
            parts.append(lax.ppermute(x, axes, [(i, i ^ flip) for i in range(devices)]))
    return parts


def body(q_proj, k_proj, v_proj, cache_k, cache_v, bias_q, bias_k, bias_v, start, dout):
    shards = lax.axis_size("seq")
    rank = lax.axis_index("seq").astype(jnp.int32)
    tokens = q_proj.shape[1]
    shifts = range(1, shards)

    def ring(x, s):
        return lax.ppermute(x, "seq", [(i, (i + s) % shards) for i in range(shards)])

    def earlier(x, s):
        return lax.ppermute(x, "seq", [(i + s, i) for i in range(shards - s)])

    hbm = functools.partial(pltpu.with_memory_space_constraint, memory_space=pltpu.HBM)
    own = [hbm(x[0]) for x in (cache_k, cache_v, k_proj, v_proj)]
    chunk = pack(own)
    far = [[ring(chunk, s) for s in shifts]]

    owners = lax.rem(rank - jnp.arange(shards, dtype=jnp.int32) + shards, shards)
    positions = start[0] + owners[:, None] * tokens + jnp.arange(tokens, dtype=jnp.int32)[None]
    lane = jnp.arange(HD, dtype=jnp.int32)
    freqs = jnp.exp(
        -(2.0 * (lane % (HD // 2)).astype(F32) / HD) * jnp.log(jnp.float32(1000000.0))
    )
    angles = positions.reshape(-1).astype(F32)[:, None] * freqs[None, :]
    cosine = jnp.cos(angles)
    sine = jnp.sin(angles) * jnp.where(lane < HD // 2, -1.0, 1.0).astype(F32)[None]

    *prepared, ck, cv, kp, vp, chunk = prep(
        hbm(q_proj[0]), hbm(dout[0]), hbm(bias_q.reshape(HQ, HD)),
        hbm(bias_k.reshape(KV, HD)), hbm(bias_v.reshape(KV, HD)), cosine, sine, own,
    )
    far.append([ring(chunk, s) for s in shifts])
    qst, dot_t, bias = prepared[1], prepared[3], prepared[4]
    ahead = [
        look_ahead(
            g, shards, start, rank.reshape(1), qst, dot_t, bias, cosine, sine, ck, cv, kp, vp
        )
        for g in range(KV)
    ]
    before, owns = None, []
    for g in range(KV):
        before, own, more = attend(
            g, shards, start, rank.reshape(1), prepared, cosine, sine, ck, cv, kp, vp,
            far[g], ahead, before,
        )
        if g == KV - 2:
            out, gq = before[:2]
        owns.append(own)
        far += [[ring(chunk, s) for s in shifts] for chunk in more]
    *columns, sums, send = before
    backs = [earlier(x, s) for s, x in zip(shifts, send)]
    sums = sum_but_last(sums, ("dp", "seq"), shards, backs)
    out, gq, gk, gv = finish(shards, cosine, sine, owns, backs, columns, out, gq)
    sums = last_sums(sums, hbm(gk))
    return (out[None], gq[None], gk[None], gv[None], *[x.reshape(-1) for x in sums])


def solution(mesh):
    split = P("dp", "seq", None)
    return jax.shard_map(
        body,
        mesh=mesh,
        in_specs=(split,) * 5 + (P(), P(), P(), P("dp"), split),
        out_specs=(split,) * 4 + (P(), P(), P()),
        check_vma=False,
    )
```

```python
import functools
import itertools
import math

import jax
import jax.numpy as jnp
from jax import lax
from jax.experimental import pallas as pl
from jax.experimental.pallas import tpu as pltpu
from jax.sharding import PartitionSpec as P

HQ = 32
KV = 4
HD = 128
GROUP = 8
HEADS = 4
NEG = -1e30
SUMS = HQ + 2 * KV
VMEM = 28 * 1024 * 1024
F32, B16 = jnp.float32, jnp.bfloat16


def turn(x):
    return pltpu.roll(x, HD // 2, 1)


def dot(a, b, dims):
    return lax.dot_general(a, b, (dims, ((), ())), preferred_element_type=F32)


NN = ((1,), (0,))


def whole(shape):
    return pl.BlockSpec(shape, lambda i: (0,) * len(shape))


def column(rows, g):
    return pl.BlockSpec((rows, HD), lambda i: (0, g))


def params():
    return pltpu.CompilerParams(dimension_semantics=("arbitrary",), vmem_limit_bytes=VMEM)


def copy_chunk(cols, sources, out_ref):
    start = 0
    for ref in sources:
        rows = ref.shape[0]
        out_ref[pl.ds(start, rows)] = ref[:, cols]
        start += rows


def pack_kernel(*refs):
    copy_chunk(pl.ds(0, HD), refs[:-1], refs[-1])


def pack(sources):
    rows = sum(x.shape[0] for x in sources)
    return pl.pallas_call(
        pack_kernel,
        grid=(1,),
        in_specs=[column(x.shape[0], 0) for x in sources],
        out_specs=pl.BlockSpec(memory_space=pltpu.VMEM),
        out_shape=pltpu.VMEM((rows, HD), B16),
        compiler_params=params(),
        cost_estimate=pl.CostEstimate(flops=0, bytes_accessed=4 * rows * HD, transcendentals=0),
        name="pack",
    )(*sources)


def turn_back(x, cosine, sine):
    return x * cosine - turn(x) * sine


def prep_kernel(
    q_ref, do_ref, bq_ref, bk_ref, bv_ref, cos_ref, sin_ref, ck_ref, cv_ref, kp_ref, vp_ref,
    qs_ref, qst_ref, dos_ref, dot_ref, bias_ref, cos_t_ref, sin_t_ref, ck_t_ref, cv_t_ref,
    ck_out, cv_out, kp_out, vp_out, pack_ref,
):
    g = pl.program_id(0)
    tokens = q_ref.shape[0]
    cosine, sine = cos_ref[pl.ds(0, tokens), :], sin_ref[pl.ds(0, tokens), :]
    bias_q = bq_ref[...].astype(F32)
    own = (ck_ref, cv_ref, kp_ref, vp_ref)

    @pl.when(g == 0)
    def _():
        bias_ref[pl.ds(0, KV), :] = bk_ref[...].astype(F32)
        bias_ref[pl.ds(KV, KV), :] = bv_ref[...].astype(F32)
        cos_t_ref[...] = cosine.T
        sin_t_ref[...] = sine.T

    @pl.when(g == 1)
    def _():
        copy_chunk(pl.ds(0, HD), own, pack_ref)

    for h in range(GROUP):
        cols = pl.ds(h * HD, HD)
        rows = pl.ds(pl.multiple_of((g * GROUP + h) * tokens, tokens), tokens)
        x = q_ref[:, cols].astype(F32) + bias_q[h:h + 1]
        x = (x * cosine + turn(x) * sine).astype(B16)
        qs_ref[rows, :] = x
        do = do_ref[:, cols]
        dos_ref[rows, :] = do
        chain, part = h // HEADS, h % HEADS
        place = pl.ds(pl.multiple_of((g * (GROUP // HEADS) + chain) * HD, HD), HD)
        qst_ref[place, pl.ds(part * tokens, tokens)] = x.T
        dot_ref[place, pl.ds(part * tokens, tokens)] = do.T
    mine = pl.ds(pl.multiple_of(g * HD, HD), HD)
    ck_t_ref[mine, :] = ck_ref[...].T
    cv_t_ref[mine, :] = cv_ref[...].T
    for ref, out in zip(own, (ck_out, cv_out, kp_out, vp_out)):
        out[:, mine] = ref[...]


def prep(q, do, bq, bk, bv, cosine, sine, own):
    tokens, slots = q.shape[0], own[0].shape[0]
    vmem = pl.BlockSpec(memory_space=pltpu.VMEM)
    wide = pl.BlockSpec((tokens, GROUP * HD), lambda i: (0, i))
    stacked = pltpu.VMEM((HQ * tokens, HD), B16)
    turned = pltpu.VMEM((HQ // HEADS * HD, HEADS * tokens), B16)
    out_shape = [
        stacked, turned, stacked, turned,
        pltpu.VMEM((2 * KV, HD), F32),
        pltpu.VMEM((HD, tokens), F32),
        pltpu.VMEM((HD, tokens), F32),
        pltpu.VMEM((KV * HD, slots), B16),
        pltpu.VMEM((KV * HD, slots), B16),
        *[pltpu.VMEM(x.shape, B16) for x in own],
        pltpu.VMEM((2 * (slots + tokens), HD), B16),
    ]
    return pl.pallas_call(
        prep_kernel,
        grid=(KV,),
        in_specs=[
            wide, wide, pl.BlockSpec((GROUP, HD), lambda i: (i, 0)),
            whole((KV, HD)), whole((KV, HD)), vmem, vmem,
            *[pl.BlockSpec((x.shape[0], HD), lambda i: (0, i)) for x in own],
        ],
        out_specs=[vmem] * len(out_shape),
        out_shape=out_shape,
        compiler_params=params(),
        cost_estimate=pl.CostEstimate(
            flops=4 * tokens * HQ * HD, bytes_accessed=12 * tokens * HQ * HD, transcendentals=0
        ),
        name="prep",
    )(q, do, bq, bk, bv, cosine, sine, *own)


def fold(x, op):
    return op(x.reshape(x.shape[0] // 8, 8, x.shape[1]), axis=0)


def allowed(start, s, first, rank, shards, slots, tokens):
    shift, at = divmod(start, slots + tokens)
    row = lax.broadcasted_iota(jnp.int32, s.shape, 0)
    if at < slots:
        owner = lax.rem(rank - shift + shards, shards)
        return row < first - owner * slots - at
    if shift == 0:
        return row <= (lax.broadcasted_iota(jnp.int32, s.shape, 1) & (tokens - 1))
    return row < jnp.where(rank >= shift, tokens, 0)


def slab_rows(g, sources, bias_ref, cosine, sine):
    kp, vp = sources
    k = kp.astype(F32) + bias_ref[g:g + 1, :]
    v = vp.astype(F32) + bias_ref[KV + g:KV + g + 1, :]
    return (k * cosine + turn(k) * sine).astype(B16), v.astype(B16)


def ahead_kernel(
    g, shards, first_ref, rank_ref, qst_ref, dot_ref, bias_ref, cos_ref, sin_ref,
    ck_ref, cv_ref, kp_ref, vp_ref, s_ref, dp_ref, top_ref, keys, values,
):
    tokens, slots, width = kp_ref.shape[0], ck_ref.shape[0], qst_ref.shape[1]
    owned = slots + tokens
    mine = pl.ds(g * HD, HD)
    rows = pl.ds(0, tokens)
    k, v = slab_rows(
        g, (kp_ref[:, mine], vp_ref[:, mine]), bias_ref, cos_ref[rows, :], sin_ref[rows, :]
    )
    keys[pl.ds(0, slots)] = ck_ref[:, mine]
    keys[pl.ds(slots, tokens)] = k
    values[pl.ds(0, slots)] = cv_ref[:, mine]
    values[pl.ds(slots, tokens)] = v
    for i in range(GROUP // HEADS):
        place = pl.ds((g * (GROUP // HEADS) + i) * HD, HD)
        s = dot(keys[...], qst_ref[place, :], NN)
        top = jnp.full((8, width), NEG, F32)
        for start in range(0, owned, tokens):
            part = s[start:start + tokens]
            seen = allowed(start, part, first_ref[0], rank_ref[0], shards, slots, tokens)
            part = jnp.where(seen, part, NEG)
            s_ref[i, pl.ds(start, tokens), :] = part
            top = jnp.maximum(top, fold(part, jnp.max))
        top_ref[i] = top
        dp_ref[i] = dot(values[...], dot_ref[place, :], NN)


def look_ahead(g, shards, first, rank, qst, dot_t, bias, cosine, sine, ck, cv, kp, vp):
    tokens, slots, width = kp.shape[0], ck.shape[0], qst.shape[1]
    owned = slots + tokens
    chains = GROUP // HEADS
    smem = pl.BlockSpec(memory_space=pltpu.SMEM)
    vmem = pl.BlockSpec(memory_space=pltpu.VMEM)
    args = [first, rank, qst, dot_t, bias, cosine, sine, ck, cv, kp, vp]
    return pl.pallas_call(
        functools.partial(ahead_kernel, g, shards),
        grid=(1,),
        in_specs=[smem] * 2 + [vmem] * (len(args) - 2),
        out_specs=[vmem] * 3,
        out_shape=[
            pltpu.VMEM((chains, owned, width), F32),
            pltpu.VMEM((chains, owned, width), F32),
            pltpu.VMEM((chains, 8, width), F32),
        ],
        scratch_shapes=[pltpu.VMEM((owned, HD), B16)] * 2,
        compiler_params=params(),
        cost_estimate=pl.CostEstimate(
            flops=4 * GROUP * tokens * HD * owned, bytes_accessed=8 * GROUP * tokens * owned,
            transcendentals=0,
        ),
        name="ahead",
    )(*args)


def attend_kernel(g, shards, *refs):
    refs = list(refs)

    def take(count):
        taken = refs[:count]
        del refs[:count]
        return taken

    (first_ref, rank_ref, qs_ref, qst_ref, dos_ref, dot_ref, bias_ref, cos_t_ref, sin_t_ref,
     ck_t_ref, cv_t_ref, cos_ref, sin_ref, ck_ref, cv_ref, kp_ref, vp_ref) = take(17)
    far = take(shards - 1)
    ahead = take(3)
    if g + 1 < KV:
        take(1)
    old_sums_ref = take(1)[0] if g else None
    old_send = take(shards - 1) if g else []
    if 0 < g < KV - 1:
        take(2)
    out_ref, gq_ref, sums_ref, own_ref = take(4)
    send = take(shards - 1)
    pack_ref = take(1)[0] if g + 2 < KV else None
    keys, values, keys_t, values_t, dk_acc, dv_acc = take(6)
    scratch = [take(3) for _ in range(GROUP // HEADS)]
    tokens = kp_ref.shape[0]
    slots = ck_ref.shape[0]
    owned = slots + tokens
    total = shards * owned
    known = owned
    first = first_ref[0]
    rank = rank_ref[0]
    mine = pl.ds(g * HD, HD)

    if pack_ref is not None:
        copy_chunk(pl.ds((g + 2) * HD, HD), (ck_ref, cv_ref, kp_ref, vp_ref), pack_ref)
    for s in range(shards):
        at = s * owned
        rows = pl.ds(s * tokens, tokens)
        if s == 0:
            sources = [ref[:, mine] for ref in (ck_ref, cv_ref, kp_ref, vp_ref)]
        else:
            sources = [
                far[s - 1][pl.ds(*part)] for part in
                ((0, slots), (slots, slots), (2 * slots, tokens), (2 * slots + tokens, tokens))
            ]
        k, v = slab_rows(g, sources[2:], bias_ref, cos_ref[rows, :], sin_ref[rows, :])
        for (natural, transposed), cache, own in zip(
            ((keys, keys_t), (values, values_t)), sources[:2], (k, v)
        ):
            if s:
                natural[pl.ds(at, slots)] = cache
                natural[pl.ds(at + slots, tokens)] = own
            transposed[:, pl.ds(at + slots, tokens)] = own.T
            if s:
                transposed[:, pl.ds(at, slots)] = cache.T
    keys_t[:, pl.ds(0, slots)] = ck_t_ref[mine, :]
    values_t[:, pl.ds(0, slots)] = cv_t_ref[mine, :]
    sums_ref[...] = jnp.zeros_like(sums_ref) if old_sums_ref is None else old_sums_ref[...]
    dk_acc[...] = jnp.zeros_like(dk_acc)
    dv_acc[...] = jnp.zeros_like(dv_acc)

    width = HEADS * tokens
    scale = HD ** -0.5
    blocks = range(0, total, tokens)

    class Chain:
        def __init__(self, index):
            self.index = g * (GROUP // HEADS) + index
            self.s, self.pb, self.ds = scratch[index]
            index = self.index
            self.rows = pl.ds(pl.multiple_of(index * width, width), width)
            self.place = pl.ds(pl.multiple_of(index * HD, HD), HD)
            self.ahead = [ref.at[self.index % len(scratch)] for ref in ahead]
            self.top = self.ahead[2][...]

        def scores(self):
            s = dot(keys[pl.ds(known, total - known), :], qst_ref[self.place, :], NN)
            for start in blocks[known // tokens:]:
                part = s[start - known:start - known + tokens]
                seen = allowed(start, part, first, rank, shards, slots, tokens)
                part = jnp.where(seen, part, NEG)
                self.s[pl.ds(start, tokens), :] = part
                self.top = jnp.maximum(self.top, fold(part, jnp.max))

        def exponents(self):
            top = jnp.max(self.top, axis=0, keepdims=True)
            weight = jnp.zeros((8, width), F32)
            for start in blocks:
                rows = pl.ds(start, tokens)
                s = (self.ahead[0] if start < known else self.s)[rows, :]
                e = jnp.exp2((s - top) * (scale * math.log2(math.e)))
                self.s[rows, :] = e
                weight = weight + fold(e, jnp.sum)
            self.inverse = 1.0 / jnp.sum(weight, axis=0, keepdims=True)

        def probs(self):
            for start in blocks:
                rows = pl.ds(start, tokens)
                p = self.s[rows, :] * self.inverse
                self.s[rows, :] = p
                self.pb[rows, :] = p.astype(B16)

        def output(self):
            self.o = dot(values_t[...], self.pb[...], NN).astype(B16)
            do = dot_ref[self.place, :].astype(F32)
            self.delta = jnp.sum(do * self.o.astype(F32), axis=0, keepdims=True)

        def heads(self):
            for i in range(HEADS):
                head = self.index * HEADS + i
                yield (
                    slice(i * tokens, (i + 1) * tokens),
                    pl.ds(pl.multiple_of((head - g * GROUP) * HD, HD), HD),
                    head,
                )

        def dprobs(self):
            rows = pl.ds(known, total - known)
            self.dp = dot(values[rows, :], dot_ref[self.place, :], NN)

        def dscores(self):
            for start in blocks:
                rows = pl.ds(start, tokens)
                if start < known:
                    part = self.ahead[1][rows, :]
                else:
                    part = self.dp[start - known:start - known + tokens]
                self.ds[rows, :] = (self.s[rows, :] * (part - self.delta)).astype(B16)

        def query_grad(self):
            self.dq = (dot(keys_t[...], self.ds[...], NN) * scale).astype(B16).astype(F32)

        def slab_grads(self):
            for s in range(shards):
                rows = pl.ds(s * owned + slots, tokens)
                place = pl.ds(s * tokens, tokens)
                dv_acc[place, :] += dot(self.pb[rows, :], dos_ref[self.rows, :], NN)
                dk_acc[place, :] += dot(self.ds[rows, :], qs_ref[self.rows, :], NN)

        def store(self):
            for part, cols, head in self.heads():
                out_ref[:, cols] = self.o[:, part].T
                x = self.dq[:, part]
                other = jnp.concatenate([x[HD // 2:], x[:HD // 2]], axis=0)
                x = (x * cos_t_ref[...] - other * sin_t_ref[...]).T
                gq_ref[:, cols] = x.astype(B16)
                sums_ref[pl.ds(head, 1), :] = jnp.sum(x, axis=0, keepdims=True)

    steps = [
        Chain.scores, Chain.exponents, Chain.dprobs, Chain.probs, Chain.output,
        Chain.dscores, Chain.query_grad, Chain.slab_grads, Chain.store,
    ]
    group = [Chain(i) for i in range(GROUP // HEADS)]
    for turn_of in range(len(steps) + len(group) - 1):
        for i, chain in reversed(list(enumerate(group))):
            if 0 <= turn_of - i < len(steps):
                steps[turn_of - i](chain)

    dk = dk_acc[...] * scale
    dv = dv_acc[...]
    gk = turn_back(dk, cos_ref[...], sin_ref[...])
    own_ref[0] = dk[:tokens]
    own_ref[1] = dv[:tokens]
    at = 2 * g
    for j in range(1, shards):
        block = slice(j * tokens, (j + 1) * tokens)
        send[j - 1][at] = dk[block].astype(B16)
        send[j - 1][at + 1] = dv[block].astype(B16)
        if g:
            send[j - 1][pl.ds(0, at)] = old_send[j - 1][...]
    sums_ref[pl.ds(HQ + g, 1), :] = jnp.sum(gk, axis=0, keepdims=True)
    sums_ref[pl.ds(HQ + KV + g, 1), :] = jnp.sum(dv, axis=0, keepdims=True)


def attend(
    g, shards, first, rank, prepared, cosine, sine, ck, cv, kp, vp, far, ahead, before
):
    tokens, slots = kp.shape[0], ck.shape[0]
    slab = shards * tokens
    total = slab + shards * slots
    smem = pl.BlockSpec(memory_space=pltpu.SMEM)
    vmem = pl.BlockSpec(memory_space=pltpu.VMEM)
    anywhere = pl.BlockSpec(memory_space=pl.ANY)
    wide = pl.BlockSpec((tokens, GROUP * HD), lambda i: (0, g))

    args = [first, rank]
    placed = [*prepared, cosine, sine, ck, cv, kp, vp, *far]
    placed += [*ahead[g], *[x[2] for x in ahead[g + 1:g + 2]]]
    aliases = {}
    if before is not None:
        out, gq, sums, send = before
        placed += [sums, *send]
    args += placed
    in_specs = [smem] * 2 + [vmem] * len(placed)
    last = g == KV - 1
    if before is not None and not last:
        aliases = {len(args): 0, len(args) + 1: 1}
        args += [out, gq]
        in_specs += [anywhere] * 2
    kept = pltpu.VMEM((tokens, GROUP * HD), B16) if last else pltpu.HBM((tokens, HQ * HD), B16)
    out_shape = [
        kept, kept,
        pltpu.VMEM((SUMS, HD), F32),
        pltpu.VMEM((2, tokens, HD), F32),
    ]
    out_specs = [vmem if last else wide] * 2 + [vmem, vmem]
    out_shape += [pltpu.VMEM((2 * g + 2, tokens, HD), B16)] * (shards - 1)
    out_specs += [vmem] * (shards - 1)
    if g + 2 < KV:
        out_shape.append(pltpu.VMEM((2 * (slots + tokens), HD), B16))
        out_specs.append(vmem)
    results = pl.pallas_call(
        functools.partial(attend_kernel, g, shards),
        grid=(1,),
        in_specs=in_specs,
        out_shape=out_shape,
        out_specs=out_specs,
        scratch_shapes=[
            pltpu.VMEM((total, HD), B16), pltpu.VMEM((total, HD), B16),
            pltpu.VMEM((HD, total), B16), pltpu.VMEM((HD, total), B16),
            pltpu.VMEM((slab, HD), F32), pltpu.VMEM((slab, HD), F32),
        ] + [
            pltpu.VMEM((total, HEADS * tokens), kind) for kind in (F32, B16, B16) * (GROUP // HEADS)
        ],
        input_output_aliases=aliases,
        compiler_params=params(),
        cost_estimate=pl.CostEstimate(
            flops=2 * GROUP * tokens * HD * (4 * total + 2 * slab),
            bytes_accessed=8 * tokens * GROUP * HD + 8 * total * HD,
            transcendentals=GROUP * tokens * total,
        ),
        name="attend",
    )(*args)
    out, gq, sums, own = results[:4]
    send = results[4:4 + shards - 1]
    return (out, gq, sums, send), own, results[4 + shards - 1:]


def finish_kernel(shards, *refs):
    cos_ref, sin_ref, *refs = refs
    owns, refs = refs[:KV], refs[KV:]
    backs, refs = refs[:shards - 1], refs[shards - 1:]
    out_part, gq_part, _, _, out_ref, gq_ref, gk_ref, gv_ref = refs
    out_ref[...] = out_part[...]
    gq_ref[...] = gq_part[...]
    tokens = gk_ref.shape[0]
    cosine, sine = cos_ref[pl.ds(0, tokens), :], sin_ref[pl.ds(0, tokens), :]
    for g in range(KV):
        dk, dv = owns[g][0], owns[g][1]
        for back in backs:
            dk = dk + back[2 * g].astype(F32)
            dv = dv + back[2 * g + 1].astype(F32)
        cols = pl.ds(g * HD, HD)
        gk_ref[:, cols] = turn_back(dk, cosine, sine).astype(B16)
        gv_ref[:, cols] = dv.astype(B16)


def finish(shards, cosine, sine, owns, backs, parts, out, gq):
    tokens = out.shape[0]
    args = [cosine, sine, *owns, *backs, *parts]
    wide = pl.BlockSpec((tokens, GROUP * HD), lambda i: (0, KV - 1))
    narrow = (tokens, KV * HD)
    return pl.pallas_call(
        functools.partial(finish_kernel, shards),
        grid=(1,),
        in_specs=[pl.BlockSpec(memory_space=pltpu.VMEM)] * len(args)
        + [pl.BlockSpec(memory_space=pl.ANY)] * 2,
        out_specs=[wide, wide, whole(narrow), whole(narrow)],
        out_shape=[pltpu.HBM(out.shape, B16)] * 2 + [pltpu.HBM(narrow, B16)] * 2,
        input_output_aliases={len(args): 0, len(args) + 1: 1},
        compiler_params=params(),
        cost_estimate=pl.CostEstimate(flops=0, bytes_accessed=1 << 21, transcendentals=0),
        name="finish",
    )(*args, out, gq)


def sums_kernel(*refs):
    sums, parts = refs[:-4], refs[-3:]
    start = 0
    for part in parts:
        rows = pl.ds(start, part.shape[0])
        part[...] = add_up([ref[rows, :] for ref in sums])
        start += part.shape[0]


def last_sums(sums, after):
    shapes = [(rows, HD) for rows in (HQ, KV, KV)]
    return pl.pallas_call(
        sums_kernel,
        grid=(1,),
        in_specs=[pl.BlockSpec(memory_space=pltpu.VMEM)] * len(sums)
        + [pl.BlockSpec(memory_space=pl.ANY)],
        out_specs=[whole(shape) for shape in shapes],
        out_shape=[pltpu.HBM(shape, F32) for shape in shapes],
        compiler_params=params(),
        cost_estimate=pl.CostEstimate(flops=0, bytes_accessed=1 << 17, transcendentals=0),
        name="sums",
    )(*sums, after)


def add_up(parts):
    while len(parts) > 1:
        parts = [a + b for a, b in zip(parts[::2], parts[1::2])]
    return parts[0]


def sum_but_last(x, axes, near):
    devices = lax.axis_size(axes)
    bits = [1 << i for i in range(devices.bit_length() - 1) if 1 << i != near]
    stages = [[near]] + [bits[i:i + 2] for i in range(0, len(bits), 2)]
    parts = [x]
    for stage in stages:
        x = add_up(parts)
        parts = [x]
        for flip in [sum(c) for n in (1, 2) for c in itertools.combinations(stage, n)]:
            parts.append(lax.ppermute(x, axes, [(i, i ^ flip) for i in range(devices)]))
    return parts


def body(q_proj, k_proj, v_proj, cache_k, cache_v, bias_q, bias_k, bias_v, start, dout):
    shards = lax.axis_size("seq")
    rank = lax.axis_index("seq").astype(jnp.int32)
    tokens = q_proj.shape[1]
    shifts = range(1, shards)

    def ring(x, s):
        return lax.ppermute(x, "seq", [(i, (i + s) % shards) for i in range(shards)])

    def earlier(x, s):
        return lax.ppermute(x, "seq", [(i + s, i) for i in range(shards - s)])

    hbm = functools.partial(pltpu.with_memory_space_constraint, memory_space=pltpu.HBM)
    own = [hbm(x[0]) for x in (cache_k, cache_v, k_proj, v_proj)]
    chunk = pack(own)
    far = [[ring(chunk, s) for s in shifts]]

    owners = lax.rem(rank - jnp.arange(shards, dtype=jnp.int32) + shards, shards)
    positions = start[0] + owners[:, None] * tokens + jnp.arange(tokens, dtype=jnp.int32)[None]
    lane = jnp.arange(HD, dtype=jnp.int32)
    freqs = jnp.exp(
        -(2.0 * (lane % (HD // 2)).astype(F32) / HD) * jnp.log(jnp.float32(1000000.0))
    )
    angles = positions.reshape(-1).astype(F32)[:, None] * freqs[None, :]
    cosine = jnp.cos(angles)
    sine = jnp.sin(angles) * jnp.where(lane < HD // 2, -1.0, 1.0).astype(F32)[None]

    *prepared, ck, cv, kp, vp, chunk = prep(
        hbm(q_proj[0]), hbm(dout[0]), hbm(bias_q.reshape(HQ, HD)),
        hbm(bias_k.reshape(KV, HD)), hbm(bias_v.reshape(KV, HD)), cosine, sine, own,
    )
    far.append([ring(chunk, s) for s in shifts])
    qst, dot_t, bias = prepared[1], prepared[3], prepared[4]
    ahead = [
        look_ahead(
            g, shards, start, rank.reshape(1), qst, dot_t, bias, cosine, sine, ck, cv, kp, vp
        )
        for g in range(KV)
    ]
    before, owns = None, []
    for g in range(KV):
        before, own, more = attend(
            g, shards, start, rank.reshape(1), prepared, cosine, sine, ck, cv, kp, vp,
            far[g], ahead, before,
        )
        if g == KV - 2:
            out, gq = before[:2]
        owns.append(own)
        far += [[ring(chunk, s) for s in shifts] for chunk in more]
    *columns, sums, send = before
    backs = [earlier(x, s) for s, x in zip(shifts, send)]
    sums = sum_but_last(sums, ("dp", "seq"), shards)
    out, gq, gk, gv = finish(shards, cosine, sine, owns, backs, columns, out, gq)
    sums = last_sums(sums, hbm(gk))
    return (out[None], gq[None], gk[None], gv[None], *[x.reshape(-1) for x in sums])


def solution(mesh):
    split = P("dp", "seq", None)
    return jax.shard_map(
        body,
        mesh=mesh,
        in_specs=(split,) * 5 + (P(), P(), P(), P("dp"), split),
        out_specs=(split,) * 4 + (P(), P(), P()),
        check_vma=False,
    )
```

```python
import functools
import itertools
import math

import jax
import jax.numpy as jnp
from jax import lax
from jax.experimental import pallas as pl
from jax.experimental.pallas import tpu as pltpu
from jax.sharding import PartitionSpec as P

HQ = 32
KV = 4
HD = 128
GROUP = 8
HEADS = 4
NEG = -1e30
SUMS = HQ + 2 * KV
VMEM = 28 * 1024 * 1024
F32, B16 = jnp.float32, jnp.bfloat16


def turn(x):
    return pltpu.roll(x, HD // 2, 1)


def dot(a, b, dims):
    return lax.dot_general(a, b, (dims, ((), ())), preferred_element_type=F32)


NN = ((1,), (0,))


def whole(shape):
    return pl.BlockSpec(shape, lambda i: (0,) * len(shape))


def column(rows, g):
    return pl.BlockSpec((rows, HD), lambda i: (0, g))


def params():
    return pltpu.CompilerParams(dimension_semantics=("arbitrary",), vmem_limit_bytes=VMEM)


def copy_chunk(cols, sources, out_ref):
    start = 0
    for ref in sources:
        rows = ref.shape[0]
        out_ref[pl.ds(start, rows)] = ref[:, cols]
        start += rows


def pack_kernel(*refs):
    copy_chunk(pl.ds(0, HD), refs[:-1], refs[-1])


def pack(sources):
    rows = sum(x.shape[0] for x in sources)
    return pl.pallas_call(
        pack_kernel,
        grid=(1,),
        in_specs=[column(x.shape[0], 0) for x in sources],
        out_specs=pl.BlockSpec(memory_space=pltpu.VMEM),
        out_shape=pltpu.VMEM((rows, HD), B16),
        compiler_params=params(),
        cost_estimate=pl.CostEstimate(flops=0, bytes_accessed=4 * rows * HD, transcendentals=0),
        name="pack",
    )(*sources)


def turn_back(x, cosine, sine):
    return x * cosine - turn(x) * sine


def prep_kernel(
    q_ref, do_ref, bq_ref, bk_ref, bv_ref, cos_ref, sin_ref, ck_ref, cv_ref, kp_ref, vp_ref,
    qs_ref, qst_ref, dos_ref, dot_ref, bias_ref, cos_t_ref, sin_t_ref, ck_t_ref, cv_t_ref,
    ck_out, cv_out, kp_out, vp_out, pack_ref,
):
    g = pl.program_id(0)
    tokens = q_ref.shape[0]
    cosine, sine = cos_ref[pl.ds(0, tokens), :], sin_ref[pl.ds(0, tokens), :]
    bias_q = bq_ref[...].astype(F32)
    own = (ck_ref, cv_ref, kp_ref, vp_ref)

    @pl.when(g == 0)
    def _():
        bias_ref[pl.ds(0, KV), :] = bk_ref[...].astype(F32)
        bias_ref[pl.ds(KV, KV), :] = bv_ref[...].astype(F32)
        cos_t_ref[...] = cosine.T
        sin_t_ref[...] = sine.T

    @pl.when(g == 1)
    def _():
        copy_chunk(pl.ds(0, HD), own, pack_ref)

    for h in range(GROUP):
        cols = pl.ds(h * HD, HD)
        rows = pl.ds(pl.multiple_of((g * GROUP + h) * tokens, tokens), tokens)
        x = q_ref[:, cols].astype(F32) + bias_q[h:h + 1]
        x = (x * cosine + turn(x) * sine).astype(B16)
        qs_ref[rows, :] = x
        do = do_ref[:, cols]
        dos_ref[rows, :] = do
        chain, part = h // HEADS, h % HEADS
        place = pl.ds(pl.multiple_of((g * (GROUP // HEADS) + chain) * HD, HD), HD)
        qst_ref[place, pl.ds(part * tokens, tokens)] = x.T
        dot_ref[place, pl.ds(part * tokens, tokens)] = do.T
    mine = pl.ds(pl.multiple_of(g * HD, HD), HD)
    ck_t_ref[mine, :] = ck_ref[...].T
    cv_t_ref[mine, :] = cv_ref[...].T
    for ref, out in zip(own, (ck_out, cv_out, kp_out, vp_out)):
        out[:, mine] = ref[...]


def prep(q, do, bq, bk, bv, cosine, sine, own):
    tokens, slots = q.shape[0], own[0].shape[0]
    vmem = pl.BlockSpec(memory_space=pltpu.VMEM)
    wide = pl.BlockSpec((tokens, GROUP * HD), lambda i: (0, i))
    stacked = pltpu.VMEM((HQ * tokens, HD), B16)
    turned = pltpu.VMEM((HQ // HEADS * HD, HEADS * tokens), B16)
    out_shape = [
        stacked, turned, stacked, turned,
        pltpu.VMEM((2 * KV, HD), F32),
        pltpu.VMEM((HD, tokens), F32),
        pltpu.VMEM((HD, tokens), F32),
        pltpu.VMEM((KV * HD, slots), B16),
        pltpu.VMEM((KV * HD, slots), B16),
        *[pltpu.VMEM(x.shape, B16) for x in own],
        pltpu.VMEM((2 * (slots + tokens), HD), B16),
    ]
    return pl.pallas_call(
        prep_kernel,
        grid=(KV,),
        in_specs=[
            wide, wide, pl.BlockSpec((GROUP, HD), lambda i: (i, 0)),
            whole((KV, HD)), whole((KV, HD)), vmem, vmem,
            *[pl.BlockSpec((x.shape[0], HD), lambda i: (0, i)) for x in own],
        ],
        out_specs=[vmem] * len(out_shape),
        out_shape=out_shape,
        compiler_params=params(),
        cost_estimate=pl.CostEstimate(
            flops=4 * tokens * HQ * HD, bytes_accessed=12 * tokens * HQ * HD, transcendentals=0
        ),
        name="prep",
    )(q, do, bq, bk, bv, cosine, sine, *own)


def fold(x, op):
    return op(x.reshape(x.shape[0] // 8, 8, x.shape[1]), axis=0)


def allowed(start, s, first, rank, shards, slots, tokens):
    shift, at = divmod(start, slots + tokens)
    row = lax.broadcasted_iota(jnp.int32, s.shape, 0)
    if at < slots:
        owner = lax.rem(rank - shift + shards, shards)
        return row < first - owner * slots - at
    if shift == 0:
        return row <= (lax.broadcasted_iota(jnp.int32, s.shape, 1) & (tokens - 1))
    return row < jnp.where(rank >= shift, tokens, 0)


def slab_rows(g, sources, bias_ref, cosine, sine):
    kp, vp = sources
    k = kp.astype(F32) + bias_ref[g:g + 1, :]
    v = vp.astype(F32) + bias_ref[KV + g:KV + g + 1, :]
    return (k * cosine + turn(k) * sine).astype(B16), v.astype(B16)


def ahead_kernel(
    g, shards, first_ref, rank_ref, qst_ref, dot_ref, bias_ref, cos_ref, sin_ref,
    ck_ref, cv_ref, kp_ref, vp_ref, s_ref, dp_ref, top_ref, keys, values,
):
    tokens, slots, width = kp_ref.shape[0], ck_ref.shape[0], qst_ref.shape[1]
    owned = slots + tokens
    mine = pl.ds(g * HD, HD)
    rows = pl.ds(0, tokens)
    k, v = slab_rows(
        g, (kp_ref[:, mine], vp_ref[:, mine]), bias_ref, cos_ref[rows, :], sin_ref[rows, :]
    )
    keys[pl.ds(0, slots)] = ck_ref[:, mine]
    keys[pl.ds(slots, tokens)] = k
    values[pl.ds(0, slots)] = cv_ref[:, mine]
    values[pl.ds(slots, tokens)] = v
    for i in range(GROUP // HEADS):
        place = pl.ds((g * (GROUP // HEADS) + i) * HD, HD)
        s = dot(keys[...], qst_ref[place, :], NN)
        top = jnp.full((8, width), NEG, F32)
        for start in range(0, owned, tokens):
            part = s[start:start + tokens]
            seen = allowed(start, part, first_ref[0], rank_ref[0], shards, slots, tokens)
            part = jnp.where(seen, part, NEG)
            s_ref[i, pl.ds(start, tokens), :] = part
            top = jnp.maximum(top, fold(part, jnp.max))
        top_ref[i] = top
        dp_ref[i] = dot(values[...], dot_ref[place, :], NN)


def look_ahead(g, shards, first, rank, qst, dot_t, bias, cosine, sine, ck, cv, kp, vp):
    tokens, slots, width = kp.shape[0], ck.shape[0], qst.shape[1]
    owned = slots + tokens
    chains = GROUP // HEADS
    smem = pl.BlockSpec(memory_space=pltpu.SMEM)
    vmem = pl.BlockSpec(memory_space=pltpu.VMEM)
    args = [first, rank, qst, dot_t, bias, cosine, sine, ck, cv, kp, vp]
    return pl.pallas_call(
        functools.partial(ahead_kernel, g, shards),
        grid=(1,),
        in_specs=[smem] * 2 + [vmem] * (len(args) - 2),
        out_specs=[vmem] * 3,
        out_shape=[
            pltpu.VMEM((chains, owned, width), F32),
            pltpu.VMEM((chains, owned, width), F32),
            pltpu.VMEM((chains, 8, width), F32),
        ],
        scratch_shapes=[pltpu.VMEM((owned, HD), B16)] * 2,
        compiler_params=params(),
        cost_estimate=pl.CostEstimate(
            flops=4 * GROUP * tokens * HD * owned, bytes_accessed=8 * GROUP * tokens * owned,
            transcendentals=0,
        ),
        name="ahead",
    )(*args)


def attend_kernel(g, shards, *refs):
    refs = list(refs)

    def take(count):
        taken = refs[:count]
        del refs[:count]
        return taken

    (first_ref, rank_ref, qs_ref, qst_ref, dos_ref, dot_ref, bias_ref, cos_t_ref, sin_t_ref,
     ck_t_ref, cv_t_ref, cos_ref, sin_ref, ck_ref, cv_ref, kp_ref, vp_ref) = take(17)
    far = take(shards - 1)
    ahead = take(3)
    if g + 1 < KV:
        take(1)
    old_sums_ref = take(1)[0] if g else None
    old_send = take(shards - 1) if g else []
    if 0 < g < KV - 1:
        take(2)
    out_ref, gq_ref, sums_ref, own_ref = take(4)
    send = take(shards - 1)
    pack_ref = take(1)[0] if g + 2 < KV else None
    keys, values, keys_t, values_t, dk_acc, dv_acc = take(6)
    scratch = [take(3) for _ in range(GROUP // HEADS)]
    tokens = kp_ref.shape[0]
    slots = ck_ref.shape[0]
    owned = slots + tokens
    total = shards * owned
    known = owned
    first = first_ref[0]
    rank = rank_ref[0]
    mine = pl.ds(g * HD, HD)

    if pack_ref is not None:
        copy_chunk(pl.ds((g + 2) * HD, HD), (ck_ref, cv_ref, kp_ref, vp_ref), pack_ref)
    for s in range(shards):
        at = s * owned
        rows = pl.ds(s * tokens, tokens)
        if s == 0:
            sources = [ref[:, mine] for ref in (ck_ref, cv_ref, kp_ref, vp_ref)]
        else:
            sources = [
                far[s - 1][pl.ds(*part)] for part in
                ((0, slots), (slots, slots), (2 * slots, tokens), (2 * slots + tokens, tokens))
            ]
        k, v = slab_rows(g, sources[2:], bias_ref, cos_ref[rows, :], sin_ref[rows, :])
        for (natural, transposed), cache, own in zip(
            ((keys, keys_t), (values, values_t)), sources[:2], (k, v)
        ):
            if s:
                natural[pl.ds(at, slots)] = cache
                natural[pl.ds(at + slots, tokens)] = own
            transposed[:, pl.ds(at + slots, tokens)] = own.T
            if s:
                transposed[:, pl.ds(at, slots)] = cache.T
    keys_t[:, pl.ds(0, slots)] = ck_t_ref[mine, :]
    values_t[:, pl.ds(0, slots)] = cv_t_ref[mine, :]
    sums_ref[...] = jnp.zeros_like(sums_ref) if old_sums_ref is None else old_sums_ref[...]
    dk_acc[...] = jnp.zeros_like(dk_acc)
    dv_acc[...] = jnp.zeros_like(dv_acc)

    width = HEADS * tokens
    scale = HD ** -0.5
    blocks = range(0, total, tokens)

    class Chain:
        def __init__(self, index):
            self.index = g * (GROUP // HEADS) + index
            self.s, self.pb, self.ds = scratch[index]
            index = self.index
            self.rows = pl.ds(pl.multiple_of(index * width, width), width)
            self.place = pl.ds(pl.multiple_of(index * HD, HD), HD)
            self.ahead = [ref.at[self.index % len(scratch)] for ref in ahead]
            self.top = self.ahead[2][...]

        def scores(self):
            s = dot(keys[pl.ds(known, total - known), :], qst_ref[self.place, :], NN)
            for start in blocks[known // tokens:]:
                part = s[start - known:start - known + tokens]
                seen = allowed(start, part, first, rank, shards, slots, tokens)
                part = jnp.where(seen, part, NEG)
                self.s[pl.ds(start, tokens), :] = part
                self.top = jnp.maximum(self.top, fold(part, jnp.max))

        def exponents(self):
            top = jnp.max(self.top, axis=0, keepdims=True)
            weight = jnp.zeros((8, width), F32)
            for start in blocks:
                rows = pl.ds(start, tokens)
                s = (self.ahead[0] if start < known else self.s)[rows, :]
                e = jnp.exp2((s - top) * (scale * math.log2(math.e)))
                self.s[rows, :] = e
                weight = weight + fold(e, jnp.sum)
            self.inverse = 1.0 / jnp.sum(weight, axis=0, keepdims=True)

        def probs(self):
            for start in blocks:
                rows = pl.ds(start, tokens)
                p = self.s[rows, :] * self.inverse
                self.s[rows, :] = p
                self.pb[rows, :] = p.astype(B16)

        def output(self):
            self.o = dot(values_t[...], self.pb[...], NN).astype(B16)
            do = dot_ref[self.place, :].astype(F32)
            self.delta = jnp.sum(do * self.o.astype(F32), axis=0, keepdims=True)

        def heads(self):
            for i in range(HEADS):
                head = self.index * HEADS + i
                yield (
                    slice(i * tokens, (i + 1) * tokens),
                    pl.ds(pl.multiple_of((head - g * GROUP) * HD, HD), HD),
                    head,
                )

        def dprobs(self):
            rows = pl.ds(known, total - known)
            self.dp = dot(values[rows, :], dot_ref[self.place, :], NN)

        def dscores(self):
            for start in blocks:
                rows = pl.ds(start, tokens)
                if start < known:
                    part = self.ahead[1][rows, :]
                else:
                    part = self.dp[start - known:start - known + tokens]
                self.ds[rows, :] = (self.s[rows, :] * (part - self.delta)).astype(B16)

        def query_grad(self):
            self.dq = (dot(keys_t[...], self.ds[...], NN) * scale).astype(B16).astype(F32)

        def slab_grads(self):
            for s in range(shards):
                rows = pl.ds(s * owned + slots, tokens)
                place = pl.ds(s * tokens, tokens)
                dv_acc[place, :] += dot(self.pb[rows, :], dos_ref[self.rows, :], NN)
                dk_acc[place, :] += dot(self.ds[rows, :], qs_ref[self.rows, :], NN)

        def store(self):
            for part, cols, head in self.heads():
                out_ref[:, cols] = self.o[:, part].T
                x = self.dq[:, part]
                other = jnp.concatenate([x[HD // 2:], x[:HD // 2]], axis=0)
                x = (x * cos_t_ref[...] - other * sin_t_ref[...]).T
                gq_ref[:, cols] = x.astype(B16)
                sums_ref[pl.ds(head, 1), :] = jnp.sum(x, axis=0, keepdims=True)

    steps = [
        Chain.scores, Chain.exponents, Chain.dprobs, Chain.probs, Chain.output,
        Chain.dscores, Chain.query_grad, Chain.slab_grads, Chain.store,
    ]
    group = [Chain(i) for i in range(GROUP // HEADS)]
    for turn_of in range(len(steps) + len(group) - 1):
        for i, chain in reversed(list(enumerate(group))):
            if 0 <= turn_of - i < len(steps):
                steps[turn_of - i](chain)

    dk = dk_acc[...] * scale
    dv = dv_acc[...]
    gk = turn_back(dk, cos_ref[...], sin_ref[...])
    own_ref[0] = dk[:tokens]
    own_ref[1] = dv[:tokens]
    at = 2 * g
    for j in range(1, shards):
        block = slice(j * tokens, (j + 1) * tokens)
        send[j - 1][at] = dk[block].astype(B16)
        send[j - 1][at + 1] = dv[block].astype(B16)
        if g:
            send[j - 1][pl.ds(0, at)] = old_send[j - 1][...]
    sums_ref[pl.ds(HQ + g, 1), :] = jnp.sum(gk, axis=0, keepdims=True)
    sums_ref[pl.ds(HQ + KV + g, 1), :] = jnp.sum(dv, axis=0, keepdims=True)


def attend(
    g, shards, first, rank, prepared, cosine, sine, ck, cv, kp, vp, far, ahead, before
):
    tokens, slots = kp.shape[0], ck.shape[0]
    slab = shards * tokens
    total = slab + shards * slots
    smem = pl.BlockSpec(memory_space=pltpu.SMEM)
    vmem = pl.BlockSpec(memory_space=pltpu.VMEM)
    anywhere = pl.BlockSpec(memory_space=pl.ANY)
    wide = pl.BlockSpec((tokens, GROUP * HD), lambda i: (0, g))

    args = [first, rank]
    placed = [*prepared, cosine, sine, ck, cv, kp, vp, *far]
    placed += [*ahead[g], *[x[2] for x in ahead[g + 1:g + 2]]]
    aliases = {}
    if before is not None:
        out, gq, sums, send = before
        placed += [sums, *send]
    args += placed
    in_specs = [smem] * 2 + [vmem] * len(placed)
    last = g == KV - 1
    if before is not None and not last:
        aliases = {len(args): 0, len(args) + 1: 1}
        args += [out, gq]
        in_specs += [anywhere] * 2
    kept = pltpu.VMEM((tokens, GROUP * HD), B16) if last else pltpu.HBM((tokens, HQ * HD), B16)
    out_shape = [
        kept, kept,
        pltpu.VMEM((SUMS, HD), F32),
        pltpu.VMEM((2, tokens, HD), F32),
    ]
    out_specs = [vmem if last else wide] * 2 + [vmem, vmem]
    out_shape += [pltpu.VMEM((2 * g + 2, tokens, HD), B16)] * (shards - 1)
    out_specs += [vmem] * (shards - 1)
    if g + 2 < KV:
        out_shape.append(pltpu.VMEM((2 * (slots + tokens), HD), B16))
        out_specs.append(vmem)
    results = pl.pallas_call(
        functools.partial(attend_kernel, g, shards),
        grid=(1,),
        in_specs=in_specs,
        out_shape=out_shape,
        out_specs=out_specs,
        scratch_shapes=[
            pltpu.VMEM((total, HD), B16), pltpu.VMEM((total, HD), B16),
            pltpu.VMEM((HD, total), B16), pltpu.VMEM((HD, total), B16),
            pltpu.VMEM((slab, HD), F32), pltpu.VMEM((slab, HD), F32),
        ] + [
            pltpu.VMEM((total, HEADS * tokens), kind) for kind in (F32, B16, B16) * (GROUP // HEADS)
        ],
        input_output_aliases=aliases,
        compiler_params=params(),
        cost_estimate=pl.CostEstimate(
            flops=2 * GROUP * tokens * HD * (4 * total + 2 * slab),
            bytes_accessed=8 * tokens * GROUP * HD + 8 * total * HD,
            transcendentals=GROUP * tokens * total,
        ),
        name="attend",
    )(*args)
    out, gq, sums, own = results[:4]
    send = results[4:4 + shards - 1]
    return (out, gq, sums, send), own, results[4 + shards - 1:]


def finish_kernel(shards, *refs):
    cos_ref, sin_ref, *refs = refs
    owns, refs = refs[:KV], refs[KV:]
    backs, refs = refs[:shards - 1], refs[shards - 1:]
    out_part, gq_part, _, _, out_ref, gq_ref, gk_ref, gv_ref = refs
    out_ref[...] = out_part[...]
    gq_ref[...] = gq_part[...]
    tokens = gk_ref.shape[0]
    cosine, sine = cos_ref[pl.ds(0, tokens), :], sin_ref[pl.ds(0, tokens), :]
    for g in range(KV):
        dk, dv = owns[g][0], owns[g][1]
        for back in backs:
            dk = dk + back[2 * g].astype(F32)
            dv = dv + back[2 * g + 1].astype(F32)
        cols = pl.ds(g * HD, HD)
        gk_ref[:, cols] = turn_back(dk, cosine, sine).astype(B16)
        gv_ref[:, cols] = dv.astype(B16)


def finish(shards, cosine, sine, owns, backs, parts, out, gq):
    tokens = out.shape[0]
    args = [cosine, sine, *owns, *backs, *parts]
    wide = pl.BlockSpec((tokens, GROUP * HD), lambda i: (0, KV - 1))
    narrow = (tokens, KV * HD)
    return pl.pallas_call(
        functools.partial(finish_kernel, shards),
        grid=(1,),
        in_specs=[pl.BlockSpec(memory_space=pltpu.VMEM)] * len(args)
        + [pl.BlockSpec(memory_space=pl.ANY)] * 2,
        out_specs=[wide, wide, whole(narrow), whole(narrow)],
        out_shape=[pltpu.HBM(out.shape, B16)] * 2 + [pltpu.HBM(narrow, B16)] * 2,
        input_output_aliases={len(args): 0, len(args) + 1: 1},
        compiler_params=params(),
        cost_estimate=pl.CostEstimate(flops=0, bytes_accessed=1 << 21, transcendentals=0),
        name="finish",
    )(*args, out, gq)


def sums_kernel(*refs):
    sums, parts = refs[:-4], refs[-3:]
    start = 0
    for part in parts:
        rows = pl.ds(start, part.shape[0])
        part[...] = add_up([ref[rows, :] for ref in sums])
        start += part.shape[0]


def last_sums(sums, after):
    shapes = [(rows, HD) for rows in (HQ, KV, KV)]
    return pl.pallas_call(
        sums_kernel,
        grid=(1,),
        in_specs=[pl.BlockSpec(memory_space=pltpu.VMEM)] * len(sums)
        + [pl.BlockSpec(memory_space=pl.ANY)],
        out_specs=[whole(shape) for shape in shapes],
        out_shape=[pltpu.HBM(shape, F32) for shape in shapes],
        compiler_params=params(),
        cost_estimate=pl.CostEstimate(flops=0, bytes_accessed=1 << 17, transcendentals=0),
        name="sums",
    )(*sums, after)


def add_up(parts):
    while len(parts) > 1:
        parts = [a + b for a, b in zip(parts[::2], parts[1::2])]
    return parts[0]


def sum_but_last(x, axes, near):
    devices = lax.axis_size(axes)
    bits = [1 << i for i in range(devices.bit_length() - 1) if 1 << i != near]
    stages = [[near], bits[:2]] + [[bit] for bit in bits[2:]]
    parts = [x]
    for stage in stages:
        x = add_up(parts)
        parts = [x]
        for flip in [sum(c) for n in (1, 2) for c in itertools.combinations(stage, n)]:
            parts.append(lax.ppermute(x, axes, [(i, i ^ flip) for i in range(devices)]))
    return parts


def body(q_proj, k_proj, v_proj, cache_k, cache_v, bias_q, bias_k, bias_v, start, dout):
    shards = lax.axis_size("seq")
    rank = lax.axis_index("seq").astype(jnp.int32)
    tokens = q_proj.shape[1]
    shifts = range(1, shards)

    def ring(x, s):
        return lax.ppermute(x, "seq", [(i, (i + s) % shards) for i in range(shards)])

    def earlier(x, s):
        return lax.ppermute(x, "seq", [(i + s, i) for i in range(shards - s)])

    hbm = functools.partial(pltpu.with_memory_space_constraint, memory_space=pltpu.HBM)
    own = [hbm(x[0]) for x in (cache_k, cache_v, k_proj, v_proj)]
    chunk = pack(own)
    far = [[ring(chunk, s) for s in shifts]]

    owners = lax.rem(rank - jnp.arange(shards, dtype=jnp.int32) + shards, shards)
    positions = start[0] + owners[:, None] * tokens + jnp.arange(tokens, dtype=jnp.int32)[None]
    lane = jnp.arange(HD, dtype=jnp.int32)
    freqs = jnp.exp(
        -(2.0 * (lane % (HD // 2)).astype(F32) / HD) * jnp.log(jnp.float32(1000000.0))
    )
    angles = positions.reshape(-1).astype(F32)[:, None] * freqs[None, :]
    cosine = jnp.cos(angles)
    sine = jnp.sin(angles) * jnp.where(lane < HD // 2, -1.0, 1.0).astype(F32)[None]

    *prepared, ck, cv, kp, vp, chunk = prep(
        hbm(q_proj[0]), hbm(dout[0]), hbm(bias_q.reshape(HQ, HD)),
        hbm(bias_k.reshape(KV, HD)), hbm(bias_v.reshape(KV, HD)), cosine, sine, own,
    )
    far.append([ring(chunk, s) for s in shifts])
    qst, dot_t, bias = prepared[1], prepared[3], prepared[4]
    ahead = [
        look_ahead(
            g, shards, start, rank.reshape(1), qst, dot_t, bias, cosine, sine, ck, cv, kp, vp
        )
        for g in range(KV)
    ]
    before, owns = None, []
    for g in range(KV):
        before, own, more = attend(
            g, shards, start, rank.reshape(1), prepared, cosine, sine, ck, cv, kp, vp,
            far[g], ahead, before,
        )
        if g == KV - 2:
            out, gq = before[:2]
        owns.append(own)
        far += [[ring(chunk, s) for s in shifts] for chunk in more]
    *columns, sums, send = before
    backs = [earlier(x, s) for s, x in zip(shifts, send)]
    sums = sum_but_last(sums, ("dp", "seq"), shards)
    out, gq, gk, gv = finish(shards, cosine, sine, owns, backs, columns, out, gq)
    sums = last_sums(sums, hbm(gk))
    return (out[None], gq[None], gk[None], gv[None], *[x.reshape(-1) for x in sums])


def solution(mesh):
    split = P("dp", "seq", None)
    return jax.shard_map(
        body,
        mesh=mesh,
        in_specs=(split,) * 5 + (P(), P(), P(), P("dp"), split),
        out_specs=(split,) * 4 + (P(), P(), P()),
        check_vma=False,
    )
```
